32 devices in a mesh: dp: 8 (over y, x, core), ctx: 4 (over z).
Axes of the slice: x: 2, y: 2, z: 4, core: 2. Of those that a mesh axis runs over, the one named last changes fastest.
Arguments:
- hidden_in: float32 [8, 512, 768], P('dp', 'ctx'), may hold values from -6 to 6
- segments: int32 [8, 512], P('dp'), may hold values from 0 to 2, as said below
- out_grad: float32 [8, 512, 768], P('dp', 'ctx'), may hold values from -6 to 6
- weights: float32 [2, 3, 768, 3072], P(None, None, 'dp', 'ctx')
- vectors: float32 [2, 12, 768], P(None, 'ctx', 'dp')
- mat_momentum: float32 [2, 3, 768, 3072], P(None, None, 'dp', 'ctx'), may hold values from -192 to 192
- vec_first: float32 [2, 12, 768], P(None, 'ctx', 'dp'), may hold values from -40 to 40
- vec_second: float32 [2, 12, 768], P(None, 'ctx', 'dp'), may hold values from 2.048 to 16.384
Outputs:
- hidden_out: float32 [8, 512, 768], P('dp', 'ctx')
- input_grad: float32 [8, 512, 768], P('dp', 'ctx')
- mat_grad: float32 [2, 3, 768, 3072], P(None, None, 'dp', 'ctx')
- mat_momentum_new: float32 [2, 3, 768, 3072], P(None, None, 'dp', 'ctx')
- weights_new: float32 [2, 3, 768, 3072], P(None, None, 'dp', 'ctx')
- vec_grad: float32 [2, 12, 768], P(None, 'ctx', 'dp')
- vec_second_new: float32 [2, 12, 768], P(None, 'ctx', 'dp')
- vectors_new: float32 [2, 12, 768], P(None, 'ctx', 'dp')
The draws below stay inside these ranges and needn't reach their ends.
Inputs may be any that keep to these rules, and one draw needn't show every extreme that they name: `segments`: each row is nondecreasing and holds three documents 0, 1, 2; documents 0 and 2 each have 1 to 64 tokens, document 1 the rest.
All inputs are finite; a program needn't handle non-finite values.
Results may differ from the reference program's by a relative error of at most 0.014.
Values may be sent and summed in bfloat16 or wider, within the bound.
No kernel may reach another device: no remote copies, remote signals or barrier semaphores. Data moves between devices by JAX's collectives and lax.ppermute only.
A program may use at most 192 MiB of HBM per device.

```python
import math
from functools import partial
import jax
import jax.numpy as jnp
from jax import lax

D = 768
HEADS = 12
HEAD = 64
FF = 3072
LAYERS = 2
NS_ITERS = 2
ADAM_STEP = 10
TOK_DEV = 128
SEQ = 512
SEQS = 8
TOKENS = 4096


def draw_segments(key, part):
    key = jax.random.fold_in(key, 11)
    first_key, second_key = jax.random.split(key)
    first_cut = jax.random.randint(first_key, (SEQS, 1), 1, TOK_DEV // 2 + 1)
    second_cut = jax.random.randint(second_key, (SEQS, 1), SEQ - TOK_DEV // 2, SEQ)
    position = jnp.arange(SEQ)[None, :]
    return (position >= first_cut).astype(jnp.int32) + (position >= second_cut).astype(jnp.int32)


def draw_weights(key, part):
    key = jax.random.fold_in(key, 5)
    standard = jax.random.normal(key, (LAYERS, 3, D, FF), jnp.float32)
    column = jnp.arange(FF)
    attention_scale = jnp.where(column < 3 * D, D ** (-0.5), (D // 16) ** (-0.5))
    pack_scale = jnp.stack([attention_scale, jnp.full((FF,), D ** (-0.5)), jnp.full((FF,), FF ** (-0.5))])
    return standard * pack_scale[None, :, None, :]


def draw_vectors(key, part):
    key = jax.random.fold_in(key, 7)
    gain_key, bias_key = jax.random.split(key)
    gain_draw = jax.random.uniform(gain_key, (LAYERS, 12, D), jnp.float32, 0.6, 1.4)
    biases = 0.3 * jax.random.normal(bias_key, (LAYERS, 12, D), jnp.float32)
    row_index = jnp.arange(12)
    gain_rows = (row_index == 0) | (row_index == 2)
    return jnp.where(gain_rows[None, :, None], gain_draw, biases)


def block_levels(key, shape, cuts, least, top_value):
    factor_of = 1.0
    for dim, shards_of in cuts:
        steps = jax.random.uniform(jax.random.fold_in(jax.random.fold_in(key, 6), dim), (shards_of,), jnp.float32, least / len(cuts), top_value / len(cuts))
        factor_of = factor_of * jnp.repeat(jnp.exp(steps), shape[dim] // shards_of).reshape((-1,) + (1,) * (len(shape) - 1 - dim))
    return factor_of


def noise(own_key, extent, scale, limit, shards=(), kind=jnp.bfloat16):
    gain = block_levels(own_key, extent, shards, -0.22, 0.18) if shards else 1.0
    array = jax.random.normal(own_key, extent, jnp.float32) * scale * gain
    return jnp.minimum(jnp.maximum(array, -limit), limit).astype(kind)


def setup_inputs(seed: int = 0) -> dict:
    key_list = jax.random.split(jax.random.key(seed), 9)
    hidden_in = noise(key_list[0], (SEQS, SEQ, D), 1.0, 6.0, ((0, 8), (1, 4)), jnp.float32)
    segments = draw_segments(jax.random.fold_in(key_list[8], 71), 0)
    out_grad = noise(key_list[2], (SEQS, SEQ, D), 1.0, 6.0, ((0, 8), (1, 4)), jnp.float32)
    weights = draw_weights(jax.random.fold_in(key_list[8], 71), 0)
    vectors = draw_vectors(jax.random.fold_in(key_list[8], 71), 0)
    mat_momentum = noise(key_list[5], (LAYERS, 3, D, FF), (0.5 * TOKENS ** 0.5), 192.0, ((2, 8), (3, 4)), jnp.float32)
    vec_first = noise(key_list[6], (LAYERS, 12, D), (0.1 * TOKENS ** 0.5), 40.0, ((1, 4), (2, 8)), jnp.float32)
    vec_second = jnp.clip(jnp.exp(math.log(16.384) - 2.0794415 * jax.random.uniform(key_list[7], (LAYERS, 12, D), jnp.float32) ** block_levels(key_list[7], (LAYERS, 12, D), ((1, 4), (2, 8)), -0.2, 0.2)), 2.048, 16.384)
    return dict(hidden_in=hidden_in, segments=segments, out_grad=out_grad, weights=weights, vectors=vectors, mat_momentum=mat_momentum, vec_first=vec_first, vec_second=vec_second)


@jax.custom_vjp
def low(v):
    return lax.optimization_barrier(v.astype(jnp.bfloat16)).astype(jnp.float32)

@jax.custom_vjp
def low_back(v):
    return v

def low_keep(v):
    return (low(v), None)

def low_pass(kept, grad):
    return (grad,)

def back_keep(v):
    return (v, None)

def back_low(kept, grad):
    return (low(grad),)
low.defvjp(low_keep, low_pass)
low_back.defvjp(back_keep, back_low)
norm_epsilon = 1e-05
quintic_one = 3.4445
quintic_two = -4.775
quintic_three = 2.0315
momentum_decay = 0.95
matrix_rate = 0.6
matrix_decay = 0.01
first_decay = 0.9
second_decay = 0.999
vector_rate = 0.5
vector_decay = 0.01
adam_epsilon = 1e-08
masked_score = -1e+30

def layer_norm(hidden, gain_vec, bias_vec):
    center = hidden - lax.optimization_barrier(jnp.mean(hidden, axis=-1, keepdims=True))
    variance = lax.optimization_barrier(jnp.mean(center * center, axis=-1, keepdims=True))
    return center * lax.rsqrt(variance + norm_epsilon) * gain_vec + bias_vec

def smooth_unit(preact):
    return jax.nn.gelu(preact, approximate=True)

def matmul(operand, other):
    return jnp.dot(operand, other, precision=lax.Precision.HIGHEST)

def forward_layer(hidden, weight_pack, vector_pack, segment):
    length_seq = hidden.shape[0]
    attention_pack = weight_pack[0]
    head_shape = (length_seq, HEADS, HEAD)
    normed = low(layer_norm(hidden, vector_pack[0], vector_pack[1]))
    queries = low(low_back(matmul(normed, attention_pack[:, 0:D]) + vector_pack[4]))
    keys_proj = low(low_back(matmul(normed, attention_pack[:, D:2 * D])))
    values_proj = low(low_back(matmul(normed, attention_pack[:, 2 * D:3 * D]) + vector_pack[5]))
    scores = jnp.einsum('qhd,khd->hqk', queries.reshape(head_shape), keys_proj.reshape(head_shape), precision=lax.Precision.HIGHEST) * HEAD ** (-0.5)
    scores = low_back(scores)
    positions = jnp.arange(length_seq)
    allowed = (positions[None, :] <= positions[:, None]) & (segment[None, :] == segment[:, None])
    masked = jnp.where(allowed[None], scores, masked_score)
    row_max = lax.optimization_barrier(jnp.max(masked, axis=-1, keepdims=True))
    unnormed = jnp.exp(masked - row_max)
    probability = low(unnormed / lax.optimization_barrier(jnp.sum(unnormed, axis=-1, keepdims=True)))
    attended = jnp.einsum('hqk,khd->qhd', probability, values_proj.reshape(head_shape), precision=lax.Precision.HIGHEST).reshape(length_seq, D)
    attended = low(low_back(attended))
    branch_one = low_back(matmul(attended, attention_pack[:, 3 * D:4 * D]) + vector_pack[6])
    middle = hidden + branch_one
    normed_two = low(layer_norm(middle, vector_pack[2], vector_pack[3]))
    preact = low_back(matmul(normed_two, weight_pack[1]) + vector_pack[8:12].reshape(FF))
    activated = low(smooth_unit(preact))
    branch_two = low_back(jnp.dot(activated, weight_pack[2].T, precision=lax.Precision.HIGHEST) + vector_pack[7])
    return middle + branch_two

def forward_all(segments, hidden_all, weight_all, vector_all):
    weight_low = low(weight_all)
    vector_low = low(vector_all)

    def one_sequence(carry, inputs):
        hidden, segment = inputs
        for layer_index in range(LAYERS):
            hidden = forward_layer(hidden, weight_low[layer_index], vector_low[layer_index], segment)
        return (carry, hidden)
    unused, outputs = lax.scan(jax.checkpoint(one_sequence), jnp.zeros((), jnp.float32), (hidden_all, segments))
    return outputs

def orthogonalize(update):
    current = low(update)
    for iteration in range(NS_ITERS):
        gram_matrix = jnp.dot(current, current.T, precision=lax.Precision.HIGHEST)
        if iteration == 0:
            norm_scale = 1.0 / (jnp.sqrt(jnp.trace(gram_matrix)) + 1e-07)
        else:
            norm_scale = 1.0
        poly_base = gram_matrix * (norm_scale * norm_scale)
        base_low = low(poly_base)
        bmat_low = low(quintic_two * poly_base + quintic_three * matmul(base_low, base_low))
        current = low(norm_scale * (quintic_one * current + matmul(bmat_low, current)))
    return current

def reference(hidden_in, segments, out_grad, weights, vectors, mat_momentum, vec_first, vec_second):
    hidden_out, pullback = jax.vjp(partial(forward_all, segments), hidden_in, weights, vectors)
    input_grad, mat_grad, vec_grad = pullback(out_grad)
    moment_new = momentum_decay * mat_momentum + mat_grad
    update_in = mat_grad + momentum_decay * moment_new
    new_blocks = []
    for layer_index in range(LAYERS):
        attention_pack = update_in[layer_index, 0]
        squares = [orthogonalize(attention_pack[:, column_block * D:(column_block + 1) * D]) * (0.2 * math.sqrt(D)) for column_block in range(4)]
        pack_list = [jnp.concatenate(squares, axis=1), orthogonalize(update_in[layer_index, 1]) * (0.2 * math.sqrt(FF)), orthogonalize(update_in[layer_index, 2]) * (0.2 * math.sqrt(FF))]
        new_blocks.append(jnp.stack(pack_list))
    ortho_all = jnp.stack(new_blocks)
    weights_new = weights * (1.0 - matrix_rate * matrix_decay) - matrix_rate * ortho_all
    first_new = first_decay * vec_first + (1.0 - first_decay) * vec_grad
    second_new = second_decay * vec_second + (1.0 - second_decay) * vec_grad * vec_grad
    first_hat = first_new / (1.0 - first_decay ** ADAM_STEP)
    second_hat = second_new / (1.0 - second_decay ** ADAM_STEP)
    vectors_new = vectors * (1.0 - vector_rate * vector_decay) - vector_rate * first_hat / (jnp.sqrt(second_hat) + adam_epsilon)
    return (hidden_out, input_grad, mat_grad, moment_new, weights_new, vec_grad, second_new, vectors_new)
```

```python
import math

import jax
import jax.numpy as jnp
from jax import lax
from jax.sharding import Mesh, PartitionSpec as P

D = 768
HEADS = 12
HEAD = 64
FF = 3072
LAYERS = 2
ADAM_STEP = 10
TP = 4
COLS = D // TP
TP_HEADS = HEADS // TP

norm_epsilon = 1e-05
quintic_one = 3.4445
quintic_two = -4.775
quintic_three = 2.0315
momentum_decay = 0.95
matrix_rate = 0.6
matrix_decay = 0.01
first_decay = 0.9
second_decay = 0.999
vector_rate = 0.5
vector_decay = 0.01
adam_epsilon = 1e-08
masked_score = -1e30

GROUP = ("jx", "jc")
REPLICAS = ("g", "ctx")
DP = ("g", "jx", "jc")
EVERY = ("g", "jx", "jc", "ctx")
SWAP = [(0, 1), (1, 0)]
bf16 = jnp.bfloat16
f32 = jnp.float32


def layer_norm(hidden, gain_vec, bias_vec):
    center = hidden - jnp.mean(hidden, axis=-1, keepdims=True)
    variance = jnp.mean(center * center, axis=-1, keepdims=True)
    return center * lax.rsqrt(variance + norm_epsilon) * gain_vec + bias_vec


def smooth_unit(preact):
    return jax.nn.gelu(preact, approximate=True)


def dot(operand, other):
    return jnp.dot(operand, other, preferred_element_type=f32)


def dot_tokens(operand, other):
    return lax.dot_general(operand, other, (((0,), (0,)), ((), ())), preferred_element_type=f32)


def dot_trans(operand, other):
    return lax.dot_general(operand, other, (((1,), (1,)), ((), ())), preferred_element_type=f32)


def bdot(operand, other, left, right):
    return lax.dot_general(
        operand, other, (((left,), (right,)), ((0,), (0,))), preferred_element_type=f32
    )


def heads_of(matrix):
    return matrix.reshape(matrix.shape[0], TP_HEADS, HEAD).transpose(1, 0, 2)


def merge_heads(stack):
    return stack.transpose(1, 0, 2).reshape(stack.shape[1], TP_HEADS * HEAD)


def core_gather(rows):
    return jnp.concatenate([rows, lax.ppermute(rows, "jc", SWAP)], axis=0)


def group_sum(partial):
    half = partial.shape[0] // 2
    mine = partial[:half] + lax.ppermute(partial[half:].astype(bf16), "jc", SWAP).astype(f32)
    return mine + lax.ppermute(mine.astype(bf16), "jx", SWAP).astype(f32)


def to_group(mats):
    count, rows, width = mats.shape
    split = mats.reshape(count, rows, TP, width // TP)
    return lax.all_to_all(split, GROUP, split_axis=2, concat_axis=1, tiled=True)[:, :, 0]


def from_group(mats):
    count, rows, width = mats.shape
    split = mats.reshape(count, TP, rows // TP, width)
    return lax.all_to_all(split, GROUP, split_axis=1, concat_axis=3, tiled=True)[:, 0]


def gather_mats(mats):
    parts = lax.all_gather(mats, REPLICAS, axis=0, tiled=False)
    groups = lax.axis_size("g")
    parts = parts.reshape(groups, -1, *mats.shape)
    return [
        parts[:, :, item].transpose(0, 2, 1, 3).reshape(D, -1) for item in range(mats.shape[0])
    ]


def scatter_mats(mats):
    groups = lax.axis_size("g")
    stack = jnp.stack([mat.astype(bf16) for mat in mats])
    count, rows, blocks, width = stack.shape
    stack = stack.reshape(count, groups, rows // groups, blocks, width).transpose(1, 3, 0, 2, 4)
    stack = stack.reshape(groups * blocks, count, rows // groups, width)
    return lax.psum_scatter(stack, REPLICAS, scatter_dimension=0, tiled=True)[0]


def local(hidden_in, segments, out_grad, weights, vectors, mat_momentum, vec_first, vec_second):
    tokens_dev = hidden_in.shape[1]
    seq_len = segments.shape[1]
    half = 2 * tokens_dev
    dp_rows = weights.shape[2]
    ctx_size = lax.axis_size("ctx")
    x_index = lax.axis_index("jx")
    c_index = lax.axis_index("jc")
    t_index = 2 * x_index + c_index
    z_index = lax.axis_index("ctx")
    dp_index = lax.axis_index(DP)
    dp_size = lax.axis_size(DP)

    to_seq = []
    for t in range(TP):
        for z in range(ctx_size):
            to_seq.append((t * ctx_size + z, ((z % 2) * 2 + z // 2) * ctx_size + t))
    from_seq = [(b, a) for a, b in to_seq]
    axes = ("jx", "jc", "ctx")

    def x_join(block):
        other = lax.ppermute(block, "jx", SWAP)
        first = jnp.where(x_index == 0, block, other)
        second = jnp.where(x_index == 0, other, block)
        return jnp.concatenate([first, second], axis=0)

    seg_row = jnp.pad(segments.astype(f32), ((0, 7), (0, D - seq_len)))
    moved = lax.ppermute(jnp.concatenate([hidden_in[0], seg_row], axis=0), axes, to_seq)
    hidden = x_join(moved[:tokens_dev])
    segment_row = moved[tokens_dev, :seq_len]
    vec_parts = lax.all_gather(vectors.astype(bf16), EVERY, axis=0, tiled=False)
    vec_rows = (
        vec_parts.reshape(dp_size, ctx_size, LAYERS, vectors.shape[1], vectors.shape[2])
        .transpose(2, 1, 3, 0, 4)
        .reshape(LAYERS, 12, D)
        .astype(f32)
    )
    low = weights.astype(bf16)
    swapped = [
        [to_group(low[layer, 0:1]), to_group(low[layer, 1:3])] for layer in range(LAYERS)
    ]
    grad_hidden = x_join(lax.ppermute(out_grad[0], axes, to_seq))

    order = [c_index * half, (1 - c_index) * half]
    pos = jnp.concatenate([start + jnp.arange(half) for start in order])
    seg = jnp.concatenate([lax.dynamic_slice_in_dim(segment_row, start, half) for start in order])
    allowed = (pos[None, :] <= pos[:, None]) & (seg[None, :] == seg[:, None])

    def mine(row):
        return lax.dynamic_slice_in_dim(row, t_index * COLS, COLS, axis=-1)

    def scores_of(q, k):
        return jnp.where(allowed[None], bdot(q, k, 2, 2) * HEAD ** (-0.5), masked_score)

    stored = []
    for layer in range(LAYERS):
        vec = vec_rows[layer]
        (attn_w,) = gather_mats(swapped[layer][0])
        w_up, w_down = gather_mats(swapped[layer][1])
        w_qkv = attn_w[:, : 3 * COLS]
        w_o = lax.all_to_all(
            attn_w[:, 3 * COLS :].reshape(TP, COLS, COLS),
            GROUP,
            split_axis=0,
            concat_axis=2,
            tiled=True,
        )[0]
        a_all = core_gather(layer_norm(hidden, vec[0], vec[1]).astype(bf16))
        proj = dot(a_all, w_qkv)
        q = heads_of((proj[:, :COLS] + mine(vec[4])).astype(bf16))
        k = heads_of(proj[:, COLS : 2 * COLS].astype(bf16))
        v = heads_of((proj[:, 2 * COLS :] + mine(vec[5])).astype(bf16))
        scores = scores_of(q, k)
        row_max = jnp.max(scores, axis=-1, keepdims=True)
        unnormed = jnp.exp(scores - row_max)
        total = jnp.sum(unnormed, axis=-1, keepdims=True)
        prob = (unnormed / total).astype(bf16)
        log_total = row_max + jnp.log(total)
        o = merge_heads(bdot(prob, v, 2, 1)).astype(bf16)
        middle = hidden + (group_sum(dot(o, w_o)) + vec[6])
        c_all = core_gather(layer_norm(middle, vec[2], vec[3]).astype(bf16))
        preact = dot(c_all, w_up) + mine(vec[8:12]).reshape(-1)
        act = smooth_unit(preact).astype(bf16)
        stored.append(
            (hidden, middle, a_all, q, k, v, log_total, o, c_all, preact, act, w_qkv, w_o, w_up, w_down)
        )
        hidden = middle + (group_sum(dot_trans(act, w_down)) + vec[7])

    def send_back(rows):
        block = lax.dynamic_slice_in_dim(rows, x_index * tokens_dev, tokens_dev, axis=0)
        return lax.ppermute(block, axes, from_seq)

    hidden_out = send_back(hidden)

    once = jnp.where(x_index == 0, 1.0, 0.0).astype(f32)
    mat_list = [None] * LAYERS
    vec_list = [None] * LAYERS
    for layer in reversed(range(LAYERS)):
        (h_in, middle, a_all, q, k, v, log_total, o, c_all, preact, act, w_qkv, w_o, w_up, w_down) = stored[
            layer
        ]
        vec = vec_rows[layer]
        gy = grad_hidden.astype(bf16)
        gy_all = core_gather(gy)
        gu = dot(gy_all, w_down)
        unused, gelu_pull = jax.vjp(smooth_unit, preact)
        gz = gelu_pull(gu)[0].astype(bf16)
        gc = group_sum(dot_trans(gz, w_up))
        unused, pull_two = jax.vjp(layer_norm, middle, vec[2], vec[3])
        g_mid, g_gain_two, g_shift_two = pull_two(gc)
        gm = grad_hidden + g_mid
        gb = gm.astype(bf16)
        gb_all = core_gather(gb)
        go = heads_of(dot_trans(gb_all, w_o).astype(bf16))
        prob = jnp.exp(scores_of(q, k) - log_total)
        prob_low = prob.astype(bf16)
        g_prob = bdot(go, v, 2, 2)
        row_dot = jnp.sum(g_prob * prob, axis=-1, keepdims=True)
        g_scores = (prob * (g_prob - row_dot)).astype(bf16)
        gq = merge_heads(bdot(g_scores, k, 2, 1) * HEAD ** (-0.5)).astype(bf16)
        gk = merge_heads(bdot(g_scores, q, 1, 1) * HEAD ** (-0.5)).astype(bf16)
        gv = merge_heads(bdot(prob_low, go, 1, 1)).astype(bf16)
        g_qkv = jnp.concatenate([gq, gk, gv], axis=1)
        ga = group_sum(dot_trans(g_qkv, w_qkv))
        unused, pull_one = jax.vjp(layer_norm, h_in, vec[0], vec[1])
        g_in, g_gain_one, g_shift_one = pull_one(ga)
        grad_hidden = gm + g_in

        mlp = [
            dot_tokens(c_all, gz).reshape(D, ctx_size, COLS),
            dot_tokens(gy_all, act).reshape(D, ctx_size, COLS),
        ]
        mlp_part = scatter_mats(mlp)
        g_wo = lax.all_to_all(
            dot_tokens(o, gb_all).astype(bf16).reshape(COLS, TP, COLS),
            GROUP,
            split_axis=1,
            concat_axis=0,
            tiled=True,
        )
        g_attn = jnp.concatenate(
            [dot_tokens(a_all, g_qkv).astype(bf16).reshape(D, 3, COLS), g_wo], axis=1
        )
        attn_part = scatter_mats([g_attn])
        mat_list[layer] = from_group(jnp.concatenate([attn_part, mlp_part], axis=0)).astype(f32)

        def place(values):
            wide = jnp.zeros(values.shape[:-1] + (D,), f32)
            return lax.dynamic_update_slice_in_dim(wide, values, t_index * COLS, axis=-1)

        def token_sum(values):
            return jnp.sum(values, axis=0, dtype=f32)

        b_qv = place(jnp.stack([token_sum(gq), token_sum(gv)]))
        b_up = place(token_sum(gz).reshape(ctx_size, COLS))
        shared = once * jnp.stack(
            [g_gain_one, g_shift_one, g_gain_two, g_shift_two, token_sum(gb), token_sum(gy)]
        )
        vec_term = jnp.concatenate([shared[:4], b_qv, shared[4:], b_up], axis=0)
        vec_sum = lax.psum(vec_term, EVERY)
        vec_list[layer] = lax.dynamic_slice(
            vec_sum,
            (z_index * vectors.shape[1], dp_index * vectors.shape[2]),
            (vectors.shape[1], vectors.shape[2]),
        )
    input_grad = send_back(grad_hidden)

    grad_mats = jnp.stack(mat_list)
    grad_vecs = jnp.stack(vec_list)
    moment_new = momentum_decay * mat_momentum + grad_mats
    update_in = grad_mats + momentum_decay * moment_new
    item_count = 3 * LAYERS
    cols_dev = update_in.shape[3]
    items = update_in.astype(bf16).reshape(item_count, dp_rows, cols_dev)
    copies = -(-dp_size // item_count)
    slots = jnp.tile(items, (copies, 1, 1))[0:dp_size]
    received = lax.all_to_all(slots[:, None], DP, split_axis=0, concat_axis=1, tiled=True)
    current = received.reshape(dp_size * dp_rows, cols_dev)
    square = (dp_index % item_count) % 3 == 0
    gram_local = dot_trans(current, current)
    gram_part = lax.psum_scatter(gram_local.astype(bf16), "ctx", scatter_dimension=0, tiled=True)
    gram_total = lax.all_gather(gram_part, "ctx", axis=0, tiled=True).astype(f32)
    gram = jnp.where(square, gram_local, gram_total)
    scale = 1.0 / (jnp.sqrt(jnp.trace(gram)) + 1e-07)
    base = gram * (scale * scale)
    base_low = base.astype(bf16)
    bmat = (quintic_two * base + quintic_three * dot(base_low, base_low)).astype(bf16)
    current = (scale * (quintic_one * current.astype(f32) + dot(bmat, current))).astype(bf16)

    def two_part(left, right):
        high = right.astype(bf16)
        rest = (right - high.astype(f32)).astype(bf16)
        return dot(left, high) + dot(left, rest)

    turned = two_part(bmat, base)
    base = (
        quintic_one * quintic_one * base
        + quintic_one * (turned + turned.T)
        + two_part(bmat, turned.T)
    )
    base_low = base.astype(bf16)
    bmat = (quintic_two * base + quintic_three * dot(base_low, base_low)).astype(bf16)
    current = (quintic_one * current.astype(f32) + dot(bmat, current)).astype(bf16)
    returned = lax.all_to_all(
        current.reshape(dp_size, 1, dp_rows, cols_dev), DP, split_axis=0, concat_axis=1, tiled=True
    )[0]
    spread = dp_size // item_count
    chosen = [
        lax.dynamic_index_in_dim(
            returned, item + item_count * (dp_index % spread), 0, keepdims=False
        )
        for item in range(item_count)
    ]
    ortho = jnp.stack(chosen).reshape(LAYERS, 3, dp_rows, cols_dev).astype(f32)
    factor = jnp.array([0.2 * math.sqrt(D), 0.2 * math.sqrt(FF), 0.2 * math.sqrt(FF)], f32)
    weights_new = weights * (1.0 - matrix_rate * matrix_decay) - matrix_rate * (
        ortho * factor[None, :, None, None]
    )
    first_new = first_decay * vec_first + (1.0 - first_decay) * grad_vecs
    second_new = second_decay * vec_second + (1.0 - second_decay) * grad_vecs * grad_vecs
    first_hat = first_new / (1.0 - first_decay**ADAM_STEP)
    second_hat = second_new / (1.0 - second_decay**ADAM_STEP)
    vectors_new = vectors * (1.0 - vector_rate * vector_decay) - vector_rate * first_hat / (
        jnp.sqrt(second_hat) + adam_epsilon
    )
    return (
        hidden_out[None],
        input_grad[None],
        grad_mats,
        moment_new,
        weights_new,
        grad_vecs,
        second_new,
        vectors_new,
    )


def solution(mesh):
    dp, ctx = mesh.shape["dp"], mesh.shape["ctx"]
    fine = Mesh(mesh.devices.reshape(dp // TP, 2, 2, ctx), EVERY)
    tokens = P(DP, "ctx", None)
    mats = P(None, None, DP, "ctx")
    vecs = P(None, "ctx", DP)
    return jax.shard_map(
        local,
        mesh=fine,
        in_specs=(tokens, P(DP, None), tokens, mats, vecs, mats, vecs, vecs),
        out_specs=(tokens, tokens, mats, mats, mats, vecs, vecs, vecs),
        check_vma=False,
    )
```

```python
import math

import jax
import jax.numpy as jnp
from jax import lax
from jax.sharding import Mesh, PartitionSpec as P

D = 768
HEADS = 12
HEAD = 64
FF = 3072
LAYERS = 2
ADAM_STEP = 10
TP = 4
COLS = D // TP
TP_HEADS = HEADS // TP

norm_epsilon = 1e-05
quintic_one = 3.4445
quintic_two = -4.775
quintic_three = 2.0315
momentum_decay = 0.95
matrix_rate = 0.6
matrix_decay = 0.01
first_decay = 0.9
second_decay = 0.999
vector_rate = 0.5
vector_decay = 0.01
adam_epsilon = 1e-08
masked_score = -1e30

GROUP = ("jx", "jc")
REPLICAS = ("g", "ctx")
DP = ("g", "jx", "jc")
EVERY = ("g", "jx", "jc", "ctx")
SWAP = [(0, 1), (1, 0)]
bf16 = jnp.bfloat16
f32 = jnp.float32


def layer_norm(hidden, gain_vec, bias_vec):
    center = hidden - jnp.mean(hidden, axis=-1, keepdims=True)
    variance = jnp.mean(center * center, axis=-1, keepdims=True)
    return center * lax.rsqrt(variance + norm_epsilon) * gain_vec + bias_vec


def smooth_unit(preact):
    return jax.nn.gelu(preact, approximate=True)


def dot(operand, other):
    return jnp.dot(operand, other, preferred_element_type=f32)


def dot_tokens(operand, other):
    return lax.dot_general(operand, other, (((0,), (0,)), ((), ())), preferred_element_type=f32)


def dot_trans(operand, other):
    return lax.dot_general(operand, other, (((1,), (1,)), ((), ())), preferred_element_type=f32)


def bdot(operand, other, left, right):
    return lax.dot_general(
        operand, other, (((left,), (right,)), ((0,), (0,))), preferred_element_type=f32
    )


def heads_of(matrix):
    return matrix.reshape(matrix.shape[0], TP_HEADS, HEAD).transpose(1, 0, 2)


def merge_heads(stack):
    return stack.transpose(1, 0, 2).reshape(stack.shape[1], TP_HEADS * HEAD)


def core_gather(rows):
    return jnp.concatenate([rows, lax.ppermute(rows, "jc", SWAP)], axis=0)


def group_sum(partial):
    half = partial.shape[0] // 2
    mine = partial[:half] + lax.ppermute(partial[half:].astype(bf16), "jc", SWAP).astype(f32)
    return mine + lax.ppermute(mine.astype(bf16), "jx", SWAP).astype(f32)


def to_group(mats):
    count, rows, width = mats.shape
    split = mats.reshape(count, rows, TP, width // TP)
    return lax.all_to_all(split, GROUP, split_axis=2, concat_axis=1, tiled=True)[:, :, 0]


def from_group(mats):
    count, rows, width = mats.shape
    split = mats.reshape(count, TP, rows // TP, width)
    return lax.all_to_all(split, GROUP, split_axis=1, concat_axis=3, tiled=True)[:, 0]


def rotate(block, axis, step):
    size = lax.axis_size(axis)
    return lax.ppermute(block, axis, [((i + step) % size, i) for i in range(size)])


def pair_join(block, axis, dim):
    other = lax.ppermute(block, axis, SWAP)
    first = lax.axis_index(axis) == 0
    return jnp.concatenate(
        [jnp.where(first, block, other), jnp.where(first, other, block)], axis=dim
    )


def from_own(stack):
    double = jnp.concatenate([stack, stack], axis=0)
    return lax.dynamic_slice_in_dim(double, lax.axis_index("ctx"), stack.shape[0], axis=0)


def to_absolute(stack):
    count = stack.shape[0]
    double = jnp.concatenate([stack, stack], axis=0)
    return lax.dynamic_slice_in_dim(double, count - lax.axis_index("ctx"), count, axis=0)


def out_moves():
    last = lax.axis_size("ctx") - 1
    size = last + 1
    moves = []
    for y in range(2):
        for x in range(2):
            for core in range(2):
                moves.append(
                    ((4 * y + 2 * x + core) * size + last, (4 * core + 2 * y + x) * size + last)
                )
    return moves


def attn_piece(mat, piece):
    half = mat.shape[1] // 2
    core = lax.axis_index("jc")
    mine = lax.dynamic_slice_in_dim(mat, core * half, half, axis=1)
    give = lax.dynamic_slice_in_dim(mat, (1 - core) * half, half, axis=1)
    got = lax.ppermute(give, "jc", SWAP)
    rows = jnp.concatenate(
        [jnp.where(core == 0, mine, got), jnp.where(core == 0, got, mine)], axis=0
    )
    rows = lax.ppermute(rows, EVERY, out_moves())
    return jnp.where(lax.axis_index("ctx") == lax.axis_size("ctx") - 1, rows, piece)


def out_back(piece):
    core = lax.axis_index("jc")
    rows = lax.ppermute(piece, EVERY, [(b, a) for a, b in out_moves()])
    half = rows.shape[0] // 2
    mine = lax.dynamic_slice_in_dim(rows, core * half, half, axis=0)
    give = lax.dynamic_slice_in_dim(rows, (1 - core) * half, half, axis=0)
    got = lax.ppermute(give, "jc", SWAP)
    return jnp.concatenate(
        [jnp.where(core == 0, mine, got), jnp.where(core == 0, got, mine)], axis=1
    )


def gather_weights(low):
    if lax.axis_size("g") != 2:
        return gather_weights_wide(low)
    layers = low.shape[0]
    first = to_group(low[0, 0:1])
    rest = to_group(jnp.concatenate([low[0, 1:3], low[1:].reshape(-1, *low.shape[2:])]))
    pieces = [attn_piece(low[0, 0], first[0].T), jnp.swapaxes(rest[0:2], 1, 2)]
    for layer in range(1, layers):
        base = 3 * layer - 1
        pieces.append(attn_piece(low[layer, 0], rest[base].T))
        pieces.append(jnp.swapaxes(rest[base + 1 : base + 3], 1, 2))
    full = []
    for number, piece in enumerate(pieces):
        if number:
            piece, full[-1][1:] = lax.optimization_barrier((piece, full[-1][1:]))
        full.append([piece] + [rotate(piece, "ctx", step) for step in range(1, 4)])
    result = []
    for layer in range(layers):
        attn, mlp = [
            jnp.stack([pair_join(block, "g", block.ndim - 1) for block in blocks])
            for blocks in full[2 * layer : 2 * layer + 2]
        ]
        result.append((to_absolute(attn), mlp[:, 0].reshape(D, D), mlp[:, 1].reshape(D, D)))
    return result


def gather_weights_wide(low):
    result = []
    for layer in range(low.shape[0]):
        mats = to_group(low[layer])
        parts = lax.all_gather(mats, REPLICAS, axis=0, tiled=False)
        parts = parts.reshape(lax.axis_size("g"), -1, *mats.shape)
        full = [parts[:, :, item].transpose(1, 3, 0, 2).reshape(D, D) for item in range(3)]
        w_o = lax.all_to_all(
            full[0][3 * COLS :].T.reshape(TP, COLS, COLS),
            GROUP,
            split_axis=0,
            concat_axis=2,
            tiled=True,
        )
        attn = jnp.concatenate([full[0][: 3 * COLS].reshape(3, COLS, D), w_o], axis=0)
        result.append((attn, full[1], full[2]))
    return result


def replica_sum(blocks, ahead):
    half = D // 2
    group = lax.axis_index("g")
    last = blocks.ndim - 1
    mine = lax.dynamic_slice_in_dim(blocks, group * half, half, axis=last)
    give = lax.dynamic_slice_in_dim(blocks, (1 - group) * half, half, axis=last)
    summed = mine.astype(f32) + lax.ppermute(give.astype(bf16), "g", SWAP).astype(f32)
    if not ahead:
        summed = from_own(summed)
    total = summed[0]
    for step in range(1, 4):
        total = total + rotate(summed[step].astype(bf16), "ctx", -step).astype(f32)
    return total


def scatter_attn(grads):
    if lax.axis_size("g") != 2:
        g_wo = lax.all_to_all(
            grads[3].reshape(COLS, TP, COLS), GROUP, split_axis=1, concat_axis=0, tiled=True
        )[:, 0]
        mats = jnp.concatenate([grads[:3], g_wo.T[None]], axis=0)
        return scatter_wide(mats[:, None])[0]
    part = replica_sum(grads, False).astype(bf16)
    columns = from_group(part.T[None])[0]
    last = lax.axis_index("ctx") == lax.axis_size("ctx") - 1
    return jnp.where(last, out_back(part), columns).astype(f32)


def scatter_mlp(grads):
    if lax.axis_size("g") != 2:
        return scatter_wide(grads)
    part = replica_sum(grads, True).astype(bf16)
    return from_group(jnp.swapaxes(part, 1, 2)).astype(f32)


def scatter_wide(mats):
    groups = lax.axis_size("g")
    blocks, count, width, depth = mats.shape
    stack = mats.astype(bf16).reshape(blocks, count, width, groups, depth // groups)
    stack = stack.transpose(3, 0, 1, 4, 2).reshape(groups * blocks, count, -1, width)
    part = lax.psum_scatter(stack, REPLICAS, scatter_dimension=0, tiled=True)[0]
    return from_group(part).astype(f32)


def gather_vectors(vectors):
    low = vectors.astype(bf16)
    low = pair_join(pair_join(low, "jc", 2), "jx", 2)
    if lax.axis_size("g") == 2:
        low = pair_join(low, "g", 2)
    else:
        low = lax.all_gather(low, "g", axis=2, tiled=True)
    stack = jnp.stack([low] + [rotate(low, "ctx", step) for step in range(1, 4)])
    return to_absolute(stack).transpose(1, 0, 2, 3).reshape(low.shape[0], -1, D).astype(f32)


def sum_vectors(terms):
    if lax.axis_size("g") == 2:
        terms = terms + lax.ppermute(terms, "g", SWAP)
    else:
        terms = lax.psum(terms, "g")
    layers, rows, width = terms.shape
    blocks = from_own(terms.reshape(layers, 4, rows // 4, width).transpose(1, 0, 2, 3))
    total = blocks[0]
    for step in range(1, 4):
        total = total + rotate(blocks[step], "ctx", -step)
    total = total + lax.ppermute(total, "jc", SWAP)
    return total + lax.ppermute(total, "jx", SWAP)


def local(hidden_in, segments, out_grad, weights, vectors, mat_momentum, vec_first, vec_second):
    tokens_dev = hidden_in.shape[1]
    seq_len = segments.shape[1]
    half = 2 * tokens_dev
    dp_rows = weights.shape[2]
    ctx_size = lax.axis_size("ctx")
    x_index = lax.axis_index("jx")
    c_index = lax.axis_index("jc")
    t_index = 2 * x_index + c_index
    z_index = lax.axis_index("ctx")
    dp_index = lax.axis_index(DP)
    dp_size = lax.axis_size(DP)

    to_seq = []
    for t in range(TP):
        for z in range(ctx_size):
            to_seq.append((t * ctx_size + z, ((z % 2) * 2 + z // 2) * ctx_size + t))
    from_seq = [(b, a) for a, b in to_seq]
    axes = ("jx", "jc", "ctx")

    def x_join(block):
        return pair_join(block, "jx", 0)

    seg_row = jnp.pad(segments.astype(f32), ((0, 7), (0, D - seq_len)))
    moved = lax.ppermute(jnp.concatenate([hidden_in[0], seg_row], axis=0), axes, to_seq)
    hidden = x_join(moved[:tokens_dev])
    segment_row = moved[tokens_dev, :seq_len]
    vec_rows = gather_vectors(vectors)
    gathered = gather_weights(weights.astype(bf16))
    grad_hidden = x_join(lax.ppermute(out_grad[0], axes, to_seq))
    relative = lax.axis_size("g") == 2

    order = [c_index * half, (1 - c_index) * half]
    pos = jnp.concatenate([start + jnp.arange(half) for start in order])
    seg = jnp.concatenate([lax.dynamic_slice_in_dim(segment_row, start, half) for start in order])
    allowed = (pos[None, :] <= pos[:, None]) & (seg[None, :] == seg[:, None])

    def mine(row):
        return lax.dynamic_slice_in_dim(row, t_index * COLS, COLS, axis=-1)

    def scores_of(q, k):
        return jnp.where(allowed[None], bdot(q, k, 2, 2) * HEAD ** (-0.5), masked_score)

    stored = []
    for layer in range(LAYERS):
        vec = [vec_rows[layer, row : row + 1] for row in range(8)]
        attn_w, w_up, w_down = gathered[layer]
        w_qkv = attn_w[:3].reshape(3 * COLS, D)
        w_o = attn_w[3]
        b_up = mine(vec_rows[layer, 8:12])
        b_up = (from_own(b_up) if relative else b_up).reshape(1, D)
        a_all = core_gather(layer_norm(hidden, vec[0], vec[1]).astype(bf16))
        proj = dot_trans(a_all, w_qkv)
        q = heads_of((proj[:, :COLS] + mine(vec[4])).astype(bf16))
        k = heads_of(proj[:, COLS : 2 * COLS].astype(bf16))
        v = heads_of((proj[:, 2 * COLS :] + mine(vec[5])).astype(bf16))
        scores = scores_of(q, k)
        row_max = jnp.max(scores, axis=-1, keepdims=True)
        unnormed = jnp.exp(scores - row_max)
        total = jnp.sum(unnormed, axis=-1, keepdims=True)
        prob = (unnormed / total).astype(bf16)
        log_total = row_max + jnp.log(total)
        o = merge_heads(bdot(prob, v, 2, 1)).astype(bf16)
        middle = hidden + (group_sum(dot(o, w_o)) + vec[6])
        c_all = core_gather(layer_norm(middle, vec[2], vec[3]).astype(bf16))
        preact = dot_trans(c_all, w_up) + b_up
        act = smooth_unit(preact).astype(bf16)
        stored.append(
            (hidden, middle, a_all, q, k, v, log_total, o, c_all, preact, act, w_qkv, w_o, w_up, w_down)
        )
        hidden = middle + (group_sum(dot(act, w_down)) + vec[7])

    def send_back(rows):
        block = lax.dynamic_slice_in_dim(rows, x_index * tokens_dev, tokens_dev, axis=0)
        return lax.ppermute(block, axes, from_seq)

    hidden_out = send_back(hidden)

    once = jnp.where(x_index == 0, 1.0, 0.0).astype(f32)
    mat_list = [None] * LAYERS
    vec_list = [None] * LAYERS
    for layer in reversed(range(LAYERS)):
        (h_in, middle, a_all, q, k, v, log_total, o, c_all, preact, act, w_qkv, w_o, w_up, w_down) = stored[
            layer
        ]
        vec = [vec_rows[layer, row : row + 1] for row in range(8)]
        gy = grad_hidden.astype(bf16)
        gy_all = core_gather(gy)
        gu = dot_trans(gy_all, w_down)
        unused, gelu_pull = jax.vjp(smooth_unit, preact)
        gz = gelu_pull(gu)[0].astype(bf16)
        gc = group_sum(dot(gz, w_up))
        unused, pull_two = jax.vjp(layer_norm, middle, vec[2], vec[3])
        g_mid, g_gain_two, g_shift_two = pull_two(gc)
        gm = grad_hidden + g_mid
        gb = gm.astype(bf16)
        gb_all = core_gather(gb)
        go = heads_of(dot_trans(gb_all, w_o).astype(bf16))
        prob = jnp.exp(scores_of(q, k) - log_total)
        prob_low = prob.astype(bf16)
        g_prob = bdot(go, v, 2, 2)
        row_dot = jnp.sum(g_prob * prob, axis=-1, keepdims=True)
        g_scores = (prob * (g_prob - row_dot)).astype(bf16)
        gq = merge_heads(bdot(g_scores, k, 2, 1) * HEAD ** (-0.5)).astype(bf16)
        gk = merge_heads(bdot(g_scores, q, 1, 1) * HEAD ** (-0.5)).astype(bf16)
        gv = merge_heads(bdot(prob_low, go, 1, 1)).astype(bf16)
        g_qkv = jnp.concatenate([gq, gk, gv], axis=1)
        ga = group_sum(dot(g_qkv, w_qkv))
        unused, pull_one = jax.vjp(layer_norm, h_in, vec[0], vec[1])
        g_in, g_gain_one, g_shift_one = pull_one(ga)
        grad_hidden = gm + g_in

        mlp_grad = scatter_mlp(
            jnp.stack(
                [
                    dot_tokens(gz, c_all).reshape(ctx_size, COLS, D),
                    dot_tokens(act, gy_all).reshape(ctx_size, COLS, D),
                ],
                axis=1,
            )
        )
        attn_grad = scatter_attn(
            jnp.concatenate([dot_tokens(g_qkv, a_all), dot_tokens(o, gb_all)]).reshape(4, COLS, D)
        )
        mat_list[layer] = jnp.concatenate([attn_grad[None], mlp_grad], axis=0)

        def place(values):
            wide = jnp.zeros((values.shape[0], D), f32)
            return lax.dynamic_update_slice_in_dim(wide, values, t_index * COLS, axis=1)

        def token_sum(values):
            return jnp.sum(values, axis=0, keepdims=True, dtype=f32)

        sum_qkv = token_sum(g_qkv)
        sum_up = token_sum(gz).reshape(ctx_size, COLS)
        placed = place(
            jnp.concatenate(
                [sum_qkv[:, :COLS], sum_qkv[:, 2 * COLS :], to_absolute(sum_up) if relative else sum_up]
            )
        )
        shared = once * jnp.concatenate(
            [g_gain_one, g_shift_one, g_gain_two, g_shift_two, token_sum(gb), token_sum(gy)]
        )
        vec_list[layer] = jnp.concatenate([shared[:4], placed[:2], shared[4:], placed[2:]], axis=0)
    input_grad = send_back(grad_hidden)

    grad_mats = jnp.stack(mat_list)
    grad_vecs = lax.dynamic_slice_in_dim(
        sum_vectors(jnp.stack(vec_list)), dp_index * vectors.shape[2], vectors.shape[2], axis=2
    )
    moment_new = momentum_decay * mat_momentum + grad_mats
    update_in = grad_mats + momentum_decay * moment_new
    item_count = 3 * LAYERS
    cols_dev = update_in.shape[3]
    items = update_in.astype(bf16).reshape(item_count, dp_rows, cols_dev)
    copies = -(-dp_size // item_count)
    slots = jnp.tile(items, (copies, 1, 1))[0:dp_size]
    received = lax.all_to_all(slots[:, None], DP, split_axis=0, concat_axis=1, tiled=True)
    current = received.reshape(dp_size * dp_rows, cols_dev)
    square = (dp_index % item_count) % 3 == 0
    gram_local = dot_trans(current, current)
    gram_part = lax.psum_scatter(gram_local.astype(bf16), "ctx", scatter_dimension=0, tiled=True)
    gram_total = lax.all_gather(gram_part, "ctx", axis=0, tiled=True).astype(f32)
    gram = jnp.where(square, gram_local, gram_total)
    scale = 1.0 / (jnp.sqrt(jnp.trace(gram)) + 1e-07)
    base = gram * (scale * scale)
    base_low = base.astype(bf16)
    bmat = (quintic_two * base + quintic_three * dot(base_low, base_low)).astype(bf16)
    current = (scale * (quintic_one * current.astype(f32) + dot(bmat, current))).astype(bf16)

    def two_part(left, right):
        high = right.astype(bf16)
        rest = (right - high.astype(f32)).astype(bf16)
        return dot(left, high) + dot(left, rest)

    turned = two_part(bmat, base)
    base = (
        quintic_one * quintic_one * base
        + quintic_one * (turned + turned.T)
        + two_part(bmat, turned.T)
    )
    base_low = base.astype(bf16)
    bmat = (quintic_two * base + quintic_three * dot(base_low, base_low)).astype(bf16)
    current = (quintic_one * current.astype(f32) + dot(bmat, current)).astype(bf16)
    returned = lax.all_to_all(
        current.reshape(dp_size, 1, dp_rows, cols_dev), DP, split_axis=0, concat_axis=1, tiled=True
    )[0]
    spread = dp_size // item_count
    chosen = [
        lax.dynamic_index_in_dim(
            returned, item + item_count * (dp_index % spread), 0, keepdims=False
        )
        for item in range(item_count)
    ]
    ortho = jnp.stack(chosen).reshape(LAYERS, 3, dp_rows, cols_dev).astype(f32)
    factor = jnp.array([0.2 * math.sqrt(D), 0.2 * math.sqrt(FF), 0.2 * math.sqrt(FF)], f32)
    weights_new = weights * (1.0 - matrix_rate * matrix_decay) - matrix_rate * (
        ortho * factor[None, :, None, None]
    )
    first_new = first_decay * vec_first + (1.0 - first_decay) * grad_vecs
    second_new = second_decay * vec_second + (1.0 - second_decay) * grad_vecs * grad_vecs
    first_hat = first_new / (1.0 - first_decay**ADAM_STEP)
    second_hat = second_new / (1.0 - second_decay**ADAM_STEP)
    vectors_new = vectors * (1.0 - vector_rate * vector_decay) - vector_rate * first_hat / (
        jnp.sqrt(second_hat) + adam_epsilon
    )
    return (
        hidden_out[None],
        input_grad[None],
        grad_mats,
        moment_new,
        weights_new,
        grad_vecs,
        second_new,
        vectors_new,
    )


def solution(mesh):
    dp, ctx = mesh.shape["dp"], mesh.shape["ctx"]
    fine = Mesh(mesh.devices.reshape(dp // TP, 2, 2, ctx), EVERY)
    tokens = P(DP, "ctx", None)
    mats = P(None, None, DP, "ctx")
    vecs = P(None, "ctx", DP)
    return jax.shard_map(
        local,
        mesh=fine,
        in_specs=(tokens, P(DP, None), tokens, mats, vecs, mats, vecs, vecs),
        out_specs=(tokens, tokens, mats, mats, mats, vecs, vecs, vecs),
        check_vma=False,
    )
```

```python
import math

import jax
import jax.numpy as jnp
from jax import lax
from jax.experimental import pallas as pl
from jax.experimental.pallas import tpu as pltpu
from jax.sharding import Mesh, PartitionSpec as P

D = 768
HEADS = 12
HEAD = 64
FF = 3072
LAYERS = 2
ADAM_STEP = 10
TP = 4
COLS = D // TP
TP_HEADS = HEADS // TP

norm_epsilon = 1e-05
quintic_one = 3.4445
quintic_two = -4.775
quintic_three = 2.0315
momentum_decay = 0.95
matrix_rate = 0.6
matrix_decay = 0.01
first_decay = 0.9
second_decay = 0.999
vector_rate = 0.5
vector_decay = 0.01
adam_epsilon = 1e-08
masked_score = -1e30

GROUP = ("jx", "jc")
REPLICAS = ("g", "ctx")
DP = ("g", "jx", "jc")
EVERY = ("g", "jx", "jc", "ctx")
SWAP = [(0, 1), (1, 0)]
bf16 = jnp.bfloat16
f32 = jnp.float32


def layer_norm(hidden, gain_vec, bias_vec):
    center = hidden - jnp.mean(hidden, axis=-1, keepdims=True)
    variance = jnp.mean(center * center, axis=-1, keepdims=True)
    return center * lax.rsqrt(variance + norm_epsilon) * gain_vec + bias_vec


def smooth_unit(preact):
    return jax.nn.gelu(preact, approximate=True)


def dot(operand, other):
    return jnp.dot(operand, other, preferred_element_type=f32)


def dot_tokens(operand, other):
    return lax.dot_general(operand, other, (((0,), (0,)), ((), ())), preferred_element_type=f32)


def dot_trans(operand, other):
    return lax.dot_general(operand, other, (((1,), (1,)), ((), ())), preferred_element_type=f32)


def bdot(operand, other, left, right):
    return lax.dot_general(
        operand, other, (((left,), (right,)), ((0,), (0,))), preferred_element_type=f32
    )


def heads_of(matrix):
    return matrix.reshape(matrix.shape[0], TP_HEADS, HEAD).transpose(1, 0, 2)


def merge_heads(stack):
    return stack.transpose(1, 0, 2).reshape(stack.shape[1], TP_HEADS * HEAD)


def core_gather(rows):
    return jnp.concatenate([rows, lax.ppermute(rows, "jc", SWAP)], axis=0)


def group_sum(partial):
    half = partial.shape[0] // 2
    mine = partial[:half] + lax.ppermute(partial[half:].astype(bf16), "jc", SWAP).astype(f32)
    return mine + lax.ppermute(mine.astype(bf16), "jx", SWAP).astype(f32)


def to_group(mats):
    count, rows, width = mats.shape
    split = mats.reshape(count, rows, TP, width // TP)
    return lax.all_to_all(split, GROUP, split_axis=2, concat_axis=1, tiled=True)[:, :, 0]


def from_group(mats):
    count, rows, width = mats.shape
    split = mats.reshape(count, TP, rows // TP, width)
    return lax.all_to_all(split, GROUP, split_axis=1, concat_axis=3, tiled=True)[:, 0]


def rotate(block, axis, step):
    size = lax.axis_size(axis)
    return lax.ppermute(block, axis, [((i + step) % size, i) for i in range(size)])


def pair_join(block, axis, dim):
    other = lax.ppermute(block, axis, SWAP)
    first = lax.axis_index(axis) == 0
    return jnp.concatenate(
        [jnp.where(first, block, other), jnp.where(first, other, block)], axis=dim
    )


def after(value, *others):
    return lax.optimization_barrier((value, *others))[0]


def roll_blocks(stack, sign):
    place = lax.axis_index("ctx")
    for bit in (1, 2):
        moved = jnp.roll(stack, sign * bit, axis=0)
        stack = jnp.where((place & bit) != 0, moved, stack)
    return stack


def from_own(stack):
    return roll_blocks(stack, -1)


def to_absolute(stack):
    return roll_blocks(stack, 1)


def out_moves():
    last = lax.axis_size("ctx") - 1
    size = last + 1
    moves = []
    for y in range(2):
        for x in range(2):
            for core in range(2):
                moves.append(
                    ((4 * y + 2 * x + core) * size + last, (4 * core + 2 * y + x) * size + last)
                )
    return moves


def attn_piece(mat, piece):
    half = mat.shape[1] // 2
    core = lax.axis_index("jc")
    mine = lax.dynamic_slice_in_dim(mat, core * half, half, axis=1)
    give = lax.dynamic_slice_in_dim(mat, (1 - core) * half, half, axis=1)
    got = lax.ppermute(give, "jc", SWAP)
    rows = jnp.concatenate(
        [jnp.where(core == 0, mine, got), jnp.where(core == 0, got, mine)], axis=0
    )
    rows = lax.ppermute(rows, EVERY, out_moves())
    return jnp.where(lax.axis_index("ctx") == lax.axis_size("ctx") - 1, rows, piece)


def out_back(piece):
    core = lax.axis_index("jc")
    rows = lax.ppermute(piece, EVERY, [(b, a) for a, b in out_moves()])
    half = rows.shape[0] // 2
    mine = lax.dynamic_slice_in_dim(rows, core * half, half, axis=0)
    give = lax.dynamic_slice_in_dim(rows, (1 - core) * half, half, axis=0)
    got = lax.ppermute(give, "jc", SWAP)
    return jnp.concatenate(
        [jnp.where(core == 0, mine, got), jnp.where(core == 0, got, mine)], axis=1
    )


def pack_pieces(low):
    first = to_group(low[0, 0:1])
    rest = to_group(after(jnp.concatenate([low[0, 1:3], low[1:].reshape(-1, *low.shape[2:])]), first))
    pieces = [(attn_piece(low[0, 0], first[0].T), jnp.swapaxes(rest[0:2], 1, 2))]
    for layer in range(1, low.shape[0]):
        base = 3 * layer - 1
        pieces.append(
            (attn_piece(low[layer, 0], rest[base].T), jnp.swapaxes(rest[base + 1 : base + 3], 1, 2))
        )
    return pieces


def ctx_gather(piece):
    return [piece] + [rotate(piece, "ctx", step) for step in (1, 3, 2)]


def group_join(blocks, pieces):
    own, near, back, far = blocks
    ordered = [own, near, far, back]
    if pieces == 1:
        other = lax.ppermute(jnp.stack(ordered), "g", SWAP)
    else:
        others = [lax.ppermute(block, "g", SWAP) for block in (own, near)]
        others.append(lax.ppermute(jnp.stack([far, back]), "g", SWAP))
        other = jnp.concatenate([others[0][None], others[1][None], others[2]])
    mine = jnp.stack(ordered)
    first = lax.axis_index("g") == 0
    return jnp.concatenate(
        [jnp.where(first, mine, other), jnp.where(first, other, mine)], axis=mine.ndim - 1
    )


def mlp_mats(stack):
    return stack[:, 0].reshape(D, D), stack[:, 1].reshape(D, D)


def gather_weights_wide(low):
    result = []
    for layer in range(low.shape[0]):
        mats = to_group(low[layer])
        parts = lax.all_gather(mats, REPLICAS, axis=0, tiled=False)
        parts = parts.reshape(lax.axis_size("g"), -1, *mats.shape)
        full = [parts[:, :, item].transpose(1, 3, 0, 2).reshape(D, D) for item in range(3)]
        w_o = lax.all_to_all(
            full[0][3 * COLS :].T.reshape(TP, COLS, COLS),
            GROUP,
            split_axis=0,
            concat_axis=2,
            tiled=True,
        )
        attn = jnp.concatenate([full[0][: 3 * COLS].reshape(3, COLS, D), w_o], axis=0)
        result.append((attn, full[1], full[2]))
    return result


def half_sum(blocks):
    half = D // 2
    group = lax.axis_index("g")
    last = blocks.ndim - 1
    mine = lax.dynamic_slice_in_dim(blocks, group * half, half, axis=last)
    give = lax.dynamic_slice_in_dim(blocks, (1 - group) * half, half, axis=last)
    return mine.astype(f32) + lax.ppermute(give.astype(bf16), "g", SWAP).astype(f32)


def ctx_sum(blocks):
    total = blocks[0]
    for step in (1, 3, 2):
        total = total + rotate(blocks[step].astype(bf16), "ctx", -step).astype(f32)
    return total


def attn_rows(part):
    columns = from_group(part.T[None])[0]
    last = lax.axis_index("ctx") == lax.axis_size("ctx") - 1
    return jnp.where(last, out_back(part), columns).astype(f32)


def mlp_rows(part):
    return from_group(jnp.swapaxes(part, 1, 2)).astype(f32)


def scatter_wide(mats):
    groups = lax.axis_size("g")
    blocks, count, width, depth = mats.shape
    stack = mats.astype(bf16).reshape(blocks, count, width, groups, depth // groups)
    stack = stack.transpose(3, 0, 1, 4, 2).reshape(groups * blocks, count, -1, width)
    part = lax.psum_scatter(stack, REPLICAS, scatter_dimension=0, tiled=True)[0]
    return from_group(part).astype(f32)


def gather_vectors(vectors):
    low = vectors.astype(bf16)
    stack = jnp.stack([low] + [rotate(low, "ctx", step) for step in range(1, 4)])
    stack = pair_join(pair_join(to_absolute(stack), "jc", 3), "jx", 3)
    if lax.axis_size("g") == 2:
        stack = pair_join(stack, "g", 3)
    else:
        stack = lax.all_gather(stack, "g", axis=3, tiled=True)
    return stack.transpose(1, 0, 2, 3).reshape(low.shape[0], -1, D).astype(f32)


def sum_vectors(terms):
    if lax.axis_size("g") == 2:
        terms = terms + lax.ppermute(terms, "g", SWAP)
    else:
        terms = lax.psum(terms, "g")
    layers, rows, width = terms.shape
    blocks = from_own(terms.reshape(layers, 4, rows // 4, width).transpose(1, 0, 2, 3))
    total = blocks[0]
    for step in range(1, 4):
        total = total + rotate(blocks[step], "ctx", -step)
    total = total + lax.ppermute(total, "jc", SWAP)
    return total + lax.ppermute(total, "jx", SWAP)


def orthogonalize_kernel(x_ref, gram_ref, out_ref, base_ref, work_ref, mat_ref, low_ref):
    size = x_ref.shape[0]
    rows = 256

    def each(body):
        for start in range(0, size, rows):
            body(pl.ds(start, rows))

    def polynomial():
        low_ref[...] = base_ref[...].astype(bf16)

        def body(block):
            square = dot(low_ref[block, :], low_ref[...])
            mat_ref[block, :] = (
                quintic_two * base_ref[block, :] + quintic_three * square
            ).astype(bf16)

        each(body)

    def two_part(left, right):
        high = left.astype(bf16)
        rest = (left - high.astype(f32)).astype(bf16)
        return dot(high, right) + dot(rest, right)

    trace = jnp.zeros((1, 1), f32)
    for start in range(0, size, rows):
        block = gram_ref[pl.ds(start, rows), pl.ds(start, rows)]
        line = lax.broadcasted_iota(jnp.int32, (rows, rows), 0)
        column = lax.broadcasted_iota(jnp.int32, (rows, rows), 1)
        trace = trace + jnp.sum(jnp.where(line == column, block, 0.0), keepdims=True)
    scale = 1.0 / (jnp.sqrt(trace) + 1e-07)
    base_ref[...] = gram_ref[...] * (scale * scale)
    polynomial()

    def first_step(block):
        value = quintic_one * x_ref[block, :].astype(f32) + dot(mat_ref[block, :], x_ref[...])
        out_ref[block, :] = (scale * value).astype(bf16)
        work_ref[block, :] = quintic_one * base_ref[block, :] + two_part(
            base_ref[block, :], mat_ref[...]
        )

    each(first_step)
    turned = work_ref[...].T
    work_ref[...] = turned

    def gram_step(block):
        base_ref[block, :] = quintic_one * work_ref[block, :] + two_part(
            work_ref[block, :], mat_ref[...]
        )

    each(gram_step)
    polynomial()
    low_ref[...] = out_ref[...]

    def second_step(block):
        value = quintic_one * low_ref[block, :].astype(f32) + dot(mat_ref[block, :], low_ref[...])
        out_ref[block, :] = value.astype(bf16)

    each(second_step)


def orthogonalize(matrix, gram):
    size = matrix.shape[0]
    return pl.pallas_call(
        orthogonalize_kernel,
        out_shape=jax.ShapeDtypeStruct(matrix.shape, bf16),
        in_specs=[pl.BlockSpec(memory_space=pltpu.VMEM)] * 2,
        out_specs=pl.BlockSpec(memory_space=pltpu.VMEM),
        scratch_shapes=[
            pltpu.VMEM((size, size), f32),
            pltpu.VMEM((size, size), f32),
            pltpu.VMEM((size, size), bf16),
            pltpu.VMEM((size, size), bf16),
        ],
        compiler_params=pltpu.CompilerParams(vmem_limit_bytes=48 * 1024 * 1024),
    )(matrix, gram)


def ctx_gram(gram):
    size = lax.axis_size("ctx")

    def shift(block, step):
        moves = [((i + step) % size, i) for i in range(size)]
        return lax.ppermute(block, ("jc", "ctx"), moves)

    rows = gram.shape[0] // size
    blocks = from_own(gram.astype(bf16).reshape(size, rows, -1))
    total = blocks[0].astype(f32)
    for step in (1, 3, 2):
        total = total + shift(blocks[step], -step).astype(f32)
    low = total.astype(bf16)
    full = [low] + [shift(low, step) for step in range(1, size)]
    return to_absolute(jnp.stack(full)).reshape(gram.shape).astype(f32)


def local(hidden_in, segments, out_grad, weights, vectors, mat_momentum, vec_first, vec_second):
    tokens_dev = hidden_in.shape[1]
    seq_len = segments.shape[1]
    half = 2 * tokens_dev
    dp_rows = weights.shape[2]
    ctx_size = lax.axis_size("ctx")
    x_index = lax.axis_index("jx")
    c_index = lax.axis_index("jc")
    t_index = 2 * x_index + c_index
    z_index = lax.axis_index("ctx")
    dp_index = lax.axis_index(DP)
    dp_size = lax.axis_size(DP)

    to_seq = []
    for t in range(TP):
        for z in range(ctx_size):
            to_seq.append((t * ctx_size + z, ((z % 2) * 2 + z // 2) * ctx_size + t))
    from_seq = [(b, a) for a, b in to_seq]
    axes = ("jx", "jc", "ctx")

    def x_join(block):
        return pair_join(block, "jx", 0)

    vec_rows = gather_vectors(vectors)
    seg_row = jnp.pad(segments.astype(f32), ((0, 7), (0, D - seq_len)))
    moved = lax.ppermute(jnp.concatenate([hidden_in[0], seg_row], axis=0), axes, to_seq)
    hidden = x_join(moved[:tokens_dev])
    segment_row = moved[tokens_dev, :seq_len]
    relative = lax.axis_size("g") == 2
    low = weights.astype(bf16)
    gathered = [None] * LAYERS
    if relative:
        pieces = pack_pieces(low)
        attn_blocks = ctx_gather(pieces[0][0])
        mlp_blocks = ctx_gather(after(pieces[0][1], *attn_blocks[1:]))
        gathered[0] = (to_absolute(group_join(attn_blocks, 3)), mlp_blocks)
    else:
        gathered = gather_weights_wide(low)

    order = [c_index * half, (1 - c_index) * half]
    pos = jnp.concatenate([start + jnp.arange(half) for start in order])
    seg = jnp.concatenate([lax.dynamic_slice_in_dim(segment_row, start, half) for start in order])
    allowed = (pos[None, :] <= pos[:, None]) & (seg[None, :] == seg[:, None])

    def mine(row):
        return lax.dynamic_slice_in_dim(row, t_index * COLS, COLS, axis=-1)

    def scores_of(q, k):
        return jnp.where(allowed[None], bdot(q, k, 2, 2) * HEAD ** (-0.5), masked_score)

    stored = []
    for layer in range(LAYERS):
        vec = [vec_rows[layer, row : row + 1] for row in range(8)]
        attn_w = gathered[layer][0]
        w_qkv = attn_w[:3].reshape(3 * COLS, D)
        w_o = attn_w[3]
        b_up = mine(vec_rows[layer, 8:12])
        b_up = (from_own(b_up) if relative else b_up).reshape(1, D)
        a_all = core_gather(layer_norm(hidden, vec[0], vec[1]).astype(bf16))
        proj = dot_trans(a_all, w_qkv)
        q = heads_of((proj[:, :COLS] + mine(vec[4])).astype(bf16))
        k = heads_of(proj[:, COLS : 2 * COLS].astype(bf16))
        v = heads_of((proj[:, 2 * COLS :] + mine(vec[5])).astype(bf16))
        scores = scores_of(q, k)
        row_max = jnp.max(scores, axis=-1, keepdims=True)
        unnormed = jnp.exp(scores - row_max)
        total = jnp.sum(unnormed, axis=-1, keepdims=True)
        prob = (unnormed / total).astype(bf16)
        log_total = row_max + jnp.log(total)
        o = merge_heads(bdot(prob, v, 2, 1)).astype(bf16)
        following = layer + 1 < LAYERS
        if relative and following:
            attn_blocks = ctx_gather(after(pieces[layer + 1][0], o))
        middle = hidden + (group_sum(dot(o, w_o)) + vec[6])
        c_all = core_gather(layer_norm(middle, vec[2], vec[3]).astype(bf16))
        if relative:
            w_up, w_down = mlp_mats(group_join(gathered[layer][1], 1))
        else:
            w_up, w_down = gathered[layer][1:]
        preact = dot_trans(c_all, w_up) + b_up
        act = smooth_unit(preact).astype(bf16)
        if relative and following:
            mlp_blocks = ctx_gather(after(pieces[layer + 1][1], act, *attn_blocks[1:]))
            gathered[layer + 1] = (to_absolute(group_join(attn_blocks, 1)), mlp_blocks)
        stored.append(
            (hidden, middle, a_all, q, k, v, log_total, o, c_all, preact, act, w_qkv, w_o, w_up, w_down)
        )
        hidden = middle + (group_sum(dot(act, w_down)) + vec[7])

    def send_back(rows):
        block = lax.dynamic_slice_in_dim(rows, x_index * tokens_dev, tokens_dev, axis=0)
        return lax.ppermute(block, axes, from_seq)

    hidden_out = send_back(hidden)
    moved_grad = lax.ppermute(after(out_grad[0], stored[-1][7]), axes, to_seq)
    grad_hidden = x_join(moved_grad)

    once = jnp.where(x_index == 0, 1.0, 0.0).astype(f32)
    mat_list = [None] * LAYERS
    vec_list = [None] * LAYERS
    parts = [None] * LAYERS
    attn_half = attn_part = up_part = down_part = None
    for layer in reversed(range(LAYERS)):
        (h_in, middle, a_all, q, k, v, log_total, o, c_all, preact, act, w_qkv, w_o, w_up, w_down) = stored[
            layer
        ]
        vec = [vec_rows[layer, row : row + 1] for row in range(8)]
        gy = grad_hidden.astype(bf16)
        gy_all = core_gather(gy)
        down_grad = dot_tokens(act, gy_all).reshape(ctx_size, COLS, D)
        if relative:
            down_half = half_sum(down_grad)
        gu = dot_trans(gy_all, w_down)
        unused, gelu_pull = jax.vjp(smooth_unit, preact)
        gz = gelu_pull(gu)[0].astype(bf16)
        if relative and attn_half is not None:
            gz, attn_half, up_part = lax.optimization_barrier((gz, attn_half, up_part))
            attn_part = ctx_sum(from_own(attn_half))
        up_grad = dot_tokens(gz, c_all).reshape(ctx_size, COLS, D)
        if relative:
            up_half = half_sum(up_grad)
        gc = group_sum(dot(gz, w_up))
        unused, pull_two = jax.vjp(layer_norm, middle, vec[2], vec[3])
        g_mid, g_gain_two, g_shift_two = pull_two(gc)
        gm = grad_hidden + g_mid
        gb = gm.astype(bf16)
        if relative:
            if attn_part is not None:
                gb, attn_part = lax.optimization_barrier((gb, attn_part))
                parts[layer + 1] = (attn_part, down_part, up_part)
            gb, down_half = lax.optimization_barrier((gb, down_half))
            down_part = ctx_sum(down_half)
        gb_all = core_gather(gb)
        go = heads_of(dot_trans(gb_all, w_o).astype(bf16))
        prob = jnp.exp(scores_of(q, k) - log_total)
        prob_low = prob.astype(bf16)
        g_prob = bdot(go, v, 2, 2)
        row_dot = jnp.sum(g_prob * prob, axis=-1, keepdims=True)
        g_scores = (prob * (g_prob - row_dot)).astype(bf16)
        gq = merge_heads(bdot(g_scores, k, 2, 1) * HEAD ** (-0.5)).astype(bf16)
        gk = merge_heads(bdot(g_scores, q, 1, 1) * HEAD ** (-0.5)).astype(bf16)
        gv = merge_heads(bdot(prob_low, go, 1, 1)).astype(bf16)
        g_qkv = jnp.concatenate([gq, gk, gv], axis=1)
        if relative:
            g_qkv, up_half = lax.optimization_barrier((g_qkv, up_half))
            up_part = ctx_sum(up_half)
        attn_grad = jnp.concatenate([dot_tokens(g_qkv, a_all), dot_tokens(o, gb_all)])
        attn_grad = attn_grad.reshape(4, COLS, D)
        if relative:
            attn_half = half_sum(attn_grad)
        ga = group_sum(dot(g_qkv, w_qkv))
        if relative:
            ga, down_part = lax.optimization_barrier((ga, down_part))
        unused, pull_one = jax.vjp(layer_norm, h_in, vec[0], vec[1])
        g_in, g_gain_one, g_shift_one = pull_one(ga)
        grad_hidden = gm + g_in

        if not relative:
            g_wo = lax.all_to_all(
                attn_grad[3].reshape(COLS, TP, COLS), GROUP, split_axis=1, concat_axis=0, tiled=True
            )[:, 0]
            attn_grad = jnp.concatenate([attn_grad[:3], g_wo.T[None]], axis=0)
            mat_list[layer] = scatter_wide(jnp.stack([attn_grad, up_grad, down_grad], axis=1))

        def place(values):
            wide = jnp.zeros((values.shape[0], D), f32)
            return lax.dynamic_update_slice_in_dim(wide, values, t_index * COLS, axis=1)

        def token_sum(values):
            return jnp.sum(values, axis=0, keepdims=True, dtype=f32)

        sum_qkv = token_sum(g_qkv)
        sum_up = token_sum(gz).reshape(ctx_size, COLS)
        placed = place(
            jnp.concatenate(
                [sum_qkv[:, :COLS], sum_qkv[:, 2 * COLS :], to_absolute(sum_up) if relative else sum_up]
            )
        )
        shared = once * jnp.concatenate(
            [g_gain_one, g_shift_one, g_gain_two, g_shift_two, token_sum(gb), token_sum(gy)]
        )
        vec_list[layer] = jnp.concatenate([shared[:4], placed[:2], shared[4:], placed[2:]], axis=0)
    input_grad = send_back(grad_hidden)

    if relative:
        parts[0] = (ctx_sum(from_own(attn_half)), down_part, up_part)
        for layer in range(LAYERS):
            attn_part, down_part, up_part = [part.astype(bf16) for part in parts[layer]]
            mat_list[layer] = jnp.concatenate(
                [attn_rows(attn_part)[None], mlp_rows(jnp.stack([up_part, down_part]))]
            )
    grad_vecs = lax.dynamic_slice_in_dim(
        sum_vectors(jnp.stack(vec_list)), dp_index * vectors.shape[2], vectors.shape[2], axis=2
    )
    cols_dev = weights.shape[3]
    grad_list, moment_list, low_list = [], [], []
    for layer in range(LAYERS):
        for item in range(3):
            grad = mat_list[layer][item]
            moment = momentum_decay * mat_momentum[layer, item] + grad
            grad_list.append(grad)
            moment_list.append(moment)
            low_list.append((grad + momentum_decay * moment).astype(bf16))
    wide = [item for item in range(3 * LAYERS) if item % 3]
    squares = [item for item in range(3, 3 * LAYERS, 3)]
    table = []
    for number in range(4):
        table += [wide[number], squares[number % len(squares)]]
    table = (table * (-(-dp_size // 8)))[:dp_size]
    slots = jnp.stack([low_list[item] for item in table])
    received = lax.all_to_all(slots[:, None], DP, split_axis=0, concat_axis=1, tiled=True)
    current = received.reshape(dp_size * dp_rows, cols_dev)
    gram_local = dot_trans(current, current)
    gram = jnp.where(c_index == 0, ctx_gram(gram_local), gram_local)
    ortho_mine = orthogonalize(current, gram)
    returned = lax.all_to_all(
        ortho_mine.reshape(dp_size, 1, dp_rows, cols_dev),
        DP,
        split_axis=0,
        concat_axis=1,
        tiled=True,
    )[0]
    first_full = lax.all_gather(low_list[0], DP, axis=0, tiled=True)
    first_ortho = orthogonalize(first_full, dot_trans(first_full, first_full))
    ortho_list = [lax.dynamic_slice_in_dim(first_ortho, dp_index * dp_rows, dp_rows, axis=0)]
    ortho_list += [returned[table.index(item)] for item in range(1, 3 * LAYERS)]
    ortho = jnp.stack(ortho_list).reshape(LAYERS, 3, dp_rows, cols_dev).astype(f32)
    grad_mats = jnp.stack(grad_list).reshape(weights.shape)
    moment_new = jnp.stack(moment_list).reshape(weights.shape)
    factor = jnp.array([0.2 * math.sqrt(D), 0.2 * math.sqrt(FF), 0.2 * math.sqrt(FF)], f32)
    weights_new = weights * (1.0 - matrix_rate * matrix_decay) - matrix_rate * (
        ortho * factor[None, :, None, None]
    )
    first_new = first_decay * vec_first + (1.0 - first_decay) * grad_vecs
    second_new = second_decay * vec_second + (1.0 - second_decay) * grad_vecs * grad_vecs
    first_hat = first_new / (1.0 - first_decay**ADAM_STEP)
    second_hat = second_new / (1.0 - second_decay**ADAM_STEP)
    vectors_new = vectors * (1.0 - vector_rate * vector_decay) - vector_rate * first_hat / (
        jnp.sqrt(second_hat) + adam_epsilon
    )
    return (
        hidden_out[None],
        input_grad[None],
        grad_mats,
        moment_new,
        weights_new,
        grad_vecs,
        second_new,
        vectors_new,
    )


def solution(mesh):
    dp, ctx = mesh.shape["dp"], mesh.shape["ctx"]
    fine = Mesh(mesh.devices.reshape(dp // TP, 2, 2, ctx), EVERY)
    tokens = P(DP, "ctx", None)
    mats = P(None, None, DP, "ctx")
    vecs = P(None, "ctx", DP)
    return jax.shard_map(
        local,
        mesh=fine,
        in_specs=(tokens, P(DP, None), tokens, mats, vecs, mats, vecs, vecs),
        out_specs=(tokens, tokens, mats, mats, mats, vecs, vecs, vecs),
        check_vma=False,
    )
```

```python
import math

import jax
import jax.numpy as jnp
from jax import lax
from jax.experimental import pallas as pl
from jax.experimental.pallas import tpu as pltpu
from jax.sharding import Mesh, PartitionSpec as P

D = 768
HEADS = 12
HEAD = 64
FF = 3072
LAYERS = 2
ADAM_STEP = 10
TP = 4
COLS = D // TP
TP_HEADS = HEADS // TP

norm_epsilon = 1e-05
quintic_one = 3.4445
quintic_two = -4.775
quintic_three = 2.0315
momentum_decay = 0.95
matrix_rate = 0.6
matrix_decay = 0.01
first_decay = 0.9
second_decay = 0.999
vector_rate = 0.5
vector_decay = 0.01
adam_epsilon = 1e-08
masked_score = -1e30

GROUP = ("jx", "jc")
REPLICAS = ("g", "ctx")
DP = ("g", "jx", "jc")
EVERY = ("g", "jx", "jc", "ctx")
SWAP = [(0, 1), (1, 0)]
bf16 = jnp.bfloat16
f32 = jnp.float32


def dot(operand, other):
    return jnp.dot(operand, other, preferred_element_type=f32)


def dot_tokens(operand, other):
    return lax.dot_general(operand, other, (((0,), (0,)), ((), ())), preferred_element_type=f32)


def dot_trans(operand, other):
    return lax.dot_general(operand, other, (((1,), (1,)), ((), ())), preferred_element_type=f32)


def to_group(mats):
    count, rows, width = mats.shape
    split = mats.reshape(count, rows, TP, width // TP)
    return lax.all_to_all(split, GROUP, split_axis=2, concat_axis=1, tiled=True)[:, :, 0]


def from_group(mats):
    count, rows, width = mats.shape
    split = mats.reshape(count, TP, rows // TP, width)
    return lax.all_to_all(split, GROUP, split_axis=1, concat_axis=3, tiled=True)[:, 0]


def rotate(block, axis, step):
    size = lax.axis_size(axis)
    return lax.ppermute(block, axis, [((i + step) % size, i) for i in range(size)])


def pair_join(block, axis, dim):
    other = lax.ppermute(block, axis, SWAP)
    first = lax.axis_index(axis) == 0
    return jnp.concatenate(
        [jnp.where(first, block, other), jnp.where(first, other, block)], axis=dim
    )


def after(value, *others):
    return lax.optimization_barrier((value, *others))[0]


def roll_blocks(stack, sign):
    place = lax.axis_index("ctx")
    for bit in (1, 2):
        moved = jnp.roll(stack, sign * bit, axis=0)
        stack = jnp.where((place & bit) != 0, moved, stack)
    return stack


def from_own(stack):
    return roll_blocks(stack, -1)


def to_absolute(stack):
    return roll_blocks(stack, 1)


def out_moves():
    last = lax.axis_size("ctx") - 1
    size = last + 1
    moves = []
    for y in range(2):
        for x in range(2):
            for core in range(2):
                moves.append(
                    ((4 * y + 2 * x + core) * size + last, (4 * core + 2 * y + x) * size + last)
                )
    return moves


def attn_piece(mat, piece):
    half = mat.shape[1] // 2
    core = lax.axis_index("jc")
    mine = lax.dynamic_slice_in_dim(mat, core * half, half, axis=1)
    give = lax.dynamic_slice_in_dim(mat, (1 - core) * half, half, axis=1)
    got = lax.ppermute(give, "jc", SWAP)
    rows = jnp.concatenate(
        [jnp.where(core == 0, mine, got), jnp.where(core == 0, got, mine)], axis=0
    )
    rows = lax.ppermute(rows, EVERY, out_moves())
    return jnp.where(lax.axis_index("ctx") == lax.axis_size("ctx") - 1, rows, piece)


def out_back(piece):
    core = lax.axis_index("jc")
    rows = lax.ppermute(piece, EVERY, [(b, a) for a, b in out_moves()])
    half = rows.shape[0] // 2
    mine = lax.dynamic_slice_in_dim(rows, core * half, half, axis=0)
    give = lax.dynamic_slice_in_dim(rows, (1 - core) * half, half, axis=0)
    got = lax.ppermute(give, "jc", SWAP)
    return jnp.concatenate(
        [jnp.where(core == 0, mine, got), jnp.where(core == 0, got, mine)], axis=1
    )


def pack_pieces(low):
    first = to_group(low[0, 0:1])
    rest = to_group(after(jnp.concatenate([low[0, 1:3], low[1:].reshape(-1, *low.shape[2:])]), first))
    pieces = [(attn_piece(low[0, 0], first[0].T), jnp.swapaxes(rest[0:2], 1, 2))]
    for layer in range(1, low.shape[0]):
        base = 3 * layer - 1
        pieces.append(
            (attn_piece(low[layer, 0], rest[base].T), jnp.swapaxes(rest[base + 1 : base + 3], 1, 2))
        )
    return pieces


def ctx_gather(piece):
    near, back, far = [rotate(piece, "ctx", step) for step in (1, 3, 2)]
    return [piece, near, far, back]


def gather_weights_wide(low):
    result = []
    for layer in range(low.shape[0]):
        mats = to_group(low[layer])
        parts = lax.all_gather(mats, REPLICAS, axis=0, tiled=False)
        parts = parts.reshape(lax.axis_size("g"), -1, *mats.shape)
        full = [parts[:, :, item].transpose(1, 3, 0, 2).reshape(D, D) for item in range(3)]
        w_o = lax.all_to_all(
            full[0][3 * COLS :].T.reshape(TP, COLS, COLS),
            GROUP,
            split_axis=0,
            concat_axis=2,
            tiled=True,
        )
        attn = jnp.concatenate([full[0][: 3 * COLS].reshape(3, COLS, D), w_o], axis=0)
        result.append((attn.reshape(D, D), jnp.stack([full[1], full[2]])))
    return result


def half_sum(mine, give):
    return mine + lax.ppermute(give, "g", SWAP).astype(f32)


def ctx_sum(blocks):
    total = blocks[0]
    for step in (1, 3, 2):
        total = total + rotate(blocks[step].astype(bf16), "ctx", -step).astype(f32)
    return total


def attn_rows(part):
    columns = from_group(part.T[None])[0]
    last = lax.axis_index("ctx") == lax.axis_size("ctx") - 1
    return jnp.where(last, out_back(part), columns).astype(f32)


def mlp_rows(part):
    return from_group(jnp.swapaxes(part, 1, 2)).astype(f32)


def scatter_wide(mats):
    groups = lax.axis_size("g")
    blocks, count, width, depth = mats.shape
    stack = mats.astype(bf16).reshape(blocks, count, width, groups, depth // groups)
    stack = stack.transpose(3, 0, 1, 4, 2).reshape(groups * blocks, count, -1, width)
    part = lax.psum_scatter(stack, REPLICAS, scatter_dimension=0, tiled=True)[0]
    return from_group(part).astype(f32)


def gather_vectors(vectors):
    low = vectors.astype(bf16)
    stack = jnp.stack([low] + [rotate(low, "ctx", step) for step in range(1, 4)])
    stack = pair_join(pair_join(to_absolute(stack), "jc", 3), "jx", 3)
    if lax.axis_size("g") == 2:
        stack = pair_join(stack, "g", 3)
    else:
        stack = lax.all_gather(stack, "g", axis=3, tiled=True)
    return stack.transpose(1, 0, 2, 3).reshape(low.shape[0], -1, D).astype(f32)


def sum_vectors(terms):
    if lax.axis_size("g") == 2:
        terms = terms + lax.ppermute(terms, "g", SWAP)
    else:
        terms = lax.psum(terms, "g")
    layers, rows, width = terms.shape
    blocks = from_own(terms.reshape(layers, 4, rows // 4, width).transpose(1, 0, 2, 3))
    total = blocks[0]
    for step in range(1, 4):
        total = total + rotate(blocks[step], "ctx", -step)
    total = total + lax.ppermute(total, "jc", SWAP)
    return total + lax.ppermute(total, "jx", SWAP)


def call(kernel, outs, *args, scratch=()):
    return pl.pallas_call(
        kernel,
        out_shape=[jax.ShapeDtypeStruct(shape, kind) for shape, kind in outs],
        in_specs=[pl.BlockSpec(memory_space=pltpu.SMEM)]
        + [pl.BlockSpec(memory_space=pltpu.VMEM)] * (len(args) - 1),
        out_specs=[pl.BlockSpec(memory_space=pltpu.VMEM)] * len(outs),
        scratch_shapes=list(scratch),
        compiler_params=pltpu.CompilerParams(vmem_limit_bytes=52 * 1024 * 1024),
    )(*args)


def block_at(place_ref, step):
    ahead = place_ref[0] + step
    return jnp.where(ahead >= 4, ahead - 4, ahead)


def put_blocks(place_ref, own_refs, other_refs, full_refs):
    half = D // 2
    mine = pl.multiple_of(place_ref[1] * half, half)
    theirs = pl.multiple_of((1 - place_ref[1]) * half, half)
    for step in range(4):
        rows = pl.ds(pl.multiple_of(block_at(place_ref, step) * COLS, COLS), COLS)
        for number, full_ref in enumerate(full_refs):
            own, other = own_refs[step], other_refs[step]
            if len(full_refs) > 1:
                own, other = own.at[number], other.at[number]
            full_ref[rows, pl.ds(mine, half)] = own[...]
            full_ref[rows, pl.ds(theirs, half)] = other[...]


def put_grads(place_ref, grad, mine_refs, give_refs, halves):
    half = D // 2
    for block in range(4):
        rows = grad[block * COLS : (block + 1) * COLS]
        if halves:
            back = block - place_ref[0]
            back = jnp.where(back < 0, back + 4, back)
            low = place_ref[1] == 0
            mine_refs(back)[...] = jnp.where(low, rows[:, :half], rows[:, half:])
            give_refs(back)[...] = jnp.where(low, rows[:, half:], rows[:, :half]).astype(bf16)
        else:
            mine_refs(block)[...] = rows


def norm_rows(hidden):
    center = hidden - jnp.mean(hidden, axis=-1, keepdims=True)
    variance = jnp.mean(center * center, axis=-1, keepdims=True)
    inverse = lax.rsqrt(variance + norm_epsilon)
    return center * inverse, inverse


def norm_stage(vecs, layer, row, hidden, mine=None, recv=None, bias=None):
    rows = hidden.shape[0]

    def kernel(unused, vec_ref, hidden_ref, *refs):
        total = hidden_ref[...]
        if mine is not None:
            mine_ref, recv_ref, total_ref, out_ref = refs
            bias_row = vec_ref[bias[0], bias[1] : bias[1] + 1, :]
            total = total + (mine_ref[...] + recv_ref[...].astype(f32) + bias_row)
            total_ref[...] = total
        else:
            (out_ref,) = refs
        normed, unused_scale = norm_rows(total)
        gain = vec_ref[layer, row : row + 1, :]
        shift = vec_ref[layer, row + 1 : row + 2, :]
        out_ref[...] = (normed * gain + shift).astype(bf16)

    outs = [((rows, D), bf16)]
    args = [hidden]
    if mine is not None:
        outs = [((rows, D), f32)] + outs
        args += [mine, recv]
    return call(kernel, outs, jnp.zeros((1,), jnp.int32), vecs, *args)


def norm_back_stage(vecs, layer, row, grad, mine, recv, hidden):
    rows = hidden.shape[0]

    def kernel(unused, vec_ref, grad_ref, mine_ref, recv_ref, hidden_ref, out_ref, low_ref, sum_ref):
        through = mine_ref[...] + recv_ref[...].astype(f32)
        normed, inverse = norm_rows(hidden_ref[...])
        scaled = through * vec_ref[layer, row : row + 1, :]
        part = jnp.mean(scaled, axis=-1, keepdims=True)
        part = part + normed * jnp.mean(scaled * normed, axis=-1, keepdims=True)
        total = grad_ref[...] + inverse * (scaled - part)
        out_ref[...] = total
        low = total.astype(bf16)
        low_ref[...] = low
        sum_ref[0:1, :] = jnp.sum(through * normed, axis=0, keepdims=True)
        sum_ref[1:2, :] = jnp.sum(through, axis=0, keepdims=True)
        sum_ref[2:3, :] = jnp.sum(low.astype(f32), axis=0, keepdims=True)

    outs = [((rows, D), f32), ((rows, D), bf16), ((8, D), f32)]
    return call(kernel, outs, jnp.zeros((1,), jnp.int32), vecs, grad, mine, recv, hidden)


def both(first_ref, second_ref):
    return jnp.concatenate([first_ref[...], second_ref[...]], axis=0)


def allowed_of(row_ref, column_ref):
    before = row_ref[0:1, :] <= column_ref[:, 0:1]
    return before & (row_ref[1:2, :] == column_ref[:, 1:2])


def attend_stage(place, row_info, column_info, bias, a_own, a_other, weights):
    half = a_own.shape[0]
    tokens = 2 * half
    wide = 3 * COLS
    own, other = weights if isinstance(weights, tuple) else ([], [])
    stacked = bool(other) and other[0].ndim == 3

    def kernel(place_ref, row_ref, column_ref, bias_ref, own_a_ref, other_a_ref, *refs):
        if own:
            own_refs, refs = refs[:4], refs[4:]
            count = len(other)
            others, refs = refs[:count], refs[count:]
            if stacked:
                others = [others[0].at[step] for step in range(4)]
            w_ref, qkv_ref, lse_ref, o_ref, mine_ref, give_ref = refs
            put_blocks(place_ref, own_refs, others, [w_ref])
        else:
            w_ref, qkv_ref, lse_ref, o_ref, mine_ref, give_ref = refs
        for start, a_ref in ((0, own_a_ref), (half, other_a_ref)):
            proj = dot_trans(a_ref[...], w_ref[0:wide, :]) + bias_ref[0:1, :]
            qkv_ref[start : start + half, :] = proj.astype(bf16)
        allowed = allowed_of(row_ref, column_ref)
        for head in range(TP_HEADS):
            lanes = head * HEAD
            k = qkv_ref[:, COLS + lanes : COLS + lanes + HEAD]
            v = qkv_ref[:, 2 * COLS + lanes : 2 * COLS + lanes + HEAD]
            for start in (0, half):
                rows = slice(start, start + half)
                q = qkv_ref[rows, lanes : lanes + HEAD]
                scores = jnp.where(allowed[rows], dot_trans(q, k) * HEAD ** (-0.5), masked_score)
                top = jnp.max(scores, axis=-1, keepdims=True)
                unnormed = jnp.exp(scores - top)
                total = jnp.sum(unnormed, axis=-1, keepdims=True)
                prob = (unnormed * (1.0 / total)).astype(bf16)
                o_ref[rows, lanes : lanes + HEAD] = dot(prob, v).astype(bf16)
                lse_ref[rows, head : head + 1] = top + jnp.log(total)
        mine_ref[...] = dot(o_ref[0:half, :], w_ref[wide:, :])
        give_ref[...] = dot(o_ref[half:, :], w_ref[wide:, :]).astype(bf16)

    outs = [
        ((tokens, wide), bf16),
        ((tokens, 128), f32),
        ((tokens, COLS), bf16),
        ((half, D), f32),
        ((half, D), bf16),
    ]
    if own:
        outs = [((D, D), bf16)] + outs
        return call(
            kernel, outs, place, row_info, column_info, bias, a_own, a_other, *own, *other
        )
    result = call(kernel, outs, place, row_info, column_info, bias, a_own, a_other, weights)
    return [weights] + list(result)


def attend_back_stage(
    place, row_info, column_info, gb_own, gb_other, a_own, a_other, qkv, lse, o, w_attn, halves
):
    half = a_own.shape[0]
    tokens = 2 * half
    wide = 3 * COLS

    def kernel(
        place_ref,
        row_ref,
        column_ref,
        own_gb_ref,
        other_gb_ref,
        own_a_ref,
        other_a_ref,
        qkv_ref,
        lse_ref,
        o_ref,
        w_ref,
        mine_ref,
        give_ref,
        sum_ref,
        *refs,
    ):
        *grad_refs, go_ref, all_ref = refs
        w_o = w_ref[wide:, :]
        for start, gb_ref in ((0, own_gb_ref), (half, other_gb_ref)):
            go_ref[start : start + half, :] = dot_trans(gb_ref[...], w_o).astype(bf16)
        allowed = allowed_of(row_ref, column_ref)
        for head in range(TP_HEADS):
            lanes = head * HEAD
            q_lanes = slice(lanes, lanes + HEAD)
            k_lanes = slice(COLS + lanes, COLS + lanes + HEAD)
            v_lanes = slice(2 * COLS + lanes, 2 * COLS + lanes + HEAD)
            k = qkv_ref[:, k_lanes]
            v = qkv_ref[:, v_lanes]
            gk = jnp.zeros((tokens, HEAD), f32)
            gv = jnp.zeros((tokens, HEAD), f32)
            for start in (0, half):
                rows = slice(start, start + half)
                q = qkv_ref[rows, q_lanes]
                go = go_ref[rows, q_lanes]
                scores = jnp.where(allowed[rows], dot_trans(q, k) * HEAD ** (-0.5), masked_score)
                prob = jnp.exp(scores - lse_ref[rows, head : head + 1])
                g_prob = dot_trans(go, v)
                row_dot = jnp.sum(g_prob * prob, axis=-1, keepdims=True)
                g_scores = (prob * (g_prob - row_dot)).astype(bf16)
                all_ref[rows, q_lanes] = (dot(g_scores, k) * HEAD ** (-0.5)).astype(bf16)
                gk = gk + dot_tokens(g_scores, q)
                gv = gv + dot_tokens(prob.astype(bf16), go)
            all_ref[:, k_lanes] = (gk * HEAD ** (-0.5)).astype(bf16)
            all_ref[:, v_lanes] = gv.astype(bf16)
        mine_ref[...] = dot(all_ref[0:half, :], w_ref[0:wide, :])
        give_ref[...] = dot(all_ref[half:, :], w_ref[0:wide, :]).astype(bf16)
        sum_ref[0:1, :] = jnp.sum(all_ref[...].astype(f32), axis=0, keepdims=True)
        grad = jnp.concatenate(
            [
                dot_tokens(all_ref[...], both(own_a_ref, other_a_ref)),
                dot_tokens(o_ref[...], both(own_gb_ref, other_gb_ref)),
            ],
            axis=0,
        )
        put_grads(
            place_ref,
            grad,
            lambda block: grad_refs[0].at[block],
            lambda block: grad_refs[1].at[block],
            halves,
        )

    width = D // 2 if halves else D
    outs = [((half, D), f32), ((half, D), bf16), ((8, wide), f32), ((4, COLS, width), f32)]
    if halves:
        outs.append(((4, COLS, width), bf16))
    return call(
        kernel,
        outs,
        place,
        row_info,
        column_info,
        gb_own,
        gb_other,
        a_own,
        a_other,
        qkv,
        lse,
        o,
        w_attn,
        scratch=[pltpu.VMEM((tokens, COLS), bf16), pltpu.VMEM((tokens, wide), bf16)],
    )


def tanh_part(preact):
    inner = math.sqrt(2.0 / math.pi) * (preact + 0.044715 * (preact * preact * preact))
    return jnp.tanh(inner)


def feed_stage(place, bias, c_own, c_other, weights):
    half = c_own.shape[0]
    own, other = weights if isinstance(weights, tuple) else ([], [])

    def kernel(place_ref, bias_ref, own_c_ref, other_c_ref, *refs):
        if own:
            own_refs, other_ref, refs = refs[:4], refs[4], refs[5:]
            others = [other_ref.at[step] for step in range(4)]
            w_ref, preact_ref, act_ref, mine_ref, give_ref = refs
            put_blocks(place_ref, own_refs, others, [w_ref.at[0], w_ref.at[1]])
        else:
            w_ref, preact_ref, act_ref, mine_ref, give_ref = refs
        for start, c_ref, out_ref in ((0, own_c_ref, mine_ref), (half, other_c_ref, give_ref)):
            rows = slice(start, start + half)
            preact = dot_trans(c_ref[...], w_ref[0]) + bias_ref[...]
            preact_ref[rows, :] = preact
            act = (0.5 * preact * (1.0 + tanh_part(preact))).astype(bf16)
            act_ref[rows, :] = act
            out_ref[...] = dot(act, w_ref[1]).astype(out_ref.dtype)

    outs = [
        ((2 * half, D), f32),
        ((2 * half, D), bf16),
        ((half, D), f32),
        ((half, D), bf16),
    ]
    if own:
        outs = [((2, D, D), bf16)] + outs
        return call(kernel, outs, place, bias, c_own, c_other, *own, *other)
    return [weights] + list(call(kernel, outs, place, bias, c_own, c_other, weights))


def feed_back_stage(place, gy_own, gy_other, c_own, c_other, preact, act, weights, halves):
    half = c_own.shape[0]

    def kernel(
        place_ref,
        own_gy_ref,
        other_gy_ref,
        own_c_ref,
        other_c_ref,
        preact_ref,
        act_ref,
        w_ref,
        mine_ref,
        give_ref,
        sum_ref,
        *refs,
    ):
        *grad_refs, gz_ref = refs
        up_sum = jnp.zeros((1, D), f32)
        for start, gy_ref, out_ref in ((0, own_gy_ref, mine_ref), (half, other_gy_ref, give_ref)):
            rows = slice(start, start + half)
            gu = dot_trans(gy_ref[...], w_ref[1])
            x = preact_ref[rows, :]
            tanh = tanh_part(x)
            slope = math.sqrt(2.0 / math.pi) * (1.0 + 3.0 * 0.044715 * (x * x))
            factor = 0.5 * (1.0 + tanh) + 0.5 * x * (1.0 - tanh * tanh) * slope
            gz = (gu * factor).astype(bf16)
            gz_ref[rows, :] = gz
            up_sum = up_sum + jnp.sum(gz.astype(f32), axis=0, keepdims=True)
            out_ref[...] = dot(gz, w_ref[0]).astype(out_ref.dtype)
        sum_ref[0:1, :] = up_sum
        sum_ref[1:2, :] = jnp.sum(own_gy_ref[...].astype(f32), axis=0, keepdims=True)
        for number, left_ref, rights in (
            (0, gz_ref, (own_c_ref, other_c_ref)),
            (1, act_ref, (own_gy_ref, other_gy_ref)),
        ):
            put_grads(
                place_ref,
                dot_tokens(left_ref[...], both(*rights)),
                lambda block: grad_refs[0].at[block, number],
                lambda block: grad_refs[1].at[block, number],
                halves,
            )

    width = D // 2 if halves else D
    outs = [((half, D), f32), ((half, D), bf16), ((8, D), f32), ((4, 2, COLS, width), f32)]
    if halves:
        outs.append(((4, 2, COLS, width), bf16))
    return call(
        kernel,
        outs,
        place,
        gy_own,
        gy_other,
        c_own,
        c_other,
        preact,
        act,
        weights,
        scratch=[pltpu.VMEM((2 * half, D), bf16)],
    )


def core_swap(block):
    return lax.ppermute(block, "jc", SWAP)


def group_sum(mine, give):
    mine = mine + core_swap(give).astype(f32)
    return mine, lax.ppermute(mine.astype(bf16), "jx", SWAP)


def orthogonalize_kernel(x_ref, gram_ref, out_ref, base_ref, work_ref, mat_ref, low_ref):
    size = x_ref.shape[0]
    rows = 256

    def each(body):
        for start in range(0, size, rows):
            body(pl.ds(start, rows))

    def polynomial():
        low_ref[...] = base_ref[...].astype(bf16)

        def body(block):
            square = dot(low_ref[block, :], low_ref[...])
            mat_ref[block, :] = (
                quintic_two * base_ref[block, :] + quintic_three * square
            ).astype(bf16)

        each(body)

    def two_part(left, right):
        high = left.astype(bf16)
        rest = (left - high.astype(f32)).astype(bf16)
        return dot(high, right) + dot(rest, right)

    trace = jnp.zeros((1, 1), f32)
    for start in range(0, size, rows):
        block = gram_ref[pl.ds(start, rows), pl.ds(start, rows)]
        line = lax.broadcasted_iota(jnp.int32, (rows, rows), 0)
        column = lax.broadcasted_iota(jnp.int32, (rows, rows), 1)
        trace = trace + jnp.sum(jnp.where(line == column, block, 0.0), keepdims=True)
    scale = 1.0 / (jnp.sqrt(trace) + 1e-07)
    base_ref[...] = gram_ref[...] * (scale * scale)
    polynomial()

    def first_step(block):
        value = quintic_one * x_ref[block, :].astype(f32) + dot(mat_ref[block, :], x_ref[...])
        out_ref[block, :] = (scale * value).astype(bf16)
        work_ref[block, :] = quintic_one * base_ref[block, :] + two_part(
            base_ref[block, :], mat_ref[...]
        )

    each(first_step)
    turned = work_ref[...].T
    work_ref[...] = turned

    def gram_step(block):
        base_ref[block, :] = quintic_one * work_ref[block, :] + two_part(
            work_ref[block, :], mat_ref[...]
        )

    each(gram_step)
    polynomial()
    low_ref[...] = out_ref[...]

    def second_step(block):
        value = quintic_one * low_ref[block, :].astype(f32) + dot(mat_ref[block, :], low_ref[...])
        out_ref[block, :] = value.astype(bf16)

    each(second_step)


def orthogonalize(matrix, gram):
    size = matrix.shape[0]
    return pl.pallas_call(
        orthogonalize_kernel,
        out_shape=jax.ShapeDtypeStruct(matrix.shape, bf16),
        in_specs=[pl.BlockSpec(memory_space=pltpu.VMEM)] * 2,
        out_specs=pl.BlockSpec(memory_space=pltpu.VMEM),
        scratch_shapes=[
            pltpu.VMEM((size, size), f32),
            pltpu.VMEM((size, size), f32),
            pltpu.VMEM((size, size), bf16),
            pltpu.VMEM((size, size), bf16),
        ],
        compiler_params=pltpu.CompilerParams(vmem_limit_bytes=48 * 1024 * 1024),
    )(matrix, gram)


def ctx_gram(gram):
    size = lax.axis_size("ctx")

    def shift(block, step):
        moves = [((i + step) % size, i) for i in range(size)]
        return lax.ppermute(block, ("jc", "ctx"), moves)

    rows = gram.shape[0] // size
    blocks = from_own(gram.astype(bf16).reshape(size, rows, -1))
    total = blocks[0].astype(f32)
    for step in (1, 3, 2):
        total = total + shift(blocks[step], -step).astype(f32)
    low = total.astype(bf16)
    full = [low] + [shift(low, step) for step in range(1, size)]
    return to_absolute(jnp.stack(full)).reshape(gram.shape).astype(f32)


def local(hidden_in, segments, out_grad, weights, vectors, mat_momentum, vec_first, vec_second):
    tokens_dev = hidden_in.shape[1]
    seq_len = segments.shape[1]
    half = 2 * tokens_dev
    dp_rows = weights.shape[2]
    ctx_size = lax.axis_size("ctx")
    x_index = lax.axis_index("jx")
    c_index = lax.axis_index("jc")
    t_index = 2 * x_index + c_index
    z_index = lax.axis_index("ctx")
    dp_index = lax.axis_index(DP)
    dp_size = lax.axis_size(DP)

    to_seq = []
    for t in range(TP):
        for z in range(ctx_size):
            to_seq.append((t * ctx_size + z, ((z % 2) * 2 + z // 2) * ctx_size + t))
    from_seq = [(b, a) for a, b in to_seq]
    axes = ("jx", "jc", "ctx")

    def x_join(block):
        return pair_join(block, "jx", 0)

    vec_rows = gather_vectors(vectors)
    seg_row = jnp.pad(segments.astype(f32), ((0, 7), (0, D - seq_len)))
    moved = lax.ppermute(jnp.concatenate([hidden_in[0], seg_row], axis=0), axes, to_seq)
    hidden = x_join(moved[:tokens_dev])
    segment_row = moved[tokens_dev, :seq_len]
    relative = lax.axis_size("g") == 2
    low = weights.astype(bf16)
    place = jnp.stack([z_index, lax.axis_index("g")]).astype(jnp.int32)
    if relative:
        pieces = pack_pieces(low)
        own_attn = ctx_gather(pieces[0][0])
        own_mlp = ctx_gather(after(pieces[0][1], *own_attn[1:]))
        swap_attn = [lax.ppermute(block, "g", SWAP) for block in own_attn]
        attn_weights = (own_attn, swap_attn)
    else:
        wide_weights = gather_weights_wide(low)

    start = c_index * half
    pos = jnp.concatenate([start + jnp.arange(half), half - start + jnp.arange(half)])
    seg = jnp.roll(segment_row.reshape(2, half), -c_index, axis=0).reshape(-1)
    info = jnp.stack([pos.astype(f32), seg])
    row_info = jnp.pad(info, ((0, 6), (0, 0)))
    column_info = jnp.pad(info.T, ((0, 0), (0, 126)))
    vec_mine = lax.dynamic_slice_in_dim(vec_rows, t_index * COLS, COLS, axis=2)
    no_bias = jnp.zeros((LAYERS, 1, COLS), f32)
    qkv_bias = jnp.concatenate([vec_mine[:, 4:5], no_bias, vec_mine[:, 5:6]], axis=2)
    up_bias = vec_mine[:, 8:12].reshape(LAYERS, 1, D)

    stored = []
    (a_own,) = norm_stage(vec_rows, 0, 0, hidden)
    for layer in range(LAYERS):
        following = layer + 1 < LAYERS
        a_other = core_swap(a_own)
        if not relative:
            attn_weights, mlp_weights = wide_weights[layer]
        w_attn, qkv, lse, o, mine, give = attend_stage(
            place, row_info, column_info, qkv_bias[layer], a_own, a_other, attn_weights
        )
        if relative:
            mlp_weights = (own_mlp, [lax.ppermute(jnp.stack(own_mlp), "g", SWAP)])
            if following:
                own_attn = ctx_gather(after(pieces[layer + 1][0], o))
        mine, recv = group_sum(mine, give)
        middle, c_own = norm_stage(vec_rows, layer, 2, hidden, mine, recv, (layer, 6))
        c_other = core_swap(c_own)
        w_mlp, preact, act, mine, give = feed_stage(
            place, up_bias[layer], c_own, c_other, mlp_weights
        )
        if relative and following:
            own_mlp = ctx_gather(after(pieces[layer + 1][1], act, *own_attn[1:]))
            attn_weights = (own_attn, [lax.ppermute(jnp.stack(own_attn), "g", SWAP)])
        mine, recv = group_sum(mine, give)
        stored.append(
            (hidden, middle, a_own, a_other, qkv, lse, o, c_own, c_other, preact, act, w_attn, w_mlp)
        )
        if following:
            hidden, a_own = norm_stage(vec_rows, layer + 1, 0, middle, mine, recv, (layer, 7))
        else:
            hidden = middle + (mine + recv.astype(f32) + vec_rows[layer, 7:8])

    def send_back(rows):
        block = lax.dynamic_slice_in_dim(rows, x_index * tokens_dev, tokens_dev, axis=0)
        return lax.ppermute(block, axes, from_seq)

    hidden_out = send_back(hidden)
    grad_hidden = x_join(lax.ppermute(after(out_grad[0], stored[-1][6]), axes, to_seq))
    gy_own = grad_hidden.astype(bf16)

    mat_list = [None] * LAYERS
    sum_list = [None] * LAYERS
    parts = [None] * LAYERS
    attn_half = None
    for layer in reversed(range(LAYERS)):
        h_in, middle, a_own, a_other, qkv, lse, o, c_own, c_other, preact, act, w_attn, w_mlp = stored[
            layer
        ]
        gy_other = core_swap(gy_own)
        mine, give, up_sums, *mlp_grads = feed_back_stage(
            place, gy_own, gy_other, c_own, c_other, preact, act, w_mlp, relative
        )
        if relative:
            if attn_half is not None:
                mine, attn_half = lax.optimization_barrier((mine, attn_half))
                attn_part = ctx_sum(attn_half)
            mlp_half = half_sum(*mlp_grads)
        mine, recv = group_sum(mine, give)
        grad_middle, gb_own, mid_sums = norm_back_stage(
            vec_rows, layer, 2, grad_hidden, mine, recv, middle
        )
        if relative and attn_half is not None:
            gb_own, mlp_part, attn_part = lax.optimization_barrier((gb_own, mlp_part, attn_part))
            parts[layer + 1] = (attn_part, mlp_part)
        gb_other = core_swap(gb_own)
        mine, give, qkv_sums, *attn_grads = attend_back_stage(
            place,
            row_info,
            column_info,
            gb_own,
            gb_other,
            a_own,
            a_other,
            qkv,
            lse,
            o,
            w_attn,
            relative,
        )
        if relative:
            mine, mlp_half = lax.optimization_barrier((mine, mlp_half))
            mlp_part = ctx_sum(mlp_half)
            attn_half = half_sum(*attn_grads)
        else:
            attn_grad = attn_grads[0]
            g_wo = lax.all_to_all(
                attn_grad[3].reshape(COLS, TP, COLS), GROUP, split_axis=1, concat_axis=0, tiled=True
            )[:, 0]
            attn_grad = jnp.concatenate([attn_grad[:3], g_wo.T[None]], axis=0)
            mat_list[layer] = scatter_wide(
                jnp.concatenate([attn_grad[:, None], mlp_grads[0]], axis=1)
            )
        mine, recv = group_sum(mine, give)
        grad_hidden, gy_own, in_sums = norm_back_stage(
            vec_rows, layer, 0, grad_middle, mine, recv, h_in
        )
        sum_list[layer] = (in_sums, mid_sums, up_sums, qkv_sums)
    input_grad = send_back(grad_hidden)

    if relative:
        parts[0] = (ctx_sum(attn_half), mlp_part)
        for layer in range(LAYERS):
            attn_part, mlp_part = [part.astype(bf16) for part in parts[layer]]
            mat_list[layer] = jnp.concatenate([attn_rows(attn_part)[None], mlp_rows(mlp_part)])
    once = jnp.where(x_index == 0, 1.0, 0.0).astype(f32)
    in_sums, mid_sums, up_sums, qkv_sums = [jnp.stack(sums) for sums in zip(*sum_list)]
    shared = once * jnp.concatenate(
        [in_sums[:, 0:2], mid_sums[:, 0:3], up_sums[:, 1:2]], axis=1
    )
    placed = jnp.concatenate(
        [
            qkv_sums[:, 0:1, :COLS],
            qkv_sums[:, 0:1, 2 * COLS :],
            up_sums[:, 0].reshape(LAYERS, ctx_size, COLS),
        ],
        axis=1,
    )
    placed = lax.dynamic_update_slice_in_dim(
        jnp.zeros((LAYERS, 6, D), f32), placed, t_index * COLS, axis=2
    )
    vec_terms = jnp.concatenate(
        [shared[:, 0:4], placed[:, 0:2], shared[:, 4:6], placed[:, 2:6]], axis=1
    )
    grad_vecs = lax.dynamic_slice_in_dim(
        sum_vectors(vec_terms), dp_index * vectors.shape[2], vectors.shape[2], axis=2
    )
    cols_dev = weights.shape[3]
    grad_list, moment_list, low_list = [], [], []
    for layer in range(LAYERS):
        for item in range(3):
            grad = mat_list[layer][item]
            moment = momentum_decay * mat_momentum[layer, item] + grad
            grad_list.append(grad)
            moment_list.append(moment)
            low_list.append((grad + momentum_decay * moment).astype(bf16))
    wide = [item for item in range(3 * LAYERS) if item % 3]
    squares = [item for item in range(3, 3 * LAYERS, 3)]
    table = []
    for number in range(4):
        table += [wide[number], squares[number % len(squares)]]
    table = (table * (-(-dp_size // 8)))[:dp_size]
    slots = jnp.stack([low_list[item] for item in table])
    received = lax.all_to_all(slots[:, None], DP, split_axis=0, concat_axis=1, tiled=True)
    current = received.reshape(dp_size * dp_rows, cols_dev)
    gram_local = dot_trans(current, current)
    gram = jnp.where(c_index == 0, ctx_gram(gram_local), gram_local)
    ortho_mine = orthogonalize(current, gram)
    returned = lax.all_to_all(
        ortho_mine.reshape(dp_size, 1, dp_rows, cols_dev),
        DP,
        split_axis=0,
        concat_axis=1,
        tiled=True,
    )[0]
    first_full = lax.all_gather(low_list[0], DP, axis=0, tiled=True)
    first_ortho = orthogonalize(first_full, dot_trans(first_full, first_full))
    ortho_list = [lax.dynamic_slice_in_dim(first_ortho, dp_index * dp_rows, dp_rows, axis=0)]
    ortho_list += [returned[table.index(item)] for item in range(1, 3 * LAYERS)]
    ortho = jnp.stack(ortho_list).reshape(LAYERS, 3, dp_rows, cols_dev).astype(f32)
    grad_mats = jnp.stack(grad_list).reshape(weights.shape)
    moment_new = jnp.stack(moment_list).reshape(weights.shape)
    factor = jnp.array([0.2 * math.sqrt(D), 0.2 * math.sqrt(FF), 0.2 * math.sqrt(FF)], f32)
    weights_new = weights * (1.0 - matrix_rate * matrix_decay) - matrix_rate * (
        ortho * factor[None, :, None, None]
    )
    first_new = first_decay * vec_first + (1.0 - first_decay) * grad_vecs
    second_new = second_decay * vec_second + (1.0 - second_decay) * grad_vecs * grad_vecs
    first_hat = first_new / (1.0 - first_decay**ADAM_STEP)
    second_hat = second_new / (1.0 - second_decay**ADAM_STEP)
    vectors_new = vectors * (1.0 - vector_rate * vector_decay) - vector_rate * first_hat / (
        jnp.sqrt(second_hat) + adam_epsilon
    )
    return (
        hidden_out[None],
        input_grad[None],
        grad_mats,
        moment_new,
        weights_new,
        grad_vecs,
        second_new,
        vectors_new,
    )


def solution(mesh):
    dp, ctx = mesh.shape["dp"], mesh.shape["ctx"]
    fine = Mesh(mesh.devices.reshape(dp // TP, 2, 2, ctx), EVERY)
    tokens = P(DP, "ctx", None)
    mats = P(None, None, DP, "ctx")
    vecs = P(None, "ctx", DP)
    return jax.shard_map(
        local,
        mesh=fine,
        in_specs=(tokens, P(DP, None), tokens, mats, vecs, mats, vecs, vecs),
        out_specs=(tokens, tokens, mats, mats, mats, vecs, vecs, vecs),
        check_vma=False,
    )
```

```python
import math

import jax
import jax.numpy as jnp
from jax import lax
from jax.experimental import pallas as pl
from jax.experimental.pallas import tpu as pltpu
from jax.sharding import Mesh, PartitionSpec as P

D = 768
HEADS = 12
HEAD = 64
FF = 3072
LAYERS = 2
ADAM_STEP = 10
TP = 4
COLS = D // TP
TP_HEADS = HEADS // TP

norm_epsilon = 1e-05
quintic_one = 3.4445
quintic_two = -4.775
quintic_three = 2.0315
momentum_decay = 0.95
matrix_rate = 0.6
matrix_decay = 0.01
first_decay = 0.9
second_decay = 0.999
vector_rate = 0.5
vector_decay = 0.01
adam_epsilon = 1e-08
masked_score = -1e30

GROUP = ("jx", "jc")
REPLICAS = ("g", "ctx")
DP = ("g", "jx", "jc")
EVERY = ("g", "jx", "jc", "ctx")
SWAP = [(0, 1), (1, 0)]
bf16 = jnp.bfloat16
f32 = jnp.float32


def dot(operand, other):
    return jnp.dot(operand, other, preferred_element_type=f32)


def dot_tokens(operand, other):
    return lax.dot_general(operand, other, (((0,), (0,)), ((), ())), preferred_element_type=f32)


def dot_trans(operand, other):
    return lax.dot_general(operand, other, (((1,), (1,)), ((), ())), preferred_element_type=f32)


def to_group(mats):
    count, rows, width = mats.shape
    split = mats.reshape(count, rows, TP, width // TP)
    return lax.all_to_all(split, GROUP, split_axis=2, concat_axis=1, tiled=True)[:, :, 0]


def from_group(mats):
    count, rows, width = mats.shape
    split = mats.reshape(count, TP, rows // TP, width)
    return lax.all_to_all(split, GROUP, split_axis=1, concat_axis=3, tiled=True)[:, 0]


def rotate(block, axis, step):
    size = lax.axis_size(axis)
    return lax.ppermute(block, axis, [((i + step) % size, i) for i in range(size)])


def pair_join(block, axis, dim):
    other = lax.ppermute(block, axis, SWAP)
    first = lax.axis_index(axis) == 0
    return jnp.concatenate(
        [jnp.where(first, block, other), jnp.where(first, other, block)], axis=dim
    )


def after(value, *others):
    return lax.optimization_barrier((value, *others))[0]


def roll_blocks(stack, sign):
    place = lax.axis_index("ctx")
    for bit in (1, 2):
        moved = jnp.roll(stack, sign * bit, axis=0)
        stack = jnp.where((place & bit) != 0, moved, stack)
    return stack


def from_own(stack):
    return roll_blocks(stack, -1)


def to_absolute(stack):
    return roll_blocks(stack, 1)


def out_moves():
    last = lax.axis_size("ctx") - 1
    size = last + 1
    moves = []
    for y in range(2):
        for x in range(2):
            for core in range(2):
                moves.append(
                    ((4 * y + 2 * x + core) * size + last, (4 * core + 2 * y + x) * size + last)
                )
    return moves


def out_pieces(mats):
    half = mats.shape[2] // 2
    core = lax.axis_index("jc")
    mine = lax.dynamic_slice_in_dim(mats, core * half, half, axis=2)
    give = lax.dynamic_slice_in_dim(mats, (1 - core) * half, half, axis=2)
    got = lax.ppermute(give, "jc", SWAP)
    rows = jnp.concatenate(
        [jnp.where(core == 0, mine, got), jnp.where(core == 0, got, mine)], axis=1
    )
    return lax.ppermute(rows, EVERY, out_moves())


def out_back(piece):
    core = lax.axis_index("jc")
    rows = lax.ppermute(piece, EVERY, [(b, a) for a, b in out_moves()])
    half = rows.shape[0] // 2
    mine = lax.dynamic_slice_in_dim(rows, core * half, half, axis=0)
    give = lax.dynamic_slice_in_dim(rows, (1 - core) * half, half, axis=0)
    got = lax.ppermute(give, "jc", SWAP)
    return jnp.concatenate(
        [jnp.where(core == 0, mine, got), jnp.where(core == 0, got, mine)], axis=1
    )


def pack_pieces(mats):
    attn = mats[:, 0].astype(bf16)
    outs = out_pieces(attn)
    first = to_group(attn[0:1])
    rest = [mats[0, 1:3]] + [mats[layer] for layer in range(1, mats.shape[0])]
    rest = to_group(after(jnp.concatenate(rest), first).astype(bf16))
    last = lax.axis_index("ctx") == lax.axis_size("ctx") - 1
    pieces = [(jnp.where(last, outs[0], first[0].T), jnp.swapaxes(rest[0:2], 1, 2))]
    for layer in range(1, mats.shape[0]):
        base = 3 * layer - 1
        pieces.append(
            (
                jnp.where(last, outs[layer], rest[base].T),
                jnp.swapaxes(rest[base + 1 : base + 3], 1, 2),
            )
        )
    return pieces


def ctx_gather(piece):
    near, back, far = [rotate(piece, "ctx", step) for step in (1, 3, 2)]
    return [piece, near, far, back]


def group_swap(blocks):
    return [lax.ppermute(block, "g", SWAP) for block in blocks]


def gather_weights_wide(low):
    result = []
    for layer in range(low.shape[0]):
        mats = to_group(low[layer])
        parts = lax.all_gather(mats, REPLICAS, axis=0, tiled=False)
        parts = parts.reshape(lax.axis_size("g"), -1, *mats.shape)
        full = [parts[:, :, item].transpose(1, 3, 0, 2).reshape(D, D) for item in range(3)]
        w_o = lax.all_to_all(
            full[0][3 * COLS :].T.reshape(TP, COLS, COLS),
            GROUP,
            split_axis=0,
            concat_axis=2,
            tiled=True,
        )
        attn = jnp.concatenate([full[0][: 3 * COLS].reshape(3, COLS, D), w_o], axis=0)
        result.append((attn.reshape(D, D), jnp.stack([full[1], full[2]])))
    return result


def half_sum(mine, give):
    return mine + lax.ppermute(give, "g", SWAP).astype(f32)


def ctx_sum(blocks):
    total = blocks[0]
    for step in (1, 3, 2):
        total = total + rotate(blocks[step].astype(bf16), "ctx", -step).astype(f32)
    return total


def attn_rows(part):
    columns = from_group(part.T[None])[0]
    last = lax.axis_index("ctx") == lax.axis_size("ctx") - 1
    return jnp.where(last, out_back(part), columns).astype(f32)


def mlp_rows(part):
    return from_group(jnp.swapaxes(part, 1, 2)).astype(f32)


def scatter_wide(mats):
    groups = lax.axis_size("g")
    blocks, count, width, depth = mats.shape
    stack = mats.astype(bf16).reshape(blocks, count, width, groups, depth // groups)
    stack = stack.transpose(3, 0, 1, 4, 2).reshape(groups * blocks, count, -1, width)
    part = lax.psum_scatter(stack, REPLICAS, scatter_dimension=0, tiled=True)[0]
    return from_group(part).astype(f32)


def gather_vectors(vectors):
    low = vectors.astype(bf16)
    stack = jnp.stack([low] + [rotate(low, "ctx", step) for step in range(1, 4)])
    stack = pair_join(pair_join(to_absolute(stack), "jc", 3), "jx", 3)
    if lax.axis_size("g") == 2:
        stack = pair_join(stack, "g", 3)
    else:
        stack = lax.all_gather(stack, "g", axis=3, tiled=True)
    return stack.transpose(1, 0, 2, 3).reshape(low.shape[0], -1, D).astype(f32)


def sum_vectors(terms):
    if lax.axis_size("g") == 2:
        terms = terms + lax.ppermute(terms, "g", SWAP)
    else:
        terms = lax.psum(terms, "g")
    layers, rows, width = terms.shape
    blocks = from_own(terms.reshape(layers, 4, rows // 4, width).transpose(1, 0, 2, 3))
    total = blocks[0]
    for step in range(1, 4):
        total = total + rotate(blocks[step], "ctx", -step)
    total = total + lax.ppermute(total, "jc", SWAP)
    return total + lax.ppermute(total, "jx", SWAP)


def call(kernel, outs, *args, scratch=()):
    return pl.pallas_call(
        kernel,
        out_shape=[jax.ShapeDtypeStruct(shape, kind) for shape, kind in outs],
        in_specs=[pl.BlockSpec(memory_space=pltpu.SMEM)]
        + [pl.BlockSpec(memory_space=pltpu.VMEM)] * (len(args) - 1),
        out_specs=[pl.BlockSpec(memory_space=pltpu.VMEM)] * len(outs),
        scratch_shapes=list(scratch),
        compiler_params=pltpu.CompilerParams(vmem_limit_bytes=52 * 1024 * 1024),
    )(*args)


def block_at(place_ref, step):
    ahead = place_ref[0] + step
    return jnp.where(ahead >= 4, ahead - 4, ahead)


def put_blocks(place_ref, own_refs, other_refs, full_refs):
    half = D // 2
    mine = pl.multiple_of(place_ref[1] * half, half)
    theirs = pl.multiple_of((1 - place_ref[1]) * half, half)
    for step in range(4):
        rows = pl.ds(pl.multiple_of(block_at(place_ref, step) * COLS, COLS), COLS)
        for number, full_ref in enumerate(full_refs):
            own, other = own_refs[step], other_refs[step]
            if len(full_refs) > 1:
                own, other = own.at[number], other.at[number]
            full_ref[rows, pl.ds(mine, half)] = own[...]
            full_ref[rows, pl.ds(theirs, half)] = other[...]


def put_grads(place_ref, grad, mine_refs, give_refs, halves):
    half = D // 2
    for block in range(4):
        rows = grad[block * COLS : (block + 1) * COLS]
        if halves:
            back = block - place_ref[0]
            back = jnp.where(back < 0, back + 4, back)
            low = place_ref[1] == 0
            mine_refs(back)[...] = jnp.where(low, rows[:, :half], rows[:, half:])
            give_refs(back)[...] = jnp.where(low, rows[:, half:], rows[:, :half]).astype(bf16)
        else:
            mine_refs(block)[...] = rows


def norm_rows(hidden):
    center = hidden - jnp.mean(hidden, axis=-1, keepdims=True)
    variance = jnp.mean(center * center, axis=-1, keepdims=True)
    inverse = lax.rsqrt(variance + norm_epsilon)
    return center * inverse, inverse


def norm_stage(vecs, layer, row, hidden, mine=None, recv=None, bias=None):
    rows = hidden.shape[0]

    def kernel(unused, vec_ref, hidden_ref, *refs):
        total = hidden_ref[...]
        if mine is not None:
            mine_ref, recv_ref, total_ref, out_ref = refs
            bias_row = vec_ref[bias[0], bias[1] : bias[1] + 1, :]
            total = total + (mine_ref[...] + recv_ref[...].astype(f32) + bias_row)
            total_ref[...] = total
        else:
            (out_ref,) = refs
        normed, unused_scale = norm_rows(total)
        gain = vec_ref[layer, row : row + 1, :]
        shift = vec_ref[layer, row + 1 : row + 2, :]
        out_ref[...] = (normed * gain + shift).astype(bf16)

    outs = [((rows, D), bf16)]
    args = [hidden]
    if mine is not None:
        outs = [((rows, D), f32)] + outs
        args += [mine, recv]
    return call(kernel, outs, jnp.zeros((1,), jnp.int32), vecs, *args)


def norm_back_stage(vecs, layer, row, grad, mine, recv, hidden):
    rows = hidden.shape[0]

    def kernel(unused, vec_ref, grad_ref, mine_ref, recv_ref, hidden_ref, out_ref, low_ref, sum_ref):
        through = mine_ref[...] + recv_ref[...].astype(f32)
        normed, inverse = norm_rows(hidden_ref[...])
        scaled = through * vec_ref[layer, row : row + 1, :]
        part = jnp.mean(scaled, axis=-1, keepdims=True)
        part = part + normed * jnp.mean(scaled * normed, axis=-1, keepdims=True)
        total = grad_ref[...] + inverse * (scaled - part)
        out_ref[...] = total
        low = total.astype(bf16)
        low_ref[...] = low
        sum_ref[0:1, :] = jnp.sum(through * normed, axis=0, keepdims=True)
        sum_ref[1:2, :] = jnp.sum(through, axis=0, keepdims=True)
        sum_ref[2:3, :] = jnp.sum(low.astype(f32), axis=0, keepdims=True)

    outs = [((rows, D), f32), ((rows, D), bf16), ((8, D), f32)]
    return call(kernel, outs, jnp.zeros((1,), jnp.int32), vecs, grad, mine, recv, hidden)


def both(first_ref, second_ref):
    return jnp.concatenate([first_ref[...], second_ref[...]], axis=0)


def allowed_of(row_ref, column_ref):
    before = row_ref[0:1, :] <= column_ref[:, 0:1]
    return before & (row_ref[1:2, :] == column_ref[:, 1:2])


def attend_stage(place, row_info, column_info, bias, a_own, a_other, weights):
    half = a_own.shape[0]
    tokens = 2 * half
    wide = 3 * COLS
    own, other = weights if isinstance(weights, tuple) else ([], [])

    def kernel(place_ref, row_ref, column_ref, bias_ref, own_a_ref, other_a_ref, *refs):
        if own:
            own_refs, refs = refs[:4], refs[4:]
            others, refs = refs[:4], refs[4:]
            w_ref, qkv_ref, lse_ref, o_ref, mine_ref, give_ref = refs
            put_blocks(place_ref, own_refs, others, [w_ref])
        else:
            w_ref, qkv_ref, lse_ref, o_ref, mine_ref, give_ref = refs
        for start, a_ref in ((0, own_a_ref), (half, other_a_ref)):
            proj = dot_trans(a_ref[...], w_ref[0:wide, :]) + bias_ref[0:1, :]
            qkv_ref[start : start + half, :] = proj.astype(bf16)
        allowed = allowed_of(row_ref, column_ref)
        for head in range(TP_HEADS):
            lanes = head * HEAD
            k = qkv_ref[:, COLS + lanes : COLS + lanes + HEAD]
            v = qkv_ref[:, 2 * COLS + lanes : 2 * COLS + lanes + HEAD]
            for start in (0, half):
                rows = slice(start, start + half)
                q = qkv_ref[rows, lanes : lanes + HEAD]
                scores = jnp.where(allowed[rows], dot_trans(q, k) * HEAD ** (-0.5), masked_score)
                top = jnp.max(scores, axis=-1, keepdims=True)
                unnormed = jnp.exp(scores - top)
                total = jnp.sum(unnormed, axis=-1, keepdims=True)
                prob = (unnormed * (1.0 / total)).astype(bf16)
                o_ref[rows, lanes : lanes + HEAD] = dot(prob, v).astype(bf16)
                lse_ref[rows, head : head + 1] = top + jnp.log(total)
        mine_ref[...] = dot(o_ref[0:half, :], w_ref[wide:, :])
        give_ref[...] = dot(o_ref[half:, :], w_ref[wide:, :]).astype(bf16)

    outs = [
        ((tokens, wide), bf16),
        ((tokens, 128), f32),
        ((tokens, COLS), bf16),
        ((half, D), f32),
        ((half, D), bf16),
    ]
    if own:
        outs = [((D, D), bf16)] + outs
        return call(
            kernel, outs, place, row_info, column_info, bias, a_own, a_other, *own, *other
        )
    result = call(kernel, outs, place, row_info, column_info, bias, a_own, a_other, weights)
    return [weights] + list(result)


def attend_back_stage(
    place, row_info, column_info, gb_own, gb_other, a_own, a_other, qkv, lse, o, w_attn, halves
):
    half = a_own.shape[0]
    tokens = 2 * half
    wide = 3 * COLS

    def kernel(
        place_ref,
        row_ref,
        column_ref,
        own_gb_ref,
        other_gb_ref,
        own_a_ref,
        other_a_ref,
        qkv_ref,
        lse_ref,
        o_ref,
        w_ref,
        mine_ref,
        give_ref,
        sum_ref,
        *refs,
    ):
        *grad_refs, go_ref, all_ref = refs
        w_o = w_ref[wide:, :]
        for start, gb_ref in ((0, own_gb_ref), (half, other_gb_ref)):
            go_ref[start : start + half, :] = dot_trans(gb_ref[...], w_o).astype(bf16)
        allowed = allowed_of(row_ref, column_ref)
        for head in range(TP_HEADS):
            lanes = head * HEAD
            q_lanes = slice(lanes, lanes + HEAD)
            k_lanes = slice(COLS + lanes, COLS + lanes + HEAD)
            v_lanes = slice(2 * COLS + lanes, 2 * COLS + lanes + HEAD)
            k = qkv_ref[:, k_lanes]
            v = qkv_ref[:, v_lanes]
            gk = jnp.zeros((tokens, HEAD), f32)
            gv = jnp.zeros((tokens, HEAD), f32)
            for start in (0, half):
                rows = slice(start, start + half)
                q = qkv_ref[rows, q_lanes]
                go = go_ref[rows, q_lanes]
                scores = jnp.where(allowed[rows], dot_trans(q, k) * HEAD ** (-0.5), masked_score)
                prob = jnp.exp(scores - lse_ref[rows, head : head + 1])
                g_prob = dot_trans(go, v)
                row_dot = jnp.sum(g_prob * prob, axis=-1, keepdims=True)
                g_scores = (prob * (g_prob - row_dot)).astype(bf16)
                all_ref[rows, q_lanes] = (dot(g_scores, k) * HEAD ** (-0.5)).astype(bf16)
                gk = gk + dot_tokens(g_scores, q)
                gv = gv + dot_tokens(prob.astype(bf16), go)
            all_ref[:, k_lanes] = (gk * HEAD ** (-0.5)).astype(bf16)
            all_ref[:, v_lanes] = gv.astype(bf16)
        mine_ref[...] = dot(all_ref[0:half, :], w_ref[0:wide, :])
        give_ref[...] = dot(all_ref[half:, :], w_ref[0:wide, :]).astype(bf16)
        sum_ref[0:1, :] = jnp.sum(all_ref[...].astype(f32), axis=0, keepdims=True)
        grad = jnp.concatenate(
            [
                dot_tokens(all_ref[...], both(own_a_ref, other_a_ref)),
                dot_tokens(o_ref[...], both(own_gb_ref, other_gb_ref)),
            ],
            axis=0,
        )
        put_grads(
            place_ref,
            grad,
            lambda block: grad_refs[0].at[block],
            lambda block: grad_refs[1].at[block],
            halves,
        )

    width = D // 2 if halves else D
    outs = [((half, D), f32), ((half, D), bf16), ((8, wide), f32), ((4, COLS, width), f32)]
    if halves:
        outs.append(((4, COLS, width), bf16))
    return call(
        kernel,
        outs,
        place,
        row_info,
        column_info,
        gb_own,
        gb_other,
        a_own,
        a_other,
        qkv,
        lse,
        o,
        w_attn,
        scratch=[pltpu.VMEM((tokens, COLS), bf16), pltpu.VMEM((tokens, wide), bf16)],
    )


def tanh_part(preact):
    inner = math.sqrt(2.0 / math.pi) * (preact + 0.044715 * (preact * preact * preact))
    return jnp.tanh(inner)


def feed_stage(place, bias, c_own, c_other, weights):
    half = c_own.shape[0]
    own, other = weights if isinstance(weights, tuple) else ([], [])

    def kernel(place_ref, bias_ref, own_c_ref, other_c_ref, *refs):
        if own:
            own_refs, others, refs = refs[:4], refs[4:8], refs[8:]
            w_ref, preact_ref, act_ref, mine_ref, give_ref = refs
            put_blocks(place_ref, own_refs, others, [w_ref.at[0], w_ref.at[1]])
        else:
            w_ref, preact_ref, act_ref, mine_ref, give_ref = refs
        for start, c_ref, out_ref in ((0, own_c_ref, mine_ref), (half, other_c_ref, give_ref)):
            rows = slice(start, start + half)
            preact = dot_trans(c_ref[...], w_ref[0]) + bias_ref[...]
            preact_ref[rows, :] = preact
            act = (0.5 * preact * (1.0 + tanh_part(preact))).astype(bf16)
            act_ref[rows, :] = act
            out_ref[...] = dot(act, w_ref[1]).astype(out_ref.dtype)

    outs = [
        ((2 * half, D), f32),
        ((2 * half, D), bf16),
        ((half, D), f32),
        ((half, D), bf16),
    ]
    if own:
        outs = [((2, D, D), bf16)] + outs
        return call(kernel, outs, place, bias, c_own, c_other, *own, *other)
    return [weights] + list(call(kernel, outs, place, bias, c_own, c_other, weights))


def feed_back_stage(place, gy_own, gy_other, c_own, c_other, preact, act, weights, halves):
    half = c_own.shape[0]

    def kernel(
        place_ref,
        own_gy_ref,
        other_gy_ref,
        own_c_ref,
        other_c_ref,
        preact_ref,
        act_ref,
        w_ref,
        mine_ref,
        give_ref,
        sum_ref,
        *refs,
    ):
        *grad_refs, gz_ref = refs
        up_sum = jnp.zeros((1, D), f32)
        for start, gy_ref, out_ref in ((0, own_gy_ref, mine_ref), (half, other_gy_ref, give_ref)):
            rows = slice(start, start + half)
            gu = dot_trans(gy_ref[...], w_ref[1])
            x = preact_ref[rows, :]
            tanh = tanh_part(x)
            slope = math.sqrt(2.0 / math.pi) * (1.0 + 3.0 * 0.044715 * (x * x))
            factor = 0.5 * (1.0 + tanh) + 0.5 * x * (1.0 - tanh * tanh) * slope
            gz = (gu * factor).astype(bf16)
            gz_ref[rows, :] = gz
            up_sum = up_sum + jnp.sum(gz.astype(f32), axis=0, keepdims=True)
            out_ref[...] = dot(gz, w_ref[0]).astype(out_ref.dtype)
        sum_ref[0:1, :] = up_sum
        sum_ref[1:2, :] = jnp.sum(own_gy_ref[...].astype(f32), axis=0, keepdims=True)
        for number, left_ref, rights in (
            (0, gz_ref, (own_c_ref, other_c_ref)),
            (1, act_ref, (own_gy_ref, other_gy_ref)),
        ):
            put_grads(
                place_ref,
                dot_tokens(left_ref[...], both(*rights)),
                lambda block: grad_refs[0].at[block, number],
                lambda block: grad_refs[1].at[block, number],
                halves,
            )

    width = D // 2 if halves else D
    outs = [((half, D), f32), ((half, D), bf16), ((8, D), f32), ((4, 2, COLS, width), f32)]
    if halves:
        outs.append(((4, 2, COLS, width), bf16))
    return call(
        kernel,
        outs,
        place,
        gy_own,
        gy_other,
        c_own,
        c_other,
        preact,
        act,
        weights,
        scratch=[pltpu.VMEM((2 * half, D), bf16)],
    )


def core_swap(block):
    return lax.ppermute(block, "jc", SWAP)


def group_sum(mine, give):
    mine = mine + core_swap(give).astype(f32)
    return mine, lax.ppermute(mine.astype(bf16), "jx", SWAP)


def orthogonalize_kernel(x_ref, gram_ref, out_ref, base_ref, work_ref, mat_ref, low_ref):
    size = x_ref.shape[0]
    rows = 256

    def each(body):
        for start in range(0, size, rows):
            body(pl.ds(start, rows))

    def polynomial():
        low_ref[...] = base_ref[...].astype(bf16)

        def body(block):
            square = dot(low_ref[block, :], low_ref[...])
            mat_ref[block, :] = (
                quintic_two * base_ref[block, :] + quintic_three * square
            ).astype(bf16)

        each(body)

    def two_part(left, right):
        high = left.astype(bf16)
        rest = (left - high.astype(f32)).astype(bf16)
        return dot(high, right) + dot(rest, right)

    trace = jnp.zeros((1, 1), f32)
    for start in range(0, size, rows):
        block = gram_ref[pl.ds(start, rows), pl.ds(start, rows)]
        line = lax.broadcasted_iota(jnp.int32, (rows, rows), 0)
        column = lax.broadcasted_iota(jnp.int32, (rows, rows), 1)
        trace = trace + jnp.sum(jnp.where(line == column, block, 0.0), keepdims=True)
    scale = 1.0 / (jnp.sqrt(trace) + 1e-07)
    base_ref[...] = gram_ref[...] * (scale * scale)
    polynomial()

    def first_step(block):
        value = quintic_one * x_ref[block, :].astype(f32) + dot(mat_ref[block, :], x_ref[...])
        out_ref[block, :] = (scale * value).astype(bf16)
        work_ref[block, :] = quintic_one * base_ref[block, :] + two_part(
            base_ref[block, :], mat_ref[...]
        )

    each(first_step)
    turned = work_ref[...].T
    work_ref[...] = turned

    def gram_step(block):
        base_ref[block, :] = quintic_one * work_ref[block, :] + two_part(
            work_ref[block, :], mat_ref[...]
        )

    each(gram_step)
    polynomial()
    low_ref[...] = out_ref[...]

    def second_step(block):
        value = quintic_one * low_ref[block, :].astype(f32) + dot(mat_ref[block, :], low_ref[...])
        out_ref[block, :] = value.astype(bf16)

    each(second_step)


def orthogonalize(matrix, gram):
    size = matrix.shape[0]
    return pl.pallas_call(
        orthogonalize_kernel,
        out_shape=jax.ShapeDtypeStruct(matrix.shape, bf16),
        in_specs=[pl.BlockSpec(memory_space=pltpu.VMEM)] * 2,
        out_specs=pl.BlockSpec(memory_space=pltpu.VMEM),
        scratch_shapes=[
            pltpu.VMEM((size, size), f32),
            pltpu.VMEM((size, size), f32),
            pltpu.VMEM((size, size), bf16),
            pltpu.VMEM((size, size), bf16),
        ],
        compiler_params=pltpu.CompilerParams(vmem_limit_bytes=48 * 1024 * 1024),
    )(matrix, gram)


def ctx_gram(gram):
    size = lax.axis_size("ctx")

    def shift(block, step):
        moves = [((i + step) % size, i) for i in range(size)]
        return lax.ppermute(block, ("jc", "ctx"), moves)

    rows = gram.shape[0] // size
    blocks = from_own(gram.astype(bf16).reshape(size, rows, -1))
    total = blocks[0].astype(f32)
    for step in (1, 3, 2):
        total = total + shift(blocks[step], -step).astype(f32)
    low = total.astype(bf16)
    full = [low] + [shift(low, step) for step in range(1, size)]
    return to_absolute(jnp.stack(full)).reshape(gram.shape).astype(f32)


def local(hidden_in, segments, out_grad, weights, vectors, mat_momentum, vec_first, vec_second):
    tokens_dev = hidden_in.shape[1]
    seq_len = segments.shape[1]
    half = 2 * tokens_dev
    dp_rows = weights.shape[2]
    ctx_size = lax.axis_size("ctx")
    x_index = lax.axis_index("jx")
    c_index = lax.axis_index("jc")
    t_index = 2 * x_index + c_index
    z_index = lax.axis_index("ctx")
    dp_index = lax.axis_index(DP)
    dp_size = lax.axis_size(DP)

    to_seq = []
    for t in range(TP):
        for z in range(ctx_size):
            to_seq.append((t * ctx_size + z, ((z % 2) * 2 + z // 2) * ctx_size + t))
    from_seq = [(b, a) for a, b in to_seq]
    axes = ("jx", "jc", "ctx")

    def x_join(block):
        return pair_join(block, "jx", 0)

    vec_rows = gather_vectors(vectors)
    seg_row = jnp.pad(segments.astype(f32), ((0, 7), (0, D - seq_len)))
    moved = lax.ppermute(jnp.concatenate([hidden_in[0], seg_row], axis=0), axes, to_seq)
    hidden = x_join(moved[:tokens_dev])
    segment_row = moved[tokens_dev, :seq_len]
    relative = lax.axis_size("g") == 2
    place = jnp.stack([z_index, lax.axis_index("g")]).astype(jnp.int32)
    if relative:
        pieces = pack_pieces(weights)
        own_attn = ctx_gather(pieces[0][0])
        own_mlp = ctx_gather(after(pieces[0][1], *own_attn[1:]))
        attn_weights = (own_attn, group_swap(own_attn))
        mlp_weights = (own_mlp, group_swap(own_mlp))
    else:
        wide_weights = gather_weights_wide(weights.astype(bf16))

    start = c_index * half
    pos = jnp.concatenate([start + jnp.arange(half), half - start + jnp.arange(half)])
    seg = jnp.roll(segment_row.reshape(2, half), -c_index, axis=0).reshape(-1)
    info = jnp.stack([pos.astype(f32), seg])
    row_info = jnp.pad(info, ((0, 6), (0, 0)))
    column_info = jnp.pad(info.T, ((0, 0), (0, 126)))
    vec_mine = lax.dynamic_slice_in_dim(vec_rows, t_index * COLS, COLS, axis=2)
    no_bias = jnp.zeros((LAYERS, 1, COLS), f32)
    qkv_bias = jnp.concatenate([vec_mine[:, 4:5], no_bias, vec_mine[:, 5:6]], axis=2)
    up_bias = vec_mine[:, 8:12].reshape(LAYERS, 1, D)

    stored = []
    (a_own,) = norm_stage(vec_rows, 0, 0, hidden)
    for layer in range(LAYERS):
        following = layer + 1 < LAYERS
        a_other = core_swap(a_own)
        if not relative:
            attn_weights, mlp_weights = wide_weights[layer]
        w_attn, qkv, lse, o, mine, give = attend_stage(
            place, row_info, column_info, qkv_bias[layer], a_own, a_other, attn_weights
        )
        if relative and layer:
            mine, own_mlp = lax.optimization_barrier((mine, own_mlp))
            mlp_weights = (own_mlp, group_swap(own_mlp))
        if relative and following:
            next_attn = ctx_gather(after(pieces[layer + 1][0], *own_mlp[1:]))
            next_mlp = ctx_gather(after(pieces[layer + 1][1], *next_attn[1:]))
        mine, recv = group_sum(mine, give)
        middle, c_own = norm_stage(vec_rows, layer, 2, hidden, mine, recv, (layer, 6))
        if relative and following:
            c_own, next_attn = lax.optimization_barrier((c_own, next_attn))
        c_other = core_swap(c_own)
        w_mlp, preact, act, mine, give = feed_stage(
            place, up_bias[layer], c_own, c_other, mlp_weights
        )
        if relative and following:
            attn_weights = (next_attn, group_swap(next_attn))
            own_mlp = next_mlp
        mine, recv = group_sum(mine, give)
        stored.append(
            (hidden, middle, a_own, a_other, qkv, lse, o, c_own, c_other, preact, act, w_attn, w_mlp)
        )
        if following:
            hidden, a_own = norm_stage(vec_rows, layer + 1, 0, middle, mine, recv, (layer, 7))
        else:
            hidden = middle + (mine + recv.astype(f32) + vec_rows[layer, 7:8])

    def send_back(rows):
        block = lax.dynamic_slice_in_dim(rows, x_index * tokens_dev, tokens_dev, axis=0)
        return lax.ppermute(block, axes, from_seq)

    hidden_out = send_back(hidden)
    grad_hidden = x_join(lax.ppermute(after(out_grad[0], stored[-1][6]), axes, to_seq))
    gy_own = grad_hidden.astype(bf16)
    attn_half = mlp_part = None

    mat_list = [None] * LAYERS
    sum_list = [None] * LAYERS
    parts = [None] * LAYERS
    for layer in reversed(range(LAYERS)):
        h_in, middle, a_own, a_other, qkv, lse, o, c_own, c_other, preact, act, w_attn, w_mlp = stored[
            layer
        ]
        if relative and attn_half is not None:
            gy_own, attn_half, mlp_part = lax.optimization_barrier((gy_own, attn_half, mlp_part))
            attn_part = ctx_sum(attn_half)
        gy_other = core_swap(gy_own)
        mine, give, up_sums, *mlp_grads = feed_back_stage(
            place, gy_own, gy_other, c_own, c_other, preact, act, w_mlp, relative
        )
        if relative:
            mlp_half = half_sum(*mlp_grads)
        mine, recv = group_sum(mine, give)
        grad_middle, gb_own, mid_sums = norm_back_stage(
            vec_rows, layer, 2, grad_hidden, mine, recv, middle
        )
        if relative and attn_half is not None:
            gb_own, attn_part = lax.optimization_barrier((gb_own, attn_part))
            parts[layer + 1] = (attn_part, mlp_part)
        if layer == LAYERS - 1:
            gb_own, hidden_out = lax.optimization_barrier((gb_own, hidden_out))
        gb_other = core_swap(gb_own)
        mine, give, qkv_sums, *attn_grads = attend_back_stage(
            place,
            row_info,
            column_info,
            gb_own,
            gb_other,
            a_own,
            a_other,
            qkv,
            lse,
            o,
            w_attn,
            relative,
        )
        if relative:
            mine, mlp_half = lax.optimization_barrier((mine, mlp_half))
            mlp_part = ctx_sum(mlp_half)
            attn_half = half_sum(*attn_grads)
        else:
            attn_grad = attn_grads[0]
            g_wo = lax.all_to_all(
                attn_grad[3].reshape(COLS, TP, COLS), GROUP, split_axis=1, concat_axis=0, tiled=True
            )[:, 0]
            attn_grad = jnp.concatenate([attn_grad[:3], g_wo.T[None]], axis=0)
            mat_list[layer] = scatter_wide(
                jnp.concatenate([attn_grad[:, None], mlp_grads[0]], axis=1)
            )
        mine, recv = group_sum(mine, give)
        grad_hidden, gy_own, in_sums = norm_back_stage(
            vec_rows, layer, 0, grad_middle, mine, recv, h_in
        )
        sum_list[layer] = (in_sums, mid_sums, up_sums, qkv_sums)
    input_grad = send_back(grad_hidden)

    if relative:
        parts[0] = (ctx_sum(attn_half), mlp_part)
        for layer in range(LAYERS):
            attn_part, mlp_part = [
                after(part, grad_hidden).astype(bf16) for part in parts[layer]
            ]
            mat_list[layer] = jnp.concatenate([attn_rows(attn_part)[None], mlp_rows(mlp_part)])
    once = jnp.where(x_index == 0, 1.0, 0.0).astype(f32)
    in_sums, mid_sums, up_sums, qkv_sums = [jnp.stack(sums) for sums in zip(*sum_list)]
    shared = once * jnp.concatenate(
        [in_sums[:, 0:2], mid_sums[:, 0:3], up_sums[:, 1:2]], axis=1
    )
    placed = jnp.concatenate(
        [
            qkv_sums[:, 0:1, :COLS],
            qkv_sums[:, 0:1, 2 * COLS :],
            up_sums[:, 0].reshape(LAYERS, ctx_size, COLS),
        ],
        axis=1,
    )
    placed = lax.dynamic_update_slice_in_dim(
        jnp.zeros((LAYERS, 6, D), f32), placed, t_index * COLS, axis=2
    )
    vec_terms = jnp.concatenate(
        [shared[:, 0:4], placed[:, 0:2], shared[:, 4:6], placed[:, 2:6]], axis=1
    )
    grad_vecs = lax.dynamic_slice_in_dim(
        sum_vectors(vec_terms), dp_index * vectors.shape[2], vectors.shape[2], axis=2
    )
    cols_dev = weights.shape[3]
    grad_list, moment_list, low_list = [], [], []
    for layer in range(LAYERS):
        for item in range(3):
            grad = mat_list[layer][item]
            moment = momentum_decay * mat_momentum[layer, item] + grad
            grad_list.append(grad)
            moment_list.append(moment)
            low_list.append((grad + momentum_decay * moment).astype(bf16))
    wide = [item for item in range(3 * LAYERS) if item % 3]
    squares = [item for item in range(3, 3 * LAYERS, 3)]
    table = []
    for number in range(4):
        table += [wide[number], squares[number % len(squares)]]
    table = (table * (-(-dp_size // 8)))[:dp_size]
    slots = jnp.stack([low_list[item] for item in table])
    received = lax.all_to_all(slots[:, None], DP, split_axis=0, concat_axis=1, tiled=True)
    current = received.reshape(dp_size * dp_rows, cols_dev)
    gram_local = dot_trans(current, current)
    gram = jnp.where(c_index == 0, ctx_gram(gram_local), gram_local)
    ortho_mine = orthogonalize(current, gram)
    returned = lax.all_to_all(
        ortho_mine.reshape(dp_size, 1, dp_rows, cols_dev),
        DP,
        split_axis=0,
        concat_axis=1,
        tiled=True,
    )[0]
    first_full = lax.all_gather(low_list[0], DP, axis=0, tiled=True)
    first_ortho = orthogonalize(first_full, dot_trans(first_full, first_full))
    ortho_list = [lax.dynamic_slice_in_dim(first_ortho, dp_index * dp_rows, dp_rows, axis=0)]
    ortho_list += [returned[table.index(item)] for item in range(1, 3 * LAYERS)]
    ortho = jnp.stack(ortho_list).reshape(LAYERS, 3, dp_rows, cols_dev).astype(f32)
    grad_mats = jnp.stack(grad_list).reshape(weights.shape)
    moment_new = jnp.stack(moment_list).reshape(weights.shape)
    factor = jnp.array([0.2 * math.sqrt(D), 0.2 * math.sqrt(FF), 0.2 * math.sqrt(FF)], f32)
    weights_new = weights * (1.0 - matrix_rate * matrix_decay) - matrix_rate * (
        ortho * factor[None, :, None, None]
    )
    first_new = first_decay * vec_first + (1.0 - first_decay) * grad_vecs
    second_new = second_decay * vec_second + (1.0 - second_decay) * grad_vecs * grad_vecs
    first_hat = first_new / (1.0 - first_decay**ADAM_STEP)
    second_hat = second_new / (1.0 - second_decay**ADAM_STEP)
    vectors_new = vectors * (1.0 - vector_rate * vector_decay) - vector_rate * first_hat / (
        jnp.sqrt(second_hat) + adam_epsilon
    )
    return (
        hidden_out[None],
        input_grad[None],
        grad_mats,
        moment_new,
        weights_new,
        grad_vecs,
        second_new,
        vectors_new,
    )


def solution(mesh):
    dp, ctx = mesh.shape["dp"], mesh.shape["ctx"]
    fine = Mesh(mesh.devices.reshape(dp // TP, 2, 2, ctx), EVERY)
    tokens = P(DP, "ctx", None)
    mats = P(None, None, DP, "ctx")
    vecs = P(None, "ctx", DP)
    return jax.shard_map(
        local,
        mesh=fine,
        in_specs=(tokens, P(DP, None), tokens, mats, vecs, mats, vecs, vecs),
        out_specs=(tokens, tokens, mats, mats, mats, vecs, vecs, vecs),
        check_vma=False,
    )
```

```python
import math

import jax
import jax.numpy as jnp
from jax import lax
from jax.experimental import pallas as pl
from jax.experimental.pallas import tpu as pltpu
from jax.sharding import Mesh, PartitionSpec as P

D = 768
HEADS = 12
HEAD = 64
FF = 3072
LAYERS = 2
ADAM_STEP = 10
TP = 4
COLS = D // TP
TP_HEADS = HEADS // TP

norm_epsilon = 1e-05
quintic_one = 3.4445
quintic_two = -4.775
quintic_three = 2.0315
momentum_decay = 0.95
matrix_rate = 0.6
matrix_decay = 0.01
first_decay = 0.9
second_decay = 0.999
vector_rate = 0.5
vector_decay = 0.01
adam_epsilon = 1e-08
masked_score = -1e30

GROUP = ("jx", "jc")
REPLICAS = ("g", "ctx")
DP = ("g", "jx", "jc")
EVERY = ("g", "jx", "jc", "ctx")
SWAP = [(0, 1), (1, 0)]
bf16 = jnp.bfloat16
f32 = jnp.float32


def dot(operand, other):
    return jnp.dot(operand, other, preferred_element_type=f32)


def dot_tokens(operand, other):
    return lax.dot_general(operand, other, (((0,), (0,)), ((), ())), preferred_element_type=f32)


def dot_trans(operand, other):
    return lax.dot_general(operand, other, (((1,), (1,)), ((), ())), preferred_element_type=f32)


def to_group(mats):
    count, rows, width = mats.shape
    split = mats.reshape(count, rows, TP, width // TP)
    return lax.all_to_all(split, GROUP, split_axis=2, concat_axis=1, tiled=True)[:, :, 0]


def from_group(mats):
    count, rows, width = mats.shape
    split = mats.reshape(count, TP, rows // TP, width)
    return lax.all_to_all(split, GROUP, split_axis=1, concat_axis=3, tiled=True)[:, 0]


def rotate(block, axis, step):
    size = lax.axis_size(axis)
    return lax.ppermute(block, axis, [((i + step) % size, i) for i in range(size)])


def pair_join(block, axis, dim):
    other = lax.ppermute(block, axis, SWAP)
    first = lax.axis_index(axis) == 0
    return jnp.concatenate(
        [jnp.where(first, block, other), jnp.where(first, other, block)], axis=dim
    )


def after(value, *others):
    return lax.optimization_barrier((value, *others))[0]


def roll_blocks(stack, sign):
    place = lax.axis_index("ctx")
    for bit in (1, 2):
        moved = jnp.roll(stack, sign * bit, axis=0)
        stack = jnp.where((place & bit) != 0, moved, stack)
    return stack


def from_own(stack):
    return roll_blocks(stack, -1)


def to_absolute(stack):
    return roll_blocks(stack, 1)


def out_moves():
    last = lax.axis_size("ctx") - 1
    size = last + 1
    moves = []
    for y in range(2):
        for x in range(2):
            for core in range(2):
                moves.append(
                    ((4 * y + 2 * x + core) * size + last, (4 * core + 2 * y + x) * size + last)
                )
    return moves


def out_pieces(mats):
    half = mats.shape[2] // 2
    core = lax.axis_index("jc")
    mine = lax.dynamic_slice_in_dim(mats, core * half, half, axis=2)
    give = lax.dynamic_slice_in_dim(mats, (1 - core) * half, half, axis=2)
    got = lax.ppermute(give, "jc", SWAP)
    rows = jnp.concatenate(
        [jnp.where(core == 0, mine, got), jnp.where(core == 0, got, mine)], axis=1
    )
    return lax.ppermute(rows, EVERY, out_moves())


def out_back(piece):
    core = lax.axis_index("jc")
    rows = lax.ppermute(piece, EVERY, [(b, a) for a, b in out_moves()])
    half = rows.shape[0] // 2
    mine = lax.dynamic_slice_in_dim(rows, core * half, half, axis=0)
    give = lax.dynamic_slice_in_dim(rows, (1 - core) * half, half, axis=0)
    got = lax.ppermute(give, "jc", SWAP)
    return jnp.concatenate(
        [jnp.where(core == 0, mine, got), jnp.where(core == 0, got, mine)], axis=1
    )


def pack_pieces(mats):
    attn = mats[:, 0].astype(bf16)
    outs = out_pieces(attn)
    first = to_group(attn[0:1])
    rest = [mats[0, 1:3]] + [mats[layer] for layer in range(1, mats.shape[0])]
    rest = to_group(after(jnp.concatenate(rest), first).astype(bf16))
    last = lax.axis_index("ctx") == lax.axis_size("ctx") - 1
    pieces = [(jnp.where(last, outs[0], first[0].T), jnp.swapaxes(rest[0:2], 1, 2))]
    for layer in range(1, mats.shape[0]):
        base = 3 * layer - 1
        pieces.append(
            (
                jnp.where(last, outs[layer], rest[base].T),
                jnp.swapaxes(rest[base + 1 : base + 3], 1, 2),
            )
        )
    return pieces


def ctx_gather(piece, *earlier):
    near = rotate(after(piece, *earlier), "ctx", 1)
    back = rotate(after(piece, near), "ctx", 3)
    far = rotate(after(piece, back), "ctx", 2)
    return [piece, near, far, back]


def group_swap(blocks, *earlier):
    others = []
    for block in blocks:
        others.append(lax.ppermute(after(block, *earlier), "g", SWAP))
        earlier = others[-1:]
    return others


def gather_weights_wide(low):
    result = []
    for layer in range(low.shape[0]):
        mats = to_group(low[layer])
        parts = lax.all_gather(mats, REPLICAS, axis=0, tiled=False)
        parts = parts.reshape(lax.axis_size("g"), -1, *mats.shape)
        full = [parts[:, :, item].transpose(1, 3, 0, 2).reshape(D, D) for item in range(3)]
        w_o = lax.all_to_all(
            full[0][3 * COLS :].T.reshape(TP, COLS, COLS),
            GROUP,
            split_axis=0,
            concat_axis=2,
            tiled=True,
        )
        attn = jnp.concatenate([full[0][: 3 * COLS].reshape(3, COLS, D), w_o], axis=0)
        result.append((attn.reshape(D, D), jnp.stack([full[1], full[2]])))
    return result


def half_sum(mine, give):
    return mine + lax.ppermute(give, "g", SWAP).astype(f32)


def ctx_sum(blocks, *earlier):
    low = after(blocks, *earlier).astype(bf16)
    total = blocks[0]
    for step in (1, 3, 2):
        got = rotate(low[step], "ctx", -step)
        total = total + got.astype(f32)
        low = after(low, got)
    return total


def attn_rows(part):
    columns = from_group(part.T[None])[0]
    last = lax.axis_index("ctx") == lax.axis_size("ctx") - 1
    return jnp.where(last, out_back(part), columns).astype(f32)


def mlp_rows(part):
    return from_group(jnp.swapaxes(part, 1, 2)).astype(f32)


def scatter_wide(mats):
    groups = lax.axis_size("g")
    blocks, count, width, depth = mats.shape
    stack = mats.astype(bf16).reshape(blocks, count, width, groups, depth // groups)
    stack = stack.transpose(3, 0, 1, 4, 2).reshape(groups * blocks, count, -1, width)
    part = lax.psum_scatter(stack, REPLICAS, scatter_dimension=0, tiled=True)[0]
    return from_group(part).astype(f32)


def gather_vectors(vectors):
    low = vectors.astype(bf16)
    stack = jnp.stack([low] + [rotate(low, "ctx", step) for step in range(1, 4)])
    stack = pair_join(pair_join(to_absolute(stack), "jc", 3), "jx", 3)
    if lax.axis_size("g") == 2:
        stack = pair_join(stack, "g", 3)
    else:
        stack = lax.all_gather(stack, "g", axis=3, tiled=True)
    return stack.transpose(1, 0, 2, 3).reshape(low.shape[0], -1, D).astype(f32)


def sum_vectors(terms):
    if lax.axis_size("g") == 2:
        terms = terms + lax.ppermute(terms, "g", SWAP)
    else:
        terms = lax.psum(terms, "g")
    layers, rows, width = terms.shape
    blocks = from_own(terms.reshape(layers, 4, rows // 4, width).transpose(1, 0, 2, 3))
    total = blocks[0]
    for step in range(1, 4):
        total = total + rotate(blocks[step], "ctx", -step)
    total = total + lax.ppermute(total, "jc", SWAP)
    return total + lax.ppermute(total, "jx", SWAP)


def call(kernel, outs, *args, scratch=()):
    return pl.pallas_call(
        kernel,
        out_shape=[jax.ShapeDtypeStruct(shape, kind) for shape, kind in outs],
        in_specs=[pl.BlockSpec(memory_space=pltpu.SMEM)]
        + [pl.BlockSpec(memory_space=pltpu.VMEM)] * (len(args) - 1),
        out_specs=[pl.BlockSpec(memory_space=pltpu.VMEM)] * len(outs),
        scratch_shapes=list(scratch),
        compiler_params=pltpu.CompilerParams(vmem_limit_bytes=52 * 1024 * 1024),
    )(*args)


def block_at(place_ref, step):
    ahead = place_ref[0] + step
    return jnp.where(ahead >= 4, ahead - 4, ahead)


def put_blocks(place_ref, own_refs, other_refs, full_refs):
    half = D // 2
    mine = pl.multiple_of(place_ref[1] * half, half)
    theirs = pl.multiple_of((1 - place_ref[1]) * half, half)
    for step in range(4):
        rows = pl.ds(pl.multiple_of(block_at(place_ref, step) * COLS, COLS), COLS)
        for number, full_ref in enumerate(full_refs):
            own, other = own_refs[step], other_refs[step]
            if len(full_refs) > 1:
                own, other = own.at[number], other.at[number]
            full_ref[rows, pl.ds(mine, half)] = own[...]
            full_ref[rows, pl.ds(theirs, half)] = other[...]


def put_grads(place_ref, grad, mine_refs, give_refs, halves):
    half = D // 2
    for block in range(4):
        rows = grad[block * COLS : (block + 1) * COLS]
        if halves:
            back = block - place_ref[0]
            back = jnp.where(back < 0, back + 4, back)
            low = place_ref[1] == 0
            mine_refs(back)[...] = jnp.where(low, rows[:, :half], rows[:, half:])
            give_refs(back)[...] = jnp.where(low, rows[:, half:], rows[:, :half]).astype(bf16)
        else:
            mine_refs(block)[...] = rows


def norm_rows(hidden):
    center = hidden - jnp.mean(hidden, axis=-1, keepdims=True)
    variance = jnp.mean(center * center, axis=-1, keepdims=True)
    inverse = lax.rsqrt(variance + norm_epsilon)
    return center * inverse, inverse


def norm_stage(vecs, layer, row, hidden, mine=None, recv=None, bias=None):
    rows = hidden.shape[0]

    def kernel(unused, vec_ref, hidden_ref, *refs):
        total = hidden_ref[...]
        if mine is not None:
            mine_ref, recv_ref, total_ref, out_ref = refs
            bias_row = vec_ref[bias[0], bias[1] : bias[1] + 1, :]
            total = total + (mine_ref[...] + recv_ref[...].astype(f32) + bias_row)
            total_ref[...] = total
        else:
            (out_ref,) = refs
        normed, unused_scale = norm_rows(total)
        gain = vec_ref[layer, row : row + 1, :]
        shift = vec_ref[layer, row + 1 : row + 2, :]
        out_ref[...] = (normed * gain + shift).astype(bf16)

    outs = [((rows, D), bf16)]
    args = [hidden]
    if mine is not None:
        outs = [((rows, D), f32)] + outs
        args += [mine, recv]
    return call(kernel, outs, jnp.zeros((1,), jnp.int32), vecs, *args)


def norm_back_stage(vecs, layer, row, grad, mine, recv, hidden):
    rows = hidden.shape[0]

    def kernel(unused, vec_ref, grad_ref, mine_ref, recv_ref, hidden_ref, out_ref, low_ref, sum_ref):
        through = mine_ref[...] + recv_ref[...].astype(f32)
        normed, inverse = norm_rows(hidden_ref[...])
        scaled = through * vec_ref[layer, row : row + 1, :]
        part = jnp.mean(scaled, axis=-1, keepdims=True)
        part = part + normed * jnp.mean(scaled * normed, axis=-1, keepdims=True)
        total = grad_ref[...] + inverse * (scaled - part)
        out_ref[...] = total
        low = total.astype(bf16)
        low_ref[...] = low
        sum_ref[0:1, :] = jnp.sum(through * normed, axis=0, keepdims=True)
        sum_ref[1:2, :] = jnp.sum(through, axis=0, keepdims=True)
        sum_ref[2:3, :] = jnp.sum(low.astype(f32), axis=0, keepdims=True)

    outs = [((rows, D), f32), ((rows, D), bf16), ((8, D), f32)]
    return call(kernel, outs, jnp.zeros((1,), jnp.int32), vecs, grad, mine, recv, hidden)


def both(first_ref, second_ref):
    return jnp.concatenate([first_ref[...], second_ref[...]], axis=0)


def allowed_of(row_ref, column_ref):
    before = row_ref[0:1, :] <= column_ref[:, 0:1]
    return before & (row_ref[1:2, :] == column_ref[:, 1:2])


def attend_stage(place, row_info, column_info, bias, a_own, a_other, weights):
    half = a_own.shape[0]
    tokens = 2 * half
    wide = 3 * COLS
    own, other = weights if isinstance(weights, tuple) else ([], [])

    def kernel(place_ref, row_ref, column_ref, bias_ref, own_a_ref, other_a_ref, *refs):
        if own:
            own_refs, refs = refs[:4], refs[4:]
            others, refs = refs[:4], refs[4:]
            w_ref, qkv_ref, lse_ref, o_ref, mine_ref, give_ref = refs
            put_blocks(place_ref, own_refs, others, [w_ref])
        else:
            w_ref, qkv_ref, lse_ref, o_ref, mine_ref, give_ref = refs
        for start, a_ref in ((0, own_a_ref), (half, other_a_ref)):
            proj = dot_trans(a_ref[...], w_ref[0:wide, :]) + bias_ref[0:1, :]
            qkv_ref[start : start + half, :] = proj.astype(bf16)
        allowed = allowed_of(row_ref, column_ref)
        for head in range(TP_HEADS):
            lanes = head * HEAD
            k = qkv_ref[:, COLS + lanes : COLS + lanes + HEAD]
            v = qkv_ref[:, 2 * COLS + lanes : 2 * COLS + lanes + HEAD]
            for start in (0, half):
                rows = slice(start, start + half)
                q = qkv_ref[rows, lanes : lanes + HEAD]
                scores = jnp.where(allowed[rows], dot_trans(q, k) * HEAD ** (-0.5), masked_score)
                top = jnp.max(scores, axis=-1, keepdims=True)
                unnormed = jnp.exp(scores - top)
                total = jnp.sum(unnormed, axis=-1, keepdims=True)
                prob = (unnormed * (1.0 / total)).astype(bf16)
                o_ref[rows, lanes : lanes + HEAD] = dot(prob, v).astype(bf16)
                lse_ref[rows, head : head + 1] = top + jnp.log(total)
        mine_ref[...] = dot(o_ref[0:half, :], w_ref[wide:, :])
        give_ref[...] = dot(o_ref[half:, :], w_ref[wide:, :]).astype(bf16)

    outs = [
        ((tokens, wide), bf16),
        ((tokens, 128), f32),
        ((tokens, COLS), bf16),
        ((half, D), f32),
        ((half, D), bf16),
    ]
    if own:
        outs = [((D, D), bf16)] + outs
        return call(
            kernel, outs, place, row_info, column_info, bias, a_own, a_other, *own, *other
        )
    result = call(kernel, outs, place, row_info, column_info, bias, a_own, a_other, weights)
    return [weights] + list(result)


def attend_back_stage(
    place, row_info, column_info, gb_own, gb_other, a_own, a_other, qkv, lse, o, w_attn, halves
):
    half = a_own.shape[0]
    tokens = 2 * half
    wide = 3 * COLS

    def kernel(
        place_ref,
        row_ref,
        column_ref,
        own_gb_ref,
        other_gb_ref,
        own_a_ref,
        other_a_ref,
        qkv_ref,
        lse_ref,
        o_ref,
        w_ref,
        mine_ref,
        give_ref,
        sum_ref,
        *refs,
    ):
        *grad_refs, go_ref, all_ref = refs
        w_o = w_ref[wide:, :]
        for start, gb_ref in ((0, own_gb_ref), (half, other_gb_ref)):
            go_ref[start : start + half, :] = dot_trans(gb_ref[...], w_o).astype(bf16)
        allowed = allowed_of(row_ref, column_ref)
        for head in range(TP_HEADS):
            lanes = head * HEAD
            q_lanes = slice(lanes, lanes + HEAD)
            k_lanes = slice(COLS + lanes, COLS + lanes + HEAD)
            v_lanes = slice(2 * COLS + lanes, 2 * COLS + lanes + HEAD)
            k = qkv_ref[:, k_lanes]
            v = qkv_ref[:, v_lanes]
            gk = jnp.zeros((tokens, HEAD), f32)
            gv = jnp.zeros((tokens, HEAD), f32)
            for start in (0, half):
                rows = slice(start, start + half)
                q = qkv_ref[rows, q_lanes]
                go = go_ref[rows, q_lanes]
                scores = jnp.where(allowed[rows], dot_trans(q, k) * HEAD ** (-0.5), masked_score)
                prob = jnp.exp(scores - lse_ref[rows, head : head + 1])
                g_prob = dot_trans(go, v)
                row_dot = jnp.sum(g_prob * prob, axis=-1, keepdims=True)
                g_scores = (prob * (g_prob - row_dot)).astype(bf16)
                all_ref[rows, q_lanes] = (dot(g_scores, k) * HEAD ** (-0.5)).astype(bf16)
                gk = gk + dot_tokens(g_scores, q)
                gv = gv + dot_tokens(prob.astype(bf16), go)
            all_ref[:, k_lanes] = (gk * HEAD ** (-0.5)).astype(bf16)
            all_ref[:, v_lanes] = gv.astype(bf16)
        mine_ref[...] = dot(all_ref[0:half, :], w_ref[0:wide, :])
        give_ref[...] = dot(all_ref[half:, :], w_ref[0:wide, :]).astype(bf16)
        sum_ref[0:1, :] = jnp.sum(all_ref[...].astype(f32), axis=0, keepdims=True)
        grad = jnp.concatenate(
            [
                dot_tokens(all_ref[...], both(own_a_ref, other_a_ref)),
                dot_tokens(o_ref[...], both(own_gb_ref, other_gb_ref)),
            ],
            axis=0,
        )
        put_grads(
            place_ref,
            grad,
            lambda block: grad_refs[0].at[block],
            lambda block: grad_refs[1].at[block],
            halves,
        )

    width = D // 2 if halves else D
    outs = [((half, D), f32), ((half, D), bf16), ((8, wide), f32), ((4, COLS, width), f32)]
    if halves:
        outs.append(((4, COLS, width), bf16))
    return call(
        kernel,
        outs,
        place,
        row_info,
        column_info,
        gb_own,
        gb_other,
        a_own,
        a_other,
        qkv,
        lse,
        o,
        w_attn,
        scratch=[pltpu.VMEM((tokens, COLS), bf16), pltpu.VMEM((tokens, wide), bf16)],
    )


def tanh_part(preact):
    inner = math.sqrt(2.0 / math.pi) * (preact + 0.044715 * (preact * preact * preact))
    return jnp.tanh(inner)


def feed_stage(place, bias, c_own, c_other, weights):
    half = c_own.shape[0]
    own, other = weights if isinstance(weights, tuple) else ([], [])

    def kernel(place_ref, bias_ref, own_c_ref, other_c_ref, *refs):
        if own:
            own_refs, others, refs = refs[:4], refs[4:8], refs[8:]
            w_ref, preact_ref, act_ref, mine_ref, give_ref = refs
            put_blocks(place_ref, own_refs, others, [w_ref.at[0], w_ref.at[1]])
        else:
            w_ref, preact_ref, act_ref, mine_ref, give_ref = refs
        for start, c_ref, out_ref in ((0, own_c_ref, mine_ref), (half, other_c_ref, give_ref)):
            rows = slice(start, start + half)
            preact = dot_trans(c_ref[...], w_ref[0]) + bias_ref[...]
            preact_ref[rows, :] = preact
            act = (0.5 * preact * (1.0 + tanh_part(preact))).astype(bf16)
            act_ref[rows, :] = act
            out_ref[...] = dot(act, w_ref[1]).astype(out_ref.dtype)

    outs = [
        ((2 * half, D), f32),
        ((2 * half, D), bf16),
        ((half, D), f32),
        ((half, D), bf16),
    ]
    if own:
        outs = [((2, D, D), bf16)] + outs
        return call(kernel, outs, place, bias, c_own, c_other, *own, *other)
    return [weights] + list(call(kernel, outs, place, bias, c_own, c_other, weights))


def feed_back_stage(place, gy_own, gy_other, c_own, c_other, preact, act, weights, halves):
    half = c_own.shape[0]

    def kernel(
        place_ref,
        own_gy_ref,
        other_gy_ref,
        own_c_ref,
        other_c_ref,
        preact_ref,
        act_ref,
        w_ref,
        mine_ref,
        give_ref,
        sum_ref,
        *refs,
    ):
        *grad_refs, gz_ref = refs
        up_sum = jnp.zeros((1, D), f32)
        for start, gy_ref, out_ref in ((0, own_gy_ref, mine_ref), (half, other_gy_ref, give_ref)):
            rows = slice(start, start + half)
            gu = dot_trans(gy_ref[...], w_ref[1])
            x = preact_ref[rows, :]
            tanh = tanh_part(x)
            slope = math.sqrt(2.0 / math.pi) * (1.0 + 3.0 * 0.044715 * (x * x))
            factor = 0.5 * (1.0 + tanh) + 0.5 * x * (1.0 - tanh * tanh) * slope
            gz = (gu * factor).astype(bf16)
            gz_ref[rows, :] = gz
            up_sum = up_sum + jnp.sum(gz.astype(f32), axis=0, keepdims=True)
            out_ref[...] = dot(gz, w_ref[0]).astype(out_ref.dtype)
        sum_ref[0:1, :] = up_sum
        sum_ref[1:2, :] = jnp.sum(own_gy_ref[...].astype(f32), axis=0, keepdims=True)
        for number, left_ref, rights in (
            (0, gz_ref, (own_c_ref, other_c_ref)),
            (1, act_ref, (own_gy_ref, other_gy_ref)),
        ):
            put_grads(
                place_ref,
                dot_tokens(left_ref[...], both(*rights)),
                lambda block: grad_refs[0].at[block, number],
                lambda block: grad_refs[1].at[block, number],
                halves,
            )

    width = D // 2 if halves else D
    outs = [((half, D), f32), ((half, D), bf16), ((8, D), f32), ((4, 2, COLS, width), f32)]
    if halves:
        outs.append(((4, 2, COLS, width), bf16))
    return call(
        kernel,
        outs,
        place,
        gy_own,
        gy_other,
        c_own,
        c_other,
        preact,
        act,
        weights,
        scratch=[pltpu.VMEM((2 * half, D), bf16)],
    )


def core_swap(block):
    return lax.ppermute(block, "jc", SWAP)


def group_sum(mine, give):
    mine = mine + core_swap(give).astype(f32)
    return mine, lax.ppermute(mine.astype(bf16), "jx", SWAP)


def orthogonalize_kernel(x_ref, gram_ref, out_ref, base_ref, work_ref, mat_ref, low_ref):
    size = x_ref.shape[0]
    rows = 256

    def each(body):
        for start in range(0, size, rows):
            body(pl.ds(start, rows))

    def polynomial():
        low_ref[...] = base_ref[...].astype(bf16)

        def body(block):
            square = dot(low_ref[block, :], low_ref[...])
            mat_ref[block, :] = (
                quintic_two * base_ref[block, :] + quintic_three * square
            ).astype(bf16)

        each(body)

    def two_part(left, right):
        high = left.astype(bf16)
        rest = (left - high.astype(f32)).astype(bf16)
        return dot(high, right) + dot(rest, right)

    trace = jnp.zeros((1, 1), f32)
    for start in range(0, size, rows):
        block = gram_ref[pl.ds(start, rows), pl.ds(start, rows)]
        line = lax.broadcasted_iota(jnp.int32, (rows, rows), 0)
        column = lax.broadcasted_iota(jnp.int32, (rows, rows), 1)
        trace = trace + jnp.sum(jnp.where(line == column, block, 0.0), keepdims=True)
    scale = 1.0 / (jnp.sqrt(trace) + 1e-07)
    base_ref[...] = gram_ref[...] * (scale * scale)
    polynomial()

    def first_step(block):
        value = quintic_one * x_ref[block, :].astype(f32) + dot(mat_ref[block, :], x_ref[...])
        out_ref[block, :] = (scale * value).astype(bf16)
        work_ref[block, :] = quintic_one * base_ref[block, :] + two_part(
            base_ref[block, :], mat_ref[...]
        )

    each(first_step)
    turned = work_ref[...].T
    work_ref[...] = turned

    def gram_step(block):
        base_ref[block, :] = quintic_one * work_ref[block, :] + two_part(
            work_ref[block, :], mat_ref[...]
        )

    each(gram_step)
    polynomial()
    low_ref[...] = out_ref[...]

    def second_step(block):
        value = quintic_one * low_ref[block, :].astype(f32) + dot(mat_ref[block, :], low_ref[...])
        out_ref[block, :] = value.astype(bf16)

    each(second_step)


def orthogonalize(matrix, gram):
    size = matrix.shape[0]
    return pl.pallas_call(
        orthogonalize_kernel,
        out_shape=jax.ShapeDtypeStruct(matrix.shape, bf16),
        in_specs=[pl.BlockSpec(memory_space=pltpu.VMEM)] * 2,
        out_specs=pl.BlockSpec(memory_space=pltpu.VMEM),
        scratch_shapes=[
            pltpu.VMEM((size, size), f32),
            pltpu.VMEM((size, size), f32),
            pltpu.VMEM((size, size), bf16),
            pltpu.VMEM((size, size), bf16),
        ],
        compiler_params=pltpu.CompilerParams(vmem_limit_bytes=48 * 1024 * 1024),
    )(matrix, gram)


def ctx_gram(gram):
    size = lax.axis_size("ctx")

    def shift(block, step):
        moves = [((i + step) % size, i) for i in range(size)]
        return lax.ppermute(block, ("jc", "ctx"), moves)

    rows = gram.shape[0] // size
    blocks = from_own(gram.astype(bf16).reshape(size, rows, -1))
    total = blocks[0].astype(f32)
    for step in (1, 3, 2):
        total = total + shift(blocks[step], -step).astype(f32)
    low = total.astype(bf16)
    full = [low] + [shift(low, step) for step in range(1, size)]
    return to_absolute(jnp.stack(full)).reshape(gram.shape).astype(f32)


def local(hidden_in, segments, out_grad, weights, vectors, mat_momentum, vec_first, vec_second):
    tokens_dev = hidden_in.shape[1]
    seq_len = segments.shape[1]
    half = 2 * tokens_dev
    dp_rows = weights.shape[2]
    ctx_size = lax.axis_size("ctx")
    x_index = lax.axis_index("jx")
    c_index = lax.axis_index("jc")
    t_index = 2 * x_index + c_index
    z_index = lax.axis_index("ctx")
    dp_index = lax.axis_index(DP)
    dp_size = lax.axis_size(DP)

    to_seq = []
    for t in range(TP):
        for z in range(ctx_size):
            to_seq.append((t * ctx_size + z, ((z % 2) * 2 + z // 2) * ctx_size + t))
    from_seq = [(b, a) for a, b in to_seq]
    axes = ("jx", "jc", "ctx")

    def x_join(block):
        return pair_join(block, "jx", 0)

    vec_rows = gather_vectors(vectors)
    seg_row = jnp.pad(segments.astype(f32), ((0, 7), (0, D - seq_len)))
    moved = lax.ppermute(jnp.concatenate([hidden_in[0], seg_row], axis=0), axes, to_seq)
    hidden = x_join(moved[:tokens_dev])
    segment_row = moved[tokens_dev, :seq_len]
    relative = lax.axis_size("g") == 2
    place = jnp.stack([z_index, lax.axis_index("g")]).astype(jnp.int32)
    if relative:
        pieces = pack_pieces(weights)
        own_attn = ctx_gather(pieces[0][0])
        own_mlp = ctx_gather(pieces[0][1], own_attn[2])
        attn_weights = (own_attn, group_swap(own_attn))
        mlp_weights = (own_mlp, group_swap(own_mlp, attn_weights[1][3]))
    else:
        wide_weights = gather_weights_wide(weights.astype(bf16))

    start = c_index * half
    pos = jnp.concatenate([start + jnp.arange(half), half - start + jnp.arange(half)])
    seg = jnp.roll(segment_row.reshape(2, half), -c_index, axis=0).reshape(-1)
    info = jnp.stack([pos.astype(f32), seg])
    row_info = jnp.pad(info, ((0, 6), (0, 0)))
    column_info = jnp.pad(info.T, ((0, 0), (0, 126)))
    vec_mine = lax.dynamic_slice_in_dim(vec_rows, t_index * COLS, COLS, axis=2)
    no_bias = jnp.zeros((LAYERS, 1, COLS), f32)
    qkv_bias = jnp.concatenate([vec_mine[:, 4:5], no_bias, vec_mine[:, 5:6]], axis=2)
    up_bias = vec_mine[:, 8:12].reshape(LAYERS, 1, D)

    stored = []
    (a_own,) = norm_stage(vec_rows, 0, 0, hidden)
    for layer in range(LAYERS):
        following = layer + 1 < LAYERS
        a_other = core_swap(a_own)
        if not relative:
            attn_weights, mlp_weights = wide_weights[layer]
        w_attn, qkv, lse, o, mine, give = attend_stage(
            place, row_info, column_info, qkv_bias[layer], a_own, a_other, attn_weights
        )
        if relative and following:
            next_attn = ctx_gather(pieces[layer + 1][0], own_mlp[2])
            next_mlp = ctx_gather(pieces[layer + 1][1], next_attn[2])
        mine, recv = group_sum(mine, give)
        middle, c_own = norm_stage(vec_rows, layer, 2, hidden, mine, recv, (layer, 6))
        c_other = core_swap(c_own)
        w_mlp, preact, act, mine, give = feed_stage(
            place, up_bias[layer], c_own, c_other, mlp_weights
        )
        if relative and following:
            attn_weights = (next_attn, group_swap(next_attn, mlp_weights[1][3]))
            own_mlp = next_mlp
            mlp_weights = (own_mlp, group_swap(own_mlp, attn_weights[1][3]))
        mine, recv = group_sum(mine, give)
        stored.append(
            (hidden, middle, a_own, a_other, qkv, lse, o, c_own, c_other, preact, act, w_attn, w_mlp)
        )
        if following:
            hidden, a_own = norm_stage(vec_rows, layer + 1, 0, middle, mine, recv, (layer, 7))
        else:
            hidden = middle + (mine + recv.astype(f32) + vec_rows[layer, 7:8])

    def send_back(rows):
        block = lax.dynamic_slice_in_dim(rows, x_index * tokens_dev, tokens_dev, axis=0)
        return lax.ppermute(block, axes, from_seq)

    hidden_out = send_back(hidden)
    grad_hidden = x_join(lax.ppermute(after(out_grad[0], next_mlp[2] if relative else stored[-1][6]), axes, to_seq))
    gy_own = grad_hidden.astype(bf16)
    attn_half = mlp_part = None

    mat_list = [None] * LAYERS
    sum_list = [None] * LAYERS
    parts = [None] * LAYERS
    for layer in reversed(range(LAYERS)):
        h_in, middle, a_own, a_other, qkv, lse, o, c_own, c_other, preact, act, w_attn, w_mlp = stored[
            layer
        ]
        if relative and attn_half is not None:
            attn_part = ctx_sum(attn_half, mlp_part)
        gy_other = core_swap(gy_own)
        mine, give, up_sums, *mlp_grads = feed_back_stage(
            place, gy_own, gy_other, c_own, c_other, preact, act, w_mlp, relative
        )
        if relative:
            mlp_half = half_sum(*mlp_grads)
        mine, recv = group_sum(mine, give)
        grad_middle, gb_own, mid_sums = norm_back_stage(
            vec_rows, layer, 2, grad_hidden, mine, recv, middle
        )
        if relative and attn_half is not None:
            gb_own, attn_part = lax.optimization_barrier((gb_own, attn_part))
            parts[layer + 1] = (attn_part, mlp_part)
        if layer == LAYERS - 1:
            gb_own, hidden_out = lax.optimization_barrier((gb_own, hidden_out))
        gb_other = core_swap(gb_own)
        mine, give, qkv_sums, *attn_grads = attend_back_stage(
            place,
            row_info,
            column_info,
            gb_own,
            gb_other,
            a_own,
            a_other,
            qkv,
            lse,
            o,
            w_attn,
            relative,
        )
        if relative:
            mine, mlp_half = lax.optimization_barrier((mine, mlp_half))
            mlp_part = ctx_sum(mlp_half, *([] if parts[-1] is None else parts[-1]))
            attn_half = half_sum(*attn_grads)
        else:
            attn_grad = attn_grads[0]
            g_wo = lax.all_to_all(
                attn_grad[3].reshape(COLS, TP, COLS), GROUP, split_axis=1, concat_axis=0, tiled=True
            )[:, 0]
            attn_grad = jnp.concatenate([attn_grad[:3], g_wo.T[None]], axis=0)
            mat_list[layer] = scatter_wide(
                jnp.concatenate([attn_grad[:, None], mlp_grads[0]], axis=1)
            )
        mine, recv = group_sum(mine, give)
        grad_hidden, gy_own, in_sums = norm_back_stage(
            vec_rows, layer, 0, grad_middle, mine, recv, h_in
        )
        sum_list[layer] = (in_sums, mid_sums, up_sums, qkv_sums)
    input_grad = send_back(grad_hidden)

    if relative:
        parts[0] = (ctx_sum(attn_half, mlp_part), mlp_part)
        for layer in range(LAYERS):
            attn_part, mlp_part = [
                after(part, grad_hidden).astype(bf16) for part in parts[layer]
            ]
            mat_list[layer] = jnp.concatenate([attn_rows(attn_part)[None], mlp_rows(mlp_part)])
    once = jnp.where(x_index == 0, 1.0, 0.0).astype(f32)
    in_sums, mid_sums, up_sums, qkv_sums = [jnp.stack(sums) for sums in zip(*sum_list)]
    shared = once * jnp.concatenate(
        [in_sums[:, 0:2], mid_sums[:, 0:3], up_sums[:, 1:2]], axis=1
    )
    placed = jnp.concatenate(
        [
            qkv_sums[:, 0:1, :COLS],
            qkv_sums[:, 0:1, 2 * COLS :],
            up_sums[:, 0].reshape(LAYERS, ctx_size, COLS),
        ],
        axis=1,
    )
    placed = lax.dynamic_update_slice_in_dim(
        jnp.zeros((LAYERS, 6, D), f32), placed, t_index * COLS, axis=2
    )
    vec_terms = jnp.concatenate(
        [shared[:, 0:4], placed[:, 0:2], shared[:, 4:6], placed[:, 2:6]], axis=1
    )
    grad_vecs = lax.dynamic_slice_in_dim(
        sum_vectors(vec_terms), dp_index * vectors.shape[2], vectors.shape[2], axis=2
    )
    cols_dev = weights.shape[3]
    grad_list, moment_list, low_list = [], [], []
    for layer in range(LAYERS):
        for item in range(3):
            grad = mat_list[layer][item]
            moment = momentum_decay * mat_momentum[layer, item] + grad
            grad_list.append(grad)
            moment_list.append(moment)
            low_list.append((grad + momentum_decay * moment).astype(bf16))
    wide = [item for item in range(3 * LAYERS) if item % 3]
    squares = [item for item in range(3, 3 * LAYERS, 3)]
    table = []
    for number in range(4):
        table += [wide[number], squares[number % len(squares)]]
    table = (table * (-(-dp_size // 8)))[:dp_size]
    slots = jnp.stack([low_list[item] for item in table])
    received = lax.all_to_all(slots[:, None], DP, split_axis=0, concat_axis=1, tiled=True)
    current = received.reshape(dp_size * dp_rows, cols_dev)
    gram_local = dot_trans(current, current)
    gram = jnp.where(c_index == 0, ctx_gram(gram_local), gram_local)
    ortho_mine = orthogonalize(current, gram)
    returned = lax.all_to_all(
        ortho_mine.reshape(dp_size, 1, dp_rows, cols_dev),
        DP,
        split_axis=0,
        concat_axis=1,
        tiled=True,
    )[0]
    first_full = lax.all_gather(low_list[0], DP, axis=0, tiled=True)
    first_ortho = orthogonalize(first_full, dot_trans(first_full, first_full))
    ortho_list = [lax.dynamic_slice_in_dim(first_ortho, dp_index * dp_rows, dp_rows, axis=0)]
    ortho_list += [returned[table.index(item)] for item in range(1, 3 * LAYERS)]
    ortho = jnp.stack(ortho_list).reshape(LAYERS, 3, dp_rows, cols_dev).astype(f32)
    grad_mats = jnp.stack(grad_list).reshape(weights.shape)
    moment_new = jnp.stack(moment_list).reshape(weights.shape)
    factor = jnp.array([0.2 * math.sqrt(D), 0.2 * math.sqrt(FF), 0.2 * math.sqrt(FF)], f32)
    weights_new = weights * (1.0 - matrix_rate * matrix_decay) - matrix_rate * (
        ortho * factor[None, :, None, None]
    )
    first_new = first_decay * vec_first + (1.0 - first_decay) * grad_vecs
    second_new = second_decay * vec_second + (1.0 - second_decay) * grad_vecs * grad_vecs
    first_hat = first_new / (1.0 - first_decay**ADAM_STEP)
    second_hat = second_new / (1.0 - second_decay**ADAM_STEP)
    vectors_new = vectors * (1.0 - vector_rate * vector_decay) - vector_rate * first_hat / (
        jnp.sqrt(second_hat) + adam_epsilon
    )
    return (
        hidden_out[None],
        input_grad[None],
        grad_mats,
        moment_new,
        weights_new,
        grad_vecs,
        second_new,
        vectors_new,
    )


def solution(mesh):
    dp, ctx = mesh.shape["dp"], mesh.shape["ctx"]
    fine = Mesh(mesh.devices.reshape(dp // TP, 2, 2, ctx), EVERY)
    tokens = P(DP, "ctx", None)
    mats = P(None, None, DP, "ctx")
    vecs = P(None, "ctx", DP)
    return jax.shard_map(
        local,
        mesh=fine,
        in_specs=(tokens, P(DP, None), tokens, mats, vecs, mats, vecs, vecs),
        out_specs=(tokens, tokens, mats, mats, mats, vecs, vecs, vecs),
        check_vma=False,
    )
```

```python
import math

import jax
import jax.numpy as jnp
from jax import lax
from jax.experimental import pallas as pl
from jax.experimental.pallas import tpu as pltpu
from jax.sharding import Mesh, PartitionSpec as P

D = 768
HEADS = 12
HEAD = 64
FF = 3072
LAYERS = 2
ADAM_STEP = 10
TP = 4
COLS = D // TP
TP_HEADS = HEADS // TP
ROWS = 256

norm_epsilon = 1e-05
quintic_one = 3.4445
quintic_two = -4.775
quintic_three = 2.0315
momentum_decay = 0.95
matrix_rate = 0.6
matrix_decay = 0.01
first_decay = 0.9
second_decay = 0.999
vector_rate = 0.5
vector_decay = 0.01
adam_epsilon = 1e-08
masked_score = -1e30

GROUP = ("jx", "jc")
REPLICAS = ("g", "ctx")
DP = ("g", "jx", "jc")
EVERY = ("g", "jx", "jc", "ctx")
SWAP = [(0, 1), (1, 0)]
bf16 = jnp.bfloat16
f32 = jnp.float32


def dot(operand, other):
    return jnp.dot(operand, other, preferred_element_type=f32)


def dot_tokens(operand, other):
    return lax.dot_general(operand, other, (((0,), (0,)), ((), ())), preferred_element_type=f32)


def dot_trans(operand, other):
    return lax.dot_general(operand, other, (((1,), (1,)), ((), ())), preferred_element_type=f32)


def to_group(mats):
    count, rows, width = mats.shape
    split = mats.reshape(count, rows, TP, width // TP)
    return lax.all_to_all(split, GROUP, split_axis=2, concat_axis=1, tiled=True)[:, :, 0]


def from_group(mats):
    count, rows, width = mats.shape
    split = mats.reshape(count, TP, rows // TP, width)
    return lax.all_to_all(split, GROUP, split_axis=1, concat_axis=3, tiled=True)[:, 0]


def rotate(block, axis, step):
    size = lax.axis_size(axis)
    return lax.ppermute(block, axis, [((i + step) % size, i) for i in range(size)])


def pair_join(block, axis, dim):
    other = lax.ppermute(block, axis, SWAP)
    first = lax.axis_index(axis) == 0
    return jnp.concatenate(
        [jnp.where(first, block, other), jnp.where(first, other, block)], axis=dim
    )


def after(value, *others):
    return lax.optimization_barrier((value, *others))[0]


def roll_blocks(stack, sign):
    place = lax.axis_index("ctx")
    for bit in (1, 2):
        moved = jnp.roll(stack, sign * bit, axis=0)
        stack = jnp.where((place & bit) != 0, moved, stack)
    return stack


def from_own(stack):
    return roll_blocks(stack, -1)


def to_absolute(stack):
    return roll_blocks(stack, 1)


def out_moves():
    last = lax.axis_size("ctx") - 1
    size = last + 1
    moves = []
    for y in range(2):
        for x in range(2):
            for core in range(2):
                moves.append(
                    ((4 * y + 2 * x + core) * size + last, (4 * core + 2 * y + x) * size + last)
                )
    return moves


def out_pieces(mats):
    half = mats.shape[2] // 2
    core = lax.axis_index("jc")
    mine = lax.dynamic_slice_in_dim(mats, core * half, half, axis=2)
    give = lax.dynamic_slice_in_dim(mats, (1 - core) * half, half, axis=2)
    got = lax.ppermute(give, "jc", SWAP)
    rows = jnp.concatenate(
        [jnp.where(core == 0, mine, got), jnp.where(core == 0, got, mine)], axis=1
    )
    return lax.ppermute(rows, EVERY, out_moves())


def out_back(pieces):
    core = lax.axis_index("jc")
    rows = lax.ppermute(pieces, EVERY, [(b, a) for a, b in out_moves()])
    half = rows.shape[1] // 2
    mine = lax.dynamic_slice_in_dim(rows, core * half, half, axis=1)
    give = lax.dynamic_slice_in_dim(rows, (1 - core) * half, half, axis=1)
    got = lax.ppermute(give, "jc", SWAP)
    return jnp.concatenate(
        [jnp.where(core == 0, mine, got), jnp.where(core == 0, got, mine)], axis=2
    )


def last_block():
    return lax.axis_index("ctx") == lax.axis_size("ctx") - 1


def first_piece(mats):
    attn = mats[:, 0].astype(bf16)
    outs = out_pieces(attn)
    return jnp.where(last_block(), outs[0], to_group(attn[0:1])[0].T), outs


def other_pieces(mats, outs, *earlier):
    rest = [mats[0, 1:3]] + [mats[layer] for layer in range(1, mats.shape[0])]
    rest = to_group(after(jnp.concatenate(rest), *earlier).astype(bf16))
    rest = jnp.swapaxes(rest, 1, 2)
    pieces = [rest[0:2]]
    for layer in range(1, mats.shape[0]):
        attn = jnp.where(last_block(), outs[layer], rest[3 * layer - 1])
        pieces.append((attn, rest[3 * layer : 3 * layer + 2]))
    return pieces


def momentum_pieces(mats):
    layers, count, rows, width = mats.shape
    columns = jnp.swapaxes(to_group(mats.reshape(layers * count, rows, width)), 1, 2)
    columns = columns.reshape(layers, count, *columns.shape[1:])
    attn = jnp.where(last_block(), out_pieces(mats[:, 0]), columns[:, 0])
    return jnp.concatenate([attn[:, None], columns[:, 1:]], axis=1)


def ctx_gather(piece, *earlier):
    piece = after(piece, *earlier)
    near, back, far = [rotate(piece, "ctx", step) for step in (1, 3, 2)]
    return [piece, near, far, back]


def group_swap(blocks):
    return [lax.ppermute(block, "g", SWAP) for block in blocks]


def group_swap_all(blocks):
    return [lax.ppermute(jnp.stack(blocks), "g", SWAP)]


def gather_weights_wide(low):
    result = []
    for layer in range(low.shape[0]):
        mats = to_group(low[layer])
        parts = lax.all_gather(mats, REPLICAS, axis=0, tiled=False)
        parts = parts.reshape(lax.axis_size("g"), -1, *mats.shape)
        full = [parts[:, :, item].transpose(1, 3, 0, 2).reshape(D, D) for item in range(3)]
        w_o = lax.all_to_all(
            full[0][3 * COLS :].T.reshape(TP, COLS, COLS),
            GROUP,
            split_axis=0,
            concat_axis=2,
            tiled=True,
        )
        attn = jnp.concatenate([full[0][: 3 * COLS].reshape(3, COLS, D), w_o], axis=0)
        result.append((attn.reshape(D, D), jnp.stack([full[1], full[2]])))
    return result


def half_sum(mine, give):
    return mine + lax.ppermute(give, "g", SWAP).astype(f32)


def ctx_sum(blocks, *earlier):
    low = after(blocks, *earlier).astype(bf16)
    total = blocks[0]
    for step in (1, 3, 2):
        total = total + rotate(low[step], "ctx", -step).astype(f32)
    return total


def grad_rows(parts):
    layers, count, width, half = parts.shape
    flat = jnp.swapaxes(parts.reshape(layers * count, width, half), 1, 2)
    rows = from_group(flat).reshape(layers, count, -1, D)
    attn = jnp.where(last_block(), out_back(parts[:, 0]), rows[:, 0])
    return jnp.concatenate([attn[:, None], rows[:, 1:]], axis=1).astype(f32)


def scatter_wide(mats):
    groups = lax.axis_size("g")
    blocks, count, width, depth = mats.shape
    stack = mats.astype(bf16).reshape(blocks, count, width, groups, depth // groups)
    stack = stack.transpose(3, 0, 1, 4, 2).reshape(groups * blocks, count, -1, width)
    part = lax.psum_scatter(stack, REPLICAS, scatter_dimension=0, tiled=True)[0]
    return from_group(part).astype(f32)


def gather_vectors(vectors):
    low = vectors.astype(bf16)
    stack = jnp.stack([low] + [rotate(low, "ctx", step) for step in range(1, 4)])
    stack = pair_join(pair_join(to_absolute(stack), "jc", 3), "jx", 3)
    if lax.axis_size("g") == 2:
        stack = pair_join(stack, "g", 3)
    else:
        stack = lax.all_gather(stack, "g", axis=3, tiled=True)
    return stack.transpose(1, 0, 2, 3).reshape(low.shape[0], -1, D).astype(f32)


def sum_vectors(terms):
    if lax.axis_size("g") == 2:
        terms = terms + lax.ppermute(terms, "g", SWAP)
    else:
        terms = lax.psum(terms, "g")
    layers, rows, width = terms.shape
    blocks = from_own(terms.reshape(layers, 4, rows // 4, width).transpose(1, 0, 2, 3))
    total = blocks[0]
    for step in range(1, 4):
        total = total + rotate(blocks[step], "ctx", -step)
    total = total + lax.ppermute(total, "jc", SWAP)
    return total + lax.ppermute(total, "jx", SWAP)


def call(kernel, outs, *args, scratch=()):
    return pl.pallas_call(
        kernel,
        out_shape=[jax.ShapeDtypeStruct(shape, kind) for shape, kind in outs],
        in_specs=[pl.BlockSpec(memory_space=pltpu.SMEM)]
        + [pl.BlockSpec(memory_space=pltpu.VMEM)] * (len(args) - 1),
        out_specs=[pl.BlockSpec(memory_space=pltpu.VMEM)] * len(outs),
        scratch_shapes=list(scratch),
        compiler_params=pltpu.CompilerParams(vmem_limit_bytes=52 * 1024 * 1024),
    )(*args)


def block_at(place_ref, step):
    ahead = place_ref[0] + step
    return jnp.where(ahead >= 4, ahead - 4, ahead)


def put_blocks(place_ref, own_refs, other_refs, full_refs):
    half = D // 2
    mine = pl.multiple_of(place_ref[1] * half, half)
    theirs = pl.multiple_of((1 - place_ref[1]) * half, half)
    for step in range(4):
        rows = pl.ds(pl.multiple_of(block_at(place_ref, step) * COLS, COLS), COLS)
        for number, full_ref in enumerate(full_refs):
            own, other = own_refs[step], other_refs[step]
            if len(full_refs) > 1:
                own, other = own.at[number], other.at[number]
            full_ref[rows, pl.ds(mine, half)] = own[...]
            full_ref[rows, pl.ds(theirs, half)] = other[...]


def put_grads(place_ref, grad, mine_refs, give_refs, halves):
    half = D // 2
    for block in range(4):
        rows = grad[block * COLS : (block + 1) * COLS]
        if halves:
            back = block - place_ref[0]
            back = jnp.where(back < 0, back + 4, back)
            low = place_ref[1] == 0
            mine_refs(back)[...] = jnp.where(low, rows[:, :half], rows[:, half:])
            give_refs(back)[...] = jnp.where(low, rows[:, half:], rows[:, :half]).astype(bf16)
        else:
            mine_refs(block)[...] = rows


def norm_rows(hidden):
    center = hidden - jnp.mean(hidden, axis=-1, keepdims=True)
    variance = jnp.mean(center * center, axis=-1, keepdims=True)
    inverse = lax.rsqrt(variance + norm_epsilon)
    return center * inverse, inverse


def norm_stage(vecs, layer, row, hidden, mine=None, recv=None, bias=None):
    rows = hidden.shape[0]

    def kernel(unused, vec_ref, hidden_ref, *refs):
        total = hidden_ref[...]
        if mine is not None:
            mine_ref, recv_ref, total_ref, out_ref = refs
            bias_row = vec_ref[bias[0], bias[1] : bias[1] + 1, :]
            total = total + (mine_ref[...] + recv_ref[...].astype(f32) + bias_row)
            total_ref[...] = total
        else:
            (out_ref,) = refs
        normed, unused_scale = norm_rows(total)
        gain = vec_ref[layer, row : row + 1, :]
        shift = vec_ref[layer, row + 1 : row + 2, :]
        out_ref[...] = (normed * gain + shift).astype(bf16)

    outs = [((rows, D), bf16)]
    args = [hidden]
    if mine is not None:
        outs = [((rows, D), f32)] + outs
        args += [mine, recv]
    return call(kernel, outs, jnp.zeros((1,), jnp.int32), vecs, *args)


def norm_back_stage(vecs, layer, row, grad, mine, recv, hidden):
    rows = hidden.shape[0]

    def kernel(unused, vec_ref, grad_ref, mine_ref, recv_ref, hidden_ref, out_ref, low_ref, sum_ref):
        through = mine_ref[...] + recv_ref[...].astype(f32)
        normed, inverse = norm_rows(hidden_ref[...])
        scaled = through * vec_ref[layer, row : row + 1, :]
        part = jnp.mean(scaled, axis=-1, keepdims=True)
        part = part + normed * jnp.mean(scaled * normed, axis=-1, keepdims=True)
        total = grad_ref[...] + inverse * (scaled - part)
        out_ref[...] = total
        low = total.astype(bf16)
        low_ref[...] = low
        sum_ref[0:1, :] = jnp.sum(through * normed, axis=0, keepdims=True)
        sum_ref[1:2, :] = jnp.sum(through, axis=0, keepdims=True)
        sum_ref[2:3, :] = jnp.sum(low.astype(f32), axis=0, keepdims=True)

    outs = [((rows, D), f32), ((rows, D), bf16), ((8, D), f32)]
    return call(kernel, outs, jnp.zeros((1,), jnp.int32), vecs, grad, mine, recv, hidden)


def both(first_ref, second_ref):
    return jnp.concatenate([first_ref[...], second_ref[...]], axis=0)


def allowed_of(row_ref, column_ref):
    before = row_ref[0:1, :] <= column_ref[:, 0:1]
    return before & (row_ref[1:2, :] == column_ref[:, 1:2])


def attend_stage(place, row_info, column_info, bias, a_own, a_other, weights):
    half = a_own.shape[0]
    tokens = 2 * half
    wide = 3 * COLS
    own, other = weights if isinstance(weights, tuple) else ([], [])

    def kernel(place_ref, row_ref, column_ref, bias_ref, own_a_ref, other_a_ref, *refs):
        if own:
            own_refs, refs = refs[:4], refs[4:]
            others, refs = refs[: len(other)], refs[len(other) :]
            if len(other) == 1:
                others = [others[0].at[step] for step in range(4)]
            w_ref, qkv_ref, lse_ref, o_ref, mine_ref, give_ref = refs
            put_blocks(place_ref, own_refs, others, [w_ref])
        else:
            w_ref, qkv_ref, lse_ref, o_ref, mine_ref, give_ref = refs
        for start, a_ref in ((0, own_a_ref), (half, other_a_ref)):
            proj = dot_trans(a_ref[...], w_ref[0:wide, :]) + bias_ref[0:1, :]
            qkv_ref[start : start + half, :] = proj.astype(bf16)
        allowed = allowed_of(row_ref, column_ref)
        for head in range(TP_HEADS):
            lanes = head * HEAD
            k = qkv_ref[:, COLS + lanes : COLS + lanes + HEAD]
            v = qkv_ref[:, 2 * COLS + lanes : 2 * COLS + lanes + HEAD]
            for start in (0, half):
                rows = slice(start, start + half)
                q = qkv_ref[rows, lanes : lanes + HEAD]
                scores = jnp.where(allowed[rows], dot_trans(q, k) * HEAD ** (-0.5), masked_score)
                top = jnp.max(scores, axis=-1, keepdims=True)
                unnormed = jnp.exp(scores - top)
                total = jnp.sum(unnormed, axis=-1, keepdims=True)
                prob = (unnormed * (1.0 / total)).astype(bf16)
                o_ref[rows, lanes : lanes + HEAD] = dot(prob, v).astype(bf16)
                lse_ref[rows, head : head + 1] = top + jnp.log(total)
        mine_ref[...] = dot(o_ref[0:half, :], w_ref[wide:, :])
        give_ref[...] = dot(o_ref[half:, :], w_ref[wide:, :]).astype(bf16)

    outs = [
        ((tokens, wide), bf16),
        ((tokens, 128), f32),
        ((tokens, COLS), bf16),
        ((half, D), f32),
        ((half, D), bf16),
    ]
    if own:
        outs = [((D, D), bf16)] + outs
        return call(
            kernel, outs, place, row_info, column_info, bias, a_own, a_other, *own, *other
        )
    result = call(kernel, outs, place, row_info, column_info, bias, a_own, a_other, weights)
    return [weights] + list(result)


def attend_back_stage(
    place, row_info, column_info, gb_own, gb_other, a_own, a_other, qkv, lse, o, w_attn, halves
):
    half = a_own.shape[0]
    tokens = 2 * half
    wide = 3 * COLS

    def kernel(
        place_ref,
        row_ref,
        column_ref,
        own_gb_ref,
        other_gb_ref,
        own_a_ref,
        other_a_ref,
        qkv_ref,
        lse_ref,
        o_ref,
        w_ref,
        mine_ref,
        give_ref,
        sum_ref,
        *refs,
    ):
        *grad_refs, go_ref, all_ref = refs
        w_o = w_ref[wide:, :]
        for start, gb_ref in ((0, own_gb_ref), (half, other_gb_ref)):
            go_ref[start : start + half, :] = dot_trans(gb_ref[...], w_o).astype(bf16)
        allowed = allowed_of(row_ref, column_ref)
        for head in range(TP_HEADS):
            lanes = head * HEAD
            q_lanes = slice(lanes, lanes + HEAD)
            k_lanes = slice(COLS + lanes, COLS + lanes + HEAD)
            v_lanes = slice(2 * COLS + lanes, 2 * COLS + lanes + HEAD)
            k = qkv_ref[:, k_lanes]
            v = qkv_ref[:, v_lanes]
            gk = jnp.zeros((tokens, HEAD), f32)
            gv = jnp.zeros((tokens, HEAD), f32)
            for start in (0, half):
                rows = slice(start, start + half)
                q = qkv_ref[rows, q_lanes]
                go = go_ref[rows, q_lanes]
                scores = jnp.where(allowed[rows], dot_trans(q, k) * HEAD ** (-0.5), masked_score)
                prob = jnp.exp(scores - lse_ref[rows, head : head + 1])
                g_prob = dot_trans(go, v)
                row_dot = jnp.sum(g_prob * prob, axis=-1, keepdims=True)
                g_scores = (prob * (g_prob - row_dot)).astype(bf16)
                all_ref[rows, q_lanes] = (dot(g_scores, k) * HEAD ** (-0.5)).astype(bf16)
                gk = gk + dot_tokens(g_scores, q)
                gv = gv + dot_tokens(prob.astype(bf16), go)
            all_ref[:, k_lanes] = (gk * HEAD ** (-0.5)).astype(bf16)
            all_ref[:, v_lanes] = gv.astype(bf16)
        mine_ref[...] = dot(all_ref[0:half, :], w_ref[0:wide, :])
        give_ref[...] = dot(all_ref[half:, :], w_ref[0:wide, :]).astype(bf16)
        sum_ref[0:1, :] = jnp.sum(all_ref[...].astype(f32), axis=0, keepdims=True)
        grad = jnp.concatenate(
            [
                dot_tokens(all_ref[...], both(own_a_ref, other_a_ref)),
                dot_tokens(o_ref[...], both(own_gb_ref, other_gb_ref)),
            ],
            axis=0,
        )
        put_grads(
            place_ref,
            grad,
            lambda block: grad_refs[0].at[block],
            lambda block: grad_refs[1].at[block],
            halves,
        )

    width = D // 2 if halves else D
    outs = [((half, D), f32), ((half, D), bf16), ((8, wide), f32), ((4, COLS, width), f32)]
    if halves:
        outs.append(((4, COLS, width), bf16))
    return call(
        kernel,
        outs,
        place,
        row_info,
        column_info,
        gb_own,
        gb_other,
        a_own,
        a_other,
        qkv,
        lse,
        o,
        w_attn,
        scratch=[pltpu.VMEM((tokens, COLS), bf16), pltpu.VMEM((tokens, wide), bf16)],
    )


def tanh_part(preact):
    inner = math.sqrt(2.0 / math.pi) * (preact + 0.044715 * (preact * preact * preact))
    return jnp.tanh(inner)


def feed_stage(place, bias, c_own, c_other, weights):
    half = c_own.shape[0]
    own, other = weights if isinstance(weights, tuple) else ([], [])

    def kernel(place_ref, bias_ref, own_c_ref, other_c_ref, *refs):
        if own:
            own_refs, other_ref, refs = refs[:4], refs[4], refs[5:]
            others = [other_ref.at[step] for step in range(4)]
            w_ref, preact_ref, act_ref, mine_ref, give_ref = refs
            put_blocks(place_ref, own_refs, others, [w_ref.at[0], w_ref.at[1]])
        else:
            w_ref, preact_ref, act_ref, mine_ref, give_ref = refs
        for start, c_ref, out_ref in ((0, own_c_ref, mine_ref), (half, other_c_ref, give_ref)):
            rows = slice(start, start + half)
            preact = dot_trans(c_ref[...], w_ref[0]) + bias_ref[...]
            preact_ref[rows, :] = preact
            act = (0.5 * preact * (1.0 + tanh_part(preact))).astype(bf16)
            act_ref[rows, :] = act
            out_ref[...] = dot(act, w_ref[1]).astype(out_ref.dtype)

    outs = [
        ((2 * half, D), f32),
        ((2 * half, D), bf16),
        ((half, D), f32),
        ((half, D), bf16),
    ]
    if own:
        outs = [((2, D, D), bf16)] + outs
        return call(kernel, outs, place, bias, c_own, c_other, *own, *other)
    return [weights] + list(call(kernel, outs, place, bias, c_own, c_other, weights))


def feed_back_stage(place, gy_own, gy_other, c_own, c_other, preact, act, weights, halves):
    half = c_own.shape[0]

    def kernel(
        place_ref,
        own_gy_ref,
        other_gy_ref,
        own_c_ref,
        other_c_ref,
        preact_ref,
        act_ref,
        w_ref,
        mine_ref,
        give_ref,
        sum_ref,
        *refs,
    ):
        *grad_refs, gz_ref = refs
        up_sum = jnp.zeros((1, D), f32)
        for start, gy_ref, out_ref in ((0, own_gy_ref, mine_ref), (half, other_gy_ref, give_ref)):
            rows = slice(start, start + half)
            gu = dot_trans(gy_ref[...], w_ref[1])
            x = preact_ref[rows, :]
            tanh = tanh_part(x)
            slope = math.sqrt(2.0 / math.pi) * (1.0 + 3.0 * 0.044715 * (x * x))
            factor = 0.5 * (1.0 + tanh) + 0.5 * x * (1.0 - tanh * tanh) * slope
            gz = (gu * factor).astype(bf16)
            gz_ref[rows, :] = gz
            up_sum = up_sum + jnp.sum(gz.astype(f32), axis=0, keepdims=True)
            out_ref[...] = dot(gz, w_ref[0]).astype(out_ref.dtype)
        sum_ref[0:1, :] = up_sum
        sum_ref[1:2, :] = jnp.sum(own_gy_ref[...].astype(f32), axis=0, keepdims=True)
        for number, left_ref, rights in (
            (0, gz_ref, (own_c_ref, other_c_ref)),
            (1, act_ref, (own_gy_ref, other_gy_ref)),
        ):
            put_grads(
                place_ref,
                dot_tokens(left_ref[...], both(*rights)),
                lambda block: grad_refs[0].at[block, number],
                lambda block: grad_refs[1].at[block, number],
                halves,
            )

    width = D // 2 if halves else D
    outs = [((half, D), f32), ((half, D), bf16), ((8, D), f32), ((4, 2, COLS, width), f32)]
    if halves:
        outs.append(((4, 2, COLS, width), bf16))
    return call(
        kernel,
        outs,
        place,
        gy_own,
        gy_other,
        c_own,
        c_other,
        preact,
        act,
        weights,
        scratch=[pltpu.VMEM((2 * half, D), bf16)],
    )


def core_swap(block):
    return lax.ppermute(block, "jc", SWAP)


def group_sum(mine, give):
    mine = mine + core_swap(give).astype(f32)
    return mine, lax.ppermute(mine.astype(bf16), "jx", SWAP)


def polynomial(base_ref, low_ref, mat_ref):
    low_ref[...] = base_ref[...].astype(bf16)
    for start in range(0, base_ref.shape[0], ROWS):
        block = pl.ds(start, ROWS)
        square = dot(low_ref[block, :], low_ref[...])
        mat_ref[block, :] = (quintic_two * base_ref[block, :] + quintic_three * square).astype(bf16)


def two_part(left, right):
    high = left.astype(bf16)
    rest = (left - high.astype(f32)).astype(bf16)
    return dot(high, right) + dot(rest, right)


def iterate(x_ref, out_ref, base_ref, work_ref, mat_ref, low_ref):
    size = x_ref.shape[0]
    blocks = [pl.ds(start, ROWS) for start in range(0, size, ROWS)]
    trace = jnp.zeros((1, 1), f32)
    line = lax.broadcasted_iota(jnp.int32, (ROWS, ROWS), 0)
    column = lax.broadcasted_iota(jnp.int32, (ROWS, ROWS), 1)
    for block in blocks:
        part = jnp.where(line == column, base_ref[block, block], 0.0)
        trace = trace + jnp.sum(part, keepdims=True)
    scale = 1.0 / (jnp.sqrt(trace) + 1e-07)
    base_ref[...] = base_ref[...] * (scale * scale)
    polynomial(base_ref, low_ref, mat_ref)

    for block in blocks:
        value = quintic_one * x_ref[block, :].astype(f32) + dot(x_ref[block, :], mat_ref[...])
        out_ref[block, :] = (scale * value).astype(bf16)
        work_ref[block, :] = quintic_one * base_ref[block, :] + two_part(
            base_ref[block, :], mat_ref[...]
        )
    turned = work_ref[...].T
    work_ref[...] = turned
    for block in blocks:
        base_ref[block, :] = quintic_one * work_ref[block, :] + two_part(
            work_ref[block, :], mat_ref[...]
        )
    polynomial(base_ref, low_ref, mat_ref)
    for block in blocks:
        x = out_ref[block, :]
        out_ref[block, :] = (quintic_one * x.astype(f32) + dot(x, mat_ref[...])).astype(bf16)


def orthogonalize(matrix, gram):
    size = matrix.shape[0]

    def kernel(unused, x_ref, gram_ref, out_ref, in_ref, base_ref, work_ref, mat_ref, low_ref):
        in_ref[...] = x_ref[...].T
        base_ref[...] = gram_ref[...]
        iterate(in_ref, out_ref, base_ref, work_ref, mat_ref, low_ref)
        out_ref[...] = out_ref[...].T

    return call(
        kernel,
        [((size, size), bf16)],
        jnp.zeros((1,), jnp.int32),
        matrix,
        gram,
        scratch=[pltpu.VMEM((size, size), kind) for kind in (bf16, f32, f32, bf16, bf16)],
    )[0]


def put_slots(slot_ref, x_ref):
    half = D // 2
    for source in range(8):
        group, number = source // TP, source % TP
        x_ref[number * COLS : (number + 1) * COLS, group * half : (group + 1) * half] = slot_ref[
            source
        ]


def slot_gram(place, slots):
    def kernel(place_ref, slot_ref, x_ref, gram_ref):
        put_slots(slot_ref, x_ref)
        half = D // 2
        for part in range(2):
            rows = dot_tokens(x_ref[:, part * half : (part + 1) * half], x_ref[...]).astype(bf16)
            for number in range(2):
                back = 2 * part + number - place_ref[0]
                back = jnp.where(back < 0, back + 4, back)
                gram_ref[back] = rows[number * COLS : (number + 1) * COLS]

    return call(kernel, [((D, D), bf16), ((4, COLS, D), bf16)], place, slots)


def slot_orthogonalize(place, x_wide, grams, square_slots):
    def kernel(
        place_ref,
        wide_ref,
        gram0_ref,
        gram1_ref,
        gram2_ref,
        gram3_ref,
        slot_ref,
        out_ref,
        x_ref,
        base_ref,
        work_ref,
        mat_ref,
        low_ref,
    ):
        core = place_ref[2]

        @pl.when(core == 0)
        def wide():
            x_ref[...] = wide_ref[...]
            for step, gram_ref in enumerate((gram0_ref, gram1_ref, gram2_ref, gram3_ref)):
                rows = pl.ds(pl.multiple_of(block_at(place_ref, step) * COLS, COLS), COLS)
                base_ref[rows, :] = gram_ref[...].astype(f32)

        @pl.when(core == 1)
        def square():
            put_slots(slot_ref, x_ref)
            base_ref[...] = dot_tokens(x_ref[...], x_ref[...])

        iterate(x_ref, out_ref, base_ref, work_ref, mat_ref, low_ref)

        @pl.when((core == 0) | (place_ref[0] < 3))
        def turn():
            out_ref[...] = out_ref[...].T

    return call(
        kernel,
        [((D, D), bf16)],
        place,
        x_wide,
        *grams,
        square_slots,
        scratch=[pltpu.VMEM((D, D), kind) for kind in (bf16, f32, f32, bf16, bf16)],
    )[0]


def slot_exchange(blocks):
    return lax.all_to_all(blocks, DP, split_axis=0, concat_axis=0, tiled=True)


def core_shift(block, step):
    size = lax.axis_size("ctx")
    return lax.ppermute(block, ("jc", "ctx"), [((i + step) % size, i) for i in range(size)])


def ctx_gram(gram):
    size = lax.axis_size("ctx")
    blocks = from_own(gram.astype(bf16).reshape(size, gram.shape[0] // size, -1))
    total = blocks[0].astype(f32)
    for step in (1, 3, 2):
        total = total + core_shift(blocks[step], -step).astype(f32)
    low = total.astype(bf16)
    full = [low] + [core_shift(low, step) for step in range(1, size)]
    return to_absolute(jnp.stack(full)).reshape(gram.shape).astype(f32)


def local(hidden_in, segments, out_grad, weights, vectors, mat_momentum, vec_first, vec_second):
    tokens_dev = hidden_in.shape[1]
    seq_len = segments.shape[1]
    half = 2 * tokens_dev
    dp_rows = weights.shape[2]
    ctx_size = lax.axis_size("ctx")
    x_index = lax.axis_index("jx")
    c_index = lax.axis_index("jc")
    t_index = 2 * x_index + c_index
    z_index = lax.axis_index("ctx")
    dp_index = lax.axis_index(DP)
    dp_size = lax.axis_size(DP)

    to_seq = []
    for t in range(TP):
        for z in range(ctx_size):
            to_seq.append((t * ctx_size + z, ((z % 2) * 2 + z // 2) * ctx_size + t))
    from_seq = [(b, a) for a, b in to_seq]
    axes = ("jx", "jc", "ctx")

    def x_join(block):
        return pair_join(block, "jx", 0)

    vec_rows = gather_vectors(vectors)
    seg_row = jnp.pad(segments.astype(f32), ((0, 7), (0, D - seq_len)))
    moved = lax.ppermute(jnp.concatenate([hidden_in[0], seg_row], axis=0), axes, to_seq)
    hidden = x_join(moved[:tokens_dev])
    segment_row = moved[tokens_dev, :seq_len]
    relative = lax.axis_size("g") == 2
    place = jnp.stack([z_index, lax.axis_index("g"), c_index]).astype(jnp.int32)
    if relative:
        piece, outs = first_piece(weights)
        own_attn = ctx_gather(piece)
        attn_weights = (own_attn, group_swap(own_attn))
        pieces = other_pieces(weights, outs, own_attn[1])
        own_mlp = ctx_gather(pieces[0], *own_attn[1:])
        mlp_weights = (own_mlp, group_swap_all(own_mlp))
    else:
        wide_weights = gather_weights_wide(weights.astype(bf16))

    start = c_index * half
    pos = jnp.concatenate([start + jnp.arange(half), half - start + jnp.arange(half)])
    seg = jnp.roll(segment_row.reshape(2, half), -c_index, axis=0).reshape(-1)
    info = jnp.stack([pos.astype(f32), seg])
    row_info = jnp.pad(info, ((0, 6), (0, 0)))
    column_info = jnp.pad(info.T, ((0, 0), (0, 126)))
    vec_mine = lax.dynamic_slice_in_dim(vec_rows, t_index * COLS, COLS, axis=2)
    no_bias = jnp.zeros((LAYERS, 1, COLS), f32)
    qkv_bias = jnp.concatenate([vec_mine[:, 4:5], no_bias, vec_mine[:, 5:6]], axis=2)
    up_bias = vec_mine[:, 8:12].reshape(LAYERS, 1, D)

    stored = []
    (a_own,) = norm_stage(vec_rows, 0, 0, hidden)
    for layer in range(LAYERS):
        following = layer + 1 < LAYERS
        a_other = core_swap(a_own)
        if not relative:
            attn_weights, mlp_weights = wide_weights[layer]
        w_attn, qkv, lse, o, mine, give = attend_stage(
            place, row_info, column_info, qkv_bias[layer], a_own, a_other, attn_weights
        )
        if relative and following:
            own_attn = ctx_gather(pieces[layer + 1][0], *own_mlp[1:])
            own_mlp = ctx_gather(pieces[layer + 1][1], *own_attn[1:])
        mine, recv = group_sum(mine, give)
        middle, c_own = norm_stage(vec_rows, layer, 2, hidden, mine, recv, (layer, 6))
        c_other = core_swap(c_own)
        w_mlp, preact, act, mine, give = feed_stage(
            place, up_bias[layer], c_own, c_other, mlp_weights
        )
        if relative and following:
            attn_weights = (own_attn, group_swap_all(own_attn))
            mlp_weights = (own_mlp, group_swap_all(own_mlp))
        mine, recv = group_sum(mine, give)
        stored.append(
            (hidden, middle, a_own, a_other, qkv, lse, o, c_own, c_other, preact, act, w_attn, w_mlp)
        )
        if following:
            hidden, a_own = norm_stage(vec_rows, layer + 1, 0, middle, mine, recv, (layer, 7))
        else:
            hidden = middle + (mine + recv.astype(f32) + vec_rows[layer, 7:8])

    def send_back(rows):
        block = lax.dynamic_slice_in_dim(rows, x_index * tokens_dev, tokens_dev, axis=0)
        return lax.ppermute(block, axes, from_seq)

    hidden_out = send_back(hidden)
    if relative:
        scaled = after(mat_momentum, stored[0][6]) * (momentum_decay * momentum_decay)
        moments = momentum_pieces(scaled.astype(bf16))
    grad_hidden = x_join(lax.ppermute(after(out_grad[0], own_mlp[2] if relative else stored[-1][6]), axes, to_seq))
    gy_own = grad_hidden.astype(bf16)
    attn_half = mlp_half = None

    mat_list = [None] * LAYERS
    sum_list = [None] * LAYERS
    parts = [None] * LAYERS
    for layer in reversed(range(LAYERS)):
        h_in, middle, a_own, a_other, qkv, lse, o, c_own, c_other, preact, act, w_attn, w_mlp = stored[
            layer
        ]
        if relative and attn_half is not None:
            gy_own, attn_half, mlp_half = lax.optimization_barrier((gy_own, attn_half, mlp_half))
            part = ctx_sum(jnp.concatenate([attn_half[:, None], mlp_half], axis=1))
        gy_other = core_swap(gy_own)
        mine, give, up_sums, *mlp_grads = feed_back_stage(
            place, gy_own, gy_other, c_own, c_other, preact, act, w_mlp, relative
        )
        if relative:
            mlp_half = half_sum(*mlp_grads)
        mine, recv = group_sum(mine, give)
        grad_middle, gb_own, mid_sums = norm_back_stage(
            vec_rows, layer, 2, grad_hidden, mine, recv, middle
        )
        if relative and attn_half is not None:
            gb_own, part = lax.optimization_barrier((gb_own, part))
            parts[layer + 1] = part
        if layer == LAYERS - 1:
            gb_own, hidden_out = lax.optimization_barrier((gb_own, hidden_out))
        gb_other = core_swap(gb_own)
        mine, give, qkv_sums, *attn_grads = attend_back_stage(
            place,
            row_info,
            column_info,
            gb_own,
            gb_other,
            a_own,
            a_other,
            qkv,
            lse,
            o,
            w_attn,
            relative,
        )
        if relative:
            mine, mlp_half = lax.optimization_barrier((mine, mlp_half))
            if layer == 0:
                mlp_part = ctx_sum(mlp_half)
            attn_half = half_sum(*attn_grads)
        else:
            attn_grad = attn_grads[0]
            g_wo = lax.all_to_all(
                attn_grad[3].reshape(COLS, TP, COLS), GROUP, split_axis=1, concat_axis=0, tiled=True
            )[:, 0]
            attn_grad = jnp.concatenate([attn_grad[:3], g_wo.T[None]], axis=0)
            mat_list[layer] = scatter_wide(
                jnp.concatenate([attn_grad[:, None], mlp_grads[0]], axis=1)
            )
        mine, recv = group_sum(mine, give)
        grad_hidden, gy_own, in_sums = norm_back_stage(
            vec_rows, layer, 0, grad_middle, mine, recv, h_in
        )
        sum_list[layer] = (in_sums, mid_sums, up_sums, qkv_sums)
    input_grad = send_back(grad_hidden)

    once = jnp.where(x_index == 0, 1.0, 0.0).astype(f32)
    in_sums, mid_sums, up_sums, qkv_sums = [jnp.stack(sums) for sums in zip(*sum_list)]
    shared = once * jnp.concatenate(
        [in_sums[:, 0:2], mid_sums[:, 0:3], up_sums[:, 1:2]], axis=1
    )
    placed = jnp.concatenate(
        [
            qkv_sums[:, 0:1, :COLS],
            qkv_sums[:, 0:1, 2 * COLS :],
            up_sums[:, 0].reshape(LAYERS, ctx_size, COLS),
        ],
        axis=1,
    )
    placed = lax.dynamic_update_slice_in_dim(
        jnp.zeros((LAYERS, 6, D), f32), placed, t_index * COLS, axis=2
    )
    vec_terms = jnp.concatenate(
        [shared[:, 0:4], placed[:, 0:2], shared[:, 4:6], placed[:, 2:6]], axis=1
    )
    grad_vecs = lax.dynamic_slice_in_dim(
        sum_vectors(vec_terms), dp_index * vectors.shape[2], vectors.shape[2], axis=2
    )
    if relative:
        wide_low = [parts[layer][1:] * (1.0 + momentum_decay) for layer in range(1, LAYERS)]
        wide_low = jnp.concatenate(wide_low + [mlp_part * (1.0 + momentum_decay)])
        moment_wide = jnp.concatenate([moments[layer, 1:] for layer in (*range(1, LAYERS), 0)])
        wide_low = (wide_low + moment_wide.astype(f32)).astype(bf16)
        received = slot_exchange(jnp.repeat(wide_low, 2, axis=0))
        x_wide, gram_blocks = slot_gram(place, received)
        attn_part = ctx_sum(attn_half)
        square_low = [parts[layer][0] for layer in range(1, LAYERS)] + [attn_part]
        square_low = jnp.stack(square_low) * (1.0 + momentum_decay)
        moment_square = jnp.stack([moments[layer, 0] for layer in (*range(1, LAYERS), 0)])
        square_low = (square_low + moment_square.astype(f32)).astype(bf16)
        square_slots = slot_exchange(jnp.tile(jnp.repeat(square_low, 2, axis=0), (2, 1, 1)))
        total = gram_blocks[0].astype(f32)
        for step in (1, 3, 2):
            total = total + core_shift(gram_blocks[step], -step).astype(f32)
        low = total.astype(bf16)
        near, back, far = [core_shift(low, step) for step in (1, 3, 2)]
        ortho_mine = slot_orthogonalize(place, x_wide, (low, near, far, back), square_slots)
        returned = slot_exchange(ortho_mine.reshape(dp_size, dp_rows, D))
        ortho = jnp.stack([returned[3], returned[4], returned[6], returned[1], returned[0], returned[2]])
        ortho = ortho.reshape(weights.shape).astype(f32)
        first = jnp.concatenate([attn_part[None], mlp_part])
        grad_mats = grad_rows(jnp.stack([first, *parts[1:]]).astype(bf16))
        moment_new = momentum_decay * mat_momentum + grad_mats
    else:
        cols_dev = weights.shape[3]
        grad_list, moment_list, low_list = [], [], []
        for layer in range(LAYERS):
            for item in range(3):
                grad = mat_list[layer][item]
                moment = momentum_decay * mat_momentum[layer, item] + grad
                grad_list.append(grad)
                moment_list.append(moment)
                low_list.append((grad + momentum_decay * moment).astype(bf16))
        wide = [item for item in range(3 * LAYERS) if item % 3]
        squares = [item for item in range(3, 3 * LAYERS, 3)]
        table = []
        for number in range(4):
            table += [wide[number], squares[number % len(squares)]]
        table = (table * (-(-dp_size // 8)))[:dp_size]
        slots = jnp.stack([low_list[item] for item in table])
        received = lax.all_to_all(slots[:, None], DP, split_axis=0, concat_axis=1, tiled=True)
        current = received.reshape(dp_size * dp_rows, cols_dev)
        gram_local = dot_trans(current, current)
        gram = jnp.where(c_index == 0, ctx_gram(gram_local), gram_local)
        ortho_mine = orthogonalize(current, gram)
        returned = lax.all_to_all(
            ortho_mine.reshape(dp_size, 1, dp_rows, cols_dev),
            DP,
            split_axis=0,
            concat_axis=1,
            tiled=True,
        )[0]
        first_full = lax.all_gather(low_list[0], DP, axis=0, tiled=True)
        first_ortho = orthogonalize(first_full, dot_trans(first_full, first_full))
        ortho_list = [lax.dynamic_slice_in_dim(first_ortho, dp_index * dp_rows, dp_rows, axis=0)]
        ortho_list += [returned[table.index(item)] for item in range(1, 3 * LAYERS)]
        ortho = jnp.stack(ortho_list).reshape(LAYERS, 3, dp_rows, cols_dev).astype(f32)
        grad_mats = jnp.stack(grad_list).reshape(weights.shape)
        moment_new = jnp.stack(moment_list).reshape(weights.shape)
    factor = jnp.array([0.2 * math.sqrt(D), 0.2 * math.sqrt(FF), 0.2 * math.sqrt(FF)], f32)
    weights_new = weights * (1.0 - matrix_rate * matrix_decay) - matrix_rate * (
        ortho * factor[None, :, None, None]
    )
    first_new = first_decay * vec_first + (1.0 - first_decay) * grad_vecs
    second_new = second_decay * vec_second + (1.0 - second_decay) * grad_vecs * grad_vecs
    first_hat = first_new / (1.0 - first_decay**ADAM_STEP)
    second_hat = second_new / (1.0 - second_decay**ADAM_STEP)
    vectors_new = vectors * (1.0 - vector_rate * vector_decay) - vector_rate * first_hat / (
        jnp.sqrt(second_hat) + adam_epsilon
    )
    return (
        hidden_out[None],
        input_grad[None],
        grad_mats,
        moment_new,
        weights_new,
        grad_vecs,
        second_new,
        vectors_new,
    )


def solution(mesh):
    dp, ctx = mesh.shape["dp"], mesh.shape["ctx"]
    fine = Mesh(mesh.devices.reshape(dp // TP, 2, 2, ctx), EVERY)
    tokens = P(DP, "ctx", None)
    mats = P(None, None, DP, "ctx")
    vecs = P(None, "ctx", DP)
    return jax.shard_map(
        local,
        mesh=fine,
        in_specs=(tokens, P(DP, None), tokens, mats, vecs, mats, vecs, vecs),
        out_specs=(tokens, tokens, mats, mats, mats, vecs, vecs, vecs),
        check_vma=False,
    )
```

```python
import math

import jax
import jax.numpy as jnp
from jax import lax
from jax.experimental import pallas as pl
from jax.experimental.pallas import tpu as pltpu
from jax.sharding import Mesh, PartitionSpec as P

D = 768
HEADS = 12
HEAD = 64
FF = 3072
LAYERS = 2
ADAM_STEP = 10
TP = 4
COLS = D // TP
TP_HEADS = HEADS // TP
ROWS = 256

norm_epsilon = 1e-05
quintic_one = 3.4445
quintic_two = -4.775
quintic_three = 2.0315
momentum_decay = 0.95
matrix_rate = 0.6
matrix_decay = 0.01
first_decay = 0.9
second_decay = 0.999
vector_rate = 0.5
vector_decay = 0.01
adam_epsilon = 1e-08
masked_score = -1e30

GROUP = ("jx", "jc")
REPLICAS = ("g", "ctx")
DP = ("g", "jx", "jc")
EVERY = ("g", "jx", "jc", "ctx")
SWAP = [(0, 1), (1, 0)]
bf16 = jnp.bfloat16
f32 = jnp.float32


def dot(operand, other):
    return jnp.dot(operand, other, preferred_element_type=f32)


def dot_tokens(operand, other):
    return lax.dot_general(operand, other, (((0,), (0,)), ((), ())), preferred_element_type=f32)


def dot_trans(operand, other):
    return lax.dot_general(operand, other, (((1,), (1,)), ((), ())), preferred_element_type=f32)


def to_group(mats):
    count, rows, width = mats.shape
    split = mats.reshape(count, rows, TP, width // TP)
    return lax.all_to_all(split, GROUP, split_axis=2, concat_axis=1, tiled=True)[:, :, 0]


def from_group(mats):
    count, rows, width = mats.shape
    split = mats.reshape(count, TP, rows // TP, width)
    return lax.all_to_all(split, GROUP, split_axis=1, concat_axis=3, tiled=True)[:, 0]


def rotate(block, axis, step):
    size = lax.axis_size(axis)
    return lax.ppermute(block, axis, [((i + step) % size, i) for i in range(size)])


def pair_join(block, axis, dim):
    other = lax.ppermute(block, axis, SWAP)
    first = lax.axis_index(axis) == 0
    return jnp.concatenate(
        [jnp.where(first, block, other), jnp.where(first, other, block)], axis=dim
    )


def after(value, *others):
    return lax.optimization_barrier((value, *others))[0]


def roll_blocks(stack, sign):
    place = lax.axis_index("ctx")
    for bit in (1, 2):
        moved = jnp.roll(stack, sign * bit, axis=0)
        stack = jnp.where((place & bit) != 0, moved, stack)
    return stack


def from_own(stack):
    return roll_blocks(stack, -1)


def to_absolute(stack):
    return roll_blocks(stack, 1)


def out_moves():
    last = lax.axis_size("ctx") - 1
    size = last + 1
    moves = []
    for y in range(2):
        for x in range(2):
            for core in range(2):
                moves.append(
                    ((4 * y + 2 * x + core) * size + last, (4 * core + 2 * y + x) * size + last)
                )
    return moves


def out_pieces(mats):
    half = mats.shape[2] // 2
    core = lax.axis_index("jc")
    mine = lax.dynamic_slice_in_dim(mats, core * half, half, axis=2)
    give = lax.dynamic_slice_in_dim(mats, (1 - core) * half, half, axis=2)
    got = lax.ppermute(give, "jc", SWAP)
    rows = jnp.concatenate(
        [jnp.where(core == 0, mine, got), jnp.where(core == 0, got, mine)], axis=1
    )
    return lax.ppermute(rows, EVERY, out_moves())


def out_back(pieces):
    core = lax.axis_index("jc")
    rows = lax.ppermute(pieces, EVERY, [(b, a) for a, b in out_moves()])
    half = rows.shape[1] // 2
    mine = lax.dynamic_slice_in_dim(rows, core * half, half, axis=1)
    give = lax.dynamic_slice_in_dim(rows, (1 - core) * half, half, axis=1)
    got = lax.ppermute(give, "jc", SWAP)
    return jnp.concatenate(
        [jnp.where(core == 0, mine, got), jnp.where(core == 0, got, mine)], axis=2
    )


def last_block():
    return lax.axis_index("ctx") == lax.axis_size("ctx") - 1


def split_columns(mats, items):
    rows = mats.shape[2]

    def kernel(unused, mats_ref, out_ref):
        for number, (layer, item) in enumerate(items):
            turned = mats_ref[layer, item].T.astype(bf16)
            for quarter in range(TP):
                out_ref[quarter, number] = turned[quarter * COLS : (quarter + 1) * COLS]

    outs = [((TP, len(items), COLS, rows), bf16)]
    return call(kernel, outs, jnp.zeros((1,), jnp.int32), mats)[0]


def join_columns(place, blocks, outs, items):
    rows = blocks.shape[3]

    def kernel(place_ref, blocks_ref, outs_ref, *out_refs):
        for number, (layer, item) in enumerate(items):
            for source in range(TP):
                lanes = slice(source * rows, (source + 1) * rows)
                out_refs[number][:, lanes] = blocks_ref[source, number]
            if item == 0:

                @pl.when(place_ref[0] == 3)
                def last(number=number, layer=layer):
                    out_refs[number][...] = outs_ref[layer]

    shapes = [((COLS, TP * rows), bf16)] * len(items)
    return call(kernel, shapes, place, blocks, outs)


def group_exchange(blocks):
    return lax.all_to_all(blocks, GROUP, split_axis=0, concat_axis=0, tiled=True)


def first_piece(place, mats):
    outs = out_pieces(mats[:, 0].astype(bf16))
    blocks = group_exchange(split_columns(mats, [(0, 0)]))
    return join_columns(place, blocks, outs, [(0, 0)])[0], outs


def other_pieces(place, mats, outs, *earlier):
    items = [(layer, item) for layer in range(mats.shape[0]) for item in range(3)][1:]
    blocks = group_exchange(split_columns(after(mats, *earlier), items))
    return join_columns(place, blocks, outs, items)


def ctx_gather(piece, *earlier):
    piece = after(piece, *earlier)
    near, back, far = [rotate(piece, "ctx", step) for step in (1, 3, 2)]
    return [piece, near, far, back]


def group_swap(blocks):
    return [lax.ppermute(block, "g", SWAP) for block in blocks]


def ctx_group_gather(pieces, *earlier):
    piece = after(jnp.stack(pieces), *earlier)
    near, back = [rotate(piece, "ctx", step) for step in (1, 3)]
    far = rotate(after(piece, near, back), "ctx", 2)
    first = lax.ppermute(jnp.stack([piece, near, back]), "g", SWAP)
    return [piece, near, far, back], [first, lax.ppermute(after(far, first), "g", SWAP)]


def gather_weights_wide(low):
    result = []
    for layer in range(low.shape[0]):
        mats = to_group(low[layer])
        parts = lax.all_gather(mats, REPLICAS, axis=0, tiled=False)
        parts = parts.reshape(lax.axis_size("g"), -1, *mats.shape)
        full = [parts[:, :, item].transpose(1, 3, 0, 2).reshape(D, D) for item in range(3)]
        w_o = lax.all_to_all(
            full[0][3 * COLS :].T.reshape(TP, COLS, COLS),
            GROUP,
            split_axis=0,
            concat_axis=2,
            tiled=True,
        )
        attn = jnp.concatenate([full[0][: 3 * COLS].reshape(3, COLS, D), w_o], axis=0)
        result.append((attn.reshape(D, D), jnp.stack([full[1], full[2]])))
    return result


def half_sum(mine, give):
    return mine + lax.ppermute(give, "g", SWAP).astype(f32)


def ctx_sum(blocks):
    return ctx_sum_last(blocks, ctx_sum_first(blocks))


def ctx_sum_first(blocks):
    low = blocks.astype(bf16)
    near, back = [rotate(low[step], "ctx", -step) for step in (1, 3)]
    return blocks[0] + near.astype(f32) + back.astype(f32)


def ctx_sum_last(blocks, total):
    far = rotate(after(blocks[2], total).astype(bf16), "ctx", -2)
    return total + far.astype(f32)


def grad_rows(place, attn_parts, mlp_parts, momentum):
    layers, count, rows, width = momentum.shape
    half = width // 2
    zero = jnp.zeros((1,), jnp.int32)

    def split(unused, *refs):
        *part_refs, out_ref = refs
        for layer in range(layers):
            for item in range(3):
                if item:
                    part = part_refs[layers + layer][item - 1]
                else:
                    part = part_refs[layer][...]
                turned = part.T.astype(bf16)
                for target in range(TP):
                    out_ref[target, 3 * layer + item] = turned[target * rows : (target + 1) * rows]

    blocks = call(split, [((TP, 3 * layers, rows, COLS), bf16)], zero, *attn_parts, *mlp_parts)[0]
    blocks = group_exchange(blocks)
    outs = out_back(jnp.stack(attn_parts).astype(bf16))

    def join(place_ref, blocks_ref, outs_ref, momentum_ref, grad_ref, new_ref):
        for layer in range(layers):
            for item in range(3):
                for source in range(TP):
                    lanes = slice(source * COLS, (source + 1) * COLS)
                    grad_ref[layer, item, :, lanes] = blocks_ref[source, 3 * layer + item].astype(f32)

            @pl.when(place_ref[0] == 3)
            def last(layer=layer):
                grad_ref[layer, 0] = outs_ref[layer].astype(f32)

        new_ref[...] = momentum_decay * momentum_ref[...] + grad_ref[...]

    shape = (momentum.shape, f32)
    return call(join, [shape, shape], place, blocks, outs, momentum)


def scatter_wide(mats):
    groups = lax.axis_size("g")
    blocks, count, width, depth = mats.shape
    stack = mats.astype(bf16).reshape(blocks, count, width, groups, depth // groups)
    stack = stack.transpose(3, 0, 1, 4, 2).reshape(groups * blocks, count, -1, width)
    part = lax.psum_scatter(stack, REPLICAS, scatter_dimension=0, tiled=True)[0]
    return from_group(part).astype(f32)


def gather_vectors(vectors):
    low = vectors.astype(bf16)
    stack = jnp.stack([low] + [rotate(low, "ctx", step) for step in range(1, 4)])
    stack = pair_join(pair_join(to_absolute(stack), "jc", 3), "jx", 3)
    if lax.axis_size("g") == 2:
        stack = pair_join(stack, "g", 3)
    else:
        stack = lax.all_gather(stack, "g", axis=3, tiled=True)
    return stack.transpose(1, 0, 2, 3).reshape(low.shape[0], -1, D).astype(f32)


def sum_vectors(terms):
    if lax.axis_size("g") == 2:
        terms = terms + lax.ppermute(terms, "g", SWAP)
    else:
        terms = lax.psum(terms, "g")
    layers, rows, width = terms.shape
    blocks = from_own(terms.reshape(layers, 4, rows // 4, width).transpose(1, 0, 2, 3))
    total = blocks[0]
    for step in range(1, 4):
        total = total + rotate(blocks[step], "ctx", -step)
    total = total + lax.ppermute(total, "jc", SWAP)
    return total + lax.ppermute(total, "jx", SWAP)


def call(kernel, outs, *args, scratch=()):
    return pl.pallas_call(
        kernel,
        out_shape=[jax.ShapeDtypeStruct(shape, kind) for shape, kind in outs],
        in_specs=[pl.BlockSpec(memory_space=pltpu.SMEM)]
        + [pl.BlockSpec(memory_space=pltpu.VMEM)] * (len(args) - 1),
        out_specs=[pl.BlockSpec(memory_space=pltpu.VMEM)] * len(outs),
        scratch_shapes=list(scratch),
        compiler_params=pltpu.CompilerParams(vmem_limit_bytes=52 * 1024 * 1024),
    )(*args)


def block_at(place_ref, step):
    ahead = place_ref[0] + step
    return jnp.where(ahead >= 4, ahead - 4, ahead)


def put_blocks(place_ref, own_refs, other_refs, full_refs):
    half = D // 2
    mine = pl.multiple_of(place_ref[1] * half, half)
    theirs = pl.multiple_of((1 - place_ref[1]) * half, half)
    for step in range(4):
        rows = pl.ds(pl.multiple_of(block_at(place_ref, step) * COLS, COLS), COLS)
        for number, full_ref in enumerate(full_refs):
            own, other = own_refs[step], other_refs[step]
            if len(full_refs) > 1:
                own, other = own.at[number], other.at[number]
            full_ref[rows, pl.ds(mine, half)] = own[...]
            full_ref[rows, pl.ds(theirs, half)] = other[...]


def put_grads(place_ref, grad, mine_refs, give_refs, halves):
    half = D // 2
    for block in range(4):
        rows = grad[block * COLS : (block + 1) * COLS]
        if halves:
            back = block - place_ref[0]
            back = jnp.where(back < 0, back + 4, back)
            low = place_ref[1] == 0
            mine_refs(back)[...] = jnp.where(low, rows[:, :half], rows[:, half:])
            give_refs(back)[...] = jnp.where(low, rows[:, half:], rows[:, :half]).astype(bf16)
        else:
            mine_refs(block)[...] = rows


def norm_rows(hidden):
    center = hidden - jnp.mean(hidden, axis=-1, keepdims=True)
    variance = jnp.mean(center * center, axis=-1, keepdims=True)
    inverse = lax.rsqrt(variance + norm_epsilon)
    return center * inverse, inverse


def norm_stage(vecs, layer, row, hidden, mine=None, recv=None, bias=None):
    rows = hidden.shape[0]

    def kernel(unused, vec_ref, hidden_ref, *refs):
        total = hidden_ref[...]
        if mine is not None:
            mine_ref, recv_ref, total_ref, out_ref = refs
            bias_row = vec_ref[bias[0], bias[1] : bias[1] + 1, :]
            total = total + (mine_ref[...] + recv_ref[...].astype(f32) + bias_row)
            total_ref[...] = total
        else:
            (out_ref,) = refs
        normed, unused_scale = norm_rows(total)
        gain = vec_ref[layer, row : row + 1, :]
        shift = vec_ref[layer, row + 1 : row + 2, :]
        out_ref[...] = (normed * gain + shift).astype(bf16)

    outs = [((rows, D), bf16)]
    args = [hidden]
    if mine is not None:
        outs = [((rows, D), f32)] + outs
        args += [mine, recv]
    return call(kernel, outs, jnp.zeros((1,), jnp.int32), vecs, *args)


def norm_back_stage(vecs, layer, row, grad, mine, recv, hidden):
    rows = hidden.shape[0]

    def kernel(unused, vec_ref, grad_ref, mine_ref, recv_ref, hidden_ref, out_ref, low_ref, sum_ref):
        through = mine_ref[...] + recv_ref[...].astype(f32)
        normed, inverse = norm_rows(hidden_ref[...])
        scaled = through * vec_ref[layer, row : row + 1, :]
        part = jnp.mean(scaled, axis=-1, keepdims=True)
        part = part + normed * jnp.mean(scaled * normed, axis=-1, keepdims=True)
        total = grad_ref[...] + inverse * (scaled - part)
        out_ref[...] = total
        low = total.astype(bf16)
        low_ref[...] = low
        sum_ref[0:1, :] = jnp.sum(through * normed, axis=0, keepdims=True)
        sum_ref[1:2, :] = jnp.sum(through, axis=0, keepdims=True)
        sum_ref[2:3, :] = jnp.sum(low.astype(f32), axis=0, keepdims=True)

    outs = [((rows, D), f32), ((rows, D), bf16), ((8, D), f32)]
    return call(kernel, outs, jnp.zeros((1,), jnp.int32), vecs, grad, mine, recv, hidden)


def both(first_ref, second_ref):
    return jnp.concatenate([first_ref[...], second_ref[...]], axis=0)


def allowed_of(row_ref, column_ref):
    before = row_ref[0:1, :] <= column_ref[:, 0:1]
    return before & (row_ref[1:2, :] == column_ref[:, 1:2])


def attend_stage(place, row_info, column_info, bias, a_own, a_other, weights):
    half = a_own.shape[0]
    tokens = 2 * half
    wide = 3 * COLS
    own, other = weights if isinstance(weights, tuple) else ([], [])

    def kernel(place_ref, row_ref, column_ref, bias_ref, own_a_ref, other_a_ref, *refs):
        if own:
            own_refs, refs = refs[:4], refs[4:]
            others, refs = refs[: len(other)], refs[len(other) :]
            if len(other) == 2:
                own_refs = [ref.at[0] for ref in own_refs]
                first, last = others
                others = [first.at[0, 0], first.at[1, 0], last.at[0], first.at[2, 0]]
            w_ref, qkv_ref, lse_ref, o_ref, mine_ref, give_ref = refs
            put_blocks(place_ref, own_refs, others, [w_ref])
        else:
            w_ref, qkv_ref, lse_ref, o_ref, mine_ref, give_ref = refs
        for start, a_ref in ((0, own_a_ref), (half, other_a_ref)):
            proj = dot_trans(a_ref[...], w_ref[0:wide, :]) + bias_ref[0:1, :]
            qkv_ref[start : start + half, :] = proj.astype(bf16)
        allowed = allowed_of(row_ref, column_ref)
        for head in range(TP_HEADS):
            lanes = head * HEAD
            k = qkv_ref[:, COLS + lanes : COLS + lanes + HEAD]
            v = qkv_ref[:, 2 * COLS + lanes : 2 * COLS + lanes + HEAD]
            for start in (0, half):
                rows = slice(start, start + half)
                q = qkv_ref[rows, lanes : lanes + HEAD]
                scores = jnp.where(allowed[rows], dot_trans(q, k) * HEAD ** (-0.5), masked_score)
                top = jnp.max(scores, axis=-1, keepdims=True)
                unnormed = jnp.exp(scores - top)
                total = jnp.sum(unnormed, axis=-1, keepdims=True)
                prob = (unnormed * (1.0 / total)).astype(bf16)
                o_ref[rows, lanes : lanes + HEAD] = dot(prob, v).astype(bf16)
                lse_ref[rows, head : head + 1] = top + jnp.log(total)
        mine_ref[...] = dot(o_ref[0:half, :], w_ref[wide:, :])
        give_ref[...] = dot(o_ref[half:, :], w_ref[wide:, :]).astype(bf16)

    outs = [
        ((tokens, wide), bf16),
        ((tokens, 128), f32),
        ((tokens, COLS), bf16),
        ((half, D), f32),
        ((half, D), bf16),
    ]
    if own:
        outs = [((D, D), bf16)] + outs
        return call(
            kernel, outs, place, row_info, column_info, bias, a_own, a_other, *own, *other
        )
    result = call(kernel, outs, place, row_info, column_info, bias, a_own, a_other, weights)
    return [weights] + list(result)


def attend_back_stage(
    place, row_info, column_info, gb_own, gb_other, a_own, a_other, qkv, lse, o, w_attn, halves
):
    half = a_own.shape[0]
    tokens = 2 * half
    wide = 3 * COLS

    def kernel(
        place_ref,
        row_ref,
        column_ref,
        own_gb_ref,
        other_gb_ref,
        own_a_ref,
        other_a_ref,
        qkv_ref,
        lse_ref,
        o_ref,
        w_ref,
        mine_ref,
        give_ref,
        sum_ref,
        *refs,
    ):
        *grad_refs, go_ref, all_ref = refs
        w_o = w_ref[wide:, :]
        for start, gb_ref in ((0, own_gb_ref), (half, other_gb_ref)):
            go_ref[start : start + half, :] = dot_trans(gb_ref[...], w_o).astype(bf16)
        allowed = allowed_of(row_ref, column_ref)
        for head in range(TP_HEADS):
            lanes = head * HEAD
            q_lanes = slice(lanes, lanes + HEAD)
            k_lanes = slice(COLS + lanes, COLS + lanes + HEAD)
            v_lanes = slice(2 * COLS + lanes, 2 * COLS + lanes + HEAD)
            k = qkv_ref[:, k_lanes]
            v = qkv_ref[:, v_lanes]
            gk = jnp.zeros((tokens, HEAD), f32)
            gv = jnp.zeros((tokens, HEAD), f32)
            for start in (0, half):
                rows = slice(start, start + half)
                q = qkv_ref[rows, q_lanes]
                go = go_ref[rows, q_lanes]
                scores = jnp.where(allowed[rows], dot_trans(q, k) * HEAD ** (-0.5), masked_score)
                prob = jnp.exp(scores - lse_ref[rows, head : head + 1])
                g_prob = dot_trans(go, v)
                row_dot = jnp.sum(g_prob * prob, axis=-1, keepdims=True)
                g_scores = (prob * (g_prob - row_dot)).astype(bf16)
                all_ref[rows, q_lanes] = (dot(g_scores, k) * HEAD ** (-0.5)).astype(bf16)
                gk = gk + dot_tokens(g_scores, q)
                gv = gv + dot_tokens(prob.astype(bf16), go)
            all_ref[:, k_lanes] = (gk * HEAD ** (-0.5)).astype(bf16)
            all_ref[:, v_lanes] = gv.astype(bf16)
        mine_ref[...] = dot(all_ref[0:half, :], w_ref[0:wide, :])
        give_ref[...] = dot(all_ref[half:, :], w_ref[0:wide, :]).astype(bf16)
        sum_ref[0:1, :] = jnp.sum(all_ref[...].astype(f32), axis=0, keepdims=True)
        grad = jnp.concatenate(
            [
                dot_tokens(all_ref[...], both(own_a_ref, other_a_ref)),
                dot_tokens(o_ref[...], both(own_gb_ref, other_gb_ref)),
            ],
            axis=0,
        )
        put_grads(
            place_ref,
            grad,
            lambda block: grad_refs[0].at[block],
            lambda block: grad_refs[1].at[block],
            halves,
        )

    width = D // 2 if halves else D
    outs = [((half, D), f32), ((half, D), bf16), ((8, wide), f32), ((4, COLS, width), f32)]
    if halves:
        outs.append(((4, COLS, width), bf16))
    return call(
        kernel,
        outs,
        place,
        row_info,
        column_info,
        gb_own,
        gb_other,
        a_own,
        a_other,
        qkv,
        lse,
        o,
        w_attn,
        scratch=[pltpu.VMEM((tokens, COLS), bf16), pltpu.VMEM((tokens, wide), bf16)],
    )


def tanh_part(preact):
    inner = math.sqrt(2.0 / math.pi) * (preact + 0.044715 * (preact * preact * preact))
    return jnp.tanh(inner)


def feed_stage(place, bias, c_own, c_other, weights):
    half = c_own.shape[0]
    own, other = weights if isinstance(weights, tuple) else ([], [])

    def kernel(place_ref, bias_ref, own_c_ref, other_c_ref, *refs):
        if own:
            own_refs, (first, last), refs = refs[:4], refs[4:6], refs[6:]
            others = [first.at[0], first.at[1], last, first.at[2]]
            w_ref, preact_ref, act_ref, mine_ref, give_ref = refs
            put_blocks(place_ref, own_refs, others, [w_ref.at[0], w_ref.at[1]])
        else:
            w_ref, preact_ref, act_ref, mine_ref, give_ref = refs
        for start, c_ref, out_ref in ((0, own_c_ref, mine_ref), (half, other_c_ref, give_ref)):
            rows = slice(start, start + half)
            preact = dot_trans(c_ref[...], w_ref[0]) + bias_ref[...]
            preact_ref[rows, :] = preact
            act = (0.5 * preact * (1.0 + tanh_part(preact))).astype(bf16)
            act_ref[rows, :] = act
            out_ref[...] = dot(act, w_ref[1]).astype(out_ref.dtype)

    outs = [
        ((2 * half, D), f32),
        ((2 * half, D), bf16),
        ((half, D), f32),
        ((half, D), bf16),
    ]
    if own:
        outs = [((2, D, D), bf16)] + outs
        return call(kernel, outs, place, bias, c_own, c_other, *own, *other)
    return [weights] + list(call(kernel, outs, place, bias, c_own, c_other, weights))


def feed_back_stage(place, gy_own, gy_other, c_own, c_other, preact, act, weights, halves):
    half = c_own.shape[0]

    def kernel(
        place_ref,
        own_gy_ref,
        other_gy_ref,
        own_c_ref,
        other_c_ref,
        preact_ref,
        act_ref,
        w_ref,
        mine_ref,
        give_ref,
        sum_ref,
        *refs,
    ):
        *grad_refs, gz_ref = refs
        up_sum = jnp.zeros((1, D), f32)
        for start, gy_ref, out_ref in ((0, own_gy_ref, mine_ref), (half, other_gy_ref, give_ref)):
            rows = slice(start, start + half)
            gu = dot_trans(gy_ref[...], w_ref[1])
            x = preact_ref[rows, :]
            tanh = tanh_part(x)
            slope = math.sqrt(2.0 / math.pi) * (1.0 + 3.0 * 0.044715 * (x * x))
            factor = 0.5 * (1.0 + tanh) + 0.5 * x * (1.0 - tanh * tanh) * slope
            gz = (gu * factor).astype(bf16)
            gz_ref[rows, :] = gz
            up_sum = up_sum + jnp.sum(gz.astype(f32), axis=0, keepdims=True)
            out_ref[...] = dot(gz, w_ref[0]).astype(out_ref.dtype)
        sum_ref[0:1, :] = up_sum
        sum_ref[1:2, :] = jnp.sum(own_gy_ref[...].astype(f32), axis=0, keepdims=True)
        for number, left_ref, rights in (
            (0, gz_ref, (own_c_ref, other_c_ref)),
            (1, act_ref, (own_gy_ref, other_gy_ref)),
        ):
            put_grads(
                place_ref,
                dot_tokens(left_ref[...], both(*rights)),
                lambda block: grad_refs[0].at[block, number],
                lambda block: grad_refs[1].at[block, number],
                halves,
            )

    width = D // 2 if halves else D
    outs = [((half, D), f32), ((half, D), bf16), ((8, D), f32), ((4, 2, COLS, width), f32)]
    if halves:
        outs.append(((4, 2, COLS, width), bf16))
    return call(
        kernel,
        outs,
        place,
        gy_own,
        gy_other,
        c_own,
        c_other,
        preact,
        act,
        weights,
        scratch=[pltpu.VMEM((2 * half, D), bf16)],
    )


def core_swap(block):
    return lax.ppermute(block, "jc", SWAP)


def group_sum(mine, give):
    mine = mine + core_swap(give).astype(f32)
    return mine, lax.ppermute(mine.astype(bf16), "jx", SWAP)


def polynomial(base_ref, low_ref, mat_ref):
    low_ref[...] = base_ref[...].astype(bf16)
    for start in range(0, base_ref.shape[0], ROWS):
        block = pl.ds(start, ROWS)
        square = dot(low_ref[block, :], low_ref[...])
        mat_ref[block, :] = (quintic_two * base_ref[block, :] + quintic_three * square).astype(bf16)


def two_part(left, right):
    high = left.astype(bf16)
    rest = (left - high.astype(f32)).astype(bf16)
    return dot(high, right) + dot(rest, right)


def iterate(x_ref, out_ref, base_ref, work_ref, mat_ref, low_ref):
    size = x_ref.shape[0]
    blocks = [pl.ds(start, ROWS) for start in range(0, size, ROWS)]
    trace = jnp.zeros((1, 1), f32)
    line = lax.broadcasted_iota(jnp.int32, (ROWS, ROWS), 0)
    column = lax.broadcasted_iota(jnp.int32, (ROWS, ROWS), 1)
    for block in blocks:
        part = jnp.where(line == column, base_ref[block, block], 0.0)
        trace = trace + jnp.sum(part, keepdims=True)
    scale = 1.0 / (jnp.sqrt(trace) + 1e-07)
    base_ref[...] = base_ref[...] * (scale * scale)
    polynomial(base_ref, low_ref, mat_ref)

    for block in blocks:
        value = quintic_one * x_ref[block, :].astype(f32) + dot(x_ref[block, :], mat_ref[...])
        out_ref[block, :] = (scale * value).astype(bf16)
        work_ref[block, :] = quintic_one * base_ref[block, :] + two_part(
            base_ref[block, :], mat_ref[...]
        )
    turned = work_ref[...].T
    work_ref[...] = turned
    for block in blocks:
        base_ref[block, :] = quintic_one * work_ref[block, :] + two_part(
            work_ref[block, :], mat_ref[...]
        )
    polynomial(base_ref, low_ref, mat_ref)
    for block in blocks:
        x = out_ref[block, :]
        out_ref[block, :] = (quintic_one * x.astype(f32) + dot(x, mat_ref[...])).astype(bf16)


def orthogonalize(matrix, gram):
    size = matrix.shape[0]

    def kernel(unused, x_ref, gram_ref, out_ref, in_ref, base_ref, work_ref, mat_ref, low_ref):
        in_ref[...] = x_ref[...].T
        base_ref[...] = gram_ref[...]
        iterate(in_ref, out_ref, base_ref, work_ref, mat_ref, low_ref)
        out_ref[...] = out_ref[...].T

    return call(
        kernel,
        [((size, size), bf16)],
        jnp.zeros((1,), jnp.int32),
        matrix,
        gram,
        scratch=[pltpu.VMEM((size, size), kind) for kind in (bf16, f32, f32, bf16, bf16)],
    )[0]


def put_slots(slot_ref, x_ref):
    half = D // 2
    for source in range(8):
        group, number = source // TP, source % TP
        x_ref[number * COLS : (number + 1) * COLS, group * half : (group + 1) * half] = slot_ref[
            source
        ]


def slot_input(place_ref, slot_ref, moment_ref, sum_ref, x_ref, turned):
    put_slots(slot_ref, sum_ref)
    moment = moment_ref[...].astype(f32) * (momentum_decay * momentum_decay)
    if turned:
        moment = moment.T
    x_ref[...] = (sum_ref[...].astype(f32) * (1.0 + momentum_decay) + moment).astype(bf16)


def slot_gram(place, slots, moments):
    def kernel(place_ref, slot_ref, moment_ref, x_ref, gram_ref, sum_ref):
        slot_input(place_ref, slot_ref, moment_ref, sum_ref, x_ref, True)
        half = D // 2
        for part in range(2):
            rows = dot_tokens(x_ref[:, part * half : (part + 1) * half], x_ref[...]).astype(bf16)
            for number in range(2):
                back = 2 * part + number - place_ref[0]
                back = jnp.where(back < 0, back + 4, back)
                gram_ref[back] = rows[number * COLS : (number + 1) * COLS]

    return call(
        kernel,
        [((D, D), bf16), ((4, COLS, D), bf16)],
        place,
        slots,
        moments,
        scratch=[pltpu.VMEM((D, D), bf16)],
    )


def slot_orthogonalize(place, x_wide, grams, square_slots, moments):
    def kernel(
        place_ref,
        wide_ref,
        gram0_ref,
        gram1_ref,
        gram2_ref,
        gram3_ref,
        slot_ref,
        moment_ref,
        out_ref,
        x_ref,
        base_ref,
        work_ref,
        mat_ref,
        low_ref,
    ):
        core = place_ref[2]
        plain = (core == 1) & (place_ref[0] == 3)

        @pl.when(core == 0)
        def wide():
            x_ref[...] = wide_ref[...]
            for step, gram_ref in enumerate((gram0_ref, gram1_ref, gram2_ref, gram3_ref)):
                rows = pl.ds(pl.multiple_of(block_at(place_ref, step) * COLS, COLS), COLS)
                base_ref[rows, :] = gram_ref[...].astype(f32)

        @pl.when(plain)
        def square_plain():
            slot_input(place_ref, slot_ref, moment_ref, low_ref, x_ref, False)

        @pl.when((core == 1) & jnp.logical_not(plain))
        def square_turned():
            slot_input(place_ref, slot_ref, moment_ref, low_ref, x_ref, True)

        @pl.when(core == 1)
        def square():
            base_ref[...] = dot_tokens(x_ref[...], x_ref[...])

        iterate(x_ref, out_ref, base_ref, work_ref, mat_ref, low_ref)

        @pl.when(jnp.logical_not(plain))
        def turn():
            out_ref[...] = out_ref[...].T

    return call(
        kernel,
        [((D, D), bf16)],
        place,
        x_wide,
        *grams,
        square_slots,
        moments,
        scratch=[pltpu.VMEM((D, D), kind) for kind in (bf16, f32, f32, bf16, bf16)],
    )[0]


def slot_exchange(blocks):
    return lax.all_to_all(blocks, DP, split_axis=0, concat_axis=0, tiled=True)


def core_shift(block, step):
    size = lax.axis_size("ctx")
    return lax.ppermute(block, ("jc", "ctx"), [((i + step) % size, i) for i in range(size)])


def ctx_gram(gram):
    size = lax.axis_size("ctx")
    blocks = from_own(gram.astype(bf16).reshape(size, gram.shape[0] // size, -1))
    total = blocks[0].astype(f32)
    for step in (1, 3, 2):
        total = total + core_shift(blocks[step], -step).astype(f32)
    low = total.astype(bf16)
    full = [low] + [core_shift(low, step) for step in range(1, size)]
    return to_absolute(jnp.stack(full)).reshape(gram.shape).astype(f32)


def local(hidden_in, segments, out_grad, weights, vectors, mat_momentum, vec_first, vec_second):
    tokens_dev = hidden_in.shape[1]
    seq_len = segments.shape[1]
    half = 2 * tokens_dev
    dp_rows = weights.shape[2]
    ctx_size = lax.axis_size("ctx")
    x_index = lax.axis_index("jx")
    c_index = lax.axis_index("jc")
    t_index = 2 * x_index + c_index
    z_index = lax.axis_index("ctx")
    dp_index = lax.axis_index(DP)
    dp_size = lax.axis_size(DP)

    to_seq = []
    for t in range(TP):
        for z in range(ctx_size):
            to_seq.append((t * ctx_size + z, ((z % 2) * 2 + z // 2) * ctx_size + t))
    from_seq = [(b, a) for a, b in to_seq]
    axes = ("jx", "jc", "ctx")

    def x_join(block):
        return pair_join(block, "jx", 0)

    vec_rows = gather_vectors(vectors)
    seg_row = jnp.pad(segments.astype(f32), ((0, 7), (0, D - seq_len)))
    moved = lax.ppermute(jnp.concatenate([hidden_in[0], seg_row], axis=0), axes, to_seq)
    hidden = x_join(moved[:tokens_dev])
    segment_row = moved[tokens_dev, :seq_len]
    relative = lax.axis_size("g") == 2
    place = jnp.stack([z_index, lax.axis_index("g"), c_index]).astype(jnp.int32)
    if relative:
        piece, outs = first_piece(place, weights)
        own_attn = ctx_gather(piece)
        attn_weights = (own_attn, group_swap(own_attn))
        pieces = other_pieces(place, weights, outs, own_attn[1])
        mlp_weights = ctx_group_gather(pieces[0:2], *own_attn[1:])
    else:
        wide_weights = gather_weights_wide(weights.astype(bf16))

    start = c_index * half
    pos = jnp.concatenate([start + jnp.arange(half), half - start + jnp.arange(half)])
    seg = jnp.roll(segment_row.reshape(2, half), -c_index, axis=0).reshape(-1)
    info = jnp.stack([pos.astype(f32), seg])
    row_info = jnp.pad(info, ((0, 6), (0, 0)))
    column_info = jnp.pad(info.T, ((0, 0), (0, 126)))
    vec_mine = lax.dynamic_slice_in_dim(vec_rows, t_index * COLS, COLS, axis=2)
    no_bias = jnp.zeros((LAYERS, 1, COLS), f32)
    qkv_bias = jnp.concatenate([vec_mine[:, 4:5], no_bias, vec_mine[:, 5:6]], axis=2)
    up_bias = vec_mine[:, 8:12].reshape(LAYERS, 1, D)

    stored = []
    (a_own,) = norm_stage(vec_rows, 0, 0, hidden)
    for layer in range(LAYERS):
        following = layer + 1 < LAYERS
        a_other = core_swap(a_own)
        if not relative:
            attn_weights, mlp_weights = wide_weights[layer]
        w_attn, qkv, lse, o, mine, give = attend_stage(
            place, row_info, column_info, qkv_bias[layer], a_own, a_other, attn_weights
        )
        mine, recv = group_sum(mine, give)
        middle, c_own = norm_stage(vec_rows, layer, 2, hidden, mine, recv, (layer, 6))
        if relative and layer == 0:
            moved_grad = lax.ppermute(after(out_grad[0], *mlp_weights[0][2:3]), axes, to_seq)
            c_own, moved_grad = lax.optimization_barrier((c_own, moved_grad))
            grad_hidden = x_join(moved_grad)
        c_other = core_swap(c_own)
        w_mlp, preact, act, mine, give = feed_stage(
            place, up_bias[layer], c_own, c_other, mlp_weights
        )
        if relative and following:
            base = 3 * layer + 2
            attn_weights = ctx_group_gather(pieces[base : base + 1], *mlp_weights[0][2:3])
            mine, grad_hidden, ready = lax.optimization_barrier(
                (mine, grad_hidden, attn_weights[0][1])
            )
            attn_weights[0][1] = ready
            mlp_weights = ctx_group_gather(pieces[base + 1 : base + 3], *attn_weights[0][2:3])
        if following:
            mine, recv = group_sum(mine, give)
        stored.append(
            (hidden, middle, a_own, a_other, qkv, lse, o, c_own, c_other, preact, act, w_attn, w_mlp)
        )
        if following:
            hidden, a_own = norm_stage(vec_rows, layer + 1, 0, middle, mine, recv, (layer, 7))

    def send_back(rows):
        block = lax.dynamic_slice_in_dim(rows, x_index * tokens_dev, tokens_dev, axis=0)
        return lax.ppermute(block, axes, from_seq)

    last_sum = (mine, give)

    def last_hidden(*earlier):
        mine, recv = group_sum(last_sum[0], after(last_sum[1], *earlier))
        return stored[-1][1] + (mine + recv.astype(f32) + vec_rows[LAYERS - 1, 7:8])

    if not relative:
        grad_hidden = x_join(lax.ppermute(out_grad[0], axes, to_seq))
        hidden_out = send_back(last_hidden())
    gy_own = grad_hidden.astype(bf16)
    attn_half = mlp_half = None

    mat_list = [None] * LAYERS
    sum_list = [None] * LAYERS
    parts = [None] * LAYERS
    for layer in reversed(range(LAYERS)):
        h_in, middle, a_own, a_other, qkv, lse, o, c_own, c_other, preact, act, w_attn, w_mlp = stored[
            layer
        ]
        if relative and attn_half is not None:
            gy_own, mlp_first = lax.optimization_barrier((gy_own, mlp_first))
            mlp_part = ctx_sum_last(mlp_half, mlp_first)
            hidden = last_hidden(gy_own)
        gy_other = core_swap(gy_own)
        mine, give, up_sums, *mlp_grads = feed_back_stage(
            place, gy_own, gy_other, c_own, c_other, preact, act, w_mlp, relative
        )
        if relative:
            if attn_half is not None:
                mine, mlp_part, hidden, attn_half = lax.optimization_barrier(
                    (mine, mlp_part, hidden, attn_half)
                )
                attn_part = ctx_sum(attn_half)
            mlp_half = half_sum(*mlp_grads)
        mine, recv = group_sum(mine, give)
        grad_middle, gb_own, mid_sums = norm_back_stage(
            vec_rows, layer, 2, grad_hidden, mine, recv, middle
        )
        if relative and layer == LAYERS - 1:
            moment_low = mat_momentum.astype(bf16)
            table = [(1, 1), (1, 0), (1, 2), (0, 0), (0, 1), (1, 0), (0, 2), (0, 0)]
            moment_slots = slot_exchange(
                after(jnp.stack([moment_low[slot] for slot in table]), gb_own)
            ).reshape(D, D)
        elif relative:
            gb_own, attn_part = lax.optimization_barrier((gb_own, attn_part))
            parts[layer + 1] = (attn_part, mlp_part)
        gb_other = core_swap(gb_own)
        mine, give, qkv_sums, *attn_grads = attend_back_stage(
            place,
            row_info,
            column_info,
            gb_own,
            gb_other,
            a_own,
            a_other,
            qkv,
            lse,
            o,
            w_attn,
            relative,
        )
        if relative:
            mine, mlp_half = lax.optimization_barrier((mine, mlp_half))
            if layer == LAYERS - 1:
                mine, moment_slots = lax.optimization_barrier((mine, moment_slots))
                mlp_first = ctx_sum_first(mlp_half)
            else:
                mlp_part = ctx_sum(mlp_half)
            attn_half = half_sum(*attn_grads)
        else:
            attn_grad = attn_grads[0]
            g_wo = lax.all_to_all(
                attn_grad[3].reshape(COLS, TP, COLS), GROUP, split_axis=1, concat_axis=0, tiled=True
            )[:, 0]
            attn_grad = jnp.concatenate([attn_grad[:3], g_wo.T[None]], axis=0)
            mat_list[layer] = scatter_wide(
                jnp.concatenate([attn_grad[:, None], mlp_grads[0]], axis=1)
            )
        if relative and layer == 0:
            wide_low = jnp.concatenate([parts[1][1], mlp_part]).astype(bf16)
            x_wide, gram_blocks = slot_gram(
                place, slot_exchange(jnp.repeat(wide_low, 2, axis=0)), moment_slots
            )
            mine = after(mine, gram_blocks)
        mine, recv = group_sum(mine, give)
        grad_hidden, gy_own, in_sums = norm_back_stage(
            vec_rows, layer, 0, grad_middle, mine, recv, h_in
        )
        sum_list[layer] = (in_sums, mid_sums, up_sums, qkv_sums)
    if not relative:
        input_grad = send_back(grad_hidden)

    once = jnp.where(x_index == 0, 1.0, 0.0).astype(f32)
    in_sums, mid_sums, up_sums, qkv_sums = [jnp.stack(sums) for sums in zip(*sum_list)]
    shared = once * jnp.concatenate(
        [in_sums[:, 0:2], mid_sums[:, 0:3], up_sums[:, 1:2]], axis=1
    )
    placed = jnp.concatenate(
        [
            qkv_sums[:, 0:1, :COLS],
            qkv_sums[:, 0:1, 2 * COLS :],
            up_sums[:, 0].reshape(LAYERS, ctx_size, COLS),
        ],
        axis=1,
    )
    placed = lax.dynamic_update_slice_in_dim(
        jnp.zeros((LAYERS, 6, D), f32), placed, t_index * COLS, axis=2
    )
    vec_terms = jnp.concatenate(
        [shared[:, 0:4], placed[:, 0:2], shared[:, 4:6], placed[:, 2:6]], axis=1
    )
    grad_vecs = lax.dynamic_slice_in_dim(
        sum_vectors(vec_terms), dp_index * vectors.shape[2], vectors.shape[2], axis=2
    )
    if relative:
        attn_part = ctx_sum(attn_half)
        square_low = jnp.stack([parts[1][0], attn_part]).astype(bf16)
        square_slots = slot_exchange(jnp.tile(jnp.repeat(square_low, 2, axis=0), (2, 1, 1)))
        total = gram_blocks[0].astype(f32)
        for step in (1, 3, 2):
            total = total + core_shift(gram_blocks[step], -step).astype(f32)
        low = total.astype(bf16)
        near, back, far = [core_shift(low, step) for step in (1, 3, 2)]
        ortho_mine = slot_orthogonalize(
            place, x_wide, (low, near, far, back), square_slots, moment_slots
        )
        returned = slot_exchange(ortho_mine.reshape(dp_size, dp_rows, D))
        ends = jnp.stack([hidden, grad_hidden])
        ends = lax.dynamic_slice_in_dim(ends, x_index * tokens_dev, tokens_dev, axis=1)
        hidden_out, input_grad = lax.ppermute(after(ends, ortho_mine), axes, from_seq)
        ortho = jnp.stack([returned[slot] for slot in (3, 4, 6, 1, 0, 2)])
        ortho = ortho.reshape(weights.shape).astype(f32)
        grad_mats, moment_new = grad_rows(
            place, [attn_part, parts[1][0]], [mlp_part, parts[1][1]], mat_momentum
        )
    else:
        cols_dev = weights.shape[3]
        grad_list, moment_list, low_list = [], [], []
        for layer in range(LAYERS):
            for item in range(3):
                grad = mat_list[layer][item]
                moment = momentum_decay * mat_momentum[layer, item] + grad
                grad_list.append(grad)
                moment_list.append(moment)
                low_list.append((grad + momentum_decay * moment).astype(bf16))
        wide = [item for item in range(3 * LAYERS) if item % 3]
        squares = [item for item in range(3, 3 * LAYERS, 3)]
        table = []
        for number in range(4):
            table += [wide[number], squares[number % len(squares)]]
        table = (table * (-(-dp_size // 8)))[:dp_size]
        slots = jnp.stack([low_list[item] for item in table])
        received = lax.all_to_all(slots[:, None], DP, split_axis=0, concat_axis=1, tiled=True)
        current = received.reshape(dp_size * dp_rows, cols_dev)
        gram_local = dot_trans(current, current)
        gram = jnp.where(c_index == 0, ctx_gram(gram_local), gram_local)
        ortho_mine = orthogonalize(current, gram)
        returned = lax.all_to_all(
            ortho_mine.reshape(dp_size, 1, dp_rows, cols_dev),
            DP,
            split_axis=0,
            concat_axis=1,
            tiled=True,
        )[0]
        first_full = lax.all_gather(low_list[0], DP, axis=0, tiled=True)
        first_ortho = orthogonalize(first_full, dot_trans(first_full, first_full))
        ortho_list = [lax.dynamic_slice_in_dim(first_ortho, dp_index * dp_rows, dp_rows, axis=0)]
        ortho_list += [returned[table.index(item)] for item in range(1, 3 * LAYERS)]
        ortho = jnp.stack(ortho_list).reshape(LAYERS, 3, dp_rows, cols_dev).astype(f32)
        grad_mats = jnp.stack(grad_list).reshape(weights.shape)
        moment_new = jnp.stack(moment_list).reshape(weights.shape)
    factor = jnp.array([0.2 * math.sqrt(D), 0.2 * math.sqrt(FF), 0.2 * math.sqrt(FF)], f32)
    weights_new = weights * (1.0 - matrix_rate * matrix_decay) - matrix_rate * (
        ortho * factor[None, :, None, None]
    )
    first_new = first_decay * vec_first + (1.0 - first_decay) * grad_vecs
    second_new = second_decay * vec_second + (1.0 - second_decay) * grad_vecs * grad_vecs
    first_hat = first_new / (1.0 - first_decay**ADAM_STEP)
    second_hat = second_new / (1.0 - second_decay**ADAM_STEP)
    vectors_new = vectors * (1.0 - vector_rate * vector_decay) - vector_rate * first_hat / (
        jnp.sqrt(second_hat) + adam_epsilon
    )
    return (
        hidden_out[None],
        input_grad[None],
        grad_mats,
        moment_new,
        weights_new,
        grad_vecs,
        second_new,
        vectors_new,
    )


def solution(mesh):
    dp, ctx = mesh.shape["dp"], mesh.shape["ctx"]
    fine = Mesh(mesh.devices.reshape(dp // TP, 2, 2, ctx), EVERY)
    tokens = P(DP, "ctx", None)
    mats = P(None, None, DP, "ctx")
    vecs = P(None, "ctx", DP)
    return jax.shard_map(
        local,
        mesh=fine,
        in_specs=(tokens, P(DP, None), tokens, mats, vecs, mats, vecs, vecs),
        out_specs=(tokens, tokens, mats, mats, mats, vecs, vecs, vecs),
        check_vma=False,
    )
```

```python
import math

import jax
import jax.numpy as jnp
from jax import lax
from jax.experimental import pallas as pl
from jax.experimental.pallas import tpu as pltpu
from jax.sharding import Mesh, PartitionSpec as P

D = 768
HEADS = 12
HEAD = 64
FF = 3072
LAYERS = 2
ADAM_STEP = 10
TP = 4
COLS = D // TP
TP_HEADS = HEADS // TP
ROWS = 256

norm_epsilon = 1e-05
quintic_one = 3.4445
quintic_two = -4.775
quintic_three = 2.0315
momentum_decay = 0.95
matrix_rate = 0.6
matrix_decay = 0.01
first_decay = 0.9
second_decay = 0.999
vector_rate = 0.5
vector_decay = 0.01
adam_epsilon = 1e-08
masked_score = -1e30

GROUP = ("jx", "jc")
REPLICAS = ("g", "ctx")
DP = ("g", "jx", "jc")
EVERY = ("g", "jx", "jc", "ctx")
SWAP = [(0, 1), (1, 0)]
bf16 = jnp.bfloat16
f32 = jnp.float32


def dot(operand, other):
    return jnp.dot(operand, other, preferred_element_type=f32)


def dot_tokens(operand, other):
    return lax.dot_general(operand, other, (((0,), (0,)), ((), ())), preferred_element_type=f32)


def dot_trans(operand, other):
    return lax.dot_general(operand, other, (((1,), (1,)), ((), ())), preferred_element_type=f32)


def to_group(mats):
    count, rows, width = mats.shape
    split = mats.reshape(count, rows, TP, width // TP)
    return lax.all_to_all(split, GROUP, split_axis=2, concat_axis=1, tiled=True)[:, :, 0]


def from_group(mats):
    count, rows, width = mats.shape
    split = mats.reshape(count, TP, rows // TP, width)
    return lax.all_to_all(split, GROUP, split_axis=1, concat_axis=3, tiled=True)[:, 0]


def rotate(block, axis, step):
    size = lax.axis_size(axis)
    return lax.ppermute(block, axis, [((i + step) % size, i) for i in range(size)])


def pair_join(block, axis, dim):
    other = lax.ppermute(block, axis, SWAP)
    first = lax.axis_index(axis) == 0
    return jnp.concatenate(
        [jnp.where(first, block, other), jnp.where(first, other, block)], axis=dim
    )


def after(value, *others):
    return lax.optimization_barrier((value, *others))[0]


def roll_blocks(stack, sign):
    place = lax.axis_index("ctx")
    for bit in (1, 2):
        moved = jnp.roll(stack, sign * bit, axis=0)
        stack = jnp.where((place & bit) != 0, moved, stack)
    return stack


def from_own(stack):
    return roll_blocks(stack, -1)


def to_absolute(stack):
    return roll_blocks(stack, 1)


def out_moves():
    last = lax.axis_size("ctx") - 1
    size = last + 1
    moves = []
    for y in range(2):
        for x in range(2):
            for core in range(2):
                moves.append(
                    ((4 * y + 2 * x + core) * size + last, (4 * core + 2 * y + x) * size + last)
                )
    return moves


def out_pieces(mats):
    half = mats.shape[2] // 2
    core = lax.axis_index("jc")
    mine = lax.dynamic_slice_in_dim(mats, core * half, half, axis=2)
    give = lax.dynamic_slice_in_dim(mats, (1 - core) * half, half, axis=2)
    got = lax.ppermute(give, "jc", SWAP)
    rows = jnp.concatenate(
        [jnp.where(core == 0, mine, got), jnp.where(core == 0, got, mine)], axis=1
    )
    return lax.ppermute(rows, EVERY, out_moves())


def out_back(pieces):
    core = lax.axis_index("jc")
    rows = lax.ppermute(pieces, EVERY, [(b, a) for a, b in out_moves()])
    half = rows.shape[1] // 2
    mine = lax.dynamic_slice_in_dim(rows, core * half, half, axis=1)
    give = lax.dynamic_slice_in_dim(rows, (1 - core) * half, half, axis=1)
    got = lax.ppermute(give, "jc", SWAP)
    return jnp.concatenate(
        [jnp.where(core == 0, mine, got), jnp.where(core == 0, got, mine)], axis=2
    )


def last_block():
    return lax.axis_index("ctx") == lax.axis_size("ctx") - 1


def split_columns(mats, items):
    rows = mats.shape[2]

    def kernel(unused, mats_ref, out_ref):
        for number, (layer, item) in enumerate(items):
            turned = mats_ref[layer, item].T.astype(bf16)
            for quarter in range(TP):
                out_ref[quarter, number] = turned[quarter * COLS : (quarter + 1) * COLS]

    outs = [((TP, len(items), COLS, rows), bf16)]
    return call(kernel, outs, jnp.zeros((1,), jnp.int32), mats)[0]


def join_columns(place, blocks, outs, items):
    rows = blocks.shape[3]

    def kernel(place_ref, blocks_ref, outs_ref, *out_refs):
        for number, (layer, item) in enumerate(items):
            for source in range(TP):
                lanes = slice(source * rows, (source + 1) * rows)
                out_refs[number][:, lanes] = blocks_ref[source, number]
            if item == 0:

                @pl.when(place_ref[0] == 3)
                def last(number=number, layer=layer):
                    out_refs[number][...] = outs_ref[layer]

    shapes = [((COLS, TP * rows), bf16)] * len(items)
    return call(kernel, shapes, place, blocks, outs)


def group_exchange(blocks):
    return lax.all_to_all(blocks, GROUP, split_axis=0, concat_axis=0, tiled=True)


def first_piece(place, mats):
    outs = out_pieces(mats[:, 0].astype(bf16))
    blocks = group_exchange(split_columns(mats, [(0, 0)]))
    return join_columns(place, blocks, outs, [(0, 0)])[0], outs


def other_pieces(place, mats, outs, *earlier):
    items = [(layer, item) for layer in range(mats.shape[0]) for item in range(3)][1:]
    blocks = group_exchange(split_columns(after(mats, *earlier), items))
    return join_columns(place, blocks, outs, items)


def ctx_gather(piece, *earlier):
    piece = after(piece, *earlier)
    near, back, far = [rotate(piece, "ctx", step) for step in (1, 3, 2)]
    return [piece, near, far, back]


def group_swap(blocks):
    return [lax.ppermute(block, "g", SWAP) for block in blocks]


def ctx_near(pieces, *earlier):
    piece = after(jnp.stack(pieces), *earlier)
    return piece, rotate(piece, "ctx", 1), rotate(piece, "ctx", 3)


def ctx_far(piece, near, back):
    return rotate(after(piece, near, back), "ctx", 2)


def group_first(piece, near, back):
    return lax.ppermute(jnp.stack([piece, near, back]), "g", SWAP)


def gather_weights_wide(low):
    result = []
    for layer in range(low.shape[0]):
        mats = to_group(low[layer])
        parts = lax.all_gather(mats, REPLICAS, axis=0, tiled=False)
        parts = parts.reshape(lax.axis_size("g"), -1, *mats.shape)
        full = [parts[:, :, item].transpose(1, 3, 0, 2).reshape(D, D) for item in range(3)]
        w_o = lax.all_to_all(
            full[0][3 * COLS :].T.reshape(TP, COLS, COLS),
            GROUP,
            split_axis=0,
            concat_axis=2,
            tiled=True,
        )
        attn = jnp.concatenate([full[0][: 3 * COLS].reshape(3, COLS, D), w_o], axis=0)
        result.append((attn.reshape(D, D), jnp.stack([full[1], full[2]])))
    return result


def half_sum(mine, give):
    return mine + lax.ppermute(give, "g", SWAP).astype(f32)


def ctx_sum(blocks):
    low = blocks.astype(bf16)
    near, back, far = [rotate(low[step], "ctx", -step) for step in (1, 3, 2)]
    return blocks[0] + near.astype(f32) + back.astype(f32) + far.astype(f32)


def ctx_sum_first(blocks):
    low = blocks.astype(bf16)
    near, back = [rotate(low[step], "ctx", -step) for step in (1, 3)]
    return blocks[0] + near.astype(f32) + back.astype(f32)


def ctx_sum_last(blocks, total):
    far = rotate(after(blocks[2], total).astype(bf16), "ctx", -2)
    return total + far.astype(f32)


def grad_blocks(attn_parts, mlp_parts, rows, *earlier):
    layers = len(attn_parts)
    zero = jnp.zeros((1,), jnp.int32)

    def split(unused, *refs):
        *part_refs, out_ref = refs
        for layer in range(layers):
            for item in range(3):
                if item:
                    part = part_refs[layers + layer][item - 1]
                else:
                    part = part_refs[layer][...]
                turned = part.T.astype(bf16)
                for target in range(TP):
                    out_ref[target, 3 * layer + item] = turned[target * rows : (target + 1) * rows]

    blocks = call(split, [((TP, 3 * layers, rows, COLS), bf16)], zero, *attn_parts, *mlp_parts)[0]
    return group_exchange(after(blocks, *earlier)), out_back(jnp.stack(attn_parts).astype(bf16))


def grad_rows(place, blocks, outs, momentum):
    layers = momentum.shape[0]

    def join(place_ref, blocks_ref, outs_ref, momentum_ref, grad_ref, new_ref):
        for layer in range(layers):
            for item in range(3):
                for source in range(TP):
                    lanes = slice(source * COLS, (source + 1) * COLS)
                    grad_ref[layer, item, :, lanes] = blocks_ref[source, 3 * layer + item].astype(f32)

            @pl.when(place_ref[0] == 3)
            def last(layer=layer):
                grad_ref[layer, 0] = outs_ref[layer].astype(f32)

        new_ref[...] = momentum_decay * momentum_ref[...] + grad_ref[...]

    shape = (momentum.shape, f32)
    return call(join, [shape, shape], place, blocks, outs, momentum)


def scatter_wide(mats):
    groups = lax.axis_size("g")
    blocks, count, width, depth = mats.shape
    stack = mats.astype(bf16).reshape(blocks, count, width, groups, depth // groups)
    stack = stack.transpose(3, 0, 1, 4, 2).reshape(groups * blocks, count, -1, width)
    part = lax.psum_scatter(stack, REPLICAS, scatter_dimension=0, tiled=True)[0]
    return from_group(part).astype(f32)


def gather_vectors(vectors, *earlier):
    low = vectors.astype(bf16)
    stack = jnp.stack([low] + [rotate(low, "ctx", step) for step in range(1, 4)])
    stack = pair_join(pair_join(after(to_absolute(stack), *earlier), "jc", 3), "jx", 3)
    if lax.axis_size("g") == 2:
        stack = pair_join(stack, "g", 3)
    else:
        stack = lax.all_gather(stack, "g", axis=3, tiled=True)
    return stack.transpose(1, 0, 2, 3).reshape(low.shape[0], -1, D).astype(f32)


def sum_vectors(terms):
    if lax.axis_size("g") == 2:
        terms = terms + lax.ppermute(terms, "g", SWAP)
    else:
        terms = lax.psum(terms, "g")
    layers, rows, width = terms.shape
    blocks = from_own(terms.reshape(layers, 4, rows // 4, width).transpose(1, 0, 2, 3))
    total = blocks[0]
    for step in range(1, 4):
        total = total + rotate(blocks[step], "ctx", -step)
    total = total + lax.ppermute(total, "jc", SWAP)
    return total + lax.ppermute(total, "jx", SWAP)


def call(kernel, outs, *args, scratch=()):
    return pl.pallas_call(
        kernel,
        out_shape=[jax.ShapeDtypeStruct(shape, kind) for shape, kind in outs],
        in_specs=[pl.BlockSpec(memory_space=pltpu.SMEM)]
        + [pl.BlockSpec(memory_space=pltpu.VMEM)] * (len(args) - 1),
        out_specs=[pl.BlockSpec(memory_space=pltpu.VMEM)] * len(outs),
        scratch_shapes=list(scratch),
        compiler_params=pltpu.CompilerParams(vmem_limit_bytes=52 * 1024 * 1024),
    )(*args)


def block_at(place_ref, step):
    ahead = place_ref[0] + step
    return jnp.where(ahead >= 4, ahead - 4, ahead)


def put_blocks(place_ref, own_refs, other_refs, full_refs):
    half = D // 2
    mine = pl.multiple_of(place_ref[1] * half, half)
    theirs = pl.multiple_of((1 - place_ref[1]) * half, half)
    for step in range(4):
        rows = pl.ds(pl.multiple_of(block_at(place_ref, step) * COLS, COLS), COLS)
        for number, full_ref in enumerate(full_refs):
            own, other = own_refs[step], other_refs[step]
            if len(full_refs) > 1:
                own, other = own.at[number], other.at[number]
            full_ref[rows, pl.ds(mine, half)] = own[...]
            full_ref[rows, pl.ds(theirs, half)] = other[...]


def put_grads(place_ref, grad, mine_refs, give_refs, halves):
    half = D // 2
    for block in range(4):
        rows = grad[block * COLS : (block + 1) * COLS]
        if halves:
            back = block - place_ref[0]
            back = jnp.where(back < 0, back + 4, back)
            low = place_ref[1] == 0
            mine_refs(back)[...] = jnp.where(low, rows[:, :half], rows[:, half:])
            give_refs(back)[...] = jnp.where(low, rows[:, half:], rows[:, :half]).astype(bf16)
        else:
            mine_refs(block)[...] = rows


def norm_rows(hidden):
    center = hidden - jnp.mean(hidden, axis=-1, keepdims=True)
    variance = jnp.mean(center * center, axis=-1, keepdims=True)
    inverse = lax.rsqrt(variance + norm_epsilon)
    return center * inverse, inverse


def norm_stage(vecs, layer, row, hidden, mine=None, recv=None, bias=None):
    rows = hidden.shape[0]

    def kernel(unused, vec_ref, hidden_ref, *refs):
        total = hidden_ref[...]
        if mine is not None:
            mine_ref, recv_ref, total_ref, out_ref = refs
            bias_row = vec_ref[bias[0], bias[1] : bias[1] + 1, :]
            total = total + (mine_ref[...] + recv_ref[...].astype(f32) + bias_row)
            total_ref[...] = total
        else:
            (out_ref,) = refs
        normed, unused_scale = norm_rows(total)
        gain = vec_ref[layer, row : row + 1, :]
        shift = vec_ref[layer, row + 1 : row + 2, :]
        out_ref[...] = (normed * gain + shift).astype(bf16)

    outs = [((rows, D), bf16)]
    args = [hidden]
    if mine is not None:
        outs = [((rows, D), f32)] + outs
        args += [mine, recv]
    return call(kernel, outs, jnp.zeros((1,), jnp.int32), vecs, *args)


def norm_back_stage(vecs, layer, row, grad, mine, recv, hidden):
    rows = hidden.shape[0]

    def kernel(unused, vec_ref, grad_ref, mine_ref, recv_ref, hidden_ref, out_ref, low_ref, sum_ref):
        through = mine_ref[...] + recv_ref[...].astype(f32)
        normed, inverse = norm_rows(hidden_ref[...])
        scaled = through * vec_ref[layer, row : row + 1, :]
        part = jnp.mean(scaled, axis=-1, keepdims=True)
        part = part + normed * jnp.mean(scaled * normed, axis=-1, keepdims=True)
        total = grad_ref[...] + inverse * (scaled - part)
        out_ref[...] = total
        low = total.astype(bf16)
        low_ref[...] = low
        sum_ref[0:1, :] = jnp.sum(through * normed, axis=0, keepdims=True)
        sum_ref[1:2, :] = jnp.sum(through, axis=0, keepdims=True)
        sum_ref[2:3, :] = jnp.sum(low.astype(f32), axis=0, keepdims=True)

    outs = [((rows, D), f32), ((rows, D), bf16), ((8, D), f32)]
    return call(kernel, outs, jnp.zeros((1,), jnp.int32), vecs, grad, mine, recv, hidden)


def both(first_ref, second_ref):
    return jnp.concatenate([first_ref[...], second_ref[...]], axis=0)


def allowed_of(row_ref, column_ref):
    before = row_ref[0:1, :] <= column_ref[:, 0:1]
    return before & (row_ref[1:2, :] == column_ref[:, 1:2])


def attend_stage(place, row_info, column_info, bias, a_own, a_other, weights):
    half = a_own.shape[0]
    tokens = 2 * half
    wide = 3 * COLS
    own, other = weights if isinstance(weights, tuple) else ([], [])

    def kernel(place_ref, row_ref, column_ref, bias_ref, own_a_ref, other_a_ref, *refs):
        if own:
            own_refs, refs = refs[:4], refs[4:]
            others, refs = refs[: len(other)], refs[len(other) :]
            if len(other) == 1:
                others = [others[0].at[step] for step in range(4)]
            w_ref, qkv_ref, lse_ref, o_ref, mine_ref, give_ref = refs
            put_blocks(place_ref, own_refs, others, [w_ref])
        else:
            w_ref, qkv_ref, lse_ref, o_ref, mine_ref, give_ref = refs
        for start, a_ref in ((0, own_a_ref), (half, other_a_ref)):
            proj = dot_trans(a_ref[...], w_ref[0:wide, :]) + bias_ref[0:1, :]
            qkv_ref[start : start + half, :] = proj.astype(bf16)
        allowed = allowed_of(row_ref, column_ref)
        for head in range(TP_HEADS):
            lanes = head * HEAD
            k = qkv_ref[:, COLS + lanes : COLS + lanes + HEAD]
            v = qkv_ref[:, 2 * COLS + lanes : 2 * COLS + lanes + HEAD]
            for start in (0, half):
                rows = slice(start, start + half)
                q = qkv_ref[rows, lanes : lanes + HEAD]
                scores = jnp.where(allowed[rows], dot_trans(q, k) * HEAD ** (-0.5), masked_score)
                top = jnp.max(scores, axis=-1, keepdims=True)
                unnormed = jnp.exp(scores - top)
                total = jnp.sum(unnormed, axis=-1, keepdims=True)
                prob = (unnormed * (1.0 / total)).astype(bf16)
                o_ref[rows, lanes : lanes + HEAD] = dot(prob, v).astype(bf16)
                lse_ref[rows, head : head + 1] = top + jnp.log(total)
        mine_ref[...] = dot(o_ref[0:half, :], w_ref[wide:, :])
        give_ref[...] = dot(o_ref[half:, :], w_ref[wide:, :]).astype(bf16)

    outs = [
        ((tokens, wide), bf16),
        ((tokens, 128), f32),
        ((tokens, COLS), bf16),
        ((half, D), f32),
        ((half, D), bf16),
    ]
    if own:
        outs = [((D, D), bf16)] + outs
        return call(
            kernel, outs, place, row_info, column_info, bias, a_own, a_other, *own, *other
        )
    result = call(kernel, outs, place, row_info, column_info, bias, a_own, a_other, weights)
    return [weights] + list(result)


def attend_back_stage(
    place, row_info, column_info, gb_own, gb_other, a_own, a_other, qkv, lse, o, w_attn, halves
):
    half = a_own.shape[0]
    tokens = 2 * half
    wide = 3 * COLS

    def kernel(
        place_ref,
        row_ref,
        column_ref,
        own_gb_ref,
        other_gb_ref,
        own_a_ref,
        other_a_ref,
        qkv_ref,
        lse_ref,
        o_ref,
        w_ref,
        mine_ref,
        give_ref,
        sum_ref,
        *refs,
    ):
        *grad_refs, go_ref, all_ref = refs
        w_o = w_ref[wide:, :]
        for start, gb_ref in ((0, own_gb_ref), (half, other_gb_ref)):
            go_ref[start : start + half, :] = dot_trans(gb_ref[...], w_o).astype(bf16)
        allowed = allowed_of(row_ref, column_ref)
        for head in range(TP_HEADS):
            lanes = head * HEAD
            q_lanes = slice(lanes, lanes + HEAD)
            k_lanes = slice(COLS + lanes, COLS + lanes + HEAD)
            v_lanes = slice(2 * COLS + lanes, 2 * COLS + lanes + HEAD)
            k = qkv_ref[:, k_lanes]
            v = qkv_ref[:, v_lanes]
            gk = jnp.zeros((tokens, HEAD), f32)
            gv = jnp.zeros((tokens, HEAD), f32)
            for start in (0, half):
                rows = slice(start, start + half)
                q = qkv_ref[rows, q_lanes]
                go = go_ref[rows, q_lanes]
                scores = jnp.where(allowed[rows], dot_trans(q, k) * HEAD ** (-0.5), masked_score)
                prob = jnp.exp(scores - lse_ref[rows, head : head + 1])
                g_prob = dot_trans(go, v)
                row_dot = jnp.sum(g_prob * prob, axis=-1, keepdims=True)
                g_scores = (prob * (g_prob - row_dot)).astype(bf16)
                all_ref[rows, q_lanes] = (dot(g_scores, k) * HEAD ** (-0.5)).astype(bf16)
                gk = gk + dot_tokens(g_scores, q)
                gv = gv + dot_tokens(prob.astype(bf16), go)
            all_ref[:, k_lanes] = (gk * HEAD ** (-0.5)).astype(bf16)
            all_ref[:, v_lanes] = gv.astype(bf16)
        mine_ref[...] = dot(all_ref[0:half, :], w_ref[0:wide, :])
        give_ref[...] = dot(all_ref[half:, :], w_ref[0:wide, :]).astype(bf16)
        sum_ref[0:1, :] = jnp.sum(all_ref[...].astype(f32), axis=0, keepdims=True)
        grad = jnp.concatenate(
            [
                dot_tokens(all_ref[...], both(own_a_ref, other_a_ref)),
                dot_tokens(o_ref[...], both(own_gb_ref, other_gb_ref)),
            ],
            axis=0,
        )
        put_grads(
            place_ref,
            grad,
            lambda block: grad_refs[0].at[block],
            lambda block: grad_refs[1].at[block],
            halves,
        )

    width = D // 2 if halves else D
    outs = [((half, D), f32), ((half, D), bf16), ((8, wide), f32), ((4, COLS, width), f32)]
    if halves:
        outs.append(((4, COLS, width), bf16))
    return call(
        kernel,
        outs,
        place,
        row_info,
        column_info,
        gb_own,
        gb_other,
        a_own,
        a_other,
        qkv,
        lse,
        o,
        w_attn,
        scratch=[pltpu.VMEM((tokens, COLS), bf16), pltpu.VMEM((tokens, wide), bf16)],
    )


def tanh_part(preact):
    inner = math.sqrt(2.0 / math.pi) * (preact + 0.044715 * (preact * preact * preact))
    return jnp.tanh(inner)


def feed_stage(place, bias, c_own, c_other, weights):
    half = c_own.shape[0]
    own, other = weights if isinstance(weights, tuple) else ([], [])

    def kernel(place_ref, bias_ref, own_c_ref, other_c_ref, *refs):
        if own:
            own_refs, (first, last), refs = refs[:4], refs[4:6], refs[6:]
            others = [first.at[0], first.at[1], last, first.at[2]]
            w_ref, preact_ref, act_ref, mine_ref, give_ref = refs
            put_blocks(place_ref, own_refs, others, [w_ref.at[0], w_ref.at[1]])
        else:
            w_ref, preact_ref, act_ref, mine_ref, give_ref = refs
        for start, c_ref, out_ref in ((0, own_c_ref, mine_ref), (half, other_c_ref, give_ref)):
            rows = slice(start, start + half)
            preact = dot_trans(c_ref[...], w_ref[0]) + bias_ref[...]
            preact_ref[rows, :] = preact
            act = (0.5 * preact * (1.0 + tanh_part(preact))).astype(bf16)
            act_ref[rows, :] = act
            out_ref[...] = dot(act, w_ref[1]).astype(out_ref.dtype)

    outs = [
        ((2 * half, D), f32),
        ((2 * half, D), bf16),
        ((half, D), f32),
        ((half, D), bf16),
    ]
    if own:
        outs = [((2, D, D), bf16)] + outs
        return call(kernel, outs, place, bias, c_own, c_other, *own, *other)
    return [weights] + list(call(kernel, outs, place, bias, c_own, c_other, weights))


def feed_back_stage(place, gy_own, gy_other, c_own, c_other, preact, act, weights, halves):
    half = c_own.shape[0]

    def kernel(
        place_ref,
        own_gy_ref,
        other_gy_ref,
        own_c_ref,
        other_c_ref,
        preact_ref,
        act_ref,
        w_ref,
        mine_ref,
        give_ref,
        sum_ref,
        *refs,
    ):
        *grad_refs, gz_ref = refs
        up_sum = jnp.zeros((1, D), f32)
        for start, gy_ref, out_ref in ((0, own_gy_ref, mine_ref), (half, other_gy_ref, give_ref)):
            rows = slice(start, start + half)
            gu = dot_trans(gy_ref[...], w_ref[1])
            x = preact_ref[rows, :]
            tanh = tanh_part(x)
            slope = math.sqrt(2.0 / math.pi) * (1.0 + 3.0 * 0.044715 * (x * x))
            factor = 0.5 * (1.0 + tanh) + 0.5 * x * (1.0 - tanh * tanh) * slope
            gz = (gu * factor).astype(bf16)
            gz_ref[rows, :] = gz
            up_sum = up_sum + jnp.sum(gz.astype(f32), axis=0, keepdims=True)
            out_ref[...] = dot(gz, w_ref[0]).astype(out_ref.dtype)
        sum_ref[0:1, :] = up_sum
        sum_ref[1:2, :] = jnp.sum(own_gy_ref[...].astype(f32), axis=0, keepdims=True)
        for number, left_ref, rights in (
            (0, gz_ref, (own_c_ref, other_c_ref)),
            (1, act_ref, (own_gy_ref, other_gy_ref)),
        ):
            put_grads(
                place_ref,
                dot_tokens(left_ref[...], both(*rights)),
                lambda block: grad_refs[0].at[block, number],
                lambda block: grad_refs[1].at[block, number],
                halves,
            )

    width = D // 2 if halves else D
    outs = [((half, D), f32), ((half, D), bf16), ((8, D), f32), ((4, 2, COLS, width), f32)]
    if halves:
        outs.append(((4, 2, COLS, width), bf16))
    return call(
        kernel,
        outs,
        place,
        gy_own,
        gy_other,
        c_own,
        c_other,
        preact,
        act,
        weights,
        scratch=[pltpu.VMEM((2 * half, D), bf16)],
    )


def core_swap(block):
    return lax.ppermute(block, "jc", SWAP)


def group_sum(mine, give):
    mine = mine + core_swap(give).astype(f32)
    return mine, lax.ppermute(mine.astype(bf16), "jx", SWAP)


def polynomial(base_ref, low_ref, mat_ref):
    low_ref[...] = base_ref[...].astype(bf16)
    for start in range(0, base_ref.shape[0], ROWS):
        block = pl.ds(start, ROWS)
        square = dot(low_ref[block, :], low_ref[...])
        mat_ref[block, :] = (quintic_two * base_ref[block, :] + quintic_three * square).astype(bf16)


def two_part(left, right):
    high = left.astype(bf16)
    rest = (left - high.astype(f32)).astype(bf16)
    return dot(high, right) + dot(rest, right)


def iterate(x_ref, out_ref, base_ref, work_ref, mat_ref, low_ref):
    size = x_ref.shape[0]
    blocks = [pl.ds(start, ROWS) for start in range(0, size, ROWS)]
    trace = jnp.zeros((1, 1), f32)
    line = lax.broadcasted_iota(jnp.int32, (ROWS, ROWS), 0)
    column = lax.broadcasted_iota(jnp.int32, (ROWS, ROWS), 1)
    for block in blocks:
        part = jnp.where(line == column, base_ref[block, block], 0.0)
        trace = trace + jnp.sum(part, keepdims=True)
    scale = 1.0 / (jnp.sqrt(trace) + 1e-07)
    base_ref[...] = base_ref[...] * (scale * scale)
    polynomial(base_ref, low_ref, mat_ref)

    for block in blocks:
        value = quintic_one * x_ref[block, :].astype(f32) + dot(x_ref[block, :], mat_ref[...])
        out_ref[block, :] = (scale * value).astype(bf16)
        work_ref[block, :] = quintic_one * base_ref[block, :] + two_part(
            base_ref[block, :], mat_ref[...]
        )
    turned = work_ref[...].T
    work_ref[...] = turned
    for block in blocks:
        base_ref[block, :] = quintic_one * work_ref[block, :] + two_part(
            work_ref[block, :], mat_ref[...]
        )
    polynomial(base_ref, low_ref, mat_ref)
    for block in blocks:
        x = out_ref[block, :]
        out_ref[block, :] = (quintic_one * x.astype(f32) + dot(x, mat_ref[...])).astype(bf16)


def orthogonalize(matrix, gram):
    size = matrix.shape[0]

    def kernel(unused, x_ref, gram_ref, out_ref, in_ref, base_ref, work_ref, mat_ref, low_ref):
        in_ref[...] = x_ref[...].T
        base_ref[...] = gram_ref[...]
        iterate(in_ref, out_ref, base_ref, work_ref, mat_ref, low_ref)
        out_ref[...] = out_ref[...].T

    return call(
        kernel,
        [((size, size), bf16)],
        jnp.zeros((1,), jnp.int32),
        matrix,
        gram,
        scratch=[pltpu.VMEM((size, size), kind) for kind in (bf16, f32, f32, bf16, bf16)],
    )[0]


def put_slots(slot_ref, x_ref):
    half = D // 2
    for source in range(8):
        group, number = source // TP, source % TP
        x_ref[number * COLS : (number + 1) * COLS, group * half : (group + 1) * half] = slot_ref[
            source
        ]


def slot_input(place_ref, slot_ref, moment_ref, sum_ref, x_ref, turned):
    put_slots(slot_ref, sum_ref)
    moment = moment_ref[...].astype(f32) * (momentum_decay * momentum_decay)
    if turned:
        moment = moment.T
    x_ref[...] = (sum_ref[...].astype(f32) * (1.0 + momentum_decay) + moment).astype(bf16)


def slot_gram(place, slots, moments):
    def kernel(place_ref, slot_ref, moment_ref, x_ref, gram_ref, sum_ref):
        slot_input(place_ref, slot_ref, moment_ref, sum_ref, x_ref, True)
        half = D // 2
        for part in range(2):
            rows = dot_tokens(x_ref[:, part * half : (part + 1) * half], x_ref[...]).astype(bf16)
            for number in range(2):
                back = 2 * part + number - place_ref[0]
                back = jnp.where(back < 0, back + 4, back)
                gram_ref[back] = rows[number * COLS : (number + 1) * COLS]

    return call(
        kernel,
        [((D, D), bf16), ((4, COLS, D), bf16)],
        place,
        slots,
        moments,
        scratch=[pltpu.VMEM((D, D), bf16)],
    )


def slot_orthogonalize(place, x_wide, grams, square_slots, moments):
    def kernel(
        place_ref,
        wide_ref,
        gram0_ref,
        gram1_ref,
        gram2_ref,
        gram3_ref,
        slot_ref,
        moment_ref,
        out_ref,
        x_ref,
        base_ref,
        work_ref,
        mat_ref,
        low_ref,
    ):
        core = place_ref[2]
        plain = (core == 1) & (place_ref[0] == 3)

        @pl.when(core == 0)
        def wide():
            x_ref[...] = wide_ref[...]
            for step, gram_ref in enumerate((gram0_ref, gram1_ref, gram2_ref, gram3_ref)):
                rows = pl.ds(pl.multiple_of(block_at(place_ref, step) * COLS, COLS), COLS)
                base_ref[rows, :] = gram_ref[...].astype(f32)

        @pl.when(plain)
        def square_plain():
            slot_input(place_ref, slot_ref, moment_ref, low_ref, x_ref, False)

        @pl.when((core == 1) & jnp.logical_not(plain))
        def square_turned():
            slot_input(place_ref, slot_ref, moment_ref, low_ref, x_ref, True)

        @pl.when(core == 1)
        def square():
            base_ref[...] = dot_tokens(x_ref[...], x_ref[...])

        iterate(x_ref, out_ref, base_ref, work_ref, mat_ref, low_ref)

        @pl.when(jnp.logical_not(plain))
        def turn():
            out_ref[...] = out_ref[...].T

    return call(
        kernel,
        [((D, D), bf16)],
        place,
        x_wide,
        *grams,
        square_slots,
        moments,
        scratch=[pltpu.VMEM((D, D), kind) for kind in (bf16, f32, f32, bf16, bf16)],
    )[0]


def slot_exchange(blocks):
    return lax.all_to_all(blocks, DP, split_axis=0, concat_axis=0, tiled=True)


def core_shift(block, step):
    size = lax.axis_size("ctx")
    return lax.ppermute(block, ("jc", "ctx"), [((i + step) % size, i) for i in range(size)])


def ctx_gram(gram):
    size = lax.axis_size("ctx")
    blocks = from_own(gram.astype(bf16).reshape(size, gram.shape[0] // size, -1))
    total = blocks[0].astype(f32)
    for step in (1, 3, 2):
        total = total + core_shift(blocks[step], -step).astype(f32)
    low = total.astype(bf16)
    full = [low] + [core_shift(low, step) for step in range(1, size)]
    return to_absolute(jnp.stack(full)).reshape(gram.shape).astype(f32)


def local(hidden_in, segments, out_grad, weights, vectors, mat_momentum, vec_first, vec_second):
    tokens_dev = hidden_in.shape[1]
    seq_len = segments.shape[1]
    half = 2 * tokens_dev
    dp_rows = weights.shape[2]
    ctx_size = lax.axis_size("ctx")
    x_index = lax.axis_index("jx")
    c_index = lax.axis_index("jc")
    t_index = 2 * x_index + c_index
    z_index = lax.axis_index("ctx")
    dp_index = lax.axis_index(DP)
    dp_size = lax.axis_size(DP)

    to_seq = []
    for t in range(TP):
        for z in range(ctx_size):
            to_seq.append((t * ctx_size + z, ((z % 2) * 2 + z // 2) * ctx_size + t))
    from_seq = [(b, a) for a, b in to_seq]
    axes = ("jx", "jc", "ctx")

    def x_join(block):
        return pair_join(block, "jx", 0)

    seg_row = jnp.pad(segments.astype(f32), ((0, 7), (0, D - seq_len)))
    moved = lax.ppermute(jnp.concatenate([hidden_in[0], seg_row], axis=0), axes, to_seq)
    segment_row = moved[tokens_dev, :seq_len]
    relative = lax.axis_size("g") == 2
    place = jnp.stack([z_index, lax.axis_index("g"), c_index]).astype(jnp.int32)
    if relative:
        piece, outs = first_piece(place, weights)
        own_attn = ctx_gather(piece)
        attn_weights = (own_attn, group_swap(own_attn))
        pieces = other_pieces(place, weights, outs, own_attn[1])
        near_blocks = ctx_near(pieces[0:2], *own_attn[1:])
        far = ctx_far(*near_blocks)
        first = group_first(*near_blocks)
    else:
        wide_weights = gather_weights_wide(weights.astype(bf16))
        outs = piece = place
    vec_rows = gather_vectors(vectors, outs)
    hidden = x_join(after(moved[:tokens_dev], piece))

    start = c_index * half
    pos = jnp.concatenate([start + jnp.arange(half), half - start + jnp.arange(half)])
    seg = jnp.roll(segment_row.reshape(2, half), -c_index, axis=0).reshape(-1)
    info = jnp.stack([pos.astype(f32), seg])
    row_info = jnp.pad(info, ((0, 6), (0, 0)))
    column_info = jnp.pad(info.T, ((0, 0), (0, 126)))
    vec_mine = lax.dynamic_slice_in_dim(vec_rows, t_index * COLS, COLS, axis=2)
    no_bias = jnp.zeros((LAYERS, 1, COLS), f32)
    qkv_bias = jnp.concatenate([vec_mine[:, 4:5], no_bias, vec_mine[:, 5:6]], axis=2)
    up_bias = vec_mine[:, 8:12].reshape(LAYERS, 1, D)

    stored = []
    (a_own,) = norm_stage(vec_rows, 0, 0, hidden)
    for layer in range(LAYERS):
        following = layer + 1 < LAYERS
        a_other = core_swap(a_own)
        if not relative:
            attn_weights, mlp_weights = wide_weights[layer]
        w_attn, qkv, lse, o, mine, give = attend_stage(
            place, row_info, column_info, qkv_bias[layer], a_own, a_other, attn_weights
        )
        if relative and not following:
            mine, gy_own = lax.optimization_barrier((mine, gy_own))
            moved_grad = lax.ppermute(after(out_grad[0], far), axes, to_seq)
        mine, recv = group_sum(mine, give)
        middle, c_own = norm_stage(vec_rows, layer, 2, hidden, mine, recv, (layer, 6))
        if relative:
            last = lax.ppermute(after(far, first), "g", SWAP)
            mlp_weights = ([near_blocks[0], near_blocks[1], far, near_blocks[2]], [first, last])
        c_other = core_swap(c_own)
        if relative and following:
            base = 3 * layer + 2
            own_attn = ctx_gather(pieces[base], far)
            c_other, own_attn = lax.optimization_barrier((c_other, own_attn))
        w_mlp, preact, act, mine, give = feed_stage(
            place, up_bias[layer], c_own, c_other, mlp_weights
        )
        if relative and following:
            attn_weights = (own_attn, [lax.ppermute(jnp.stack(own_attn), "g", SWAP)])
            near_blocks = ctx_near(pieces[base + 1 : base + 3], *own_attn[1:])
            moved_low = lax.ppermute(after(out_grad[0].astype(bf16), own_attn[2]), axes, to_seq)
        if following:
            mine, recv = group_sum(mine, give)
        stored.append(
            (hidden, middle, a_own, a_other, qkv, lse, o, c_own, c_other, preact, act, w_attn, w_mlp)
        )
        if following:
            hidden, a_own = norm_stage(vec_rows, layer + 1, 0, middle, mine, recv, (layer, 7))
            if relative:
                a_own, near_blocks, moved_low = lax.optimization_barrier(
                    (a_own, near_blocks, moved_low)
                )
                far = ctx_far(*near_blocks)
                first = group_first(*near_blocks)
                gy_own = x_join(moved_low)

    def send_back(rows):
        block = lax.dynamic_slice_in_dim(rows, x_index * tokens_dev, tokens_dev, axis=0)
        return lax.ppermute(block, axes, from_seq)

    last_sum = (mine, give)

    def last_hidden(*earlier):
        mine, recv = group_sum(last_sum[0], after(last_sum[1], *earlier))
        return stored[-1][1] + (mine + recv.astype(f32) + vec_rows[LAYERS - 1, 7:8])

    if not relative:
        grad_hidden = x_join(lax.ppermute(out_grad[0], axes, to_seq))
        hidden_out = send_back(last_hidden())
        gy_own = grad_hidden.astype(bf16)
    attn_half = mlp_half = None

    mat_list = [None] * LAYERS
    sum_list = [None] * LAYERS
    parts = [None] * LAYERS
    for layer in reversed(range(LAYERS)):
        h_in, middle, a_own, a_other, qkv, lse, o, c_own, c_other, preact, act, w_attn, w_mlp = stored[
            layer
        ]
        if relative and attn_half is not None:
            gy_own, mlp_first = lax.optimization_barrier((gy_own, mlp_first))
            mlp_part = ctx_sum_last(mlp_half, mlp_first)
            hidden = last_hidden(gy_own)
        gy_other = core_swap(gy_own)
        if relative and attn_half is None:
            gy_other, moved_grad = lax.optimization_barrier((gy_other, moved_grad))
            grad_hidden = x_join(moved_grad)
        mine, give, up_sums, *mlp_grads = feed_back_stage(
            place, gy_own, gy_other, c_own, c_other, preact, act, w_mlp, relative
        )
        if relative:
            if attn_half is None:
                mine, grad_hidden = lax.optimization_barrier((mine, grad_hidden))
            else:
                mine, hidden, attn_half, wide_part = lax.optimization_barrier(
                    (mine, hidden, attn_half, mlp_part)
                )
                attn_part = ctx_sum(attn_half)
            mlp_half = half_sum(*mlp_grads)
        mine, recv = group_sum(mine, give)
        grad_middle, gb_own, mid_sums = norm_back_stage(
            vec_rows, layer, 2, grad_hidden, mine, recv, middle
        )
        if relative and layer == LAYERS - 1:
            moment_low = mat_momentum.astype(bf16)
            table = [(1, 1), (1, 0), (1, 2), (0, 0), (0, 1), (1, 0), (0, 2), (0, 0)]
            moment_slots = slot_exchange(
                after(jnp.stack([moment_low[slot] for slot in table]), gb_own)
            ).reshape(D, D)
        gb_other = core_swap(gb_own)
        if relative and layer < LAYERS - 1:
            gb_other, attn_part, mlp_half = lax.optimization_barrier(
                (gb_other, attn_part, mlp_half)
            )
            parts[layer + 1] = (attn_part, wide_part)
            mlp_part = ctx_sum(mlp_half)
        mine, give, qkv_sums, *attn_grads = attend_back_stage(
            place,
            row_info,
            column_info,
            gb_own,
            gb_other,
            a_own,
            a_other,
            qkv,
            lse,
            o,
            w_attn,
            relative,
        )
        if relative:
            if layer == LAYERS - 1:
                mine, mlp_half, moment_slots = lax.optimization_barrier(
                    (mine, mlp_half, moment_slots)
                )
                mlp_first = ctx_sum_first(mlp_half)
            attn_half = half_sum(*attn_grads)
        else:
            attn_grad = attn_grads[0]
            g_wo = lax.all_to_all(
                attn_grad[3].reshape(COLS, TP, COLS), GROUP, split_axis=1, concat_axis=0, tiled=True
            )[:, 0]
            attn_grad = jnp.concatenate([attn_grad[:3], g_wo.T[None]], axis=0)
            mat_list[layer] = scatter_wide(
                jnp.concatenate([attn_grad[:, None], mlp_grads[0]], axis=1)
            )
        mine, recv = group_sum(mine, give)
        grad_hidden, gy_own, in_sums = norm_back_stage(
            vec_rows, layer, 0, grad_middle, mine, recv, h_in
        )
        sum_list[layer] = (in_sums, mid_sums, up_sums, qkv_sums)
    if not relative:
        input_grad = send_back(grad_hidden)

    once = jnp.where(x_index == 0, 1.0, 0.0).astype(f32)
    in_sums, mid_sums, up_sums, qkv_sums = [jnp.stack(sums) for sums in zip(*sum_list)]
    shared = once * jnp.concatenate(
        [in_sums[:, 0:2], mid_sums[:, 0:3], up_sums[:, 1:2]], axis=1
    )
    placed = jnp.concatenate(
        [
            qkv_sums[:, 0:1, :COLS],
            qkv_sums[:, 0:1, 2 * COLS :],
            up_sums[:, 0].reshape(LAYERS, ctx_size, COLS),
        ],
        axis=1,
    )
    placed = lax.dynamic_update_slice_in_dim(
        jnp.zeros((LAYERS, 6, D), f32), placed, t_index * COLS, axis=2
    )
    vec_terms = jnp.concatenate(
        [shared[:, 0:4], placed[:, 0:2], shared[:, 4:6], placed[:, 2:6]], axis=1
    )
    grad_vecs = lax.dynamic_slice_in_dim(
        sum_vectors(vec_terms), dp_index * vectors.shape[2], vectors.shape[2], axis=2
    )
    if relative:
        attn_part = ctx_sum(attn_half)
        wide_low = jnp.concatenate([parts[1][1], mlp_part]).astype(bf16)
        wide_slots = slot_exchange(jnp.repeat(after(wide_low, give), 2, axis=0))
        wide_slots, attn_part, grad_hidden = lax.optimization_barrier(
            (wide_slots, attn_part, grad_hidden)
        )
        x_wide, gram_blocks = slot_gram(place, wide_slots, moment_slots)
        total = gram_blocks[0].astype(f32)
        for step in (1, 3, 2):
            total = total + core_shift(gram_blocks[step], -step).astype(f32)
        gram_low = total.astype(bf16)
        square_low = after(jnp.stack([parts[1][0], attn_part]).astype(bf16), gram_low)
        square_slots = slot_exchange(jnp.tile(jnp.repeat(square_low, 2, axis=0), (2, 1, 1)))
        near, back, far = [core_shift(gram_low, step) for step in (1, 3, 2)]
        near, grad_vecs = lax.optimization_barrier((near, grad_vecs))
        ortho_mine = slot_orthogonalize(
            place, x_wide, (gram_low, near, far, back), square_slots, moment_slots
        )
        blocks, outs = grad_blocks(
            [attn_part, parts[1][0]], [mlp_part, parts[1][1]], dp_rows, square_slots
        )
        ortho_mine, blocks = lax.optimization_barrier((ortho_mine, blocks))
        returned = slot_exchange(ortho_mine.reshape(dp_size, dp_rows, D))
        ends = jnp.stack([hidden, grad_hidden])
        ends = lax.dynamic_slice_in_dim(ends, x_index * tokens_dev, tokens_dev, axis=1)
        hidden_out, input_grad = lax.ppermute(after(ends, near, back, far), axes, from_seq)
        ortho = jnp.stack([returned[slot] for slot in (3, 4, 6, 1, 0, 2)])
        ortho = ortho.reshape(weights.shape).astype(f32)
        grad_mats, moment_new = grad_rows(place, blocks, outs, mat_momentum)
    else:
        cols_dev = weights.shape[3]
        grad_list, moment_list, low_list = [], [], []
        for layer in range(LAYERS):
            for item in range(3):
                grad = mat_list[layer][item]
                moment = momentum_decay * mat_momentum[layer, item] + grad
                grad_list.append(grad)
                moment_list.append(moment)
                low_list.append((grad + momentum_decay * moment).astype(bf16))
        wide = [item for item in range(3 * LAYERS) if item % 3]
        squares = [item for item in range(3, 3 * LAYERS, 3)]
        table = []
        for number in range(4):
            table += [wide[number], squares[number % len(squares)]]
        table = (table * (-(-dp_size // 8)))[:dp_size]
        slots = jnp.stack([low_list[item] for item in table])
        received = lax.all_to_all(slots[:, None], DP, split_axis=0, concat_axis=1, tiled=True)
        current = received.reshape(dp_size * dp_rows, cols_dev)
        gram_local = dot_trans(current, current)
        gram = jnp.where(c_index == 0, ctx_gram(gram_local), gram_local)
        ortho_mine = orthogonalize(current, gram)
        returned = lax.all_to_all(
            ortho_mine.reshape(dp_size, 1, dp_rows, cols_dev),
            DP,
            split_axis=0,
            concat_axis=1,
            tiled=True,
        )[0]
        first_full = lax.all_gather(low_list[0], DP, axis=0, tiled=True)
        first_ortho = orthogonalize(first_full, dot_trans(first_full, first_full))
        ortho_list = [lax.dynamic_slice_in_dim(first_ortho, dp_index * dp_rows, dp_rows, axis=0)]
        ortho_list += [returned[table.index(item)] for item in range(1, 3 * LAYERS)]
        ortho = jnp.stack(ortho_list).reshape(LAYERS, 3, dp_rows, cols_dev).astype(f32)
        grad_mats = jnp.stack(grad_list).reshape(weights.shape)
        moment_new = jnp.stack(moment_list).reshape(weights.shape)
    factor = jnp.array([0.2 * math.sqrt(D), 0.2 * math.sqrt(FF), 0.2 * math.sqrt(FF)], f32)
    weights_new = weights * (1.0 - matrix_rate * matrix_decay) - matrix_rate * (
        ortho * factor[None, :, None, None]
    )
    first_new = first_decay * vec_first + (1.0 - first_decay) * grad_vecs
    second_new = second_decay * vec_second + (1.0 - second_decay) * grad_vecs * grad_vecs
    first_hat = first_new / (1.0 - first_decay**ADAM_STEP)
    second_hat = second_new / (1.0 - second_decay**ADAM_STEP)
    vectors_new = vectors * (1.0 - vector_rate * vector_decay) - vector_rate * first_hat / (
        jnp.sqrt(second_hat) + adam_epsilon
    )
    return (
        hidden_out[None],
        input_grad[None],
        grad_mats,
        moment_new,
        weights_new,
        grad_vecs,
        second_new,
        vectors_new,
    )


def solution(mesh):
    dp, ctx = mesh.shape["dp"], mesh.shape["ctx"]
    fine = Mesh(mesh.devices.reshape(dp // TP, 2, 2, ctx), EVERY)
    tokens = P(DP, "ctx", None)
    mats = P(None, None, DP, "ctx")
    vecs = P(None, "ctx", DP)
    return jax.shard_map(
        local,
        mesh=fine,
        in_specs=(tokens, P(DP, None), tokens, mats, vecs, mats, vecs, vecs),
        out_specs=(tokens, tokens, mats, mats, mats, vecs, vecs, vecs),
        check_vma=False,
    )
```

```python
import math

import jax
import jax.numpy as jnp
from jax import lax
from jax.experimental import pallas as pl
from jax.experimental.pallas import tpu as pltpu
from jax.sharding import Mesh, PartitionSpec as P

D = 768
HEADS = 12
HEAD = 64
FF = 3072
LAYERS = 2
ADAM_STEP = 10
TP = 4
COLS = D // TP
TP_HEADS = HEADS // TP
ROWS = 256

norm_epsilon = 1e-05
quintic_one = 3.4445
quintic_two = -4.775
quintic_three = 2.0315
momentum_decay = 0.95
matrix_rate = 0.6
matrix_decay = 0.01
first_decay = 0.9
second_decay = 0.999
vector_rate = 0.5
vector_decay = 0.01
adam_epsilon = 1e-08
masked_score = -1e30

GROUP = ("jx", "jc")
REPLICAS = ("g", "ctx")
DP = ("g", "jx", "jc")
EVERY = ("g", "jx", "jc", "ctx")
SWAP = [(0, 1), (1, 0)]
bf16 = jnp.bfloat16
f32 = jnp.float32


def dot(operand, other):
    return jnp.dot(operand, other, preferred_element_type=f32)


def dot_tokens(operand, other):
    return lax.dot_general(operand, other, (((0,), (0,)), ((), ())), preferred_element_type=f32)


def dot_trans(operand, other):
    return lax.dot_general(operand, other, (((1,), (1,)), ((), ())), preferred_element_type=f32)


def to_group(mats):
    count, rows, width = mats.shape
    split = mats.reshape(count, rows, TP, width // TP)
    return lax.all_to_all(split, GROUP, split_axis=2, concat_axis=1, tiled=True)[:, :, 0]


def from_group(mats):
    count, rows, width = mats.shape
    split = mats.reshape(count, TP, rows // TP, width)
    return lax.all_to_all(split, GROUP, split_axis=1, concat_axis=3, tiled=True)[:, 0]


def rotate(block, axis, step):
    size = lax.axis_size(axis)
    return lax.ppermute(block, axis, [((i + step) % size, i) for i in range(size)])


def pair_join(block, axis, dim):
    other = lax.ppermute(block, axis, SWAP)
    first = lax.axis_index(axis) == 0
    return jnp.concatenate(
        [jnp.where(first, block, other), jnp.where(first, other, block)], axis=dim
    )


def after(value, *others):
    return lax.optimization_barrier((value, *others))[0]


def roll_blocks(stack, sign):
    place = lax.axis_index("ctx")
    for bit in (1, 2):
        moved = jnp.roll(stack, sign * bit, axis=0)
        stack = jnp.where((place & bit) != 0, moved, stack)
    return stack


def from_own(stack):
    return roll_blocks(stack, -1)


def to_absolute(stack):
    return roll_blocks(stack, 1)


def out_moves():
    last = lax.axis_size("ctx") - 1
    size = last + 1
    moves = []
    for y in range(2):
        for x in range(2):
            for core in range(2):
                moves.append(
                    ((4 * y + 2 * x + core) * size + last, (4 * core + 2 * y + x) * size + last)
                )
    return moves


def out_pieces(mats):
    half = mats.shape[2] // 2
    core = lax.axis_index("jc")
    mine = lax.dynamic_slice_in_dim(mats, core * half, half, axis=2)
    give = lax.dynamic_slice_in_dim(mats, (1 - core) * half, half, axis=2)
    got = lax.ppermute(give, "jc", SWAP)
    rows = jnp.concatenate(
        [jnp.where(core == 0, mine, got), jnp.where(core == 0, got, mine)], axis=1
    )
    return lax.ppermute(rows, EVERY, out_moves())


def out_back(pieces):
    core = lax.axis_index("jc")
    rows = lax.ppermute(pieces, EVERY, [(b, a) for a, b in out_moves()])
    half = rows.shape[1] // 2
    mine = lax.dynamic_slice_in_dim(rows, core * half, half, axis=1)
    give = lax.dynamic_slice_in_dim(rows, (1 - core) * half, half, axis=1)
    got = lax.ppermute(give, "jc", SWAP)
    return jnp.concatenate(
        [jnp.where(core == 0, mine, got), jnp.where(core == 0, got, mine)], axis=2
    )


def last_block():
    return lax.axis_index("ctx") == lax.axis_size("ctx") - 1


def split_columns(mats, items):
    rows = mats.shape[2]

    def kernel(unused, mats_ref, out_ref):
        for number, (layer, item) in enumerate(items):
            turned = mats_ref[layer, item].T.astype(bf16)
            for quarter in range(TP):
                out_ref[quarter, number] = turned[quarter * COLS : (quarter + 1) * COLS]

    outs = [((TP, len(items), COLS, rows), bf16)]
    return call(kernel, outs, jnp.zeros((1,), jnp.int32), mats)[0]


def join_columns(place, blocks, outs, items):
    rows = blocks.shape[3]

    def kernel(place_ref, blocks_ref, outs_ref, *out_refs):
        for number, (layer, item) in enumerate(items):
            for source in range(TP):
                lanes = slice(source * rows, (source + 1) * rows)
                out_refs[number][:, lanes] = blocks_ref[source, number]
            if item == 0:

                @pl.when(place_ref[0] == 3)
                def last(number=number, layer=layer):
                    out_refs[number][...] = outs_ref[layer]

    shapes = [((COLS, TP * rows), bf16)] * len(items)
    return call(kernel, shapes, place, blocks, outs)


def group_exchange(blocks):
    return lax.all_to_all(blocks, GROUP, split_axis=0, concat_axis=0, tiled=True)


def first_piece(place, mats):
    outs = out_pieces(mats[:, 0].astype(bf16))
    blocks = group_exchange(split_columns(mats, [(0, 0)]))
    return join_columns(place, blocks, outs, [(0, 0)])[0], outs


def other_pieces(place, mats, outs, *earlier):
    items = [(layer, item) for layer in range(mats.shape[0]) for item in range(3)][1:]
    blocks = group_exchange(split_columns(after(mats, *earlier), items))
    return join_columns(place, blocks, outs, items)


def ctx_gather(piece, *earlier):
    piece = after(piece, *earlier)
    near, back, far = [rotate(piece, "ctx", step) for step in (1, 3, 2)]
    return [piece, near, far, back]


def group_swap(blocks):
    return [lax.ppermute(block, "g", SWAP) for block in blocks]


def ctx_near(pieces, *earlier):
    piece = after(jnp.stack(pieces), *earlier)
    return piece, rotate(piece, "ctx", 1), rotate(piece, "ctx", 3)


def ctx_far(piece, near, back):
    return rotate(after(piece, near, back), "ctx", 2)


def group_first(piece, near, back):
    return lax.ppermute(jnp.stack([piece, near, back]), "g", SWAP)


def gather_weights_wide(low):
    result = []
    for layer in range(low.shape[0]):
        mats = to_group(low[layer])
        parts = lax.all_gather(mats, REPLICAS, axis=0, tiled=False)
        parts = parts.reshape(lax.axis_size("g"), -1, *mats.shape)
        full = [parts[:, :, item].transpose(1, 3, 0, 2).reshape(D, D) for item in range(3)]
        w_o = lax.all_to_all(
            full[0][3 * COLS :].T.reshape(TP, COLS, COLS),
            GROUP,
            split_axis=0,
            concat_axis=2,
            tiled=True,
        )
        attn = jnp.concatenate([full[0][: 3 * COLS].reshape(3, COLS, D), w_o], axis=0)
        result.append((attn.reshape(D, D), jnp.stack([full[1], full[2]])))
    return result


def half_sum(mine, give):
    return mine + lax.ppermute(give, "g", SWAP).astype(f32)


def ctx_sum(blocks):
    low = blocks.astype(bf16)
    near, back, far = [rotate(low[step], "ctx", -step) for step in (1, 3, 2)]
    return blocks[0] + near.astype(f32) + back.astype(f32) + far.astype(f32)


def grad_blocks(attn_parts, mlp_parts, rows, *earlier):
    layers = len(attn_parts)
    zero = jnp.zeros((1,), jnp.int32)

    def split(unused, *refs):
        *part_refs, out_ref = refs
        for layer in range(layers):
            for item in range(3):
                if item:
                    part = part_refs[layers + layer][item - 1]
                else:
                    part = part_refs[layer][...]
                turned = part.T.astype(bf16)
                for target in range(TP):
                    out_ref[target, 3 * layer + item] = turned[target * rows : (target + 1) * rows]

    blocks = call(split, [((TP, 3 * layers, rows, COLS), bf16)], zero, *attn_parts, *mlp_parts)[0]
    return group_exchange(after(blocks, *earlier)), out_back(jnp.stack(attn_parts).astype(bf16))


def grad_rows(place, blocks, outs, momentum):
    layers = momentum.shape[0]

    def join(place_ref, blocks_ref, outs_ref, momentum_ref, grad_ref, new_ref):
        for layer in range(layers):
            for item in range(3):
                for source in range(TP):
                    lanes = slice(source * COLS, (source + 1) * COLS)
                    grad_ref[layer, item, :, lanes] = blocks_ref[source, 3 * layer + item].astype(f32)

            @pl.when(place_ref[0] == 3)
            def last(layer=layer):
                grad_ref[layer, 0] = outs_ref[layer].astype(f32)

        new_ref[...] = momentum_decay * momentum_ref[...] + grad_ref[...]

    shape = (momentum.shape, f32)
    return call(join, [shape, shape], place, blocks, outs, momentum)


def scatter_wide(mats):
    groups = lax.axis_size("g")
    blocks, count, width, depth = mats.shape
    stack = mats.astype(bf16).reshape(blocks, count, width, groups, depth // groups)
    stack = stack.transpose(3, 0, 1, 4, 2).reshape(groups * blocks, count, -1, width)
    part = lax.psum_scatter(stack, REPLICAS, scatter_dimension=0, tiled=True)[0]
    return from_group(part).astype(f32)


def gather_vectors(vectors, *earlier):
    low = vectors.astype(bf16)
    stack = jnp.stack([low] + [rotate(low, "ctx", step) for step in range(1, 4)])
    stack = pair_join(pair_join(after(to_absolute(stack), *earlier), "jc", 3), "jx", 3)
    if lax.axis_size("g") == 2:
        stack = pair_join(stack, "g", 3)
    else:
        stack = lax.all_gather(stack, "g", axis=3, tiled=True)
    return stack.transpose(1, 0, 2, 3).reshape(low.shape[0], -1, D).astype(f32)


def sum_vectors(terms):
    if lax.axis_size("g") == 2:
        terms = terms + lax.ppermute(terms, "g", SWAP)
    else:
        terms = lax.psum(terms, "g")
    layers, rows, width = terms.shape
    blocks = from_own(terms.reshape(layers, 4, rows // 4, width).transpose(1, 0, 2, 3))
    total = blocks[0]
    for step in range(1, 4):
        total = total + rotate(blocks[step], "ctx", -step)
    return total


def sum_group(total):
    total = total + lax.ppermute(total, "jc", SWAP)
    return total + lax.ppermute(total, "jx", SWAP)


def call(kernel, outs, *args, scratch=()):
    return pl.pallas_call(
        kernel,
        out_shape=[jax.ShapeDtypeStruct(shape, kind) for shape, kind in outs],
        in_specs=[pl.BlockSpec(memory_space=pltpu.SMEM)]
        + [pl.BlockSpec(memory_space=pltpu.VMEM)] * (len(args) - 1),
        out_specs=[pl.BlockSpec(memory_space=pltpu.VMEM)] * len(outs),
        scratch_shapes=list(scratch),
        compiler_params=pltpu.CompilerParams(vmem_limit_bytes=52 * 1024 * 1024),
    )(*args)


def block_at(place_ref, step):
    ahead = place_ref[0] + step
    return jnp.where(ahead >= 4, ahead - 4, ahead)


def put_blocks(place_ref, own_refs, other_refs, full_refs):
    half = D // 2
    mine = pl.multiple_of(place_ref[1] * half, half)
    theirs = pl.multiple_of((1 - place_ref[1]) * half, half)
    for step in range(4):
        rows = pl.ds(pl.multiple_of(block_at(place_ref, step) * COLS, COLS), COLS)
        for number, full_ref in enumerate(full_refs):
            own, other = own_refs[step], other_refs[step]
            if len(full_refs) > 1:
                own, other = own.at[number], other.at[number]
            full_ref[rows, pl.ds(mine, half)] = own[...]
            full_ref[rows, pl.ds(theirs, half)] = other[...]


def put_grads(place_ref, grad, mine_refs, give_refs, halves):
    half = D // 2
    for block in range(4):
        rows = grad[block * COLS : (block + 1) * COLS]
        if halves:
            back = block - place_ref[0]
            back = jnp.where(back < 0, back + 4, back)
            low = place_ref[1] == 0
            mine_refs(back)[...] = jnp.where(low, rows[:, :half], rows[:, half:])
            give_refs(back)[...] = jnp.where(low, rows[:, half:], rows[:, :half]).astype(bf16)
        else:
            mine_refs(block)[...] = rows


def norm_rows(hidden):
    center = hidden - jnp.mean(hidden, axis=-1, keepdims=True)
    variance = jnp.mean(center * center, axis=-1, keepdims=True)
    inverse = lax.rsqrt(variance + norm_epsilon)
    return center * inverse, inverse


def norm_stage(vecs, layer, row, hidden, mine=None, recv=None, bias=None):
    rows = hidden.shape[0]

    def kernel(unused, vec_ref, hidden_ref, *refs):
        total = hidden_ref[...]
        if mine is not None:
            mine_ref, recv_ref, total_ref, out_ref = refs
            bias_row = vec_ref[bias[0], bias[1] : bias[1] + 1, :]
            total = total + (mine_ref[...] + recv_ref[...].astype(f32) + bias_row)
            total_ref[...] = total
        else:
            (out_ref,) = refs
        normed, unused_scale = norm_rows(total)
        gain = vec_ref[layer, row : row + 1, :]
        shift = vec_ref[layer, row + 1 : row + 2, :]
        out_ref[...] = (normed * gain + shift).astype(bf16)

    outs = [((rows, D), bf16)]
    args = [hidden]
    if mine is not None:
        outs = [((rows, D), f32)] + outs
        args += [mine, recv]
    return call(kernel, outs, jnp.zeros((1,), jnp.int32), vecs, *args)


def norm_back_stage(vecs, layer, row, grad, mine, recv, hidden):
    rows = hidden.shape[0]

    def kernel(unused, vec_ref, grad_ref, mine_ref, recv_ref, hidden_ref, out_ref, low_ref, sum_ref):
        through = mine_ref[...] + recv_ref[...].astype(f32)
        normed, inverse = norm_rows(hidden_ref[...])
        scaled = through * vec_ref[layer, row : row + 1, :]
        part = jnp.mean(scaled, axis=-1, keepdims=True)
        part = part + normed * jnp.mean(scaled * normed, axis=-1, keepdims=True)
        total = grad_ref[...] + inverse * (scaled - part)
        out_ref[...] = total
        low = total.astype(bf16)
        low_ref[...] = low
        sum_ref[0:1, :] = jnp.sum(through * normed, axis=0, keepdims=True)
        sum_ref[1:2, :] = jnp.sum(through, axis=0, keepdims=True)
        sum_ref[2:3, :] = jnp.sum(low.astype(f32), axis=0, keepdims=True)

    outs = [((rows, D), f32), ((rows, D), bf16), ((8, D), f32)]
    return call(kernel, outs, jnp.zeros((1,), jnp.int32), vecs, grad, mine, recv, hidden)


def both(first_ref, second_ref):
    return jnp.concatenate([first_ref[...], second_ref[...]], axis=0)


def allowed_of(row_ref, column_ref):
    before = row_ref[0:1, :] <= column_ref[:, 0:1]
    return before & (row_ref[1:2, :] == column_ref[:, 1:2])


def attend_stage(place, row_info, column_info, bias, a_own, a_other, weights):
    half = a_own.shape[0]
    tokens = 2 * half
    wide = 3 * COLS
    own, other = weights if isinstance(weights, tuple) else ([], [])

    def kernel(place_ref, row_ref, column_ref, bias_ref, own_a_ref, other_a_ref, *refs):
        if own:
            own_refs, refs = refs[:4], refs[4:]
            others, refs = refs[: len(other)], refs[len(other) :]
            if len(other) == 1:
                others = [others[0].at[step] for step in range(4)]
            w_ref, qkv_ref, lse_ref, o_ref, mine_ref, give_ref = refs
            put_blocks(place_ref, own_refs, others, [w_ref])
        else:
            w_ref, qkv_ref, lse_ref, o_ref, mine_ref, give_ref = refs
        for start, a_ref in ((0, own_a_ref), (half, other_a_ref)):
            proj = dot_trans(a_ref[...], w_ref[0:wide, :]) + bias_ref[0:1, :]
            qkv_ref[start : start + half, :] = proj.astype(bf16)
        allowed = allowed_of(row_ref, column_ref)
        for head in range(TP_HEADS):
            lanes = head * HEAD
            k = qkv_ref[:, COLS + lanes : COLS + lanes + HEAD]
            v = qkv_ref[:, 2 * COLS + lanes : 2 * COLS + lanes + HEAD]
            for start in (0, half):
                rows = slice(start, start + half)
                q = qkv_ref[rows, lanes : lanes + HEAD]
                scores = jnp.where(allowed[rows], dot_trans(q, k) * HEAD ** (-0.5), masked_score)
                top = jnp.max(scores, axis=-1, keepdims=True)
                unnormed = jnp.exp(scores - top)
                total = jnp.sum(unnormed, axis=-1, keepdims=True)
                prob = (unnormed * (1.0 / total)).astype(bf16)
                o_ref[rows, lanes : lanes + HEAD] = dot(prob, v).astype(bf16)
                lse_ref[rows, head : head + 1] = top + jnp.log(total)
        mine_ref[...] = dot(o_ref[0:half, :], w_ref[wide:, :])
        give_ref[...] = dot(o_ref[half:, :], w_ref[wide:, :]).astype(bf16)

    outs = [
        ((tokens, wide), bf16),
        ((tokens, 128), f32),
        ((tokens, COLS), bf16),
        ((half, D), f32),
        ((half, D), bf16),
    ]
    if own:
        outs = [((D, D), bf16)] + outs
        return call(
            kernel, outs, place, row_info, column_info, bias, a_own, a_other, *own, *other
        )
    result = call(kernel, outs, place, row_info, column_info, bias, a_own, a_other, weights)
    return [weights] + list(result)


def attend_back_stage(
    place, row_info, column_info, gb_own, gb_other, a_own, a_other, qkv, lse, o, w_attn, halves
):
    half = a_own.shape[0]
    tokens = 2 * half
    wide = 3 * COLS

    def kernel(
        place_ref,
        row_ref,
        column_ref,
        own_gb_ref,
        other_gb_ref,
        own_a_ref,
        other_a_ref,
        qkv_ref,
        lse_ref,
        o_ref,
        w_ref,
        mine_ref,
        give_ref,
        sum_ref,
        *refs,
    ):
        *grad_refs, go_ref, all_ref = refs
        w_o = w_ref[wide:, :]
        for start, gb_ref in ((0, own_gb_ref), (half, other_gb_ref)):
            go_ref[start : start + half, :] = dot_trans(gb_ref[...], w_o).astype(bf16)
        allowed = allowed_of(row_ref, column_ref)
        for head in range(TP_HEADS):
            lanes = head * HEAD
            q_lanes = slice(lanes, lanes + HEAD)
            k_lanes = slice(COLS + lanes, COLS + lanes + HEAD)
            v_lanes = slice(2 * COLS + lanes, 2 * COLS + lanes + HEAD)
            k = qkv_ref[:, k_lanes]
            v = qkv_ref[:, v_lanes]
            gk = jnp.zeros((tokens, HEAD), f32)
            gv = jnp.zeros((tokens, HEAD), f32)
            for start in (0, half):
                rows = slice(start, start + half)
                q = qkv_ref[rows, q_lanes]
                go = go_ref[rows, q_lanes]
                scores = jnp.where(allowed[rows], dot_trans(q, k) * HEAD ** (-0.5), masked_score)
                prob = jnp.exp(scores - lse_ref[rows, head : head + 1])
                g_prob = dot_trans(go, v)
                row_dot = jnp.sum(g_prob * prob, axis=-1, keepdims=True)
                g_scores = (prob * (g_prob - row_dot)).astype(bf16)
                all_ref[rows, q_lanes] = (dot(g_scores, k) * HEAD ** (-0.5)).astype(bf16)
                gk = gk + dot_tokens(g_scores, q)
                gv = gv + dot_tokens(prob.astype(bf16), go)
            all_ref[:, k_lanes] = (gk * HEAD ** (-0.5)).astype(bf16)
            all_ref[:, v_lanes] = gv.astype(bf16)
        mine_ref[...] = dot(all_ref[0:half, :], w_ref[0:wide, :])
        give_ref[...] = dot(all_ref[half:, :], w_ref[0:wide, :]).astype(bf16)
        sum_ref[0:1, :] = jnp.sum(all_ref[...].astype(f32), axis=0, keepdims=True)
        grad = jnp.concatenate(
            [
                dot_tokens(all_ref[...], both(own_a_ref, other_a_ref)),
                dot_tokens(o_ref[...], both(own_gb_ref, other_gb_ref)),
            ],
            axis=0,
        )
        put_grads(
            place_ref,
            grad,
            lambda block: grad_refs[0].at[block],
            lambda block: grad_refs[1].at[block],
            halves,
        )

    width = D // 2 if halves else D
    outs = [((half, D), f32), ((half, D), bf16), ((8, wide), f32), ((4, COLS, width), f32)]
    if halves:
        outs.append(((4, COLS, width), bf16))
    return call(
        kernel,
        outs,
        place,
        row_info,
        column_info,
        gb_own,
        gb_other,
        a_own,
        a_other,
        qkv,
        lse,
        o,
        w_attn,
        scratch=[pltpu.VMEM((tokens, COLS), bf16), pltpu.VMEM((tokens, wide), bf16)],
    )


def tanh_part(preact):
    inner = math.sqrt(2.0 / math.pi) * (preact + 0.044715 * (preact * preact * preact))
    return jnp.tanh(inner)


def feed_stage(place, bias, c_own, c_other, weights):
    half = c_own.shape[0]
    own, other = weights if isinstance(weights, tuple) else ([], [])

    def kernel(place_ref, bias_ref, own_c_ref, other_c_ref, *refs):
        if own:
            own_refs, (first, last), refs = refs[:4], refs[4:6], refs[6:]
            others = [first.at[0], first.at[1], last, first.at[2]]
            w_ref, preact_ref, act_ref, mine_ref, give_ref = refs
            put_blocks(place_ref, own_refs, others, [w_ref.at[0], w_ref.at[1]])
        else:
            w_ref, preact_ref, act_ref, mine_ref, give_ref = refs
        for start, c_ref, out_ref in ((0, own_c_ref, mine_ref), (half, other_c_ref, give_ref)):
            rows = slice(start, start + half)
            preact = dot_trans(c_ref[...], w_ref[0]) + bias_ref[...]
            preact_ref[rows, :] = preact
            act = (0.5 * preact * (1.0 + tanh_part(preact))).astype(bf16)
            act_ref[rows, :] = act
            out_ref[...] = dot(act, w_ref[1]).astype(out_ref.dtype)

    outs = [
        ((2 * half, D), f32),
        ((2 * half, D), bf16),
        ((half, D), f32),
        ((half, D), bf16),
    ]
    if own:
        outs = [((2, D, D), bf16)] + outs
        return call(kernel, outs, place, bias, c_own, c_other, *own, *other)
    return [weights] + list(call(kernel, outs, place, bias, c_own, c_other, weights))


def feed_back_stage(place, gy_own, gy_other, c_own, c_other, preact, act, weights, halves):
    half = c_own.shape[0]

    def kernel(
        place_ref,
        own_gy_ref,
        other_gy_ref,
        own_c_ref,
        other_c_ref,
        preact_ref,
        act_ref,
        w_ref,
        mine_ref,
        give_ref,
        sum_ref,
        *refs,
    ):
        *grad_refs, gz_ref = refs
        up_sum = jnp.zeros((1, D), f32)
        for start, gy_ref, out_ref in ((0, own_gy_ref, mine_ref), (half, other_gy_ref, give_ref)):
            rows = slice(start, start + half)
            gu = dot_trans(gy_ref[...], w_ref[1])
            x = preact_ref[rows, :]
            tanh = tanh_part(x)
            slope = math.sqrt(2.0 / math.pi) * (1.0 + 3.0 * 0.044715 * (x * x))
            factor = 0.5 * (1.0 + tanh) + 0.5 * x * (1.0 - tanh * tanh) * slope
            gz = (gu * factor).astype(bf16)
            gz_ref[rows, :] = gz
            up_sum = up_sum + jnp.sum(gz.astype(f32), axis=0, keepdims=True)
            out_ref[...] = dot(gz, w_ref[0]).astype(out_ref.dtype)
        sum_ref[0:1, :] = up_sum
        sum_ref[1:2, :] = jnp.sum(own_gy_ref[...].astype(f32), axis=0, keepdims=True)
        for number, left_ref, rights in (
            (0, gz_ref, (own_c_ref, other_c_ref)),
            (1, act_ref, (own_gy_ref, other_gy_ref)),
        ):
            put_grads(
                place_ref,
                dot_tokens(left_ref[...], both(*rights)),
                lambda block: grad_refs[0].at[block, number],
                lambda block: grad_refs[1].at[block, number],
                halves,
            )

    width = D // 2 if halves else D
    outs = [((half, D), f32), ((half, D), bf16), ((8, D), f32), ((4, 2, COLS, width), f32)]
    if halves:
        outs.append(((4, 2, COLS, width), bf16))
    return call(
        kernel,
        outs,
        place,
        gy_own,
        gy_other,
        c_own,
        c_other,
        preact,
        act,
        weights,
        scratch=[pltpu.VMEM((2 * half, D), bf16)],
    )


def core_swap(block):
    return lax.ppermute(block, "jc", SWAP)


def group_sum(mine, give):
    mine = mine + core_swap(give).astype(f32)
    return mine, lax.ppermute(mine.astype(bf16), "jx", SWAP)


def polynomial(base_ref, low_ref, mat_ref):
    low_ref[...] = base_ref[...].astype(bf16)
    for start in range(0, base_ref.shape[0], ROWS):
        block = pl.ds(start, ROWS)
        square = dot(low_ref[block, :], low_ref[...])
        mat_ref[block, :] = (quintic_two * base_ref[block, :] + quintic_three * square).astype(bf16)


def two_part(left, right):
    high = left.astype(bf16)
    rest = (left - high.astype(f32)).astype(bf16)
    return dot(high, right) + dot(rest, right)


def iterate(x_ref, out_ref, base_ref, work_ref, mat_ref, low_ref):
    size = x_ref.shape[0]
    blocks = [pl.ds(start, ROWS) for start in range(0, size, ROWS)]
    trace = jnp.zeros((1, 1), f32)
    line = lax.broadcasted_iota(jnp.int32, (ROWS, ROWS), 0)
    column = lax.broadcasted_iota(jnp.int32, (ROWS, ROWS), 1)
    for block in blocks:
        part = jnp.where(line == column, base_ref[block, block], 0.0)
        trace = trace + jnp.sum(part, keepdims=True)
    scale = 1.0 / (jnp.sqrt(trace) + 1e-07)
    base_ref[...] = base_ref[...] * (scale * scale)
    polynomial(base_ref, low_ref, mat_ref)

    for block in blocks:
        value = quintic_one * x_ref[block, :].astype(f32) + dot(x_ref[block, :], mat_ref[...])
        out_ref[block, :] = (scale * value).astype(bf16)
        work_ref[block, :] = quintic_one * base_ref[block, :] + two_part(
            base_ref[block, :], mat_ref[...]
        )
    turned = work_ref[...].T
    work_ref[...] = turned
    for block in blocks:
        base_ref[block, :] = quintic_one * work_ref[block, :] + two_part(
            work_ref[block, :], mat_ref[...]
        )
    polynomial(base_ref, low_ref, mat_ref)
    for block in blocks:
        x = out_ref[block, :]
        out_ref[block, :] = (quintic_one * x.astype(f32) + dot(x, mat_ref[...])).astype(bf16)


def orthogonalize(matrix, gram):
    size = matrix.shape[0]

    def kernel(unused, x_ref, gram_ref, out_ref, in_ref, base_ref, work_ref, mat_ref, low_ref):
        in_ref[...] = x_ref[...].T
        base_ref[...] = gram_ref[...]
        iterate(in_ref, out_ref, base_ref, work_ref, mat_ref, low_ref)
        out_ref[...] = out_ref[...].T

    return call(
        kernel,
        [((size, size), bf16)],
        jnp.zeros((1,), jnp.int32),
        matrix,
        gram,
        scratch=[pltpu.VMEM((size, size), kind) for kind in (bf16, f32, f32, bf16, bf16)],
    )[0]


def put_slots(slot_ref, x_ref):
    half = D // 2
    for source in range(8):
        group, number = source // TP, source % TP
        x_ref[number * COLS : (number + 1) * COLS, group * half : (group + 1) * half] = slot_ref[
            source
        ]


def slot_input(place_ref, slot_ref, moment_ref, sum_ref, x_ref, turned):
    put_slots(slot_ref, sum_ref)
    moment = moment_ref[...].astype(f32) * (momentum_decay * momentum_decay)
    if turned:
        moment = moment.T
    x_ref[...] = (sum_ref[...].astype(f32) * (1.0 + momentum_decay) + moment).astype(bf16)


def slot_gram(place, slots, moments):
    def kernel(place_ref, slot_ref, moment_ref, x_ref, gram_ref, sum_ref):
        slot_input(place_ref, slot_ref, moment_ref, sum_ref, x_ref, True)
        half = D // 2
        for part in range(2):
            rows = dot_tokens(x_ref[:, part * half : (part + 1) * half], x_ref[...]).astype(bf16)
            for number in range(2):
                back = 2 * part + number - place_ref[0]
                back = jnp.where(back < 0, back + 4, back)
                gram_ref[back] = rows[number * COLS : (number + 1) * COLS]

    return call(
        kernel,
        [((D, D), bf16), ((4, COLS, D), bf16)],
        place,
        slots,
        moments,
        scratch=[pltpu.VMEM((D, D), bf16)],
    )


def slot_orthogonalize(place, x_wide, grams, square_slots, moments):
    def kernel(
        place_ref,
        wide_ref,
        gram0_ref,
        gram1_ref,
        gram2_ref,
        gram3_ref,
        slot_ref,
        moment_ref,
        out_ref,
        x_ref,
        base_ref,
        work_ref,
        mat_ref,
        low_ref,
    ):
        core = place_ref[2]
        plain = (core == 1) & (place_ref[0] == 3)

        @pl.when(core == 0)
        def wide():
            x_ref[...] = wide_ref[...]
            for step, gram_ref in enumerate((gram0_ref, gram1_ref, gram2_ref, gram3_ref)):
                rows = pl.ds(pl.multiple_of(block_at(place_ref, step) * COLS, COLS), COLS)
                base_ref[rows, :] = gram_ref[...].astype(f32)

        @pl.when(plain)
        def square_plain():
            slot_input(place_ref, slot_ref, moment_ref, low_ref, x_ref, False)

        @pl.when((core == 1) & jnp.logical_not(plain))
        def square_turned():
            slot_input(place_ref, slot_ref, moment_ref, low_ref, x_ref, True)

        @pl.when(core == 1)
        def square():
            base_ref[...] = dot_tokens(x_ref[...], x_ref[...])

        iterate(x_ref, out_ref, base_ref, work_ref, mat_ref, low_ref)

        @pl.when(jnp.logical_not(plain))
        def turn():
            out_ref[...] = out_ref[...].T

    return call(
        kernel,
        [((D, D), bf16)],
        place,
        x_wide,
        *grams,
        square_slots,
        moments,
        scratch=[pltpu.VMEM((D, D), kind) for kind in (bf16, f32, f32, bf16, bf16)],
    )[0]


def slot_exchange(blocks):
    return lax.all_to_all(blocks, DP, split_axis=0, concat_axis=0, tiled=True)


def core_shift(block, step):
    size = lax.axis_size("ctx")
    return lax.ppermute(block, ("jc", "ctx"), [((i + step) % size, i) for i in range(size)])


def ctx_gram(gram):
    size = lax.axis_size("ctx")
    blocks = from_own(gram.astype(bf16).reshape(size, gram.shape[0] // size, -1))
    total = blocks[0].astype(f32)
    for step in (1, 3, 2):
        total = total + core_shift(blocks[step], -step).astype(f32)
    low = total.astype(bf16)
    full = [low] + [core_shift(low, step) for step in range(1, size)]
    return to_absolute(jnp.stack(full)).reshape(gram.shape).astype(f32)


def local(hidden_in, segments, out_grad, weights, vectors, mat_momentum, vec_first, vec_second):
    tokens_dev = hidden_in.shape[1]
    seq_len = segments.shape[1]
    half = 2 * tokens_dev
    dp_rows = weights.shape[2]
    ctx_size = lax.axis_size("ctx")
    x_index = lax.axis_index("jx")
    c_index = lax.axis_index("jc")
    t_index = 2 * x_index + c_index
    z_index = lax.axis_index("ctx")
    dp_index = lax.axis_index(DP)
    dp_size = lax.axis_size(DP)

    to_seq = []
    for t in range(TP):
        for z in range(ctx_size):
            to_seq.append((t * ctx_size + z, ((z % 2) * 2 + z // 2) * ctx_size + t))
    from_seq = [(b, a) for a, b in to_seq]
    axes = ("jx", "jc", "ctx")

    def x_join(block):
        return pair_join(block, "jx", 0)

    seg_row = jnp.pad(segments.astype(f32), ((0, 7), (0, D - seq_len)))
    moved = lax.ppermute(jnp.concatenate([hidden_in[0], seg_row], axis=0), axes, to_seq)
    segment_row = moved[tokens_dev, :seq_len]
    relative = lax.axis_size("g") == 2
    place = jnp.stack([z_index, lax.axis_index("g"), c_index]).astype(jnp.int32)
    if relative:
        piece, outs = first_piece(place, weights)
        own_attn = ctx_gather(piece)
        attn_weights = (own_attn, group_swap(own_attn))
        pieces = other_pieces(place, weights, outs, own_attn[1])
        near_blocks = ctx_near(pieces[0:2], *own_attn[1:])
        far = ctx_far(*near_blocks)
        first = group_first(*near_blocks)
    else:
        wide_weights = gather_weights_wide(weights.astype(bf16))
        outs = piece = place
    vec_rows = gather_vectors(vectors, outs)
    hidden = x_join(after(moved[:tokens_dev], piece))

    start = c_index * half
    pos = jnp.concatenate([start + jnp.arange(half), half - start + jnp.arange(half)])
    seg = jnp.roll(segment_row.reshape(2, half), -c_index, axis=0).reshape(-1)
    info = jnp.stack([pos.astype(f32), seg])
    row_info = jnp.pad(info, ((0, 6), (0, 0)))
    column_info = jnp.pad(info.T, ((0, 0), (0, 126)))
    vec_mine = lax.dynamic_slice_in_dim(vec_rows, t_index * COLS, COLS, axis=2)
    no_bias = jnp.zeros((LAYERS, 1, COLS), f32)
    qkv_bias = jnp.concatenate([vec_mine[:, 4:5], no_bias, vec_mine[:, 5:6]], axis=2)
    up_bias = vec_mine[:, 8:12].reshape(LAYERS, 1, D)

    stored = []
    (a_own,) = norm_stage(vec_rows, 0, 0, hidden)
    for layer in range(LAYERS):
        following = layer + 1 < LAYERS
        a_other = core_swap(a_own)
        if not relative:
            attn_weights, mlp_weights = wide_weights[layer]
        w_attn, qkv, lse, o, mine, give = attend_stage(
            place, row_info, column_info, qkv_bias[layer], a_own, a_other, attn_weights
        )
        if relative and not following:
            mine, gy_own = lax.optimization_barrier((mine, gy_own))
            moved_grad = lax.ppermute(after(out_grad[0], far), axes, to_seq)
        mine, recv = group_sum(mine, give)
        middle, c_own = norm_stage(vec_rows, layer, 2, hidden, mine, recv, (layer, 6))
        if relative:
            last = lax.ppermute(after(far, first), "g", SWAP)
            mlp_weights = ([near_blocks[0], near_blocks[1], far, near_blocks[2]], [first, last])
        c_other = core_swap(c_own)
        if relative and following:
            base = 3 * layer + 2
            own_attn = ctx_gather(pieces[base], far)
            c_other, own_attn = lax.optimization_barrier((c_other, own_attn))
        w_mlp, preact, act, mine, give = feed_stage(
            place, up_bias[layer], c_own, c_other, mlp_weights
        )
        if relative and following:
            attn_weights = (own_attn, [lax.ppermute(jnp.stack(own_attn), "g", SWAP)])
            near_blocks = ctx_near(pieces[base + 1 : base + 3], *own_attn[1:])
            moved_low = lax.ppermute(after(out_grad[0].astype(bf16), own_attn[2]), axes, to_seq)
        if following:
            mine, recv = group_sum(mine, give)
        stored.append(
            (hidden, middle, a_own, a_other, qkv, lse, o, c_own, c_other, preact, act, w_attn, w_mlp)
        )
        if following:
            hidden, a_own = norm_stage(vec_rows, layer + 1, 0, middle, mine, recv, (layer, 7))
            if relative:
                a_own, near_blocks, moved_low = lax.optimization_barrier(
                    (a_own, near_blocks, moved_low)
                )
                far = ctx_far(*near_blocks)
                first = group_first(*near_blocks)
                gy_own = x_join(moved_low)

    def send_back(rows):
        block = lax.dynamic_slice_in_dim(rows, x_index * tokens_dev, tokens_dev, axis=0)
        return lax.ppermute(block, axes, from_seq)

    last_sum = (mine, give)

    def last_hidden(*earlier):
        mine, recv = group_sum(last_sum[0], after(last_sum[1], *earlier))
        return stored[-1][1] + (mine + recv.astype(f32) + vec_rows[LAYERS - 1, 7:8])

    if not relative:
        grad_hidden = x_join(lax.ppermute(out_grad[0], axes, to_seq))
        hidden_out = send_back(last_hidden())
        gy_own = grad_hidden.astype(bf16)
    attn_half = mlp_half = None

    mat_list = [None] * LAYERS
    sum_list = [None] * LAYERS
    parts = [None] * LAYERS
    for layer in reversed(range(LAYERS)):
        h_in, middle, a_own, a_other, qkv, lse, o, c_own, c_other, preact, act, w_attn, w_mlp = stored[
            layer
        ]
        if relative and attn_half is not None:
            gy_own, attn_half = lax.optimization_barrier((gy_own, attn_half))
            hidden = last_hidden(gy_own)
        gy_other = core_swap(gy_own)
        if relative and attn_half is None:
            gy_other, moved_grad = lax.optimization_barrier((gy_other, moved_grad))
            grad_hidden = x_join(moved_grad)
        mine, give, up_sums, *mlp_grads = feed_back_stage(
            place, gy_own, gy_other, c_own, c_other, preact, act, w_mlp, relative
        )
        if relative:
            if attn_half is None:
                mine, grad_hidden = lax.optimization_barrier((mine, grad_hidden))
            else:
                mine, hidden, wide_part = lax.optimization_barrier((mine, hidden, mlp_part))
                attn_part = ctx_sum(attn_half)
            mlp_half = half_sum(*mlp_grads)
        mine, recv = group_sum(mine, give)
        grad_middle, gb_own, mid_sums = norm_back_stage(
            vec_rows, layer, 2, grad_hidden, mine, recv, middle
        )
        if relative and layer == LAYERS - 1:
            moment_low = mat_momentum.astype(bf16)
            table = [(1, 1), (1, 0), (1, 2), (0, 0), (0, 1), (1, 0), (0, 2), (0, 0)]
            moment_slots = slot_exchange(
                after(jnp.stack([moment_low[slot] for slot in table]), gb_own)
            ).reshape(D, D)
        gb_other = core_swap(gb_own)
        if relative and layer < LAYERS - 1:
            gb_other, attn_part, mlp_half = lax.optimization_barrier(
                (gb_other, attn_part, mlp_half)
            )
            parts[layer + 1] = (attn_part, wide_part)
            mlp_part = ctx_sum(mlp_half)
        mine, give, qkv_sums, *attn_grads = attend_back_stage(
            place,
            row_info,
            column_info,
            gb_own,
            gb_other,
            a_own,
            a_other,
            qkv,
            lse,
            o,
            w_attn,
            relative,
        )
        if relative:
            if layer == LAYERS - 1:
                mine, mlp_half, moment_slots = lax.optimization_barrier(
                    (mine, mlp_half, moment_slots)
                )
                mlp_part = ctx_sum(mlp_half)
            attn_half = half_sum(*attn_grads)
        else:
            attn_grad = attn_grads[0]
            g_wo = lax.all_to_all(
                attn_grad[3].reshape(COLS, TP, COLS), GROUP, split_axis=1, concat_axis=0, tiled=True
            )[:, 0]
            attn_grad = jnp.concatenate([attn_grad[:3], g_wo.T[None]], axis=0)
            mat_list[layer] = scatter_wide(
                jnp.concatenate([attn_grad[:, None], mlp_grads[0]], axis=1)
            )
        mine, recv = group_sum(mine, give)
        grad_hidden, gy_own, in_sums = norm_back_stage(
            vec_rows, layer, 0, grad_middle, mine, recv, h_in
        )
        sum_list[layer] = (in_sums, mid_sums, up_sums, qkv_sums)
    if not relative:
        input_grad = send_back(grad_hidden)

    once = jnp.where(x_index == 0, 1.0, 0.0).astype(f32)
    in_sums, mid_sums, up_sums, qkv_sums = [jnp.stack(sums) for sums in zip(*sum_list)]
    shared = once * jnp.concatenate(
        [in_sums[:, 0:2], mid_sums[:, 0:3], up_sums[:, 1:2]], axis=1
    )
    placed = jnp.concatenate(
        [
            qkv_sums[:, 0:1, :COLS],
            qkv_sums[:, 0:1, 2 * COLS :],
            up_sums[:, 0].reshape(LAYERS, ctx_size, COLS),
        ],
        axis=1,
    )
    placed = lax.dynamic_update_slice_in_dim(
        jnp.zeros((LAYERS, 6, D), f32), placed, t_index * COLS, axis=2
    )
    vec_terms = jnp.concatenate(
        [shared[:, 0:4], placed[:, 0:2], shared[:, 4:6], placed[:, 2:6]], axis=1
    )
    vec_sums = sum_vectors(vec_terms)
    if relative:
        attn_low = attn_half.astype(bf16)
        attn_sums = [rotate(attn_low[step], "ctx", -step) for step in (1, 3, 2)]
        wide_low = jnp.concatenate([parts[1][1], mlp_part]).astype(bf16)
        wide_slots = slot_exchange(jnp.repeat(after(wide_low, give), 2, axis=0))
        wide_slots, grad_hidden = lax.optimization_barrier((wide_slots, grad_hidden))
        x_wide, gram_blocks = slot_gram(place, wide_slots, moment_slots)
        attn_sums, unused = lax.optimization_barrier((attn_sums, gram_blocks))
        attn_part = attn_half[0] + sum(block.astype(f32) for block in attn_sums)
        total = gram_blocks[0].astype(f32)
        for step in (1, 3, 2):
            total = total + core_shift(gram_blocks[step], -step).astype(f32)
        gram_low = total.astype(bf16)
        square_low, vec_sums, unused = lax.optimization_barrier(
            (jnp.stack([parts[1][0], attn_part]).astype(bf16), vec_sums, gram_low)
        )
        square_slots = slot_exchange(jnp.tile(jnp.repeat(square_low, 2, axis=0), (2, 1, 1)))
        near, back, far = [core_shift(gram_low, step) for step in (1, 3, 2)]
        ortho_mine = slot_orthogonalize(
            place, x_wide, (gram_low, near, far, back), square_slots, moment_slots
        )
        blocks, outs = grad_blocks(
            [attn_part, parts[1][0]], [mlp_part, parts[1][1]], dp_rows, square_slots, near, back, far
        )
        ortho_mine, blocks = lax.optimization_barrier((ortho_mine, blocks))
        returned = slot_exchange(ortho_mine.reshape(dp_size, dp_rows, D))
        ends = jnp.stack([hidden, grad_hidden])
        ends = lax.dynamic_slice_in_dim(ends, x_index * tokens_dev, tokens_dev, axis=1)
        hidden_out, input_grad = lax.ppermute(after(ends, near, back, far), axes, from_seq)
        ortho = jnp.stack([returned[slot] for slot in (3, 4, 6, 1, 0, 2)])
        ortho = ortho.reshape(weights.shape).astype(f32)
        grad_mats, moment_new = grad_rows(place, blocks, outs, mat_momentum)
    else:
        cols_dev = weights.shape[3]
        grad_list, moment_list, low_list = [], [], []
        for layer in range(LAYERS):
            for item in range(3):
                grad = mat_list[layer][item]
                moment = momentum_decay * mat_momentum[layer, item] + grad
                grad_list.append(grad)
                moment_list.append(moment)
                low_list.append((grad + momentum_decay * moment).astype(bf16))
        wide = [item for item in range(3 * LAYERS) if item % 3]
        squares = [item for item in range(3, 3 * LAYERS, 3)]
        table = []
        for number in range(4):
            table += [wide[number], squares[number % len(squares)]]
        table = (table * (-(-dp_size // 8)))[:dp_size]
        slots = jnp.stack([low_list[item] for item in table])
        received = lax.all_to_all(slots[:, None], DP, split_axis=0, concat_axis=1, tiled=True)
        current = received.reshape(dp_size * dp_rows, cols_dev)
        gram_local = dot_trans(current, current)
        gram = jnp.where(c_index == 0, ctx_gram(gram_local), gram_local)
        ortho_mine = orthogonalize(current, gram)
        returned = lax.all_to_all(
            ortho_mine.reshape(dp_size, 1, dp_rows, cols_dev),
            DP,
            split_axis=0,
            concat_axis=1,
            tiled=True,
        )[0]
        first_full = lax.all_gather(low_list[0], DP, axis=0, tiled=True)
        first_ortho = orthogonalize(first_full, dot_trans(first_full, first_full))
        ortho_list = [lax.dynamic_slice_in_dim(first_ortho, dp_index * dp_rows, dp_rows, axis=0)]
        ortho_list += [returned[table.index(item)] for item in range(1, 3 * LAYERS)]
        ortho = jnp.stack(ortho_list).reshape(LAYERS, 3, dp_rows, cols_dev).astype(f32)
        grad_mats = jnp.stack(grad_list).reshape(weights.shape)
        moment_new = jnp.stack(moment_list).reshape(weights.shape)
    grad_vecs = lax.dynamic_slice_in_dim(
        sum_group(vec_sums), dp_index * vectors.shape[2], vectors.shape[2], axis=2
    )
    factor = jnp.array([0.2 * math.sqrt(D), 0.2 * math.sqrt(FF), 0.2 * math.sqrt(FF)], f32)
    weights_new = weights * (1.0 - matrix_rate * matrix_decay) - matrix_rate * (
        ortho * factor[None, :, None, None]
    )
    first_new = first_decay * vec_first + (1.0 - first_decay) * grad_vecs
    second_new = second_decay * vec_second + (1.0 - second_decay) * grad_vecs * grad_vecs
    first_hat = first_new / (1.0 - first_decay**ADAM_STEP)
    second_hat = second_new / (1.0 - second_decay**ADAM_STEP)
    vectors_new = vectors * (1.0 - vector_rate * vector_decay) - vector_rate * first_hat / (
        jnp.sqrt(second_hat) + adam_epsilon
    )
    return (
        hidden_out[None],
        input_grad[None],
        grad_mats,
        moment_new,
        weights_new,
        grad_vecs,
        second_new,
        vectors_new,
    )


def solution(mesh):
    dp, ctx = mesh.shape["dp"], mesh.shape["ctx"]
    fine = Mesh(mesh.devices.reshape(dp // TP, 2, 2, ctx), EVERY)
    tokens = P(DP, "ctx", None)
    mats = P(None, None, DP, "ctx")
    vecs = P(None, "ctx", DP)
    return jax.shard_map(
        local,
        mesh=fine,
        in_specs=(tokens, P(DP, None), tokens, mats, vecs, mats, vecs, vecs),
        out_specs=(tokens, tokens, mats, mats, mats, vecs, vecs, vecs),
        check_vma=False,
    )
```

```python
import math

import jax
import jax.numpy as jnp
from jax import lax
from jax.experimental import pallas as pl
from jax.experimental.pallas import tpu as pltpu
from jax.sharding import Mesh, PartitionSpec as P

D = 768
HEADS = 12
HEAD = 64
FF = 3072
LAYERS = 2
ADAM_STEP = 10
TP = 4
COLS = D // TP
TP_HEADS = HEADS // TP
ROWS = 256

norm_epsilon = 1e-05
quintic_one = 3.4445
quintic_two = -4.775
quintic_three = 2.0315
momentum_decay = 0.95
matrix_rate = 0.6
matrix_decay = 0.01
first_decay = 0.9
second_decay = 0.999
vector_rate = 0.5
vector_decay = 0.01
adam_epsilon = 1e-08
masked_score = -1e30

GROUP = ("jx", "jc")
REPLICAS = ("g", "ctx")
DP = ("g", "jx", "jc")
EVERY = ("g", "jx", "jc", "ctx")
SWAP = [(0, 1), (1, 0)]
bf16 = jnp.bfloat16
f32 = jnp.float32


def dot(operand, other):
    return jnp.dot(operand, other, preferred_element_type=f32)


def dot_tokens(operand, other):
    return lax.dot_general(operand, other, (((0,), (0,)), ((), ())), preferred_element_type=f32)


def dot_trans(operand, other):
    return lax.dot_general(operand, other, (((1,), (1,)), ((), ())), preferred_element_type=f32)


def to_group(mats):
    count, rows, width = mats.shape
    split = mats.reshape(count, rows, TP, width // TP)
    return lax.all_to_all(split, GROUP, split_axis=2, concat_axis=1, tiled=True)[:, :, 0]


def from_group(mats):
    count, rows, width = mats.shape
    split = mats.reshape(count, TP, rows // TP, width)
    return lax.all_to_all(split, GROUP, split_axis=1, concat_axis=3, tiled=True)[:, 0]


def rotate(block, axis, step):
    size = lax.axis_size(axis)
    return lax.ppermute(block, axis, [((i + step) % size, i) for i in range(size)])


def pair_join(block, axis, dim):
    other = lax.ppermute(block, axis, SWAP)
    first = lax.axis_index(axis) == 0
    return jnp.concatenate(
        [jnp.where(first, block, other), jnp.where(first, other, block)], axis=dim
    )


def after(value, *others):
    return lax.optimization_barrier((value, *others))[0]


def roll_blocks(stack, sign):
    place = lax.axis_index("ctx")
    for bit in (1, 2):
        moved = jnp.roll(stack, sign * bit, axis=0)
        stack = jnp.where((place & bit) != 0, moved, stack)
    return stack


def from_own(stack):
    return roll_blocks(stack, -1)


def to_absolute(stack):
    return roll_blocks(stack, 1)


def out_moves():
    last = lax.axis_size("ctx") - 1
    size = last + 1
    moves = []
    for y in range(2):
        for x in range(2):
            for core in range(2):
                moves.append(
                    ((4 * y + 2 * x + core) * size + last, (4 * core + 2 * y + x) * size + last)
                )
    return moves


def out_pieces(mats):
    half = mats.shape[2] // 2
    core = lax.axis_index("jc")
    mine = lax.dynamic_slice_in_dim(mats, core * half, half, axis=2)
    give = lax.dynamic_slice_in_dim(mats, (1 - core) * half, half, axis=2)
    got = lax.ppermute(give, "jc", SWAP)
    rows = jnp.concatenate(
        [jnp.where(core == 0, mine, got), jnp.where(core == 0, got, mine)], axis=1
    )
    return lax.ppermute(rows, EVERY, out_moves())


def out_back(pieces):
    core = lax.axis_index("jc")
    rows = lax.ppermute(pieces, EVERY, [(b, a) for a, b in out_moves()])
    half = rows.shape[1] // 2
    mine = lax.dynamic_slice_in_dim(rows, core * half, half, axis=1)
    give = lax.dynamic_slice_in_dim(rows, (1 - core) * half, half, axis=1)
    got = lax.ppermute(give, "jc", SWAP)
    return jnp.concatenate(
        [jnp.where(core == 0, mine, got), jnp.where(core == 0, got, mine)], axis=2
    )


def last_block():
    return lax.axis_index("ctx") == lax.axis_size("ctx") - 1


def split_columns(mats, items):
    rows = mats.shape[2]

    def kernel(unused, mats_ref, out_ref):
        for number, (layer, item) in enumerate(items):
            turned = mats_ref[layer, item].T.astype(bf16)
            for quarter in range(TP):
                out_ref[quarter, number] = turned[quarter * COLS : (quarter + 1) * COLS]

    outs = [((TP, len(items), COLS, rows), bf16)]
    return call(kernel, outs, jnp.zeros((1,), jnp.int32), mats)[0]


def join_columns(place, blocks, outs, items):
    rows = blocks.shape[3]

    def kernel(place_ref, blocks_ref, outs_ref, *out_refs):
        for number, (layer, item) in enumerate(items):
            for source in range(TP):
                lanes = slice(source * rows, (source + 1) * rows)
                out_refs[number][:, lanes] = blocks_ref[source, number]
            if item == 0:

                @pl.when(place_ref[0] == 3)
                def last(number=number, layer=layer):
                    out_refs[number][...] = outs_ref[layer]

    shapes = [((COLS, TP * rows), bf16)] * len(items)
    return call(kernel, shapes, place, blocks, outs)


def group_exchange(blocks):
    return lax.all_to_all(blocks, GROUP, split_axis=0, concat_axis=0, tiled=True)


def first_piece(place, mats):
    outs = out_pieces(mats[:, 0].astype(bf16))
    blocks = group_exchange(split_columns(mats, [(0, 0)]))
    return join_columns(place, blocks, outs, [(0, 0)])[0], outs


def other_pieces(place, mats, outs, *earlier):
    items = [(layer, item) for layer in range(mats.shape[0]) for item in range(3)][1:]
    blocks = group_exchange(split_columns(after(mats, *earlier), items))
    return join_columns(place, blocks, outs, items)


def ctx_gather(piece, *earlier):
    piece = after(piece, *earlier)
    near, back, far = [rotate(piece, "ctx", step) for step in (1, 3, 2)]
    return [piece, near, far, back]


def group_swap(blocks):
    return [lax.ppermute(block, "g", SWAP) for block in blocks]


def ctx_near(pieces, *earlier):
    piece = after(jnp.stack(pieces), *earlier)
    return piece, rotate(piece, "ctx", 1), rotate(piece, "ctx", 3)


def ctx_far(piece, near, back):
    return rotate(after(piece, near, back), "ctx", 2)


def group_first(piece, near, back):
    return lax.ppermute(jnp.stack([piece, near, back]), "g", SWAP)


def gather_weights_wide(low):
    result = []
    for layer in range(low.shape[0]):
        mats = to_group(low[layer])
        parts = lax.all_gather(mats, REPLICAS, axis=0, tiled=False)
        parts = parts.reshape(lax.axis_size("g"), -1, *mats.shape)
        full = [parts[:, :, item].transpose(1, 3, 0, 2).reshape(D, D) for item in range(3)]
        w_o = lax.all_to_all(
            full[0][3 * COLS :].T.reshape(TP, COLS, COLS),
            GROUP,
            split_axis=0,
            concat_axis=2,
            tiled=True,
        )
        attn = jnp.concatenate([full[0][: 3 * COLS].reshape(3, COLS, D), w_o], axis=0)
        result.append((attn.reshape(D, D), jnp.stack([full[1], full[2]])))
    return result


def half_sum(mine, give):
    return mine + lax.ppermute(give, "g", SWAP).astype(f32)


def ctx_sum(blocks):
    low = blocks.astype(bf16)
    near, back, far = [rotate(low[step], "ctx", -step) for step in (1, 3, 2)]
    return blocks[0] + near.astype(f32) + back.astype(f32) + far.astype(f32)


def grad_blocks(attn_parts, mlp_parts, rows, *earlier):
    layers = len(attn_parts)
    zero = jnp.zeros((1,), jnp.int32)

    def split(unused, *refs):
        *part_refs, out_ref = refs
        for layer in range(layers):
            for item in range(3):
                if item:
                    part = part_refs[layers + layer][item - 1]
                else:
                    part = part_refs[layer][...]
                turned = part.T.astype(bf16)
                for target in range(TP):
                    out_ref[target, 3 * layer + item] = turned[target * rows : (target + 1) * rows]

    blocks = call(split, [((TP, 3 * layers, rows, COLS), bf16)], zero, *attn_parts, *mlp_parts)[0]
    return group_exchange(after(blocks, *earlier)), out_back(jnp.stack(attn_parts).astype(bf16))


def grad_rows(place, blocks, outs, momentum):
    layers = momentum.shape[0]

    def join(place_ref, blocks_ref, outs_ref, momentum_ref, grad_ref, new_ref):
        for layer in range(layers):
            for item in range(3):
                for source in range(TP):
                    lanes = slice(source * COLS, (source + 1) * COLS)
                    grad_ref[layer, item, :, lanes] = blocks_ref[source, 3 * layer + item].astype(f32)

            @pl.when(place_ref[0] == 3)
            def last(layer=layer):
                grad_ref[layer, 0] = outs_ref[layer].astype(f32)

        new_ref[...] = momentum_decay * momentum_ref[...] + grad_ref[...]

    shape = (momentum.shape, f32)
    return call(join, [shape, shape], place, blocks, outs, momentum)


def scatter_wide(mats):
    groups = lax.axis_size("g")
    blocks, count, width, depth = mats.shape
    stack = mats.astype(bf16).reshape(blocks, count, width, groups, depth // groups)
    stack = stack.transpose(3, 0, 1, 4, 2).reshape(groups * blocks, count, -1, width)
    part = lax.psum_scatter(stack, REPLICAS, scatter_dimension=0, tiled=True)[0]
    return from_group(part).astype(f32)


def gather_vectors(vectors, *earlier):
    low = vectors.astype(bf16)
    stack = jnp.stack([low] + [rotate(low, "ctx", step) for step in range(1, 4)])
    stack = pair_join(pair_join(after(to_absolute(stack), *earlier), "jc", 3), "jx", 3)
    if lax.axis_size("g") == 2:
        stack = pair_join(stack, "g", 3)
    else:
        stack = lax.all_gather(stack, "g", axis=3, tiled=True)
    return stack.transpose(1, 0, 2, 3).reshape(low.shape[0], -1, D).astype(f32)


def sum_vectors(terms):
    if lax.axis_size("g") == 2:
        terms = terms + lax.ppermute(terms, "g", SWAP)
    else:
        terms = lax.psum(terms, "g")
    layers, rows, width = terms.shape
    blocks = from_own(terms.reshape(layers, 4, rows // 4, width).transpose(1, 0, 2, 3))
    total = blocks[0]
    for step in range(1, 4):
        total = total + rotate(blocks[step], "ctx", -step)
    return total


def sum_group(total):
    total = total + lax.ppermute(total, "jc", SWAP)
    return total + lax.ppermute(total, "jx", SWAP)


def call(kernel, outs, *args, scratch=()):
    return pl.pallas_call(
        kernel,
        out_shape=[jax.ShapeDtypeStruct(shape, kind) for shape, kind in outs],
        in_specs=[pl.BlockSpec(memory_space=pltpu.SMEM)]
        + [pl.BlockSpec(memory_space=pltpu.VMEM)] * (len(args) - 1),
        out_specs=[pl.BlockSpec(memory_space=pltpu.VMEM)] * len(outs),
        scratch_shapes=list(scratch),
        compiler_params=pltpu.CompilerParams(vmem_limit_bytes=52 * 1024 * 1024),
    )(*args)


def block_at(place_ref, step):
    ahead = place_ref[0] + step
    return jnp.where(ahead >= 4, ahead - 4, ahead)


def put_blocks(place_ref, own_refs, other_refs, full_refs):
    half = D // 2
    mine = pl.multiple_of(place_ref[1] * half, half)
    theirs = pl.multiple_of((1 - place_ref[1]) * half, half)
    for step in range(4):
        rows = pl.ds(pl.multiple_of(block_at(place_ref, step) * COLS, COLS), COLS)
        for number, full_ref in enumerate(full_refs):
            own, other = own_refs[step], other_refs[step]
            if len(full_refs) > 1:
                own, other = own.at[number], other.at[number]
            full_ref[rows, pl.ds(mine, half)] = own[...]
            full_ref[rows, pl.ds(theirs, half)] = other[...]


def put_grads(place_ref, grad, mine_refs, give_refs, halves):
    half = D // 2
    for block in range(4):
        rows = grad[block * COLS : (block + 1) * COLS]
        if halves:
            back = block - place_ref[0]
            back = jnp.where(back < 0, back + 4, back)
            low = place_ref[1] == 0
            mine_refs(back)[...] = jnp.where(low, rows[:, :half], rows[:, half:])
            give_refs(back)[...] = jnp.where(low, rows[:, half:], rows[:, :half]).astype(bf16)
        else:
            mine_refs(block)[...] = rows


def norm_rows(hidden):
    center = hidden - jnp.mean(hidden, axis=-1, keepdims=True)
    variance = jnp.mean(center * center, axis=-1, keepdims=True)
    inverse = lax.rsqrt(variance + norm_epsilon)
    return center * inverse, inverse


def norm_stage(vecs, layer, row, hidden, mine=None, recv=None, bias=None):
    rows = hidden.shape[0]

    def kernel(unused, vec_ref, hidden_ref, *refs):
        total = hidden_ref[...]
        if mine is not None:
            mine_ref, recv_ref, total_ref, out_ref = refs
            bias_row = vec_ref[bias[0], bias[1] : bias[1] + 1, :]
            total = total + (mine_ref[...] + recv_ref[...].astype(f32) + bias_row)
            total_ref[...] = total
        else:
            (out_ref,) = refs
        normed, unused_scale = norm_rows(total)
        gain = vec_ref[layer, row : row + 1, :]
        shift = vec_ref[layer, row + 1 : row + 2, :]
        out_ref[...] = (normed * gain + shift).astype(bf16)

    outs = [((rows, D), bf16)]
    args = [hidden]
    if mine is not None:
        outs = [((rows, D), f32)] + outs
        args += [mine, recv]
    return call(kernel, outs, jnp.zeros((1,), jnp.int32), vecs, *args)


def norm_back_stage(vecs, layer, row, grad, mine, recv, hidden):
    rows = hidden.shape[0]

    def kernel(unused, vec_ref, grad_ref, mine_ref, recv_ref, hidden_ref, out_ref, low_ref, sum_ref):
        through = mine_ref[...] + recv_ref[...].astype(f32)
        normed, inverse = norm_rows(hidden_ref[...])
        scaled = through * vec_ref[layer, row : row + 1, :]
        part = jnp.mean(scaled, axis=-1, keepdims=True)
        part = part + normed * jnp.mean(scaled * normed, axis=-1, keepdims=True)
        total = grad_ref[...] + inverse * (scaled - part)
        out_ref[...] = total
        low = total.astype(bf16)
        low_ref[...] = low
        sum_ref[0:1, :] = jnp.sum(through * normed, axis=0, keepdims=True)
        sum_ref[1:2, :] = jnp.sum(through, axis=0, keepdims=True)
        sum_ref[2:3, :] = jnp.sum(low.astype(f32), axis=0, keepdims=True)

    outs = [((rows, D), f32), ((rows, D), bf16), ((8, D), f32)]
    return call(kernel, outs, jnp.zeros((1,), jnp.int32), vecs, grad, mine, recv, hidden)


def both(first_ref, second_ref):
    return jnp.concatenate([first_ref[...], second_ref[...]], axis=0)


def allowed_of(row_ref, column_ref):
    before = row_ref[0:1, :] <= column_ref[:, 0:1]
    return before & (row_ref[1:2, :] == column_ref[:, 1:2])


def attend_stage(place, row_info, column_info, bias, a_own, a_other, weights):
    half = a_own.shape[0]
    tokens = 2 * half
    wide = 3 * COLS
    own, other = weights if isinstance(weights, tuple) else ([], [])

    def kernel(place_ref, row_ref, column_ref, bias_ref, own_a_ref, other_a_ref, *refs):
        if own:
            own_refs, refs = refs[:4], refs[4:]
            others, refs = refs[: len(other)], refs[len(other) :]
            if len(other) == 1:
                others = [others[0].at[step] for step in range(4)]
            w_ref, qkv_ref, lse_ref, o_ref, mine_ref, give_ref = refs
            put_blocks(place_ref, own_refs, others, [w_ref])
        else:
            w_ref, qkv_ref, lse_ref, o_ref, mine_ref, give_ref = refs
        for start, a_ref in ((0, own_a_ref), (half, other_a_ref)):
            proj = dot_trans(a_ref[...], w_ref[0:wide, :]) + bias_ref[0:1, :]
            qkv_ref[start : start + half, :] = proj.astype(bf16)
        allowed = allowed_of(row_ref, column_ref)
        for head in range(TP_HEADS):
            lanes = head * HEAD
            k = qkv_ref[:, COLS + lanes : COLS + lanes + HEAD]
            v = qkv_ref[:, 2 * COLS + lanes : 2 * COLS + lanes + HEAD]
            for start in (0, half):
                rows = slice(start, start + half)
                q = qkv_ref[rows, lanes : lanes + HEAD]
                scores = jnp.where(allowed[rows], dot_trans(q, k) * HEAD ** (-0.5), masked_score)
                top = jnp.max(scores, axis=-1, keepdims=True)
                unnormed = jnp.exp(scores - top)
                total = jnp.sum(unnormed, axis=-1, keepdims=True)
                prob = (unnormed * (1.0 / total)).astype(bf16)
                o_ref[rows, lanes : lanes + HEAD] = dot(prob, v).astype(bf16)
                lse_ref[rows, head : head + 1] = top + jnp.log(total)
        mine_ref[...] = dot(o_ref[0:half, :], w_ref[wide:, :])
        give_ref[...] = dot(o_ref[half:, :], w_ref[wide:, :]).astype(bf16)

    outs = [
        ((tokens, wide), bf16),
        ((tokens, 128), f32),
        ((tokens, COLS), bf16),
        ((half, D), f32),
        ((half, D), bf16),
    ]
    if own:
        outs = [((D, D), bf16)] + outs
        return call(
            kernel, outs, place, row_info, column_info, bias, a_own, a_other, *own, *other
        )
    result = call(kernel, outs, place, row_info, column_info, bias, a_own, a_other, weights)
    return [weights] + list(result)


def attend_back_stage(
    place, row_info, column_info, gb_own, gb_other, a_own, a_other, qkv, lse, o, w_attn, halves
):
    half = a_own.shape[0]
    tokens = 2 * half
    wide = 3 * COLS

    def kernel(
        place_ref,
        row_ref,
        column_ref,
        own_gb_ref,
        other_gb_ref,
        own_a_ref,
        other_a_ref,
        qkv_ref,
        lse_ref,
        o_ref,
        w_ref,
        mine_ref,
        give_ref,
        sum_ref,
        *refs,
    ):
        *grad_refs, go_ref, all_ref = refs
        w_o = w_ref[wide:, :]
        for start, gb_ref in ((0, own_gb_ref), (half, other_gb_ref)):
            go_ref[start : start + half, :] = dot_trans(gb_ref[...], w_o).astype(bf16)
        allowed = allowed_of(row_ref, column_ref)
        for head in range(TP_HEADS):
            lanes = head * HEAD
            q_lanes = slice(lanes, lanes + HEAD)
            k_lanes = slice(COLS + lanes, COLS + lanes + HEAD)
            v_lanes = slice(2 * COLS + lanes, 2 * COLS + lanes + HEAD)
            k = qkv_ref[:, k_lanes]
            v = qkv_ref[:, v_lanes]
            gk = jnp.zeros((tokens, HEAD), f32)
            gv = jnp.zeros((tokens, HEAD), f32)
            for start in (0, half):
                rows = slice(start, start + half)
                q = qkv_ref[rows, q_lanes]
                go = go_ref[rows, q_lanes]
                scores = jnp.where(allowed[rows], dot_trans(q, k) * HEAD ** (-0.5), masked_score)
                prob = jnp.exp(scores - lse_ref[rows, head : head + 1])
                g_prob = dot_trans(go, v)
                row_dot = jnp.sum(g_prob * prob, axis=-1, keepdims=True)
                g_scores = (prob * (g_prob - row_dot)).astype(bf16)
                all_ref[rows, q_lanes] = (dot(g_scores, k) * HEAD ** (-0.5)).astype(bf16)
                gk = gk + dot_tokens(g_scores, q)
                gv = gv + dot_tokens(prob.astype(bf16), go)
            all_ref[:, k_lanes] = (gk * HEAD ** (-0.5)).astype(bf16)
            all_ref[:, v_lanes] = gv.astype(bf16)
        mine_ref[...] = dot(all_ref[0:half, :], w_ref[0:wide, :])
        give_ref[...] = dot(all_ref[half:, :], w_ref[0:wide, :]).astype(bf16)
        sum_ref[0:1, :] = jnp.sum(all_ref[...].astype(f32), axis=0, keepdims=True)
        grad = jnp.concatenate(
            [
                dot_tokens(all_ref[...], both(own_a_ref, other_a_ref)),
                dot_tokens(o_ref[...], both(own_gb_ref, other_gb_ref)),
            ],
            axis=0,
        )
        put_grads(
            place_ref,
            grad,
            lambda block: grad_refs[0].at[block],
            lambda block: grad_refs[1].at[block],
            halves,
        )

    width = D // 2 if halves else D
    outs = [((half, D), f32), ((half, D), bf16), ((8, wide), f32), ((4, COLS, width), f32)]
    if halves:
        outs.append(((4, COLS, width), bf16))
    return call(
        kernel,
        outs,
        place,
        row_info,
        column_info,
        gb_own,
        gb_other,
        a_own,
        a_other,
        qkv,
        lse,
        o,
        w_attn,
        scratch=[pltpu.VMEM((tokens, COLS), bf16), pltpu.VMEM((tokens, wide), bf16)],
    )


def tanh_part(preact):
    inner = math.sqrt(2.0 / math.pi) * (preact + 0.044715 * (preact * preact * preact))
    return jnp.tanh(inner)


def feed_stage(place, bias, c_own, c_other, weights):
    half = c_own.shape[0]
    own, other = weights if isinstance(weights, tuple) else ([], [])

    def kernel(place_ref, bias_ref, own_c_ref, other_c_ref, *refs):
        if own:
            own_refs, (first, last), refs = refs[:4], refs[4:6], refs[6:]
            others = [first.at[0], first.at[1], last, first.at[2]]
            w_ref, preact_ref, act_ref, mine_ref, give_ref = refs
            put_blocks(place_ref, own_refs, others, [w_ref.at[0], w_ref.at[1]])
        else:
            w_ref, preact_ref, act_ref, mine_ref, give_ref = refs
        for start, c_ref, out_ref in ((0, own_c_ref, mine_ref), (half, other_c_ref, give_ref)):
            rows = slice(start, start + half)
            preact = dot_trans(c_ref[...], w_ref[0]) + bias_ref[...]
            preact_ref[rows, :] = preact
            act = (0.5 * preact * (1.0 + tanh_part(preact))).astype(bf16)
            act_ref[rows, :] = act
            out_ref[...] = dot(act, w_ref[1]).astype(out_ref.dtype)

    outs = [
        ((2 * half, D), f32),
        ((2 * half, D), bf16),
        ((half, D), f32),
        ((half, D), bf16),
    ]
    if own:
        outs = [((2, D, D), bf16)] + outs
        return call(kernel, outs, place, bias, c_own, c_other, *own, *other)
    return [weights] + list(call(kernel, outs, place, bias, c_own, c_other, weights))


def feed_back_stage(place, gy_own, gy_other, c_own, c_other, preact, act, weights, halves):
    half = c_own.shape[0]

    def kernel(
        place_ref,
        own_gy_ref,
        other_gy_ref,
        own_c_ref,
        other_c_ref,
        preact_ref,
        act_ref,
        w_ref,
        mine_ref,
        give_ref,
        sum_ref,
        *refs,
    ):
        *grad_refs, gz_ref = refs
        up_sum = jnp.zeros((1, D), f32)
        for start, gy_ref, out_ref in ((0, own_gy_ref, mine_ref), (half, other_gy_ref, give_ref)):
            rows = slice(start, start + half)
            gu = dot_trans(gy_ref[...], w_ref[1])
            x = preact_ref[rows, :]
            tanh = tanh_part(x)
            slope = math.sqrt(2.0 / math.pi) * (1.0 + 3.0 * 0.044715 * (x * x))
            factor = 0.5 * (1.0 + tanh) + 0.5 * x * (1.0 - tanh * tanh) * slope
            gz = (gu * factor).astype(bf16)
            gz_ref[rows, :] = gz
            up_sum = up_sum + jnp.sum(gz.astype(f32), axis=0, keepdims=True)
            out_ref[...] = dot(gz, w_ref[0]).astype(out_ref.dtype)
        sum_ref[0:1, :] = up_sum
        sum_ref[1:2, :] = jnp.sum(own_gy_ref[...].astype(f32), axis=0, keepdims=True)
        for number, left_ref, rights in (
            (0, gz_ref, (own_c_ref, other_c_ref)),
            (1, act_ref, (own_gy_ref, other_gy_ref)),
        ):
            put_grads(
                place_ref,
                dot_tokens(left_ref[...], both(*rights)),
                lambda block: grad_refs[0].at[block, number],
                lambda block: grad_refs[1].at[block, number],
                halves,
            )

    width = D // 2 if halves else D
    outs = [((half, D), f32), ((half, D), bf16), ((8, D), f32), ((4, 2, COLS, width), f32)]
    if halves:
        outs.append(((4, 2, COLS, width), bf16))
    return call(
        kernel,
        outs,
        place,
        gy_own,
        gy_other,
        c_own,
        c_other,
        preact,
        act,
        weights,
        scratch=[pltpu.VMEM((2 * half, D), bf16)],
    )


def core_swap(block):
    return lax.ppermute(block, "jc", SWAP)


def group_sum(mine, give):
    mine = mine + core_swap(give).astype(f32)
    return mine, lax.ppermute(mine.astype(bf16), "jx", SWAP)


def polynomial(base_ref, low_ref, mat_ref):
    low_ref[...] = base_ref[...].astype(bf16)
    for start in range(0, base_ref.shape[0], ROWS):
        block = pl.ds(start, ROWS)
        square = dot(low_ref[block, :], low_ref[...])
        mat_ref[block, :] = (quintic_two * base_ref[block, :] + quintic_three * square).astype(bf16)


def two_part(left, right):
    high = left.astype(bf16)
    rest = (left - high.astype(f32)).astype(bf16)
    return dot(high, right) + dot(rest, right)


def iterate(x_ref, out_ref, base_ref, work_ref, mat_ref, low_ref):
    size = x_ref.shape[0]
    blocks = [pl.ds(start, ROWS) for start in range(0, size, ROWS)]
    trace = jnp.zeros((1, 1), f32)
    line = lax.broadcasted_iota(jnp.int32, (ROWS, ROWS), 0)
    column = lax.broadcasted_iota(jnp.int32, (ROWS, ROWS), 1)
    for block in blocks:
        part = jnp.where(line == column, base_ref[block, block], 0.0)
        trace = trace + jnp.sum(part, keepdims=True)
    scale = 1.0 / (jnp.sqrt(trace) + 1e-07)
    base_ref[...] = base_ref[...] * (scale * scale)
    polynomial(base_ref, low_ref, mat_ref)

    for block in blocks:
        value = quintic_one * x_ref[block, :].astype(f32) + dot(x_ref[block, :], mat_ref[...])
        out_ref[block, :] = (scale * value).astype(bf16)
        work_ref[block, :] = quintic_one * base_ref[block, :] + two_part(
            base_ref[block, :], mat_ref[...]
        )
    turned = work_ref[...].T
    work_ref[...] = turned
    for block in blocks:
        base_ref[block, :] = quintic_one * work_ref[block, :] + two_part(
            work_ref[block, :], mat_ref[...]
        )
    polynomial(base_ref, low_ref, mat_ref)
    for block in blocks:
        x = out_ref[block, :]
        out_ref[block, :] = (quintic_one * x.astype(f32) + dot(x, mat_ref[...])).astype(bf16)


def orthogonalize(matrix, gram):
    size = matrix.shape[0]

    def kernel(unused, x_ref, gram_ref, out_ref, in_ref, base_ref, work_ref, mat_ref, low_ref):
        in_ref[...] = x_ref[...].T
        base_ref[...] = gram_ref[...]
        iterate(in_ref, out_ref, base_ref, work_ref, mat_ref, low_ref)
        out_ref[...] = out_ref[...].T

    return call(
        kernel,
        [((size, size), bf16)],
        jnp.zeros((1,), jnp.int32),
        matrix,
        gram,
        scratch=[pltpu.VMEM((size, size), kind) for kind in (bf16, f32, f32, bf16, bf16)],
    )[0]


def put_slots(slot_ref, x_ref):
    half = D // 2
    for source in range(8):
        group, number = source // TP, source % TP
        x_ref[number * COLS : (number + 1) * COLS, group * half : (group + 1) * half] = slot_ref[
            source
        ]


def slot_input(place_ref, slot_ref, moment_ref, sum_ref, x_ref, turned):
    put_slots(slot_ref, sum_ref)
    moment = moment_ref[...].astype(f32) * (momentum_decay * momentum_decay)
    if turned:
        moment = moment.T
    x_ref[...] = (sum_ref[...].astype(f32) * (1.0 + momentum_decay) + moment).astype(bf16)


def slot_gram(place, slots, moments):
    def kernel(place_ref, slot_ref, moment_ref, x_ref, gram_ref, sum_ref):
        slot_input(place_ref, slot_ref, moment_ref, sum_ref, x_ref, True)
        half = D // 2
        for part in range(2):
            rows = dot_tokens(x_ref[:, part * half : (part + 1) * half], x_ref[...]).astype(bf16)
            for number in range(2):
                back = 2 * part + number - place_ref[0]
                back = jnp.where(back < 0, back + 4, back)
                gram_ref[back] = rows[number * COLS : (number + 1) * COLS]

    return call(
        kernel,
        [((D, D), bf16), ((4, COLS, D), bf16)],
        place,
        slots,
        moments,
        scratch=[pltpu.VMEM((D, D), bf16)],
    )


def slot_orthogonalize(place, x_wide, grams, square_slots, moments):
    def kernel(
        place_ref,
        wide_ref,
        gram0_ref,
        gram1_ref,
        gram2_ref,
        gram3_ref,
        slot_ref,
        moment_ref,
        out_ref,
        x_ref,
        base_ref,
        work_ref,
        mat_ref,
        low_ref,
    ):
        core = place_ref[2]
        plain = (core == 1) & (place_ref[0] == 3)

        @pl.when(core == 0)
        def wide():
            x_ref[...] = wide_ref[...]
            for step, gram_ref in enumerate((gram0_ref, gram1_ref, gram2_ref, gram3_ref)):
                rows = pl.ds(pl.multiple_of(block_at(place_ref, step) * COLS, COLS), COLS)
                base_ref[rows, :] = gram_ref[...].astype(f32)

        @pl.when(plain)
        def square_plain():
            slot_input(place_ref, slot_ref, moment_ref, low_ref, x_ref, False)

        @pl.when((core == 1) & jnp.logical_not(plain))
        def square_turned():
            slot_input(place_ref, slot_ref, moment_ref, low_ref, x_ref, True)

        @pl.when(core == 1)
        def square():
            base_ref[...] = dot_tokens(x_ref[...], x_ref[...])

        iterate(x_ref, out_ref, base_ref, work_ref, mat_ref, low_ref)

        @pl.when(jnp.logical_not(plain))
        def turn():
            out_ref[...] = out_ref[...].T

    return call(
        kernel,
        [((D, D), bf16)],
        place,
        x_wide,
        *grams,
        square_slots,
        moments,
        scratch=[pltpu.VMEM((D, D), kind) for kind in (bf16, f32, f32, bf16, bf16)],
    )[0]


def slot_exchange(blocks):
    return lax.all_to_all(blocks, DP, split_axis=0, concat_axis=0, tiled=True)


def core_shift(block, step):
    size = lax.axis_size("ctx")
    return lax.ppermute(block, ("jc", "ctx"), [((i + step) % size, i) for i in range(size)])


def ctx_gram(gram):
    size = lax.axis_size("ctx")
    blocks = from_own(gram.astype(bf16).reshape(size, gram.shape[0] // size, -1))
    total = blocks[0].astype(f32)
    for step in (1, 3, 2):
        total = total + core_shift(blocks[step], -step).astype(f32)
    low = total.astype(bf16)
    full = [low] + [core_shift(low, step) for step in range(1, size)]
    return to_absolute(jnp.stack(full)).reshape(gram.shape).astype(f32)


def local(hidden_in, segments, out_grad, weights, vectors, mat_momentum, vec_first, vec_second):
    tokens_dev = hidden_in.shape[1]
    seq_len = segments.shape[1]
    half = 2 * tokens_dev
    dp_rows = weights.shape[2]
    ctx_size = lax.axis_size("ctx")
    x_index = lax.axis_index("jx")
    c_index = lax.axis_index("jc")
    t_index = 2 * x_index + c_index
    z_index = lax.axis_index("ctx")
    dp_index = lax.axis_index(DP)
    dp_size = lax.axis_size(DP)

    to_seq = []
    for t in range(TP):
        for z in range(ctx_size):
            to_seq.append((t * ctx_size + z, ((z % 2) * 2 + z // 2) * ctx_size + t))
    from_seq = [(b, a) for a, b in to_seq]
    axes = ("jx", "jc", "ctx")

    def x_join(block):
        return pair_join(block, "jx", 0)

    seg_row = jnp.pad(segments.astype(f32), ((0, 7), (0, D - seq_len)))
    moved = lax.ppermute(jnp.concatenate([hidden_in[0], seg_row], axis=0), axes, to_seq)
    segment_row = moved[tokens_dev, :seq_len]
    relative = lax.axis_size("g") == 2
    place = jnp.stack([z_index, lax.axis_index("g"), c_index]).astype(jnp.int32)
    if relative:
        piece, outs = first_piece(place, weights)
        own_attn = ctx_gather(piece)
        attn_weights = (own_attn, group_swap(own_attn))
        pieces = other_pieces(place, weights, outs, own_attn[1])
        near_blocks = ctx_near(pieces[0:2], *own_attn[1:])
        far = ctx_far(*near_blocks)
        first = group_first(*near_blocks)
    else:
        wide_weights = gather_weights_wide(weights.astype(bf16))
        outs = piece = place
    vec_rows = gather_vectors(vectors, outs)
    hidden = x_join(after(moved[:tokens_dev], piece))

    start = c_index * half
    pos = jnp.concatenate([start + jnp.arange(half), half - start + jnp.arange(half)])
    seg = jnp.roll(segment_row.reshape(2, half), -c_index, axis=0).reshape(-1)
    info = jnp.stack([pos.astype(f32), seg])
    row_info = jnp.pad(info, ((0, 6), (0, 0)))
    column_info = jnp.pad(info.T, ((0, 0), (0, 126)))
    vec_mine = lax.dynamic_slice_in_dim(vec_rows, t_index * COLS, COLS, axis=2)
    no_bias = jnp.zeros((LAYERS, 1, COLS), f32)
    qkv_bias = jnp.concatenate([vec_mine[:, 4:5], no_bias, vec_mine[:, 5:6]], axis=2)
    up_bias = vec_mine[:, 8:12].reshape(LAYERS, 1, D)

    stored = []
    (a_own,) = norm_stage(vec_rows, 0, 0, hidden)
    for layer in range(LAYERS):
        following = layer + 1 < LAYERS
        a_other = core_swap(a_own)
        if not relative:
            attn_weights, mlp_weights = wide_weights[layer]
        w_attn, qkv, lse, o, mine, give = attend_stage(
            place, row_info, column_info, qkv_bias[layer], a_own, a_other, attn_weights
        )
        if relative and not following:
            mine, gy_own = lax.optimization_barrier((mine, gy_own))
            moved_grad = lax.ppermute(after(out_grad[0], far), axes, to_seq)
        mine, recv = group_sum(mine, give)
        middle, c_own = norm_stage(vec_rows, layer, 2, hidden, mine, recv, (layer, 6))
        if relative:
            last = lax.ppermute(after(far, first), "g", SWAP)
            mlp_weights = ([near_blocks[0], near_blocks[1], far, near_blocks[2]], [first, last])
        c_other = core_swap(c_own)
        if relative and following:
            base = 3 * layer + 2
            own_attn = ctx_gather(pieces[base], far)
            c_other, own_attn = lax.optimization_barrier((c_other, own_attn))
        w_mlp, preact, act, mine, give = feed_stage(
            place, up_bias[layer], c_own, c_other, mlp_weights
        )
        if relative and following:
            attn_weights = (own_attn, [lax.ppermute(jnp.stack(own_attn), "g", SWAP)])
            near_blocks = ctx_near(pieces[base + 1 : base + 3], *own_attn[1:])
            moved_low = lax.ppermute(after(out_grad[0].astype(bf16), own_attn[2]), axes, to_seq)
        if following:
            mine, recv = group_sum(mine, give)
        stored.append(
            (hidden, middle, a_own, a_other, qkv, lse, o, c_own, c_other, preact, act, w_attn, w_mlp)
        )
        if following:
            hidden, a_own = norm_stage(vec_rows, layer + 1, 0, middle, mine, recv, (layer, 7))
            if relative:
                a_own, near_blocks, moved_low = lax.optimization_barrier(
                    (a_own, near_blocks, moved_low)
                )
                far = ctx_far(*near_blocks)
                first = group_first(*near_blocks)
                gy_own = x_join(moved_low)

    def send_back(rows):
        block = lax.dynamic_slice_in_dim(rows, x_index * tokens_dev, tokens_dev, axis=0)
        return lax.ppermute(block, axes, from_seq)

    last_sum = (mine, give)

    def last_hidden(*earlier):
        mine, recv = group_sum(last_sum[0], after(last_sum[1], *earlier))
        return stored[-1][1] + (mine + recv.astype(f32) + vec_rows[LAYERS - 1, 7:8])

    if not relative:
        grad_hidden = x_join(lax.ppermute(out_grad[0], axes, to_seq))
        hidden_out = send_back(last_hidden())
        gy_own = grad_hidden.astype(bf16)
    attn_half = None

    mat_list = [None] * LAYERS
    sum_list = [None] * LAYERS
    parts = [None] * LAYERS
    for layer in reversed(range(LAYERS)):
        h_in, middle, a_own, a_other, qkv, lse, o, c_own, c_other, preact, act, w_attn, w_mlp = stored[
            layer
        ]
        if relative and attn_half is not None:
            gy_own, attn_half = lax.optimization_barrier((gy_own, attn_half))
            hidden = last_hidden(gy_own)
            attn_part = ctx_sum(attn_half)
        gy_other = core_swap(gy_own)
        if relative and attn_half is None:
            gy_other, moved_grad = lax.optimization_barrier((gy_other, moved_grad))
            grad_hidden = x_join(moved_grad)
        mine, give, up_sums, *mlp_grads = feed_back_stage(
            place, gy_own, gy_other, c_own, c_other, preact, act, w_mlp, relative
        )
        if relative:
            mlp_mine, mlp_give = mlp_grads
            mlp_recv = lax.ppermute(mlp_give, "g", SWAP)
            if attn_half is None:
                mine, grad_hidden = lax.optimization_barrier((mine, grad_hidden))
            else:
                mine, hidden, attn_part = lax.optimization_barrier((mine, hidden, attn_part))
                wide_part = ctx_sum(late_half[0] + after(late_half[1], mine).astype(f32))
        mine, recv = group_sum(mine, give)
        grad_middle, gb_own, mid_sums = norm_back_stage(
            vec_rows, layer, 2, grad_hidden, mine, recv, middle
        )
        if relative and layer == LAYERS - 1:
            moment_low = mat_momentum.astype(bf16)
            table = [(1, 1), (1, 0), (1, 2), (0, 0), (0, 1), (1, 0), (0, 2), (0, 0)]
            moment_slots = slot_exchange(
                after(jnp.stack([moment_low[slot] for slot in table]), gb_own)
            ).reshape(D, D)
        gb_other = core_swap(gb_own)
        if relative and layer < LAYERS - 1:
            gb_other, wide_part = lax.optimization_barrier((gb_other, wide_part))
        mine, give, qkv_sums, *attn_grads = attend_back_stage(
            place,
            row_info,
            column_info,
            gb_own,
            gb_other,
            a_own,
            a_other,
            qkv,
            lse,
            o,
            w_attn,
            relative,
        )
        if relative:
            if layer == LAYERS - 1:
                mine, moment_slots = lax.optimization_barrier((mine, moment_slots))
                late_half = (mlp_mine, mlp_recv)
            else:
                parts[layer + 1] = (attn_part, wide_part)
                mlp_half = mlp_mine + after(mlp_recv, give).astype(f32)
                mlp_part = ctx_sum(mlp_half)
            attn_half = half_sum(*attn_grads)
        else:
            attn_grad = attn_grads[0]
            g_wo = lax.all_to_all(
                attn_grad[3].reshape(COLS, TP, COLS), GROUP, split_axis=1, concat_axis=0, tiled=True
            )[:, 0]
            attn_grad = jnp.concatenate([attn_grad[:3], g_wo.T[None]], axis=0)
            mat_list[layer] = scatter_wide(
                jnp.concatenate([attn_grad[:, None], mlp_grads[0]], axis=1)
            )
        mine, recv = group_sum(mine, give)
        grad_hidden, gy_own, in_sums = norm_back_stage(
            vec_rows, layer, 0, grad_middle, mine, recv, h_in
        )
        sum_list[layer] = (in_sums, mid_sums, up_sums, qkv_sums)
    if not relative:
        input_grad = send_back(grad_hidden)

    once = jnp.where(x_index == 0, 1.0, 0.0).astype(f32)
    in_sums, mid_sums, up_sums, qkv_sums = [jnp.stack(sums) for sums in zip(*sum_list)]
    shared = once * jnp.concatenate(
        [in_sums[:, 0:2], mid_sums[:, 0:3], up_sums[:, 1:2]], axis=1
    )
    placed = jnp.concatenate(
        [
            qkv_sums[:, 0:1, :COLS],
            qkv_sums[:, 0:1, 2 * COLS :],
            up_sums[:, 0].reshape(LAYERS, ctx_size, COLS),
        ],
        axis=1,
    )
    placed = lax.dynamic_update_slice_in_dim(
        jnp.zeros((LAYERS, 6, D), f32), placed, t_index * COLS, axis=2
    )
    vec_terms = jnp.concatenate(
        [shared[:, 0:4], placed[:, 0:2], shared[:, 4:6], placed[:, 2:6]], axis=1
    )
    if relative:
        attn_low = attn_half.astype(bf16)
        attn_sums = [rotate(attn_low[step], "ctx", -step) for step in (1, 3, 2)]
        wide_low = jnp.concatenate([parts[1][1], mlp_part]).astype(bf16)
        wide_low = after(wide_low, attn_half)
        wide_slots = slot_exchange(jnp.repeat(wide_low, 2, axis=0))
        wide_slots, grad_hidden, attn_sums = lax.optimization_barrier(
            (wide_slots, grad_hidden, attn_sums)
        )
        x_wide, gram_blocks = slot_gram(place, wide_slots, moment_slots)
        vec_sums = sum_group(sum_vectors(after(vec_terms, gram_blocks)))
        attn_part = attn_half[0] + sum(block.astype(f32) for block in attn_sums)
        total = gram_blocks[0].astype(f32)
        for step in (1, 3, 2):
            total = total + core_shift(gram_blocks[step], -step).astype(f32)
        gram_low = total.astype(bf16)
        square_low, vec_sums, unused = lax.optimization_barrier(
            (jnp.stack([parts[1][0], attn_part]).astype(bf16), vec_sums, gram_low)
        )
        square_slots = slot_exchange(jnp.tile(jnp.repeat(square_low, 2, axis=0), (2, 1, 1)))
        near, back, far = [core_shift(gram_low, step) for step in (1, 3, 2)]
        ortho_mine = slot_orthogonalize(
            place, x_wide, (gram_low, near, far, back), square_slots, moment_slots
        )
        blocks, outs = grad_blocks(
            [attn_part, parts[1][0]], [mlp_part, parts[1][1]], dp_rows, square_slots, near, back, far
        )
        returned = slot_exchange(ortho_mine.reshape(dp_size, dp_rows, D))
        ends = jnp.stack([hidden, grad_hidden])
        ends = lax.dynamic_slice_in_dim(ends, x_index * tokens_dev, tokens_dev, axis=1)
        hidden_out, input_grad = lax.ppermute(after(ends, near, back, far), axes, from_seq)
        ortho = jnp.stack([returned[slot] for slot in (3, 4, 6, 1, 0, 2)])
        ortho = ortho.reshape(weights.shape).astype(f32)
        grad_mats, moment_new = grad_rows(place, blocks, outs, mat_momentum)
    else:
        vec_sums = sum_group(sum_vectors(vec_terms))
        cols_dev = weights.shape[3]
        grad_list, moment_list, low_list = [], [], []
        for layer in range(LAYERS):
            for item in range(3):
                grad = mat_list[layer][item]
                moment = momentum_decay * mat_momentum[layer, item] + grad
                grad_list.append(grad)
                moment_list.append(moment)
                low_list.append((grad + momentum_decay * moment).astype(bf16))
        wide = [item for item in range(3 * LAYERS) if item % 3]
        squares = [item for item in range(3, 3 * LAYERS, 3)]
        table = []
        for number in range(4):
            table += [wide[number], squares[number % len(squares)]]
        table = (table * (-(-dp_size // 8)))[:dp_size]
        slots = jnp.stack([low_list[item] for item in table])
        received = lax.all_to_all(slots[:, None], DP, split_axis=0, concat_axis=1, tiled=True)
        current = received.reshape(dp_size * dp_rows, cols_dev)
        gram_local = dot_trans(current, current)
        gram = jnp.where(c_index == 0, ctx_gram(gram_local), gram_local)
        ortho_mine = orthogonalize(current, gram)
        returned = lax.all_to_all(
            ortho_mine.reshape(dp_size, 1, dp_rows, cols_dev),
            DP,
            split_axis=0,
            concat_axis=1,
            tiled=True,
        )[0]
        first_full = lax.all_gather(low_list[0], DP, axis=0, tiled=True)
        first_ortho = orthogonalize(first_full, dot_trans(first_full, first_full))
        ortho_list = [lax.dynamic_slice_in_dim(first_ortho, dp_index * dp_rows, dp_rows, axis=0)]
        ortho_list += [returned[table.index(item)] for item in range(1, 3 * LAYERS)]
        ortho = jnp.stack(ortho_list).reshape(LAYERS, 3, dp_rows, cols_dev).astype(f32)
        grad_mats = jnp.stack(grad_list).reshape(weights.shape)
        moment_new = jnp.stack(moment_list).reshape(weights.shape)
    grad_vecs = lax.dynamic_slice_in_dim(
        vec_sums, dp_index * vectors.shape[2], vectors.shape[2], axis=2
    )
    factor = jnp.array([0.2 * math.sqrt(D), 0.2 * math.sqrt(FF), 0.2 * math.sqrt(FF)], f32)
    weights_new = weights * (1.0 - matrix_rate * matrix_decay) - matrix_rate * (
        ortho * factor[None, :, None, None]
    )
    first_new = first_decay * vec_first + (1.0 - first_decay) * grad_vecs
    second_new = second_decay * vec_second + (1.0 - second_decay) * grad_vecs * grad_vecs
    first_hat = first_new / (1.0 - first_decay**ADAM_STEP)
    second_hat = second_new / (1.0 - second_decay**ADAM_STEP)
    vectors_new = vectors * (1.0 - vector_rate * vector_decay) - vector_rate * first_hat / (
        jnp.sqrt(second_hat) + adam_epsilon
    )
    return (
        hidden_out[None],
        input_grad[None],
        grad_mats,
        moment_new,
        weights_new,
        grad_vecs,
        second_new,
        vectors_new,
    )


def solution(mesh):
    dp, ctx = mesh.shape["dp"], mesh.shape["ctx"]
    fine = Mesh(mesh.devices.reshape(dp // TP, 2, 2, ctx), EVERY)
    tokens = P(DP, "ctx", None)
    mats = P(None, None, DP, "ctx")
    vecs = P(None, "ctx", DP)
    return jax.shard_map(
        local,
        mesh=fine,
        in_specs=(tokens, P(DP, None), tokens, mats, vecs, mats, vecs, vecs),
        out_specs=(tokens, tokens, mats, mats, mats, vecs, vecs, vecs),
        check_vma=False,
    )
```

```python
import math

import jax
import jax.numpy as jnp
from jax import lax
from jax.experimental import pallas as pl
from jax.experimental.pallas import tpu as pltpu
from jax.sharding import Mesh, PartitionSpec as P

D = 768
HEADS = 12
HEAD = 64
FF = 3072
LAYERS = 2
ADAM_STEP = 10
TP = 4
COLS = D // TP
TP_HEADS = HEADS // TP
ROWS = 256

norm_epsilon = 1e-05
quintic_one = 3.4445
quintic_two = -4.775
quintic_three = 2.0315
momentum_decay = 0.95
matrix_rate = 0.6
matrix_decay = 0.01
first_decay = 0.9
second_decay = 0.999
vector_rate = 0.5
vector_decay = 0.01
adam_epsilon = 1e-08
masked_score = -1e30

GROUP = ("jx", "jc")
REPLICAS = ("g", "ctx")
DP = ("g", "jx", "jc")
EVERY = ("g", "jx", "jc", "ctx")
SWAP = [(0, 1), (1, 0)]
bf16 = jnp.bfloat16
f32 = jnp.float32


def dot(operand, other):
    return jnp.dot(operand, other, preferred_element_type=f32)


def dot_tokens(operand, other):
    return lax.dot_general(operand, other, (((0,), (0,)), ((), ())), preferred_element_type=f32)


def dot_trans(operand, other):
    return lax.dot_general(operand, other, (((1,), (1,)), ((), ())), preferred_element_type=f32)


def to_group(mats):
    count, rows, width = mats.shape
    split = mats.reshape(count, rows, TP, width // TP)
    return lax.all_to_all(split, GROUP, split_axis=2, concat_axis=1, tiled=True)[:, :, 0]


def from_group(mats):
    count, rows, width = mats.shape
    split = mats.reshape(count, TP, rows // TP, width)
    return lax.all_to_all(split, GROUP, split_axis=1, concat_axis=3, tiled=True)[:, 0]


def rotate(block, axis, step):
    size = lax.axis_size(axis)
    return lax.ppermute(block, axis, [((i + step) % size, i) for i in range(size)])


def pair_join(block, axis, dim):
    other = lax.ppermute(block, axis, SWAP)
    first = lax.axis_index(axis) == 0
    return jnp.concatenate(
        [jnp.where(first, block, other), jnp.where(first, other, block)], axis=dim
    )


def after(value, *others):
    return lax.optimization_barrier((value, *others))[0]


def roll_blocks(stack, sign):
    place = lax.axis_index("ctx")
    for bit in (1, 2):
        moved = jnp.roll(stack, sign * bit, axis=0)
        stack = jnp.where((place & bit) != 0, moved, stack)
    return stack


def from_own(stack):
    return roll_blocks(stack, -1)


def to_absolute(stack):
    return roll_blocks(stack, 1)


def out_moves():
    last = lax.axis_size("ctx") - 1
    size = last + 1
    moves = []
    for y in range(2):
        for x in range(2):
            for core in range(2):
                moves.append(
                    ((4 * y + 2 * x + core) * size + last, (4 * core + 2 * y + x) * size + last)
                )
    return moves


def out_pieces(mats):
    half = mats.shape[2] // 2
    core = lax.axis_index("jc")
    mine = lax.dynamic_slice_in_dim(mats, core * half, half, axis=2)
    give = lax.dynamic_slice_in_dim(mats, (1 - core) * half, half, axis=2)
    got = lax.ppermute(give, "jc", SWAP)
    rows = jnp.concatenate(
        [jnp.where(core == 0, mine, got), jnp.where(core == 0, got, mine)], axis=1
    )
    return lax.ppermute(rows, EVERY, out_moves())


def out_back(pieces):
    core = lax.axis_index("jc")
    rows = lax.ppermute(pieces, EVERY, [(b, a) for a, b in out_moves()])
    half = rows.shape[1] // 2
    mine = lax.dynamic_slice_in_dim(rows, core * half, half, axis=1)
    give = lax.dynamic_slice_in_dim(rows, (1 - core) * half, half, axis=1)
    got = lax.ppermute(give, "jc", SWAP)
    return jnp.concatenate(
        [jnp.where(core == 0, mine, got), jnp.where(core == 0, got, mine)], axis=2
    )


def last_block():
    return lax.axis_index("ctx") == lax.axis_size("ctx") - 1


def split_columns(mats, items):
    rows = mats.shape[2]

    def kernel(unused, mats_ref, out_ref):
        for number, (layer, item) in enumerate(items):
            turned = mats_ref[layer, item].T.astype(bf16)
            for quarter in range(TP):
                out_ref[quarter, number] = turned[quarter * COLS : (quarter + 1) * COLS]

    outs = [((TP, len(items), COLS, rows), bf16)]
    return call(kernel, outs, jnp.zeros((1,), jnp.int32), mats)[0]


def join_columns(place, blocks, outs, items):
    rows = blocks.shape[3]

    def kernel(place_ref, blocks_ref, outs_ref, *out_refs):
        for number, (layer, item) in enumerate(items):
            for source in range(TP):
                lanes = slice(source * rows, (source + 1) * rows)
                out_refs[number][:, lanes] = blocks_ref[source, number]
            if item == 0:

                @pl.when(place_ref[0] == 3)
                def last(number=number, layer=layer):
                    out_refs[number][...] = outs_ref[layer]

    shapes = [((COLS, TP * rows), bf16)] * len(items)
    return call(kernel, shapes, place, blocks, outs)


def group_exchange(blocks):
    return lax.all_to_all(blocks, GROUP, split_axis=0, concat_axis=0, tiled=True)


def first_piece(place, mats):
    outs = out_pieces(mats[:, 0].astype(bf16))
    blocks = group_exchange(split_columns(mats, [(0, 0)]))
    return join_columns(place, blocks, outs, [(0, 0)])[0], outs


def other_pieces(place, mats, outs, *earlier):
    items = [(layer, item) for layer in range(mats.shape[0]) for item in range(3)][1:]
    blocks = group_exchange(split_columns(after(mats, *earlier), items))
    return join_columns(place, blocks, outs, items)


def ctx_gather(piece, *earlier):
    piece = after(piece, *earlier)
    near, back, far = [rotate(piece, "ctx", step) for step in (1, 3, 2)]
    return [piece, near, far, back]


def group_swap(blocks):
    return [lax.ppermute(block, "g", SWAP) for block in blocks]


def ctx_near(pieces, *earlier):
    piece = after(jnp.stack(pieces), *earlier)
    return piece, rotate(piece, "ctx", 1), rotate(piece, "ctx", 3)


def ctx_far(piece, near, back):
    return rotate(after(piece, near, back), "ctx", 2)


def group_first(piece, near, back):
    return lax.ppermute(jnp.stack([piece, near, back]), "g", SWAP)


def gather_weights_wide(low):
    result = []
    for layer in range(low.shape[0]):
        mats = to_group(low[layer])
        parts = lax.all_gather(mats, REPLICAS, axis=0, tiled=False)
        parts = parts.reshape(lax.axis_size("g"), -1, *mats.shape)
        full = [parts[:, :, item].transpose(1, 3, 0, 2).reshape(D, D) for item in range(3)]
        w_o = lax.all_to_all(
            full[0][3 * COLS :].T.reshape(TP, COLS, COLS),
            GROUP,
            split_axis=0,
            concat_axis=2,
            tiled=True,
        )
        attn = jnp.concatenate([full[0][: 3 * COLS].reshape(3, COLS, D), w_o], axis=0)
        result.append((attn.reshape(D, D), jnp.stack([full[1], full[2]])))
    return result


def half_sum(mine, give):
    return mine + lax.ppermute(give, "g", SWAP).astype(f32)


def ctx_sum(blocks):
    low = blocks.astype(bf16)
    near, back, far = [rotate(low[step], "ctx", -step) for step in (1, 3, 2)]
    return blocks[0] + near.astype(f32) + back.astype(f32) + far.astype(f32)


def grad_blocks(attn_parts, mlp_parts, rows, *earlier):
    layers = len(attn_parts)
    zero = jnp.zeros((1,), jnp.int32)

    def split(unused, *refs):
        *part_refs, out_ref = refs
        for layer in range(layers):
            for item in range(3):
                if item:
                    part = part_refs[layers + layer][item - 1]
                else:
                    part = part_refs[layer][...]
                turned = part.T.astype(bf16)
                for target in range(TP):
                    out_ref[target, 3 * layer + item] = turned[target * rows : (target + 1) * rows]

    blocks = call(split, [((TP, 3 * layers, rows, COLS), bf16)], zero, *attn_parts, *mlp_parts)[0]
    return group_exchange(after(blocks, *earlier)), out_back(jnp.stack(attn_parts).astype(bf16))


def grad_rows(place, blocks, outs, momentum):
    layers = momentum.shape[0]

    def join(place_ref, blocks_ref, outs_ref, momentum_ref, grad_ref, new_ref):
        for layer in range(layers):
            for item in range(3):
                for source in range(TP):
                    lanes = slice(source * COLS, (source + 1) * COLS)
                    grad_ref[layer, item, :, lanes] = blocks_ref[source, 3 * layer + item].astype(f32)

            @pl.when(place_ref[0] == 3)
            def last(layer=layer):
                grad_ref[layer, 0] = outs_ref[layer].astype(f32)

        new_ref[...] = momentum_decay * momentum_ref[...] + grad_ref[...]

    shape = (momentum.shape, f32)
    return call(join, [shape, shape], place, blocks, outs, momentum)


def scatter_wide(mats):
    groups = lax.axis_size("g")
    blocks, count, width, depth = mats.shape
    stack = mats.astype(bf16).reshape(blocks, count, width, groups, depth // groups)
    stack = stack.transpose(3, 0, 1, 4, 2).reshape(groups * blocks, count, -1, width)
    part = lax.psum_scatter(stack, REPLICAS, scatter_dimension=0, tiled=True)[0]
    return from_group(part).astype(f32)


def gather_vectors(vectors, *earlier):
    low = vectors.astype(bf16)
    stack = jnp.stack([low] + [rotate(low, "ctx", step) for step in range(1, 4)])
    stack = pair_join(pair_join(after(to_absolute(stack), *earlier), "jc", 3), "jx", 3)
    if lax.axis_size("g") == 2:
        stack = pair_join(stack, "g", 3)
    else:
        stack = lax.all_gather(stack, "g", axis=3, tiled=True)
    return stack.transpose(1, 0, 2, 3).reshape(low.shape[0], -1, D).astype(f32)


def sum_vectors(terms):
    if lax.axis_size("g") == 2:
        terms = terms + lax.ppermute(terms, "g", SWAP)
    else:
        terms = lax.psum(terms, "g")
    layers, rows, width = terms.shape
    blocks = from_own(terms.reshape(layers, 4, rows // 4, width).transpose(1, 0, 2, 3))
    total = blocks[0]
    for step in range(1, 4):
        total = total + rotate(blocks[step], "ctx", -step)
    return total


def sum_group(total):
    total = total + lax.ppermute(total, "jc", SWAP)
    return total + lax.ppermute(total, "jx", SWAP)


def call(kernel, outs, *args, scratch=()):
    return pl.pallas_call(
        kernel,
        out_shape=[jax.ShapeDtypeStruct(shape, kind) for shape, kind in outs],
        in_specs=[pl.BlockSpec(memory_space=pltpu.SMEM)]
        + [pl.BlockSpec(memory_space=pltpu.VMEM)] * (len(args) - 1),
        out_specs=[pl.BlockSpec(memory_space=pltpu.VMEM)] * len(outs),
        scratch_shapes=list(scratch),
        compiler_params=pltpu.CompilerParams(vmem_limit_bytes=52 * 1024 * 1024),
    )(*args)


def block_at(place_ref, step):
    ahead = place_ref[0] + step
    return jnp.where(ahead >= 4, ahead - 4, ahead)


def put_blocks(place_ref, own_refs, other_refs, full_refs):
    half = D // 2
    mine = pl.multiple_of(place_ref[1] * half, half)
    theirs = pl.multiple_of((1 - place_ref[1]) * half, half)
    for step in range(4):
        rows = pl.ds(pl.multiple_of(block_at(place_ref, step) * COLS, COLS), COLS)
        for number, full_ref in enumerate(full_refs):
            own, other = own_refs[step], other_refs[step]
            if len(full_refs) > 1:
                own, other = own.at[number], other.at[number]
            full_ref[rows, pl.ds(mine, half)] = own[...]
            full_ref[rows, pl.ds(theirs, half)] = other[...]


def put_grads(place_ref, grad, mine_refs, give_refs, halves):
    half = D // 2
    for block in range(4):
        rows = grad[block * COLS : (block + 1) * COLS]
        if halves:
            back = block - place_ref[0]
            back = jnp.where(back < 0, back + 4, back)
            low = place_ref[1] == 0
            mine_refs(back)[...] = jnp.where(low, rows[:, :half], rows[:, half:])
            give_refs(back)[...] = jnp.where(low, rows[:, half:], rows[:, :half]).astype(bf16)
        else:
            mine_refs(block)[...] = rows


def norm_rows(hidden):
    center = hidden - jnp.mean(hidden, axis=-1, keepdims=True)
    variance = jnp.mean(center * center, axis=-1, keepdims=True)
    inverse = lax.rsqrt(variance + norm_epsilon)
    return center * inverse, inverse


def norm_stage(vecs, layer, row, hidden, mine=None, recv=None, bias=None):
    rows = hidden.shape[0]

    def kernel(unused, vec_ref, hidden_ref, *refs):
        total = hidden_ref[...]
        if mine is not None:
            mine_ref, recv_ref, total_ref, out_ref = refs
            bias_row = vec_ref[bias[0], bias[1] : bias[1] + 1, :]
            total = total + (mine_ref[...] + recv_ref[...].astype(f32) + bias_row)
            total_ref[...] = total
        else:
            (out_ref,) = refs
        normed, unused_scale = norm_rows(total)
        gain = vec_ref[layer, row : row + 1, :]
        shift = vec_ref[layer, row + 1 : row + 2, :]
        out_ref[...] = (normed * gain + shift).astype(bf16)

    outs = [((rows, D), bf16)]
    args = [hidden]
    if mine is not None:
        outs = [((rows, D), f32)] + outs
        args += [mine, recv]
    return call(kernel, outs, jnp.zeros((1,), jnp.int32), vecs, *args)


def norm_back_stage(vecs, layer, row, grad, mine, recv, hidden):
    rows = hidden.shape[0]

    def kernel(unused, vec_ref, grad_ref, mine_ref, recv_ref, hidden_ref, out_ref, low_ref, sum_ref):
        through = mine_ref[...] + recv_ref[...].astype(f32)
        normed, inverse = norm_rows(hidden_ref[...])
        scaled = through * vec_ref[layer, row : row + 1, :]
        part = jnp.mean(scaled, axis=-1, keepdims=True)
        part = part + normed * jnp.mean(scaled * normed, axis=-1, keepdims=True)
        total = grad_ref[...] + inverse * (scaled - part)
        out_ref[...] = total
        low = total.astype(bf16)
        low_ref[...] = low
        sum_ref[0:1, :] = jnp.sum(through * normed, axis=0, keepdims=True)
        sum_ref[1:2, :] = jnp.sum(through, axis=0, keepdims=True)
        sum_ref[2:3, :] = jnp.sum(low.astype(f32), axis=0, keepdims=True)

    outs = [((rows, D), f32), ((rows, D), bf16), ((8, D), f32)]
    return call(kernel, outs, jnp.zeros((1,), jnp.int32), vecs, grad, mine, recv, hidden)


def both(first_ref, second_ref):
    return jnp.concatenate([first_ref[...], second_ref[...]], axis=0)


def allowed_of(row_ref, column_ref):
    before = row_ref[0:1, :] <= column_ref[:, 0:1]
    return before & (row_ref[1:2, :] == column_ref[:, 1:2])


def attend_stage(place, row_info, column_info, bias, a_own, a_other, weights):
    half = a_own.shape[0]
    tokens = 2 * half
    wide = 3 * COLS
    own, other = weights if isinstance(weights, tuple) else ([], [])

    def kernel(place_ref, row_ref, column_ref, bias_ref, own_a_ref, other_a_ref, *refs):
        if own:
            own_refs, refs = refs[:4], refs[4:]
            others, refs = refs[: len(other)], refs[len(other) :]
            if len(other) == 1:
                others = [others[0].at[step] for step in range(4)]
            w_ref, qkv_ref, lse_ref, o_ref, mine_ref, give_ref = refs
            put_blocks(place_ref, own_refs, others, [w_ref])
        else:
            w_ref, qkv_ref, lse_ref, o_ref, mine_ref, give_ref = refs
        for start, a_ref in ((0, own_a_ref), (half, other_a_ref)):
            proj = dot_trans(a_ref[...], w_ref[0:wide, :]) + bias_ref[0:1, :]
            qkv_ref[start : start + half, :] = proj.astype(bf16)
        allowed = allowed_of(row_ref, column_ref)
        for head in range(TP_HEADS):
            lanes = head * HEAD
            k = qkv_ref[:, COLS + lanes : COLS + lanes + HEAD]
            v = qkv_ref[:, 2 * COLS + lanes : 2 * COLS + lanes + HEAD]
            for start in (0, half):
                rows = slice(start, start + half)
                q = qkv_ref[rows, lanes : lanes + HEAD]
                scores = jnp.where(allowed[rows], dot_trans(q, k) * HEAD ** (-0.5), masked_score)
                top = jnp.max(scores, axis=-1, keepdims=True)
                unnormed = jnp.exp(scores - top)
                total = jnp.sum(unnormed, axis=-1, keepdims=True)
                prob = (unnormed * (1.0 / total)).astype(bf16)
                o_ref[rows, lanes : lanes + HEAD] = dot(prob, v).astype(bf16)
                lse_ref[rows, head : head + 1] = top + jnp.log(total)
        mine_ref[...] = dot(o_ref[0:half, :], w_ref[wide:, :])
        give_ref[...] = dot(o_ref[half:, :], w_ref[wide:, :]).astype(bf16)

    outs = [
        ((tokens, wide), bf16),
        ((tokens, 128), f32),
        ((tokens, COLS), bf16),
        ((half, D), f32),
        ((half, D), bf16),
    ]
    if own:
        outs = [((D, D), bf16)] + outs
        return call(
            kernel, outs, place, row_info, column_info, bias, a_own, a_other, *own, *other
        )
    result = call(kernel, outs, place, row_info, column_info, bias, a_own, a_other, weights)
    return [weights] + list(result)


def attend_back_stage(
    place, row_info, column_info, gb_own, gb_other, a_own, a_other, qkv, lse, o, w_attn, halves
):
    half = a_own.shape[0]
    tokens = 2 * half
    wide = 3 * COLS

    def kernel(
        place_ref,
        row_ref,
        column_ref,
        own_gb_ref,
        other_gb_ref,
        own_a_ref,
        other_a_ref,
        qkv_ref,
        lse_ref,
        o_ref,
        w_ref,
        mine_ref,
        give_ref,
        sum_ref,
        *refs,
    ):
        *grad_refs, go_ref, all_ref = refs
        w_o = w_ref[wide:, :]
        for start, gb_ref in ((0, own_gb_ref), (half, other_gb_ref)):
            go_ref[start : start + half, :] = dot_trans(gb_ref[...], w_o).astype(bf16)
        allowed = allowed_of(row_ref, column_ref)
        for head in range(TP_HEADS):
            lanes = head * HEAD
            q_lanes = slice(lanes, lanes + HEAD)
            k_lanes = slice(COLS + lanes, COLS + lanes + HEAD)
            v_lanes = slice(2 * COLS + lanes, 2 * COLS + lanes + HEAD)
            k = qkv_ref[:, k_lanes]
            v = qkv_ref[:, v_lanes]
            gk = jnp.zeros((tokens, HEAD), f32)
            gv = jnp.zeros((tokens, HEAD), f32)
            for start in (0, half):
                rows = slice(start, start + half)
                q = qkv_ref[rows, q_lanes]
                go = go_ref[rows, q_lanes]
                scores = jnp.where(allowed[rows], dot_trans(q, k) * HEAD ** (-0.5), masked_score)
                prob = jnp.exp(scores - lse_ref[rows, head : head + 1])
                g_prob = dot_trans(go, v)
                row_dot = jnp.sum(g_prob * prob, axis=-1, keepdims=True)
                g_scores = (prob * (g_prob - row_dot)).astype(bf16)
                all_ref[rows, q_lanes] = (dot(g_scores, k) * HEAD ** (-0.5)).astype(bf16)
                gk = gk + dot_tokens(g_scores, q)
                gv = gv + dot_tokens(prob.astype(bf16), go)
            all_ref[:, k_lanes] = (gk * HEAD ** (-0.5)).astype(bf16)
            all_ref[:, v_lanes] = gv.astype(bf16)
        mine_ref[...] = dot(all_ref[0:half, :], w_ref[0:wide, :])
        give_ref[...] = dot(all_ref[half:, :], w_ref[0:wide, :]).astype(bf16)
        sum_ref[0:1, :] = jnp.sum(all_ref[...].astype(f32), axis=0, keepdims=True)
        grad = jnp.concatenate(
            [
                dot_tokens(all_ref[...], both(own_a_ref, other_a_ref)),
                dot_tokens(o_ref[...], both(own_gb_ref, other_gb_ref)),
            ],
            axis=0,
        )
        put_grads(
            place_ref,
            grad,
            lambda block: grad_refs[0].at[block],
            lambda block: grad_refs[1].at[block],
            halves,
        )

    width = D // 2 if halves else D
    outs = [((half, D), f32), ((half, D), bf16), ((8, wide), f32), ((4, COLS, width), f32)]
    if halves:
        outs.append(((4, COLS, width), bf16))
    return call(
        kernel,
        outs,
        place,
        row_info,
        column_info,
        gb_own,
        gb_other,
        a_own,
        a_other,
        qkv,
        lse,
        o,
        w_attn,
        scratch=[pltpu.VMEM((tokens, COLS), bf16), pltpu.VMEM((tokens, wide), bf16)],
    )


def tanh_part(preact):
    inner = math.sqrt(2.0 / math.pi) * (preact + 0.044715 * (preact * preact * preact))
    return jnp.tanh(inner)


def feed_stage(place, bias, c_own, c_other, weights):
    half = c_own.shape[0]
    own, other = weights if isinstance(weights, tuple) else ([], [])

    def kernel(place_ref, bias_ref, own_c_ref, other_c_ref, *refs):
        if own:
            own_refs, (first, last), refs = refs[:4], refs[4:6], refs[6:]
            others = [first.at[0], first.at[1], last, first.at[2]]
            w_ref, preact_ref, act_ref, mine_ref, give_ref = refs
            put_blocks(place_ref, own_refs, others, [w_ref.at[0], w_ref.at[1]])
        else:
            w_ref, preact_ref, act_ref, mine_ref, give_ref = refs
        for start, c_ref, out_ref in ((0, own_c_ref, mine_ref), (half, other_c_ref, give_ref)):
            rows = slice(start, start + half)
            preact = dot_trans(c_ref[...], w_ref[0]) + bias_ref[...]
            preact_ref[rows, :] = preact
            act = (0.5 * preact * (1.0 + tanh_part(preact))).astype(bf16)
            act_ref[rows, :] = act
            out_ref[...] = dot(act, w_ref[1]).astype(out_ref.dtype)

    outs = [
        ((2 * half, D), f32),
        ((2 * half, D), bf16),
        ((half, D), f32),
        ((half, D), bf16),
    ]
    if own:
        outs = [((2, D, D), bf16)] + outs
        return call(kernel, outs, place, bias, c_own, c_other, *own, *other)
    return [weights] + list(call(kernel, outs, place, bias, c_own, c_other, weights))


def feed_back_stage(place, gy_own, gy_other, c_own, c_other, preact, act, weights, halves):
    half = c_own.shape[0]

    def kernel(
        place_ref,
        own_gy_ref,
        other_gy_ref,
        own_c_ref,
        other_c_ref,
        preact_ref,
        act_ref,
        w_ref,
        mine_ref,
        give_ref,
        sum_ref,
        *refs,
    ):
        *grad_refs, gz_ref = refs
        up_sum = jnp.zeros((1, D), f32)
        for start, gy_ref, out_ref in ((0, own_gy_ref, mine_ref), (half, other_gy_ref, give_ref)):
            rows = slice(start, start + half)
            gu = dot_trans(gy_ref[...], w_ref[1])
            x = preact_ref[rows, :]
            tanh = tanh_part(x)
            slope = math.sqrt(2.0 / math.pi) * (1.0 + 3.0 * 0.044715 * (x * x))
            factor = 0.5 * (1.0 + tanh) + 0.5 * x * (1.0 - tanh * tanh) * slope
            gz = (gu * factor).astype(bf16)
            gz_ref[rows, :] = gz
            up_sum = up_sum + jnp.sum(gz.astype(f32), axis=0, keepdims=True)
            out_ref[...] = dot(gz, w_ref[0]).astype(out_ref.dtype)
        sum_ref[0:1, :] = up_sum
        sum_ref[1:2, :] = jnp.sum(own_gy_ref[...].astype(f32), axis=0, keepdims=True)
        for number, left_ref, rights in (
            (0, gz_ref, (own_c_ref, other_c_ref)),
            (1, act_ref, (own_gy_ref, other_gy_ref)),
        ):
            put_grads(
                place_ref,
                dot_tokens(left_ref[...], both(*rights)),
                lambda block: grad_refs[0].at[block, number],
                lambda block: grad_refs[1].at[block, number],
                halves,
            )

    width = D // 2 if halves else D
    outs = [((half, D), f32), ((half, D), bf16), ((8, D), f32), ((4, 2, COLS, width), f32)]
    if halves:
        outs.append(((4, 2, COLS, width), bf16))
    return call(
        kernel,
        outs,
        place,
        gy_own,
        gy_other,
        c_own,
        c_other,
        preact,
        act,
        weights,
        scratch=[pltpu.VMEM((2 * half, D), bf16)],
    )


def core_swap(block):
    return lax.ppermute(block, "jc", SWAP)


def group_sum(mine, give):
    mine = mine + core_swap(give).astype(f32)
    return mine, lax.ppermute(mine.astype(bf16), "jx", SWAP)


def polynomial(base_ref, low_ref, mat_ref):
    low_ref[...] = base_ref[...].astype(bf16)
    for start in range(0, base_ref.shape[0], ROWS):
        block = pl.ds(start, ROWS)
        square = dot(low_ref[block, :], low_ref[...])
        mat_ref[block, :] = (quintic_two * base_ref[block, :] + quintic_three * square).astype(bf16)


def two_part(left, right):
    high = left.astype(bf16)
    rest = (left - high.astype(f32)).astype(bf16)
    return dot(high, right) + dot(rest, right)


def iterate(x_ref, out_ref, base_ref, work_ref, mat_ref, low_ref):
    size = x_ref.shape[0]
    blocks = [pl.ds(start, ROWS) for start in range(0, size, ROWS)]
    trace = jnp.zeros((1, 1), f32)
    line = lax.broadcasted_iota(jnp.int32, (ROWS, ROWS), 0)
    column = lax.broadcasted_iota(jnp.int32, (ROWS, ROWS), 1)
    for block in blocks:
        part = jnp.where(line == column, base_ref[block, block], 0.0)
        trace = trace + jnp.sum(part, keepdims=True)
    scale = 1.0 / (jnp.sqrt(trace) + 1e-07)
    base_ref[...] = base_ref[...] * (scale * scale)
    polynomial(base_ref, low_ref, mat_ref)

    for block in blocks:
        value = quintic_one * x_ref[block, :].astype(f32) + dot(x_ref[block, :], mat_ref[...])
        out_ref[block, :] = (scale * value).astype(bf16)
        work_ref[block, :] = quintic_one * base_ref[block, :] + two_part(
            base_ref[block, :], mat_ref[...]
        )
    turned = work_ref[...].T
    work_ref[...] = turned
    for block in blocks:
        base_ref[block, :] = quintic_one * work_ref[block, :] + two_part(
            work_ref[block, :], mat_ref[...]
        )
    polynomial(base_ref, low_ref, mat_ref)
    for block in blocks:
        x = out_ref[block, :]
        out_ref[block, :] = (quintic_one * x.astype(f32) + dot(x, mat_ref[...])).astype(bf16)


def orthogonalize(matrix, gram):
    size = matrix.shape[0]

    def kernel(unused, x_ref, gram_ref, out_ref, in_ref, base_ref, work_ref, mat_ref, low_ref):
        in_ref[...] = x_ref[...].T
        base_ref[...] = gram_ref[...]
        iterate(in_ref, out_ref, base_ref, work_ref, mat_ref, low_ref)
        out_ref[...] = out_ref[...].T

    return call(
        kernel,
        [((size, size), bf16)],
        jnp.zeros((1,), jnp.int32),
        matrix,
        gram,
        scratch=[pltpu.VMEM((size, size), kind) for kind in (bf16, f32, f32, bf16, bf16)],
    )[0]


def put_slots(slot_ref, x_ref):
    half = D // 2
    for source in range(8):
        group, number = source // TP, source % TP
        x_ref[number * COLS : (number + 1) * COLS, group * half : (group + 1) * half] = slot_ref[
            source
        ]


def slot_input(place_ref, slot_ref, moment_ref, sum_ref, x_ref, turned):
    put_slots(slot_ref, sum_ref)
    moment = moment_ref[...].astype(f32) * (momentum_decay * momentum_decay)
    if turned:
        moment = moment.T
    x_ref[...] = (sum_ref[...].astype(f32) * (1.0 + momentum_decay) + moment).astype(bf16)


def slot_gram(place, slots, moments):
    def kernel(place_ref, slot_ref, moment_ref, x_ref, gram_ref, sum_ref):
        slot_input(place_ref, slot_ref, moment_ref, sum_ref, x_ref, True)
        half = D // 2
        for part in range(2):
            rows = dot_tokens(x_ref[:, part * half : (part + 1) * half], x_ref[...]).astype(bf16)
            for number in range(2):
                back = 2 * part + number - place_ref[0]
                back = jnp.where(back < 0, back + 4, back)
                gram_ref[back] = rows[number * COLS : (number + 1) * COLS]

    return call(
        kernel,
        [((D, D), bf16), ((4, COLS, D), bf16)],
        place,
        slots,
        moments,
        scratch=[pltpu.VMEM((D, D), bf16)],
    )


def slot_orthogonalize(place, x_wide, grams, square_slots, moments):
    def kernel(
        place_ref,
        wide_ref,
        gram0_ref,
        gram1_ref,
        gram2_ref,
        gram3_ref,
        slot_ref,
        moment_ref,
        out_ref,
        x_ref,
        base_ref,
        work_ref,
        mat_ref,
        low_ref,
    ):
        core = place_ref[2]
        plain = (core == 1) & (place_ref[0] == 3)

        @pl.when(core == 0)
        def wide():
            x_ref[...] = wide_ref[...]
            for step, gram_ref in enumerate((gram0_ref, gram1_ref, gram2_ref, gram3_ref)):
                rows = pl.ds(pl.multiple_of(block_at(place_ref, step) * COLS, COLS), COLS)
                base_ref[rows, :] = gram_ref[...].astype(f32)

        @pl.when(plain)
        def square_plain():
            slot_input(place_ref, slot_ref, moment_ref, low_ref, x_ref, False)

        @pl.when((core == 1) & jnp.logical_not(plain))
        def square_turned():
            slot_input(place_ref, slot_ref, moment_ref, low_ref, x_ref, True)

        @pl.when(core == 1)
        def square():
            base_ref[...] = dot_tokens(x_ref[...], x_ref[...])

        iterate(x_ref, out_ref, base_ref, work_ref, mat_ref, low_ref)

        @pl.when(jnp.logical_not(plain))
        def turn():
            out_ref[...] = out_ref[...].T

    return call(
        kernel,
        [((D, D), bf16)],
        place,
        x_wide,
        *grams,
        square_slots,
        moments,
        scratch=[pltpu.VMEM((D, D), kind) for kind in (bf16, f32, f32, bf16, bf16)],
    )[0]


def slot_exchange(blocks):
    return lax.all_to_all(blocks, DP, split_axis=0, concat_axis=0, tiled=True)


def core_shift(block, step):
    size = lax.axis_size("ctx")
    return lax.ppermute(block, ("jc", "ctx"), [((i + step) % size, i) for i in range(size)])


def ctx_gram(gram):
    size = lax.axis_size("ctx")
    blocks = from_own(gram.astype(bf16).reshape(size, gram.shape[0] // size, -1))
    total = blocks[0].astype(f32)
    for step in (1, 3, 2):
        total = total + core_shift(blocks[step], -step).astype(f32)
    low = total.astype(bf16)
    full = [low] + [core_shift(low, step) for step in range(1, size)]
    return to_absolute(jnp.stack(full)).reshape(gram.shape).astype(f32)


def local(hidden_in, segments, out_grad, weights, vectors, mat_momentum, vec_first, vec_second):
    tokens_dev = hidden_in.shape[1]
    seq_len = segments.shape[1]
    half = 2 * tokens_dev
    dp_rows = weights.shape[2]
    ctx_size = lax.axis_size("ctx")
    x_index = lax.axis_index("jx")
    c_index = lax.axis_index("jc")
    t_index = 2 * x_index + c_index
    z_index = lax.axis_index("ctx")
    dp_index = lax.axis_index(DP)
    dp_size = lax.axis_size(DP)

    to_seq = []
    for t in range(TP):
        for z in range(ctx_size):
            to_seq.append((t * ctx_size + z, ((z % 2) * 2 + z // 2) * ctx_size + t))
    from_seq = [(b, a) for a, b in to_seq]
    axes = ("jx", "jc", "ctx")

    def x_join(block):
        return pair_join(block, "jx", 0)

    seg_row = jnp.pad(segments.astype(f32), ((0, 7), (0, D - seq_len)))
    moved = lax.ppermute(jnp.concatenate([hidden_in[0], seg_row], axis=0), axes, to_seq)
    segment_row = moved[tokens_dev, :seq_len]
    relative = lax.axis_size("g") == 2
    place = jnp.stack([z_index, lax.axis_index("g"), c_index]).astype(jnp.int32)
    if relative:
        piece, outs = first_piece(place, weights)
        own_attn = ctx_gather(piece)
        attn_weights = (own_attn, group_swap(own_attn))
        pieces = other_pieces(place, weights, outs, own_attn[1])
        near_blocks = ctx_near(pieces[0:2], *own_attn[1:])
        far = ctx_far(*near_blocks)
        first = group_first(*near_blocks)
    else:
        wide_weights = gather_weights_wide(weights.astype(bf16))
        outs = piece = place
    vec_rows = gather_vectors(vectors, outs)
    hidden = x_join(after(moved[:tokens_dev], piece))

    start = c_index * half
    pos = jnp.concatenate([start + jnp.arange(half), half - start + jnp.arange(half)])
    seg = jnp.roll(segment_row.reshape(2, half), -c_index, axis=0).reshape(-1)
    info = jnp.stack([pos.astype(f32), seg])
    row_info = jnp.pad(info, ((0, 6), (0, 0)))
    column_info = jnp.pad(info.T, ((0, 0), (0, 126)))
    vec_mine = lax.dynamic_slice_in_dim(vec_rows, t_index * COLS, COLS, axis=2)
    no_bias = jnp.zeros((LAYERS, 1, COLS), f32)
    qkv_bias = jnp.concatenate([vec_mine[:, 4:5], no_bias, vec_mine[:, 5:6]], axis=2)
    up_bias = vec_mine[:, 8:12].reshape(LAYERS, 1, D)

    stored = []
    (a_own,) = norm_stage(vec_rows, 0, 0, hidden)
    for layer in range(LAYERS):
        following = layer + 1 < LAYERS
        a_other = core_swap(a_own)
        if not relative:
            attn_weights, mlp_weights = wide_weights[layer]
        w_attn, qkv, lse, o, mine, give = attend_stage(
            place, row_info, column_info, qkv_bias[layer], a_own, a_other, attn_weights
        )
        if relative and not following:
            mine, gy_own = lax.optimization_barrier((mine, gy_own))
        mine, recv = group_sum(mine, give)
        middle, c_own = norm_stage(vec_rows, layer, 2, hidden, mine, recv, (layer, 6))
        if relative:
            last = lax.ppermute(after(far, first), "g", SWAP)
            mlp_weights = ([near_blocks[0], near_blocks[1], far, near_blocks[2]], [first, last])
        c_other = core_swap(c_own)
        if relative and following:
            base = 3 * layer + 2
            own_attn = ctx_gather(pieces[base], far)
            c_other, own_attn = lax.optimization_barrier((c_other, own_attn))
        w_mlp, preact, act, mine, give = feed_stage(
            place, up_bias[layer], c_own, c_other, mlp_weights
        )
        if relative and following:
            attn_weights = (own_attn, [lax.ppermute(jnp.stack(own_attn), "g", SWAP)])
            near_blocks = ctx_near(pieces[base + 1 : base + 3], *own_attn[1:])
            moved_low = lax.ppermute(after(out_grad[0].astype(bf16), own_attn[2]), axes, to_seq)
        if following:
            mine, recv = group_sum(mine, give)
        stored.append(
            (hidden, middle, a_own, a_other, qkv, lse, o, c_own, c_other, preact, act, w_attn, w_mlp)
        )
        if following:
            hidden, a_own = norm_stage(vec_rows, layer + 1, 0, middle, mine, recv, (layer, 7))
            if relative:
                a_own, near_blocks, moved_low = lax.optimization_barrier(
                    (a_own, near_blocks, moved_low)
                )
                far = ctx_far(*near_blocks)
                first = group_first(*near_blocks)
                gy_own = x_join(moved_low)

    def send_back(rows):
        block = lax.dynamic_slice_in_dim(rows, x_index * tokens_dev, tokens_dev, axis=0)
        return lax.ppermute(block, axes, from_seq)

    last_sum = (mine, give)

    def last_hidden(*earlier):
        mine, recv = group_sum(last_sum[0], after(last_sum[1], *earlier))
        return stored[-1][1] + (mine + recv.astype(f32) + vec_rows[LAYERS - 1, 7:8])

    if not relative:
        grad_hidden = x_join(lax.ppermute(out_grad[0], axes, to_seq))
        hidden_out = send_back(last_hidden())
        gy_own = grad_hidden.astype(bf16)
    else:
        grad_hidden = gy_own.astype(f32)
    attn_half = None

    mat_list = [None] * LAYERS
    sum_list = [None] * LAYERS
    parts = [None] * LAYERS
    for layer in reversed(range(LAYERS)):
        h_in, middle, a_own, a_other, qkv, lse, o, c_own, c_other, preact, act, w_attn, w_mlp = stored[
            layer
        ]
        if relative and attn_half is not None:
            gy_own, attn_half = lax.optimization_barrier((gy_own, attn_half))
            hidden = last_hidden(gy_own)
            attn_part = ctx_sum(attn_half)
        gy_other = core_swap(gy_own)
        mine, give, up_sums, *mlp_grads = feed_back_stage(
            place, gy_own, gy_other, c_own, c_other, preact, act, w_mlp, relative
        )
        if relative:
            mlp_mine, mlp_give = mlp_grads
            mlp_recv = lax.ppermute(mlp_give, "g", SWAP)
            if attn_half is not None:
                mine, hidden, attn_part = lax.optimization_barrier((mine, hidden, attn_part))
                wide_part = ctx_sum(late_half[0] + after(late_half[1], mine).astype(f32))
        mine, recv = group_sum(mine, give)
        grad_middle, gb_own, mid_sums = norm_back_stage(
            vec_rows, layer, 2, grad_hidden, mine, recv, middle
        )
        if relative and layer == LAYERS - 1:
            moment_low = mat_momentum.astype(bf16)
            table = [(1, 1), (1, 0), (1, 2), (0, 0), (0, 1), (1, 0), (0, 2), (0, 0)]
            moment_slots = slot_exchange(
                after(jnp.stack([moment_low[slot] for slot in table]), gb_own)
            ).reshape(D, D)
        gb_other = core_swap(gb_own)
        if relative and layer < LAYERS - 1:
            gb_other, wide_part = lax.optimization_barrier((gb_other, wide_part))
        mine, give, qkv_sums, *attn_grads = attend_back_stage(
            place,
            row_info,
            column_info,
            gb_own,
            gb_other,
            a_own,
            a_other,
            qkv,
            lse,
            o,
            w_attn,
            relative,
        )
        if relative:
            if layer == LAYERS - 1:
                mine, mlp_recv, moment_slots = lax.optimization_barrier(
                    (mine, mlp_recv, moment_slots)
                )
                late_half = (mlp_mine, mlp_recv)
            else:
                parts[layer + 1] = (attn_part, wide_part)
                mlp_half = mlp_mine + after(mlp_recv, give).astype(f32)
                mlp_part = ctx_sum(mlp_half)
            attn_half = half_sum(*attn_grads)
        else:
            attn_grad = attn_grads[0]
            g_wo = lax.all_to_all(
                attn_grad[3].reshape(COLS, TP, COLS), GROUP, split_axis=1, concat_axis=0, tiled=True
            )[:, 0]
            attn_grad = jnp.concatenate([attn_grad[:3], g_wo.T[None]], axis=0)
            mat_list[layer] = scatter_wide(
                jnp.concatenate([attn_grad[:, None], mlp_grads[0]], axis=1)
            )
        mine, recv = group_sum(mine, give)
        grad_hidden, gy_own, in_sums = norm_back_stage(
            vec_rows, layer, 0, grad_middle, mine, recv, h_in
        )
        sum_list[layer] = (in_sums, mid_sums, up_sums, qkv_sums)
    if not relative:
        input_grad = send_back(grad_hidden)

    once = jnp.where(x_index == 0, 1.0, 0.0).astype(f32)
    in_sums, mid_sums, up_sums, qkv_sums = [jnp.stack(sums) for sums in zip(*sum_list)]
    shared = once * jnp.concatenate(
        [in_sums[:, 0:2], mid_sums[:, 0:3], up_sums[:, 1:2]], axis=1
    )
    placed = jnp.concatenate(
        [
            qkv_sums[:, 0:1, :COLS],
            qkv_sums[:, 0:1, 2 * COLS :],
            up_sums[:, 0].reshape(LAYERS, ctx_size, COLS),
        ],
        axis=1,
    )
    placed = lax.dynamic_update_slice_in_dim(
        jnp.zeros((LAYERS, 6, D), f32), placed, t_index * COLS, axis=2
    )
    vec_terms = jnp.concatenate(
        [shared[:, 0:4], placed[:, 0:2], shared[:, 4:6], placed[:, 2:6]], axis=1
    )
    if relative:
        attn_low = attn_half.astype(bf16)
        attn_sums = [rotate(attn_low[step], "ctx", -step) for step in (1, 3, 2)]
        wide_low = jnp.concatenate([parts[1][1], mlp_part]).astype(bf16)
        wide_low = after(wide_low, attn_half, grad_hidden)
        wide_slots = slot_exchange(jnp.repeat(wide_low, 2, axis=0))
        wide_slots, attn_sums = lax.optimization_barrier((wide_slots, attn_sums))
        x_wide, gram_blocks = slot_gram(place, wide_slots, moment_slots)
        vec_sums = sum_group(sum_vectors(after(vec_terms, gram_blocks)))
        attn_part = attn_half[0] + sum(block.astype(f32) for block in attn_sums)
        total = gram_blocks[0].astype(f32)
        for step in (1, 3, 2):
            total = total + core_shift(gram_blocks[step], -step).astype(f32)
        gram_low = total.astype(bf16)
        blocks, outs = grad_blocks(
            [attn_part, parts[1][0]], [mlp_part, parts[1][1]], dp_rows, gram_blocks
        )
        square_low, vec_sums, blocks, unused = lax.optimization_barrier(
            (jnp.stack([parts[1][0], attn_part]).astype(bf16), vec_sums, blocks, gram_low)
        )
        square_slots = slot_exchange(jnp.tile(jnp.repeat(square_low, 2, axis=0), (2, 1, 1)))
        near, back, far = [core_shift(gram_low, step) for step in (1, 3, 2)]
        ortho_mine = slot_orthogonalize(
            place, x_wide, (gram_low, near, far, back), square_slots, moment_slots
        )
        grad_mats, moment_new = grad_rows(place, blocks, outs, mat_momentum)
        returned = slot_exchange(ortho_mine.reshape(dp_size, dp_rows, D))
        ends = jnp.stack([hidden, grad_hidden]).astype(bf16)
        ends = lax.dynamic_slice_in_dim(ends, x_index * tokens_dev, tokens_dev, axis=1)
        ends = lax.ppermute(after(ends, near, back, far), axes, from_seq)
        hidden_out, input_grad = ends.astype(f32)
        ortho = jnp.stack([returned[slot] for slot in (3, 4, 6, 1, 0, 2)])
        ortho = ortho.reshape(weights.shape).astype(f32)
    else:
        vec_sums = sum_group(sum_vectors(vec_terms))
        cols_dev = weights.shape[3]
        grad_list, moment_list, low_list = [], [], []
        for layer in range(LAYERS):
            for item in range(3):
                grad = mat_list[layer][item]
                moment = momentum_decay * mat_momentum[layer, item] + grad
                grad_list.append(grad)
                moment_list.append(moment)
                low_list.append((grad + momentum_decay * moment).astype(bf16))
        wide = [item for item in range(3 * LAYERS) if item % 3]
        squares = [item for item in range(3, 3 * LAYERS, 3)]
        table = []
        for number in range(4):
            table += [wide[number], squares[number % len(squares)]]
        table = (table * (-(-dp_size // 8)))[:dp_size]
        slots = jnp.stack([low_list[item] for item in table])
        received = lax.all_to_all(slots[:, None], DP, split_axis=0, concat_axis=1, tiled=True)
        current = received.reshape(dp_size * dp_rows, cols_dev)
        gram_local = dot_trans(current, current)
        gram = jnp.where(c_index == 0, ctx_gram(gram_local), gram_local)
        ortho_mine = orthogonalize(current, gram)
        returned = lax.all_to_all(
            ortho_mine.reshape(dp_size, 1, dp_rows, cols_dev),
            DP,
            split_axis=0,
            concat_axis=1,
            tiled=True,
        )[0]
        first_full = lax.all_gather(low_list[0], DP, axis=0, tiled=True)
        first_ortho = orthogonalize(first_full, dot_trans(first_full, first_full))
        ortho_list = [lax.dynamic_slice_in_dim(first_ortho, dp_index * dp_rows, dp_rows, axis=0)]
        ortho_list += [returned[table.index(item)] for item in range(1, 3 * LAYERS)]
        ortho = jnp.stack(ortho_list).reshape(LAYERS, 3, dp_rows, cols_dev).astype(f32)
        grad_mats = jnp.stack(grad_list).reshape(weights.shape)
        moment_new = jnp.stack(moment_list).reshape(weights.shape)
    grad_vecs = lax.dynamic_slice_in_dim(
        vec_sums, dp_index * vectors.shape[2], vectors.shape[2], axis=2
    )
    factor = jnp.array([0.2 * math.sqrt(D), 0.2 * math.sqrt(FF), 0.2 * math.sqrt(FF)], f32)
    weights_new = weights * (1.0 - matrix_rate * matrix_decay) - matrix_rate * (
        ortho * factor[None, :, None, None]
    )
    first_new = first_decay * vec_first + (1.0 - first_decay) * grad_vecs
    second_new = second_decay * vec_second + (1.0 - second_decay) * grad_vecs * grad_vecs
    first_hat = first_new / (1.0 - first_decay**ADAM_STEP)
    second_hat = second_new / (1.0 - second_decay**ADAM_STEP)
    vectors_new = vectors * (1.0 - vector_rate * vector_decay) - vector_rate * first_hat / (
        jnp.sqrt(second_hat) + adam_epsilon
    )
    return (
        hidden_out[None],
        input_grad[None],
        grad_mats,
        moment_new,
        weights_new,
        grad_vecs,
        second_new,
        vectors_new,
    )


def solution(mesh):
    dp, ctx = mesh.shape["dp"], mesh.shape["ctx"]
    fine = Mesh(mesh.devices.reshape(dp // TP, 2, 2, ctx), EVERY)
    tokens = P(DP, "ctx", None)
    mats = P(None, None, DP, "ctx")
    vecs = P(None, "ctx", DP)
    return jax.shard_map(
        local,
        mesh=fine,
        in_specs=(tokens, P(DP, None), tokens, mats, vecs, mats, vecs, vecs),
        out_specs=(tokens, tokens, mats, mats, mats, vecs, vecs, vecs),
        check_vma=False,
    )
```

```python
import math

import jax
import jax.numpy as jnp
from jax import lax
from jax.experimental import pallas as pl
from jax.experimental.pallas import tpu as pltpu
from jax.sharding import Mesh, PartitionSpec as P

D = 768
HEADS = 12
HEAD = 64
FF = 3072
LAYERS = 2
ADAM_STEP = 10
TP = 4
COLS = D // TP
TP_HEADS = HEADS // TP
ROWS = 256

norm_epsilon = 1e-05
quintic_one = 3.4445
quintic_two = -4.775
quintic_three = 2.0315
momentum_decay = 0.95
matrix_rate = 0.6
matrix_decay = 0.01
first_decay = 0.9
second_decay = 0.999
vector_rate = 0.5
vector_decay = 0.01
adam_epsilon = 1e-08
masked_score = -1e30

GROUP = ("jx", "jc")
REPLICAS = ("g", "ctx")
DP = ("g", "jx", "jc")
EVERY = ("g", "jx", "jc", "ctx")
SWAP = [(0, 1), (1, 0)]
bf16 = jnp.bfloat16
f32 = jnp.float32


def dot(operand, other):
    return jnp.dot(operand, other, preferred_element_type=f32)


def dot_tokens(operand, other):
    return lax.dot_general(operand, other, (((0,), (0,)), ((), ())), preferred_element_type=f32)


def dot_trans(operand, other):
    return lax.dot_general(operand, other, (((1,), (1,)), ((), ())), preferred_element_type=f32)


def to_group(mats):
    count, rows, width = mats.shape
    split = mats.reshape(count, rows, TP, width // TP)
    return lax.all_to_all(split, GROUP, split_axis=2, concat_axis=1, tiled=True)[:, :, 0]


def from_group(mats):
    count, rows, width = mats.shape
    split = mats.reshape(count, TP, rows // TP, width)
    return lax.all_to_all(split, GROUP, split_axis=1, concat_axis=3, tiled=True)[:, 0]


def rotate(block, axis, step):
    size = lax.axis_size(axis)
    return lax.ppermute(block, axis, [((i + step) % size, i) for i in range(size)])


def pair_join(block, axis, dim):
    other = lax.ppermute(block, axis, SWAP)
    first = lax.axis_index(axis) == 0
    return jnp.concatenate(
        [jnp.where(first, block, other), jnp.where(first, other, block)], axis=dim
    )


def after(value, *others):
    return lax.optimization_barrier((value, *others))[0]


def roll_blocks(stack, sign):
    place = lax.axis_index("ctx")
    for bit in (1, 2):
        moved = jnp.roll(stack, sign * bit, axis=0)
        stack = jnp.where((place & bit) != 0, moved, stack)
    return stack


def from_own(stack):
    return roll_blocks(stack, -1)


def to_absolute(stack):
    return roll_blocks(stack, 1)


def out_moves():
    last = lax.axis_size("ctx") - 1
    size = last + 1
    moves = []
    for y in range(2):
        for x in range(2):
            for core in range(2):
                moves.append(
                    ((4 * y + 2 * x + core) * size + last, (4 * core + 2 * y + x) * size + last)
                )
    return moves


def out_pieces(mats):
    half = mats.shape[2] // 2
    core = lax.axis_index("jc")
    mine = lax.dynamic_slice_in_dim(mats, core * half, half, axis=2)
    give = lax.dynamic_slice_in_dim(mats, (1 - core) * half, half, axis=2)
    got = lax.ppermute(give, "jc", SWAP)
    rows = jnp.concatenate(
        [jnp.where(core == 0, mine, got), jnp.where(core == 0, got, mine)], axis=1
    )
    return lax.ppermute(rows, EVERY, out_moves())


def out_back(pieces):
    core = lax.axis_index("jc")
    rows = lax.ppermute(pieces, EVERY, [(b, a) for a, b in out_moves()])
    half = rows.shape[1] // 2
    mine = lax.dynamic_slice_in_dim(rows, core * half, half, axis=1)
    give = lax.dynamic_slice_in_dim(rows, (1 - core) * half, half, axis=1)
    got = lax.ppermute(give, "jc", SWAP)
    return jnp.concatenate(
        [jnp.where(core == 0, mine, got), jnp.where(core == 0, got, mine)], axis=2
    )


def last_block():
    return lax.axis_index("ctx") == lax.axis_size("ctx") - 1


def split_columns(mats, items):
    rows = mats.shape[2]

    def kernel(unused, mats_ref, out_ref):
        for number, (layer, item) in enumerate(items):
            turned = mats_ref[layer, item].T.astype(bf16)
            for quarter in range(TP):
                out_ref[quarter, number] = turned[quarter * COLS : (quarter + 1) * COLS]

    outs = [((TP, len(items), COLS, rows), bf16)]
    return call(kernel, outs, jnp.zeros((1,), jnp.int32), mats)[0]


def join_columns(place, blocks, outs, items):
    rows = blocks.shape[3]

    def kernel(place_ref, blocks_ref, outs_ref, *out_refs):
        for number, (layer, item) in enumerate(items):
            for source in range(TP):
                lanes = slice(source * rows, (source + 1) * rows)
                out_refs[number][:, lanes] = blocks_ref[source, number]
            if item == 0:

                @pl.when(place_ref[0] == 3)
                def last(number=number, layer=layer):
                    out_refs[number][...] = outs_ref[layer]

    shapes = [((COLS, TP * rows), bf16)] * len(items)
    return call(kernel, shapes, place, blocks, outs)


def group_exchange(blocks):
    return lax.all_to_all(blocks, GROUP, split_axis=0, concat_axis=0, tiled=True)


def first_piece(place, mats):
    outs = out_pieces(mats[:, 0].astype(bf16))
    blocks = group_exchange(split_columns(mats, [(0, 0)]))
    return join_columns(place, blocks, outs, [(0, 0)])[0], outs


def other_pieces(place, mats, outs, *earlier):
    items = [(layer, item) for layer in range(mats.shape[0]) for item in range(3)][1:]
    blocks = group_exchange(split_columns(after(mats, *earlier), items))
    return join_columns(place, blocks, outs, items)


def ctx_gather(piece, *earlier):
    piece = after(piece, *earlier)
    near, back, far = [rotate(piece, "ctx", step) for step in (1, 3, 2)]
    return [piece, near, far, back]


def group_swap(blocks):
    return [lax.ppermute(block, "g", SWAP) for block in blocks]


def ctx_near(pieces, *earlier):
    piece = after(jnp.stack(pieces), *earlier)
    return piece, rotate(piece, "ctx", 1), rotate(piece, "ctx", 3)


def ctx_far(piece, near, back):
    return rotate(after(piece, near, back), "ctx", 2)


def group_first(piece, near, back):
    return lax.ppermute(jnp.stack([piece, near, back]), "g", SWAP)


def gather_weights_wide(low):
    result = []
    for layer in range(low.shape[0]):
        mats = to_group(low[layer])
        parts = lax.all_gather(mats, REPLICAS, axis=0, tiled=False)
        parts = parts.reshape(lax.axis_size("g"), -1, *mats.shape)
        full = [parts[:, :, item].transpose(1, 3, 0, 2).reshape(D, D) for item in range(3)]
        w_o = lax.all_to_all(
            full[0][3 * COLS :].T.reshape(TP, COLS, COLS),
            GROUP,
            split_axis=0,
            concat_axis=2,
            tiled=True,
        )
        attn = jnp.concatenate([full[0][: 3 * COLS].reshape(3, COLS, D), w_o], axis=0)
        result.append((attn.reshape(D, D), jnp.stack([full[1], full[2]])))
    return result


def half_sum(mine, give):
    return mine + lax.ppermute(give, "g", SWAP).astype(f32)


def ctx_sum(blocks):
    low = blocks.astype(bf16)
    near, back, far = [rotate(low[step], "ctx", -step) for step in (1, 3, 2)]
    return blocks[0] + near.astype(f32) + back.astype(f32) + far.astype(f32)


def grad_blocks(attn_parts, mlp_parts, rows, *earlier):
    layers = len(attn_parts)
    zero = jnp.zeros((1,), jnp.int32)

    def split(unused, *refs):
        *part_refs, out_ref = refs
        for layer in range(layers):
            for item in range(3):
                if item:
                    part = part_refs[layers + layer][item - 1]
                else:
                    part = part_refs[layer][...]
                turned = part.T.astype(bf16)
                for target in range(TP):
                    out_ref[target, 3 * layer + item] = turned[target * rows : (target + 1) * rows]

    blocks = call(split, [((TP, 3 * layers, rows, COLS), bf16)], zero, *attn_parts, *mlp_parts)[0]
    return group_exchange(after(blocks, *earlier)), out_back(jnp.stack(attn_parts).astype(bf16))


def grad_rows(place, blocks, outs, momentum):
    layers = momentum.shape[0]

    def join(place_ref, blocks_ref, outs_ref, momentum_ref, grad_ref, new_ref):
        for layer in range(layers):
            for item in range(3):
                for source in range(TP):
                    lanes = slice(source * COLS, (source + 1) * COLS)
                    grad_ref[layer, item, :, lanes] = blocks_ref[source, 3 * layer + item].astype(f32)

            @pl.when(place_ref[0] == 3)
            def last(layer=layer):
                grad_ref[layer, 0] = outs_ref[layer].astype(f32)

        new_ref[...] = momentum_decay * momentum_ref[...] + grad_ref[...]

    shape = (momentum.shape, f32)
    return call(join, [shape, shape], place, blocks, outs, momentum)


def scatter_wide(mats):
    groups = lax.axis_size("g")
    blocks, count, width, depth = mats.shape
    stack = mats.astype(bf16).reshape(blocks, count, width, groups, depth // groups)
    stack = stack.transpose(3, 0, 1, 4, 2).reshape(groups * blocks, count, -1, width)
    part = lax.psum_scatter(stack, REPLICAS, scatter_dimension=0, tiled=True)[0]
    return from_group(part).astype(f32)


def gather_vectors(vectors, *earlier):
    low = vectors.astype(bf16)
    stack = jnp.stack([low] + [rotate(low, "ctx", step) for step in range(1, 4)])
    stack = pair_join(pair_join(after(to_absolute(stack), *earlier), "jc", 3), "jx", 3)
    if lax.axis_size("g") == 2:
        stack = pair_join(stack, "g", 3)
    else:
        stack = lax.all_gather(stack, "g", axis=3, tiled=True)
    return stack.transpose(1, 0, 2, 3).reshape(low.shape[0], -1, D).astype(f32)


def sum_vectors(terms):
    if lax.axis_size("g") == 2:
        terms = terms + lax.ppermute(terms, "g", SWAP)
    else:
        terms = lax.psum(terms, "g")
    layers, rows, width = terms.shape
    blocks = from_own(terms.reshape(layers, 4, rows // 4, width).transpose(1, 0, 2, 3))
    total = blocks[0]
    for step in range(1, 4):
        total = total + rotate(blocks[step], "ctx", -step)
    return total


def sum_group(total):
    total = total + lax.ppermute(total, "jc", SWAP)
    return total + lax.ppermute(total, "jx", SWAP)


def call(kernel, outs, *args, scratch=()):
    return pl.pallas_call(
        kernel,
        out_shape=[jax.ShapeDtypeStruct(shape, kind) for shape, kind in outs],
        in_specs=[pl.BlockSpec(memory_space=pltpu.SMEM)]
        + [pl.BlockSpec(memory_space=pltpu.VMEM)] * (len(args) - 1),
        out_specs=[pl.BlockSpec(memory_space=pltpu.VMEM)] * len(outs),
        scratch_shapes=list(scratch),
        compiler_params=pltpu.CompilerParams(vmem_limit_bytes=52 * 1024 * 1024),
    )(*args)


def block_at(place_ref, step):
    ahead = place_ref[0] + step
    return jnp.where(ahead >= 4, ahead - 4, ahead)


def put_blocks(place_ref, own_refs, other_refs, full_refs):
    half = D // 2
    mine = pl.multiple_of(place_ref[1] * half, half)
    theirs = pl.multiple_of((1 - place_ref[1]) * half, half)
    for step in range(4):
        rows = pl.ds(pl.multiple_of(block_at(place_ref, step) * COLS, COLS), COLS)
        for number, full_ref in enumerate(full_refs):
            own, other = own_refs[step], other_refs[step]
            if len(full_refs) > 1:
                own, other = own.at[number], other.at[number]
            full_ref[rows, pl.ds(mine, half)] = own[...]
            full_ref[rows, pl.ds(theirs, half)] = other[...]


def put_grads(place_ref, grad, mine_refs, give_refs, halves):
    half = D // 2
    for block in range(4):
        rows = grad[block * COLS : (block + 1) * COLS]
        if halves:
            back = block - place_ref[0]
            back = jnp.where(back < 0, back + 4, back)
            low = place_ref[1] == 0
            mine_refs(back)[...] = jnp.where(low, rows[:, :half], rows[:, half:])
            give_refs(back)[...] = jnp.where(low, rows[:, half:], rows[:, :half]).astype(bf16)
        else:
            mine_refs(block)[...] = rows


def norm_rows(hidden):
    center = hidden - jnp.mean(hidden, axis=-1, keepdims=True)
    variance = jnp.mean(center * center, axis=-1, keepdims=True)
    inverse = lax.rsqrt(variance + norm_epsilon)
    return center * inverse, inverse


def norm_stage(vecs, layer, row, hidden, mine=None, recv=None, bias=None):
    rows = hidden.shape[0]

    def kernel(unused, vec_ref, hidden_ref, *refs):
        total = hidden_ref[...]
        if mine is not None:
            mine_ref, recv_ref, total_ref, out_ref = refs
            bias_row = vec_ref[bias[0], bias[1] : bias[1] + 1, :]
            total = total + (mine_ref[...] + recv_ref[...].astype(f32) + bias_row)
            total_ref[...] = total
        else:
            (out_ref,) = refs
        normed, unused_scale = norm_rows(total)
        gain = vec_ref[layer, row : row + 1, :]
        shift = vec_ref[layer, row + 1 : row + 2, :]
        out_ref[...] = (normed * gain + shift).astype(bf16)

    outs = [((rows, D), bf16)]
    args = [hidden]
    if mine is not None:
        outs = [((rows, D), f32)] + outs
        args += [mine, recv]
    return call(kernel, outs, jnp.zeros((1,), jnp.int32), vecs, *args)


def norm_back_stage(vecs, layer, row, grad, mine, recv, hidden):
    rows = hidden.shape[0]

    def kernel(unused, vec_ref, grad_ref, mine_ref, recv_ref, hidden_ref, out_ref, low_ref, sum_ref):
        through = mine_ref[...] + recv_ref[...].astype(f32)
        normed, inverse = norm_rows(hidden_ref[...])
        scaled = through * vec_ref[layer, row : row + 1, :]
        part = jnp.mean(scaled, axis=-1, keepdims=True)
        part = part + normed * jnp.mean(scaled * normed, axis=-1, keepdims=True)
        total = grad_ref[...] + inverse * (scaled - part)
        out_ref[...] = total
        low = total.astype(bf16)
        low_ref[...] = low
        sum_ref[0:1, :] = jnp.sum(through * normed, axis=0, keepdims=True)
        sum_ref[1:2, :] = jnp.sum(through, axis=0, keepdims=True)
        sum_ref[2:3, :] = jnp.sum(low.astype(f32), axis=0, keepdims=True)

    outs = [((rows, D), f32), ((rows, D), bf16), ((8, D), f32)]
    return call(kernel, outs, jnp.zeros((1,), jnp.int32), vecs, grad, mine, recv, hidden)


def both(first_ref, second_ref):
    return jnp.concatenate([first_ref[...], second_ref[...]], axis=0)


def allowed_of(row_ref, column_ref):
    before = row_ref[0:1, :] <= column_ref[:, 0:1]
    return before & (row_ref[1:2, :] == column_ref[:, 1:2])


def attend_stage(place, row_info, column_info, bias, a_own, a_other, weights):
    half = a_own.shape[0]
    tokens = 2 * half
    wide = 3 * COLS
    own, other = weights if isinstance(weights, tuple) else ([], [])

    def kernel(place_ref, row_ref, column_ref, bias_ref, own_a_ref, other_a_ref, *refs):
        if own:
            own_refs, refs = refs[:4], refs[4:]
            others, refs = refs[: len(other)], refs[len(other) :]
            if len(other) == 1:
                others = [others[0].at[step] for step in range(4)]
            w_ref, qkv_ref, lse_ref, o_ref, mine_ref, give_ref = refs
            put_blocks(place_ref, own_refs, others, [w_ref])
        else:
            w_ref, qkv_ref, lse_ref, o_ref, mine_ref, give_ref = refs
        for start, a_ref in ((0, own_a_ref), (half, other_a_ref)):
            proj = dot_trans(a_ref[...], w_ref[0:wide, :]) + bias_ref[0:1, :]
            qkv_ref[start : start + half, :] = proj.astype(bf16)
        allowed = allowed_of(row_ref, column_ref)
        for head in range(TP_HEADS):
            lanes = head * HEAD
            k = qkv_ref[:, COLS + lanes : COLS + lanes + HEAD]
            v = qkv_ref[:, 2 * COLS + lanes : 2 * COLS + lanes + HEAD]
            for start in (0, half):
                rows = slice(start, start + half)
                q = qkv_ref[rows, lanes : lanes + HEAD]
                scores = jnp.where(allowed[rows], dot_trans(q, k) * HEAD ** (-0.5), masked_score)
                top = jnp.max(scores, axis=-1, keepdims=True)
                unnormed = jnp.exp(scores - top)
                total = jnp.sum(unnormed, axis=-1, keepdims=True)
                prob = (unnormed * (1.0 / total)).astype(bf16)
                o_ref[rows, lanes : lanes + HEAD] = dot(prob, v).astype(bf16)
                lse_ref[rows, head : head + 1] = top + jnp.log(total)
        mine_ref[...] = dot(o_ref[0:half, :], w_ref[wide:, :])
        give_ref[...] = dot(o_ref[half:, :], w_ref[wide:, :]).astype(bf16)

    outs = [
        ((tokens, wide), bf16),
        ((tokens, 128), f32),
        ((tokens, COLS), bf16),
        ((half, D), f32),
        ((half, D), bf16),
    ]
    if own:
        outs = [((D, D), bf16)] + outs
        return call(
            kernel, outs, place, row_info, column_info, bias, a_own, a_other, *own, *other
        )
    result = call(kernel, outs, place, row_info, column_info, bias, a_own, a_other, weights)
    return [weights] + list(result)


def attend_back_stage(
    place, row_info, column_info, gb_own, gb_other, a_own, a_other, qkv, lse, o, w_attn, halves
):
    half = a_own.shape[0]
    tokens = 2 * half
    wide = 3 * COLS

    def kernel(
        place_ref,
        row_ref,
        column_ref,
        own_gb_ref,
        other_gb_ref,
        own_a_ref,
        other_a_ref,
        qkv_ref,
        lse_ref,
        o_ref,
        w_ref,
        mine_ref,
        give_ref,
        sum_ref,
        *refs,
    ):
        *grad_refs, go_ref, all_ref = refs
        w_o = w_ref[wide:, :]
        for start, gb_ref in ((0, own_gb_ref), (half, other_gb_ref)):
            go_ref[start : start + half, :] = dot_trans(gb_ref[...], w_o).astype(bf16)
        allowed = allowed_of(row_ref, column_ref)
        for head in range(TP_HEADS):
            lanes = head * HEAD
            q_lanes = slice(lanes, lanes + HEAD)
            k_lanes = slice(COLS + lanes, COLS + lanes + HEAD)
            v_lanes = slice(2 * COLS + lanes, 2 * COLS + lanes + HEAD)
            k = qkv_ref[:, k_lanes]
            v = qkv_ref[:, v_lanes]
            gk = jnp.zeros((tokens, HEAD), f32)
            gv = jnp.zeros((tokens, HEAD), f32)
            for start in (0, half):
                rows = slice(start, start + half)
                q = qkv_ref[rows, q_lanes]
                go = go_ref[rows, q_lanes]
                scores = jnp.where(allowed[rows], dot_trans(q, k) * HEAD ** (-0.5), masked_score)
                prob = jnp.exp(scores - lse_ref[rows, head : head + 1])
                g_prob = dot_trans(go, v)
                row_dot = jnp.sum(g_prob * prob, axis=-1, keepdims=True)
                g_scores = (prob * (g_prob - row_dot)).astype(bf16)
                all_ref[rows, q_lanes] = (dot(g_scores, k) * HEAD ** (-0.5)).astype(bf16)
                gk = gk + dot_tokens(g_scores, q)
                gv = gv + dot_tokens(prob.astype(bf16), go)
            all_ref[:, k_lanes] = (gk * HEAD ** (-0.5)).astype(bf16)
            all_ref[:, v_lanes] = gv.astype(bf16)
        mine_ref[...] = dot(all_ref[0:half, :], w_ref[0:wide, :])
        give_ref[...] = dot(all_ref[half:, :], w_ref[0:wide, :]).astype(bf16)
        sum_ref[0:1, :] = jnp.sum(all_ref[...].astype(f32), axis=0, keepdims=True)
        grad = jnp.concatenate(
            [
                dot_tokens(all_ref[...], both(own_a_ref, other_a_ref)),
                dot_tokens(o_ref[...], both(own_gb_ref, other_gb_ref)),
            ],
            axis=0,
        )
        put_grads(
            place_ref,
            grad,
            lambda block: grad_refs[0].at[block],
            lambda block: grad_refs[1].at[block],
            halves,
        )

    width = D // 2 if halves else D
    outs = [((half, D), f32), ((half, D), bf16), ((8, wide), f32), ((4, COLS, width), f32)]
    if halves:
        outs.append(((4, COLS, width), bf16))
    return call(
        kernel,
        outs,
        place,
        row_info,
        column_info,
        gb_own,
        gb_other,
        a_own,
        a_other,
        qkv,
        lse,
        o,
        w_attn,
        scratch=[pltpu.VMEM((tokens, COLS), bf16), pltpu.VMEM((tokens, wide), bf16)],
    )


def tanh_part(preact):
    inner = math.sqrt(2.0 / math.pi) * (preact + 0.044715 * (preact * preact * preact))
    return jnp.tanh(inner)


def feed_stage(place, bias, c_own, c_other, weights):
    half = c_own.shape[0]
    own, other = weights if isinstance(weights, tuple) else ([], [])

    def kernel(place_ref, bias_ref, own_c_ref, other_c_ref, *refs):
        if own:
            own_refs, (first, last), refs = refs[:4], refs[4:6], refs[6:]
            others = [first.at[0], first.at[1], last, first.at[2]]
            w_ref, preact_ref, act_ref, mine_ref, give_ref = refs
            put_blocks(place_ref, own_refs, others, [w_ref.at[0], w_ref.at[1]])
        else:
            w_ref, preact_ref, act_ref, mine_ref, give_ref = refs
        for start, c_ref, out_ref in ((0, own_c_ref, mine_ref), (half, other_c_ref, give_ref)):
            rows = slice(start, start + half)
            preact = dot_trans(c_ref[...], w_ref[0]) + bias_ref[...]
            preact_ref[rows, :] = preact
            act = (0.5 * preact * (1.0 + tanh_part(preact))).astype(bf16)
            act_ref[rows, :] = act
            out_ref[...] = dot(act, w_ref[1]).astype(out_ref.dtype)

    outs = [
        ((2 * half, D), f32),
        ((2 * half, D), bf16),
        ((half, D), f32),
        ((half, D), bf16),
    ]
    if own:
        outs = [((2, D, D), bf16)] + outs
        return call(kernel, outs, place, bias, c_own, c_other, *own, *other)
    return [weights] + list(call(kernel, outs, place, bias, c_own, c_other, weights))


def feed_back_stage(place, gy_own, gy_other, c_own, c_other, preact, act, weights, halves):
    half = c_own.shape[0]

    def kernel(
        place_ref,
        own_gy_ref,
        other_gy_ref,
        own_c_ref,
        other_c_ref,
        preact_ref,
        act_ref,
        w_ref,
        mine_ref,
        give_ref,
        sum_ref,
        *refs,
    ):
        *grad_refs, gz_ref = refs
        up_sum = jnp.zeros((1, D), f32)
        for start, gy_ref, out_ref in ((0, own_gy_ref, mine_ref), (half, other_gy_ref, give_ref)):
            rows = slice(start, start + half)
            gu = dot_trans(gy_ref[...], w_ref[1])
            x = preact_ref[rows, :]
            tanh = tanh_part(x)
            slope = math.sqrt(2.0 / math.pi) * (1.0 + 3.0 * 0.044715 * (x * x))
            factor = 0.5 * (1.0 + tanh) + 0.5 * x * (1.0 - tanh * tanh) * slope
            gz = (gu * factor).astype(bf16)
            gz_ref[rows, :] = gz
            up_sum = up_sum + jnp.sum(gz.astype(f32), axis=0, keepdims=True)
            out_ref[...] = dot(gz, w_ref[0]).astype(out_ref.dtype)
        sum_ref[0:1, :] = up_sum
        sum_ref[1:2, :] = jnp.sum(own_gy_ref[...].astype(f32), axis=0, keepdims=True)
        for number, left_ref, rights in (
            (0, gz_ref, (own_c_ref, other_c_ref)),
            (1, act_ref, (own_gy_ref, other_gy_ref)),
        ):
            put_grads(
                place_ref,
                dot_tokens(left_ref[...], both(*rights)),
                lambda block: grad_refs[0].at[block, number],
                lambda block: grad_refs[1].at[block, number],
                halves,
            )

    width = D // 2 if halves else D
    outs = [((half, D), f32), ((half, D), bf16), ((8, D), f32), ((4, 2, COLS, width), f32)]
    if halves:
        outs.append(((4, 2, COLS, width), bf16))
    return call(
        kernel,
        outs,
        place,
        gy_own,
        gy_other,
        c_own,
        c_other,
        preact,
        act,
        weights,
        scratch=[pltpu.VMEM((2 * half, D), bf16)],
    )


def core_swap(block):
    return lax.ppermute(block, "jc", SWAP)


def group_sum(mine, give):
    mine = mine + core_swap(give).astype(f32)
    return mine, lax.ppermute(mine.astype(bf16), "jx", SWAP)


def polynomial(base_ref, low_ref, mat_ref):
    low_ref[...] = base_ref[...].astype(bf16)
    for start in range(0, base_ref.shape[0], ROWS):
        block = pl.ds(start, ROWS)
        square = dot(low_ref[block, :], low_ref[...])
        mat_ref[block, :] = (quintic_two * base_ref[block, :] + quintic_three * square).astype(bf16)


def two_part(left, right):
    high = left.astype(bf16)
    rest = (left - high.astype(f32)).astype(bf16)
    return dot(high, right) + dot(rest, right)


def iterate(x_ref, out_ref, base_ref, work_ref, mat_ref, low_ref):
    size = x_ref.shape[0]
    blocks = [pl.ds(start, ROWS) for start in range(0, size, ROWS)]
    trace = jnp.zeros((1, 1), f32)
    line = lax.broadcasted_iota(jnp.int32, (ROWS, ROWS), 0)
    column = lax.broadcasted_iota(jnp.int32, (ROWS, ROWS), 1)
    for block in blocks:
        part = jnp.where(line == column, base_ref[block, block], 0.0)
        trace = trace + jnp.sum(part, keepdims=True)
    scale = 1.0 / (jnp.sqrt(trace) + 1e-07)
    base_ref[...] = base_ref[...] * (scale * scale)
    polynomial(base_ref, low_ref, mat_ref)

    for block in blocks:
        value = quintic_one * x_ref[block, :].astype(f32) + dot(x_ref[block, :], mat_ref[...])
        out_ref[block, :] = (scale * value).astype(bf16)
        work_ref[block, :] = quintic_one * base_ref[block, :] + two_part(
            base_ref[block, :], mat_ref[...]
        )
    turned = work_ref[...].T
    work_ref[...] = turned
    for block in blocks:
        base_ref[block, :] = quintic_one * work_ref[block, :] + two_part(
            work_ref[block, :], mat_ref[...]
        )
    polynomial(base_ref, low_ref, mat_ref)
    for block in blocks:
        x = out_ref[block, :]
        out_ref[block, :] = (quintic_one * x.astype(f32) + dot(x, mat_ref[...])).astype(bf16)


def orthogonalize(matrix, gram):
    size = matrix.shape[0]

    def kernel(unused, x_ref, gram_ref, out_ref, in_ref, base_ref, work_ref, mat_ref, low_ref):
        in_ref[...] = x_ref[...].T
        base_ref[...] = gram_ref[...]
        iterate(in_ref, out_ref, base_ref, work_ref, mat_ref, low_ref)
        out_ref[...] = out_ref[...].T

    return call(
        kernel,
        [((size, size), bf16)],
        jnp.zeros((1,), jnp.int32),
        matrix,
        gram,
        scratch=[pltpu.VMEM((size, size), kind) for kind in (bf16, f32, f32, bf16, bf16)],
    )[0]


def put_slots(slot_ref, x_ref):
    half = D // 2
    for source in range(8):
        group, number = source // TP, source % TP
        x_ref[number * COLS : (number + 1) * COLS, group * half : (group + 1) * half] = slot_ref[
            source
        ]


def slot_input(place_ref, slot_ref, moment_ref, sum_ref, x_ref, turned):
    put_slots(slot_ref, sum_ref)
    moment = moment_ref[...].astype(f32) * (momentum_decay * momentum_decay)
    if turned:
        moment = moment.T
    x_ref[...] = (sum_ref[...].astype(f32) * (1.0 + momentum_decay) + moment).astype(bf16)


def slot_gram(place, slots, moments):
    def kernel(place_ref, slot_ref, moment_ref, x_ref, gram_ref, sum_ref):
        slot_input(place_ref, slot_ref, moment_ref, sum_ref, x_ref, True)
        half = D // 2
        for part in range(2):
            rows = dot_tokens(x_ref[:, part * half : (part + 1) * half], x_ref[...]).astype(bf16)
            for number in range(2):
                back = 2 * part + number - place_ref[0]
                back = jnp.where(back < 0, back + 4, back)
                gram_ref[back] = rows[number * COLS : (number + 1) * COLS]

    return call(
        kernel,
        [((D, D), bf16), ((4, COLS, D), bf16)],
        place,
        slots,
        moments,
        scratch=[pltpu.VMEM((D, D), bf16)],
    )


def slot_orthogonalize(place, x_wide, grams, square_slots, moments):
    def kernel(
        place_ref,
        wide_ref,
        gram0_ref,
        gram1_ref,
        gram2_ref,
        gram3_ref,
        slot_ref,
        moment_ref,
        out_ref,
        x_ref,
        base_ref,
        work_ref,
        mat_ref,
        low_ref,
    ):
        core = place_ref[2]
        plain = (core == 1) & (place_ref[0] == 3)

        @pl.when(core == 0)
        def wide():
            x_ref[...] = wide_ref[...]
            for step, gram_ref in enumerate((gram0_ref, gram1_ref, gram2_ref, gram3_ref)):
                rows = pl.ds(pl.multiple_of(block_at(place_ref, step) * COLS, COLS), COLS)
                base_ref[rows, :] = gram_ref[...].astype(f32)

        @pl.when(plain)
        def square_plain():
            slot_input(place_ref, slot_ref, moment_ref, low_ref, x_ref, False)

        @pl.when((core == 1) & jnp.logical_not(plain))
        def square_turned():
            slot_input(place_ref, slot_ref, moment_ref, low_ref, x_ref, True)

        @pl.when(core == 1)
        def square():
            base_ref[...] = dot_tokens(x_ref[...], x_ref[...])

        iterate(x_ref, out_ref, base_ref, work_ref, mat_ref, low_ref)

        @pl.when(jnp.logical_not(plain))
        def turn():
            out_ref[...] = out_ref[...].T

    return call(
        kernel,
        [((D, D), bf16)],
        place,
        x_wide,
        *grams,
        square_slots,
        moments,
        scratch=[pltpu.VMEM((D, D), kind) for kind in (bf16, f32, f32, bf16, bf16)],
    )[0]


def slot_exchange(blocks):
    return lax.all_to_all(blocks, DP, split_axis=0, concat_axis=0, tiled=True)


def core_shift(block, step):
    size = lax.axis_size("ctx")
    return lax.ppermute(block, ("jc", "ctx"), [((i + step) % size, i) for i in range(size)])


def ctx_gram(gram):
    size = lax.axis_size("ctx")
    blocks = from_own(gram.astype(bf16).reshape(size, gram.shape[0] // size, -1))
    total = blocks[0].astype(f32)
    for step in (1, 3, 2):
        total = total + core_shift(blocks[step], -step).astype(f32)
    low = total.astype(bf16)
    full = [low] + [core_shift(low, step) for step in range(1, size)]
    return to_absolute(jnp.stack(full)).reshape(gram.shape).astype(f32)


def local(hidden_in, segments, out_grad, weights, vectors, mat_momentum, vec_first, vec_second):
    tokens_dev = hidden_in.shape[1]
    seq_len = segments.shape[1]
    half = 2 * tokens_dev
    dp_rows = weights.shape[2]
    ctx_size = lax.axis_size("ctx")
    x_index = lax.axis_index("jx")
    c_index = lax.axis_index("jc")
    t_index = 2 * x_index + c_index
    z_index = lax.axis_index("ctx")
    dp_index = lax.axis_index(DP)
    dp_size = lax.axis_size(DP)

    to_seq = []
    for t in range(TP):
        for z in range(ctx_size):
            to_seq.append((t * ctx_size + z, ((z % 2) * 2 + z // 2) * ctx_size + t))
    from_seq = [(b, a) for a, b in to_seq]
    axes = ("jx", "jc", "ctx")

    def x_join(block):
        return pair_join(block, "jx", 0)

    seg_row = jnp.pad(segments.astype(f32), ((0, 7), (0, D - seq_len)))
    moved = lax.ppermute(jnp.concatenate([hidden_in[0], seg_row], axis=0), axes, to_seq)
    segment_row = moved[tokens_dev, :seq_len]
    relative = lax.axis_size("g") == 2
    place = jnp.stack([z_index, lax.axis_index("g"), c_index]).astype(jnp.int32)
    if relative:
        piece, outs = first_piece(place, weights)
        own_attn = ctx_gather(piece)
        attn_weights = (own_attn, group_swap(own_attn))
        pieces = other_pieces(place, weights, outs, own_attn[1])
        near_blocks = ctx_near(pieces[0:2], *own_attn[1:])
        far = ctx_far(*near_blocks)
        first = group_first(*near_blocks)
    else:
        wide_weights = gather_weights_wide(weights.astype(bf16))
        outs = piece = place
    vec_rows = gather_vectors(vectors, outs)
    hidden = x_join(after(moved[:tokens_dev], piece))

    start = c_index * half
    pos = jnp.concatenate([start + jnp.arange(half), half - start + jnp.arange(half)])
    seg = jnp.roll(segment_row.reshape(2, half), -c_index, axis=0).reshape(-1)
    info = jnp.stack([pos.astype(f32), seg])
    row_info = jnp.pad(info, ((0, 6), (0, 0)))
    column_info = jnp.pad(info.T, ((0, 0), (0, 126)))
    vec_mine = lax.dynamic_slice_in_dim(vec_rows, t_index * COLS, COLS, axis=2)
    no_bias = jnp.zeros((LAYERS, 1, COLS), f32)
    qkv_bias = jnp.concatenate([vec_mine[:, 4:5], no_bias, vec_mine[:, 5:6]], axis=2)
    up_bias = vec_mine[:, 8:12].reshape(LAYERS, 1, D)

    stored = []
    (a_own,) = norm_stage(vec_rows, 0, 0, hidden)
    for layer in range(LAYERS):
        following = layer + 1 < LAYERS
        a_other = core_swap(a_own)
        if not relative:
            attn_weights, mlp_weights = wide_weights[layer]
        w_attn, qkv, lse, o, mine, give = attend_stage(
            place, row_info, column_info, qkv_bias[layer], a_own, a_other, attn_weights
        )
        if relative and not following:
            mine, gy_own = lax.optimization_barrier((mine, gy_own))
        mine, recv = group_sum(mine, give)
        middle, c_own = norm_stage(vec_rows, layer, 2, hidden, mine, recv, (layer, 6))
        if relative:
            last = lax.ppermute(after(far, first), "g", SWAP)
            mlp_weights = ([near_blocks[0], near_blocks[1], far, near_blocks[2]], [first, last])
        c_other = core_swap(c_own)
        if relative and following:
            base = 3 * layer + 2
            own_attn = ctx_gather(pieces[base], far)
            c_other, own_attn = lax.optimization_barrier((c_other, own_attn))
        w_mlp, preact, act, mine, give = feed_stage(
            place, up_bias[layer], c_own, c_other, mlp_weights
        )
        if relative and following:
            attn_weights = (own_attn, [lax.ppermute(jnp.stack(own_attn), "g", SWAP)])
            near_blocks = ctx_near(pieces[base + 1 : base + 3], *own_attn[1:])
            moved_low = lax.ppermute(after(out_grad[0].astype(bf16), own_attn[2]), axes, to_seq)
        if following:
            mine, recv = group_sum(mine, give)
        stored.append(
            (hidden, middle, a_own, a_other, qkv, lse, o, c_own, c_other, preact, act, w_attn, w_mlp)
        )
        if following:
            hidden, a_own = norm_stage(vec_rows, layer + 1, 0, middle, mine, recv, (layer, 7))
            if relative:
                a_own, near_blocks, moved_low = lax.optimization_barrier(
                    (a_own, near_blocks, moved_low)
                )
                far = ctx_far(*near_blocks)
                first = group_first(*near_blocks)
                gy_own = x_join(moved_low)

    def send_back(rows):
        block = lax.dynamic_slice_in_dim(rows, x_index * tokens_dev, tokens_dev, axis=0)
        return lax.ppermute(block, axes, from_seq)

    last_sum = (mine, give)

    def last_hidden(*earlier):
        mine, recv = group_sum(last_sum[0], after(last_sum[1], *earlier))
        return stored[-1][1] + (mine + recv.astype(f32) + vec_rows[LAYERS - 1, 7:8])

    if not relative:
        grad_hidden = x_join(lax.ppermute(out_grad[0], axes, to_seq))
        hidden_out = send_back(last_hidden())
        gy_own = grad_hidden.astype(bf16)
    else:
        grad_hidden = gy_own.astype(f32)
    attn_half = None

    mat_list = [None] * LAYERS
    sum_list = [None] * LAYERS
    parts = [None] * LAYERS
    for layer in reversed(range(LAYERS)):
        h_in, middle, a_own, a_other, qkv, lse, o, c_own, c_other, preact, act, w_attn, w_mlp = stored[
            layer
        ]
        if relative and attn_half is not None:
            gy_own, attn_half = lax.optimization_barrier((gy_own, attn_half))
            hidden = last_hidden(gy_own)
            attn_part = ctx_sum(attn_half)
        gy_other = core_swap(gy_own)
        mine, give, up_sums, *mlp_grads = feed_back_stage(
            place, gy_own, gy_other, c_own, c_other, preact, act, w_mlp, relative
        )
        if relative:
            mlp_mine, mlp_give = mlp_grads
            mlp_recv = lax.ppermute(mlp_give, "g", SWAP)
            if attn_half is not None:
                mine, hidden, attn_part = lax.optimization_barrier((mine, hidden, attn_part))
                wide_part = ctx_sum(late_half[0] + after(late_half[1], mine).astype(f32))
        mine, recv = group_sum(mine, give)
        grad_middle, gb_own, mid_sums = norm_back_stage(
            vec_rows, layer, 2, grad_hidden, mine, recv, middle
        )
        if relative and layer == LAYERS - 1:
            moment_low = mat_momentum.astype(bf16)
            table = [(1, 1), (1, 0), (1, 2), (0, 0), (0, 1), (1, 0), (0, 2), (0, 0)]
            moment_slots = slot_exchange(
                after(jnp.stack([moment_low[slot] for slot in table]), gb_own)
            ).reshape(D, D)
        gb_other = core_swap(gb_own)
        if relative and layer < LAYERS - 1:
            gb_other, wide_part = lax.optimization_barrier((gb_other, wide_part))
        mine, give, qkv_sums, *attn_grads = attend_back_stage(
            place,
            row_info,
            column_info,
            gb_own,
            gb_other,
            a_own,
            a_other,
            qkv,
            lse,
            o,
            w_attn,
            relative,
        )
        if relative:
            if layer == LAYERS - 1:
                mine, mlp_recv, moment_slots = lax.optimization_barrier(
                    (mine, mlp_recv, moment_slots)
                )
                late_half = (mlp_mine, mlp_recv)
            else:
                parts[layer + 1] = (attn_part, wide_part)
                mlp_half = mlp_mine + after(mlp_recv, give).astype(f32)
                mlp_part = ctx_sum(mlp_half)
            attn_half = half_sum(*attn_grads)
        else:
            attn_grad = attn_grads[0]
            g_wo = lax.all_to_all(
                attn_grad[3].reshape(COLS, TP, COLS), GROUP, split_axis=1, concat_axis=0, tiled=True
            )[:, 0]
            attn_grad = jnp.concatenate([attn_grad[:3], g_wo.T[None]], axis=0)
            mat_list[layer] = scatter_wide(
                jnp.concatenate([attn_grad[:, None], mlp_grads[0]], axis=1)
            )
        mine, recv = group_sum(mine, give)
        grad_hidden, gy_own, in_sums = norm_back_stage(
            vec_rows, layer, 0, grad_middle, mine, recv, h_in
        )
        sum_list[layer] = (in_sums, mid_sums, up_sums, qkv_sums)
    if not relative:
        input_grad = send_back(grad_hidden)

    once = jnp.where(x_index == 0, 1.0, 0.0).astype(f32)
    in_sums, mid_sums, up_sums, qkv_sums = [jnp.stack(sums) for sums in zip(*sum_list)]
    shared = once * jnp.concatenate(
        [in_sums[:, 0:2], mid_sums[:, 0:3], up_sums[:, 1:2]], axis=1
    )
    placed = jnp.concatenate(
        [
            qkv_sums[:, 0:1, :COLS],
            qkv_sums[:, 0:1, 2 * COLS :],
            up_sums[:, 0].reshape(LAYERS, ctx_size, COLS),
        ],
        axis=1,
    )
    placed = lax.dynamic_update_slice_in_dim(
        jnp.zeros((LAYERS, 6, D), f32), placed, t_index * COLS, axis=2
    )
    vec_terms = jnp.concatenate(
        [shared[:, 0:4], placed[:, 0:2], shared[:, 4:6], placed[:, 2:6]], axis=1
    )
    if relative:
        attn_low = attn_half.astype(bf16)
        attn_sums = [rotate(attn_low[step], "ctx", -step) for step in (1, 3, 2)]
        wide_low = jnp.concatenate([parts[1][1], mlp_part]).astype(bf16)
        wide_low = after(wide_low, attn_half)
        wide_slots = slot_exchange(jnp.repeat(wide_low, 2, axis=0))
        wide_slots, grad_hidden, attn_sums = lax.optimization_barrier(
            (wide_slots, grad_hidden, attn_sums)
        )
        x_wide, gram_blocks = slot_gram(place, wide_slots, moment_slots)
        vec_sums = sum_group(sum_vectors(after(vec_terms, gram_blocks)))
        attn_part = attn_half[0] + sum(block.astype(f32) for block in attn_sums)
        total = gram_blocks[0].astype(f32)
        for step in (1, 3, 2):
            total = total + core_shift(gram_blocks[step], -step).astype(f32)
        gram_low = total.astype(bf16)
        blocks, outs = grad_blocks(
            [attn_part, parts[1][0]], [mlp_part, parts[1][1]], dp_rows, gram_blocks
        )
        square_low, vec_sums, blocks, unused = lax.optimization_barrier(
            (jnp.stack([parts[1][0], attn_part]).astype(bf16), vec_sums, blocks, gram_low)
        )
        square_slots = slot_exchange(jnp.tile(jnp.repeat(square_low, 2, axis=0), (2, 1, 1)))
        near, back, far = [core_shift(gram_low, step) for step in (1, 3, 2)]
        ortho_mine = slot_orthogonalize(
            place, x_wide, (gram_low, near, far, back), square_slots, moment_slots
        )
        grad_mats, moment_new = grad_rows(place, blocks, outs, mat_momentum)
        returned = slot_exchange(ortho_mine.reshape(dp_size, dp_rows, D))
        ends = jnp.stack([hidden, grad_hidden]).astype(bf16)
        ends = lax.dynamic_slice_in_dim(ends, x_index * tokens_dev, tokens_dev, axis=1)
        ends = lax.ppermute(after(ends, near, back, far), axes, from_seq)
        hidden_out, input_grad = ends.astype(f32)
        ortho = jnp.stack([returned[slot] for slot in (3, 4, 6, 1, 0, 2)])
        ortho = ortho.reshape(weights.shape).astype(f32)
    else:
        vec_sums = sum_group(sum_vectors(vec_terms))
        cols_dev = weights.shape[3]
        grad_list, moment_list, low_list = [], [], []
        for layer in range(LAYERS):
            for item in range(3):
                grad = mat_list[layer][item]
                moment = momentum_decay * mat_momentum[layer, item] + grad
                grad_list.append(grad)
                moment_list.append(moment)
                low_list.append((grad + momentum_decay * moment).astype(bf16))
        wide = [item for item in range(3 * LAYERS) if item % 3]
        squares = [item for item in range(3, 3 * LAYERS, 3)]
        table = []
        for number in range(4):
            table += [wide[number], squares[number % len(squares)]]
        table = (table * (-(-dp_size // 8)))[:dp_size]
        slots = jnp.stack([low_list[item] for item in table])
        received = lax.all_to_all(slots[:, None], DP, split_axis=0, concat_axis=1, tiled=True)
        current = received.reshape(dp_size * dp_rows, cols_dev)
        gram_local = dot_trans(current, current)
        gram = jnp.where(c_index == 0, ctx_gram(gram_local), gram_local)
        ortho_mine = orthogonalize(current, gram)
        returned = lax.all_to_all(
            ortho_mine.reshape(dp_size, 1, dp_rows, cols_dev),
            DP,
            split_axis=0,
            concat_axis=1,
            tiled=True,
        )[0]
        first_full = lax.all_gather(low_list[0], DP, axis=0, tiled=True)
        first_ortho = orthogonalize(first_full, dot_trans(first_full, first_full))
        ortho_list = [lax.dynamic_slice_in_dim(first_ortho, dp_index * dp_rows, dp_rows, axis=0)]
        ortho_list += [returned[table.index(item)] for item in range(1, 3 * LAYERS)]
        ortho = jnp.stack(ortho_list).reshape(LAYERS, 3, dp_rows, cols_dev).astype(f32)
        grad_mats = jnp.stack(grad_list).reshape(weights.shape)
        moment_new = jnp.stack(moment_list).reshape(weights.shape)
    grad_vecs = lax.dynamic_slice_in_dim(
        vec_sums, dp_index * vectors.shape[2], vectors.shape[2], axis=2
    )
    factor = jnp.array([0.2 * math.sqrt(D), 0.2 * math.sqrt(FF), 0.2 * math.sqrt(FF)], f32)
    weights_new = weights * (1.0 - matrix_rate * matrix_decay) - matrix_rate * (
        ortho * factor[None, :, None, None]
    )
    first_new = first_decay * vec_first + (1.0 - first_decay) * grad_vecs
    second_new = second_decay * vec_second + (1.0 - second_decay) * grad_vecs * grad_vecs
    first_hat = first_new / (1.0 - first_decay**ADAM_STEP)
    second_hat = second_new / (1.0 - second_decay**ADAM_STEP)
    vectors_new = vectors * (1.0 - vector_rate * vector_decay) - vector_rate * first_hat / (
        jnp.sqrt(second_hat) + adam_epsilon
    )
    return (
        hidden_out[None],
        input_grad[None],
        grad_mats,
        moment_new,
        weights_new,
        grad_vecs,
        second_new,
        vectors_new,
    )


def solution(mesh):
    dp, ctx = mesh.shape["dp"], mesh.shape["ctx"]
    fine = Mesh(mesh.devices.reshape(dp // TP, 2, 2, ctx), EVERY)
    tokens = P(DP, "ctx", None)
    mats = P(None, None, DP, "ctx")
    vecs = P(None, "ctx", DP)
    return jax.shard_map(
        local,
        mesh=fine,
        in_specs=(tokens, P(DP, None), tokens, mats, vecs, mats, vecs, vecs),
        out_specs=(tokens, tokens, mats, mats, mats, vecs, vecs, vecs),
        check_vma=False,
    )
```
